32 devices in a mesh: groups: 2 (over y), mp: 8 (over z, x), batch: 2 (over core).
Axes of the slice: x: 2, y: 2, z: 4, core: 2. Of those that a mesh axis runs over, the one named last changes fastest.
Arguments:
- hidden: bfloat16 [64, 8192], P(('groups', 'mp', 'batch')), parts along dimension 0, may hold values from -6 to 6
- attention_norm_gain: bfloat16 [8192], replicated, may hold values from 0.25 to 1.75
- query_key_value_weight: bfloat16 [8192, 10240], P(None, ('mp', 'batch')), may hold values from -0.0625 to 0.0625
- output_weight: bfloat16 [8192, 8192], P(None, 'mp'), may hold values from -0.0625 to 0.0625
- key_cache: bfloat16 [64, 256, 1024], P(('groups', 'mp', 'batch')), parts along dimension 0, may hold values from -180 to 180
- value_cache: bfloat16 [64, 256, 1024], P(('groups', 'mp', 'batch')), parts along dimension 0, may hold values from -6 to 6
- lengths: int32 [64], P(('groups', 'mp', 'batch')), parts along dimension 0, may hold values from 1 to 256
- slots: int32 [64], P(('groups', 'mp', 'batch')), parts along dimension 0, may hold values from 0 to 1
- requests: int32 [32, 2], P(('groups', 'mp', 'batch')), parts along dimension 0, may hold values from 0 to 63, as said below
- adapter_down_matrices: bfloat16 [64, 8192, 64], P(None, 'mp'), may hold values from -0.0625 to 0.0625
- adapter_up_matrices: bfloat16 [64, 64, 8192], P(None, None, 'mp'), may hold values from -0.75 to 0.75
Outputs:
- result: bfloat16 [64, 8192], P(('groups', 'mp', 'batch')), parts along dimension 0
The draws below stay inside these ranges and needn't reach their ends.
There are 2 independent parts, one for each index of `groups`. The reference program is written for one: setup_inputs(seed, part) draws one part's arguments, and reference() takes and returns one part's arrays. A program takes and returns all parts, laid end to end along the dimension named above; an argument that names none is the same for every part. Nothing has to cross between parts.
Inputs may be any that keep to these rules, and one draw needn't show every extreme that they name: `requests`: the 2 entries of one device's list are distinct adapters.
All inputs are finite; a program needn't handle non-finite values.
Results may differ from the reference program's by a relative error of at most 0.012.
The reference program's roundings to bfloat16 on the way count: a program that leaves them out, or rounds other values in their place, can miss the bound.
Values may be sent and summed in bfloat16 or wider, within the bound.
No kernel may reach another device: no remote copies, remote signals or barrier semaphores. Data moves between devices by JAX's collectives and lax.ppermute only.
A program may use at most 128 MiB of HBM per device.

```python
import jax
import jax.numpy as jnp
from jax import lax

MODEL_WIDTH = 8192
HEADS = 64
KV_HEADS = 8
HEAD_DIM = 128
ADAPTER_COUNT = 64
ADAPTER_RANK = 64
ROW_DEV = 2
CTX = 256
QUERY_FEATURES = 8192
KVD = 1024
QKVC = 10240
REQ = 2
DEVS = 16
ROWS = 32


def draw_key_cache(key, part):
    key = jax.random.fold_in(key, 7)
    base_output = jnp.clip(jax.random.normal(key, (ROWS, CTX, KV_HEADS * HEAD_DIM), jnp.float32), -6.0, 6.0)
    return base_output.astype(jnp.bfloat16)


def draw_lengths(key, part):
    key = jax.random.fold_in(key, 5)
    base_output = jax.random.randint(key, (ROWS,), 0, CTX)
    skewed = base_output * base_output // CTX + 1
    spot = jax.random.randint(jax.random.fold_in(key, 1), (), 0, ROWS)
    return skewed.at[spot].set(CTX).astype(jnp.int32)


def draw_slots(key, part):
    key = jax.random.fold_in(key, 3)
    base_output = jax.random.randint(key, (ROWS,), 0, REQ)
    return base_output.at[0].set(REQ - 1).astype(jnp.int32)


def draw_requests(key, part):
    key = jax.random.fold_in(key, 9)
    noise = jax.random.randint(key, (DEVS, ADAPTER_COUNT), 0, 4096) * ADAPTER_COUNT + jnp.arange(ADAPTER_COUNT)[None, :]
    noise = noise.at[0, ADAPTER_COUNT - 1].add(1 << 24).at[0, 0].add(1 << 24)
    scores, chosen = lax.top_k(noise, REQ)
    return chosen.astype(jnp.int32)


def levels(rng, shape, shards, smallest, largest):
    loudness = 1.0
    for position, blocks in shards:
        draws = jax.random.uniform(jax.random.fold_in(jax.random.fold_in(rng, 6), position), (blocks,), jnp.float32, smallest / len(shards), largest / len(shards))
        loudness = loudness * jnp.repeat(jnp.exp(draws), shape[position] // blocks).reshape((-1,) + (1,) * (len(shape) - 1 - position))
    return loudness


def gaussian(own_key, shape, deviation, bound, split=(), held_as=jnp.bfloat16):
    factor_of = levels(own_key, shape, split, -0.22, 0.18) if split else 1.0
    drawn = jax.random.normal(own_key, shape, jnp.float32) * deviation * factor_of
    return jnp.minimum(jnp.maximum(drawn, -bound), bound).astype(held_as)


def setup_inputs(seed: int = 0, part: int = 0) -> dict:
    splits = jax.random.split(jax.random.key(seed), 12)
    own_keys = jax.random.split(jax.random.fold_in(splits[11], part), 12)
    hidden = gaussian(own_keys[0], (ROWS, MODEL_WIDTH), 1.0, 6.0, ((0, 16),))
    attention_norm_gain = jnp.clip(1.0 + 0.15 * jax.random.normal(splits[1], (MODEL_WIDTH,), jnp.float32), 0.25, 1.75).astype(jnp.bfloat16)
    query_key_value_weight = gaussian(splits[2], (MODEL_WIDTH, QKVC), MODEL_WIDTH ** -0.5, 0.0625, ((1, 16),))
    output_weight = gaussian(splits[3], (QUERY_FEATURES, MODEL_WIDTH), QUERY_FEATURES ** -0.5, 0.0625, ((1, 8),))
    key_cache = draw_key_cache(jax.random.fold_in(jax.random.fold_in(splits[11], part), 71), part)
    value_cache = gaussian(own_keys[5], (ROWS, CTX, KVD), 1.0, 6.0, ((0, 16),))
    lengths = draw_lengths(jax.random.fold_in(jax.random.fold_in(splits[11], part), 71), part)
    slots = draw_slots(jax.random.fold_in(jax.random.fold_in(splits[11], part), 71), part)
    requests = draw_requests(jax.random.fold_in(jax.random.fold_in(splits[11], part), 71), part)
    adapter_down_matrices = gaussian(splits[9], (ADAPTER_COUNT, QUERY_FEATURES, ADAPTER_RANK), QUERY_FEATURES ** -0.5, 0.0625, ((1, 8),))
    adapter_up_matrices = gaussian(splits[10], (ADAPTER_COUNT, ADAPTER_RANK, MODEL_WIDTH), ADAPTER_RANK ** -0.5, 0.75, ((2, 8),))
    return {"hidden": hidden, "attention_norm_gain": attention_norm_gain, "query_key_value_weight": query_key_value_weight, "output_weight": output_weight, "key_cache": key_cache, "value_cache": value_cache, "lengths": lengths, "slots": slots, "requests": requests, "adapter_down_matrices": adapter_down_matrices, "adapter_up_matrices": adapter_up_matrices}


EPS = 1e-05
THETA = 500000.0
ADAPTER_SCALE = 2.0

def rotate(vec, pos):
    width = vec.shape[-1]
    half = width // 2
    freq = THETA ** (-(jnp.arange(half, dtype=jnp.float32) * 2.0) / width)
    angle = pos[..., None, None] * freq
    cosine = jnp.concatenate([jnp.cos(angle), jnp.cos(angle)], -1)
    sine = jnp.concatenate([jnp.sin(angle), jnp.sin(angle)], -1)
    turned = jnp.concatenate([-vec[..., half:], vec[..., :half]], -1)
    return vec * cosine + turned * sine

def attend_row(qkv_row, keys, values, length):
    query_width = HEADS * HEAD_DIM
    kv_width = KV_HEADS * HEAD_DIM
    group = HEADS // KV_HEADS
    scale = HEAD_DIM ** (-0.5)
    pos = length.astype(jnp.float32)
    query = rotate(qkv_row[:query_width].astype(jnp.float32).reshape(HEADS, HEAD_DIM), pos).astype(jnp.bfloat16)
    fresh_key = rotate(qkv_row[query_width:query_width + kv_width].astype(jnp.float32).reshape(KV_HEADS, HEAD_DIM), pos).astype(jnp.bfloat16)
    fresh_value = qkv_row[query_width + kv_width:].astype(jnp.float32).reshape(KV_HEADS, HEAD_DIM)
    grouped = query.astype(jnp.float32).reshape(KV_HEADS, group, HEAD_DIM)
    cached = keys.astype(jnp.float32).reshape(CTX, KV_HEADS, HEAD_DIM)
    scores = jnp.einsum('gqd,tgd->gqt', grouped, cached) * scale
    live = jnp.arange(CTX) < length
    scores = jnp.where(live[None, None, :], scores, -jnp.inf)
    own = jnp.einsum('gqd,gd->gq', grouped, fresh_key.astype(jnp.float32)) * scale
    top = jnp.maximum(lax.optimization_barrier(jnp.max(scores, -1)), own)
    expo = jnp.exp(scores - top[..., None])
    own_exp = jnp.exp(own - top)
    total = lax.optimization_barrier(jnp.sum(expo, -1)) + own_exp
    probs = (expo / total[..., None]).astype(jnp.bfloat16)
    own_prob = (own_exp / total).astype(jnp.bfloat16)
    stored = values.astype(jnp.float32).reshape(CTX, KV_HEADS, HEAD_DIM)
    context_vector = jnp.einsum('gqt,tgd->gqd', probs.astype(jnp.float32), stored)
    context_vector = context_vector + own_prob.astype(jnp.float32)[..., None] * fresh_value[:, None, :]
    return context_vector.reshape(query_width).astype(jnp.bfloat16)

def reference(hidden, attention_norm_gain, query_key_value_weight, output_weight, key_cache, value_cache, lengths, slots, requests, adapter_down_matrices, adapter_up_matrices):
    widened = hidden.astype(jnp.float32)
    normed = (widened * lax.rsqrt(lax.optimization_barrier(jnp.mean(widened * widened, -1, keepdims=True)) + EPS) * attention_norm_gain.astype(jnp.float32)).astype(jnp.bfloat16)
    qkv = jnp.dot(normed, query_key_value_weight, preferred_element_type=jnp.float32).astype(jnp.bfloat16)
    context_vector = lax.map(lambda packed_weights: attend_row(packed_weights[0], packed_weights[1], packed_weights[2], packed_weights[3]), (qkv, key_cache, value_cache, lengths))
    adapter = jnp.take_along_axis(requests, slots.reshape(-1, ROW_DEV).astype(jnp.int32), 1).reshape(-1).astype(jnp.int32)

    def down_row(packed_weights):
        attention_block = lax.dynamic_index_in_dim(adapter_down_matrices, packed_weights[1], 0, keepdims=False).astype(jnp.float32)
        return jnp.dot(packed_weights[0].astype(jnp.float32), attention_block, precision=lax.Precision.HIGHEST).astype(jnp.bfloat16)
    down_result = lax.map(down_row, (context_vector, adapter))

    def up_row(packed_weights):
        attention_block = lax.dynamic_index_in_dim(adapter_up_matrices, packed_weights[1], 0, keepdims=False).astype(jnp.float32)
        return jnp.dot(packed_weights[0].astype(jnp.float32), attention_block, precision=lax.Precision.HIGHEST)
    adapter_delta = lax.map(up_row, (down_result, adapter))
    base_output = jnp.dot(context_vector, output_weight, preferred_element_type=jnp.float32)
    projection_result = (base_output + ADAPTER_SCALE * adapter_delta).astype(jnp.bfloat16)
    return (widened + projection_result.astype(jnp.float32)).astype(jnp.bfloat16)
```

```python
import jax
import jax.numpy as jnp
from jax import lax
from jax.sharding import PartitionSpec as P

HEADS = 64
KV_HEADS = 8
HEAD_DIM = 128
ADAPTER_COUNT = 64


EPS = 1e-05
THETA = 500000.0
ADAPTER_SCALE = 2.0


def rotate(vec, pos):
    width = vec.shape[-1]
    half = width // 2
    freq = THETA ** (-(jnp.arange(half, dtype=jnp.float32) * 2.0) / width)
    angle = pos[..., None, None] * freq
    cosine = jnp.concatenate([jnp.cos(angle), jnp.cos(angle)], -1)
    sine = jnp.concatenate([jnp.sin(angle), jnp.sin(angle)], -1)
    turned = jnp.concatenate([-vec[..., half:], vec[..., :half]], -1)
    return vec * cosine + turned * sine


def apply_up_matrix(
    context_vector, adapter_selector, down_result, output_weight, adapter_up_matrices
):
    base_output = jnp.dot(context_vector, output_weight, preferred_element_type=jnp.float32)
    spread = (adapter_selector[:, :, None] * down_result[:, None, :]).reshape(
        adapter_selector.shape[0], -1
    )
    adapter_table = adapter_up_matrices.reshape(-1, adapter_up_matrices.shape[2])
    adapter_delta = jnp.dot(spread, adapter_table, preferred_element_type=jnp.float32)
    return (base_output + ADAPTER_SCALE * adapter_delta).astype(jnp.bfloat16)


def general_body(
    hidden,
    attention_norm_gain,
    query_key_value_weight,
    output_weight,
    key_cache,
    value_cache,
    lengths,
    slots,
    requests,
    adapter_down_matrices,
    adapter_up_matrices,
):
    widened = hidden.astype(jnp.float32)
    normed = (
        widened
        * lax.rsqrt(jnp.mean(widened * widened, -1, keepdims=True) + EPS)
        * attention_norm_gain.astype(jnp.float32)
    ).astype(jnp.bfloat16)
    rows = normed.shape[0]
    columns = jnp.dot(
        lax.all_gather(normed, ("mp", "batch"), axis=0, tiled=True),
        query_key_value_weight,
        preferred_element_type=jnp.float32,
    ).astype(jnp.bfloat16)
    mixed = lax.all_to_all(
        lax.all_to_all(columns, "mp", split_axis=0, concat_axis=1, tiled=True),
        "batch",
        split_axis=0,
        concat_axis=1,
        tiled=True,
    )
    width = query_key_value_weight.shape[1]
    qkv = (
        mixed.reshape(rows, lax.axis_size("batch"), lax.axis_size("mp"), width)
        .transpose(0, 2, 1, 3)
        .reshape(rows, -1)
    )
    query_width = HEADS * HEAD_DIM
    kv_width = KV_HEADS * HEAD_DIM
    group = HEADS // KV_HEADS
    scale = HEAD_DIM ** (-0.5)
    pos = lengths.astype(jnp.float32)
    query = rotate(
        qkv[:, :query_width].astype(jnp.float32).reshape(rows, HEADS, HEAD_DIM), pos
    ).astype(jnp.bfloat16)
    fresh_key = rotate(
        qkv[:, query_width : query_width + kv_width]
        .astype(jnp.float32)
        .reshape(rows, KV_HEADS, HEAD_DIM),
        pos,
    ).astype(jnp.bfloat16)
    fresh_value = (
        qkv[:, query_width + kv_width :].astype(jnp.float32).reshape(rows, KV_HEADS, HEAD_DIM)
    )
    grouped = query.reshape(rows, KV_HEADS, group, HEAD_DIM)
    cached = key_cache.reshape(rows, -1, KV_HEADS, HEAD_DIM)
    stored = value_cache.reshape(rows, -1, KV_HEADS, HEAD_DIM)
    scores = (
        jnp.einsum("rgqd,rtgd->rgqt", grouped, cached, preferred_element_type=jnp.float32) * scale
    )
    live = jnp.arange(cached.shape[1])[None, :] < lengths[:, None]
    scores = jnp.where(live[:, None, None, :], scores, -jnp.inf)
    own = (
        jnp.einsum("rgqd,rgd->rgq", grouped, fresh_key, preferred_element_type=jnp.float32) * scale
    )
    top = jnp.maximum(jnp.max(scores, -1), own)
    expo = jnp.exp(scores - top[..., None])
    own_exp = jnp.exp(own - top)
    total = jnp.sum(expo, -1) + own_exp
    probs = (expo / total[..., None]).astype(jnp.bfloat16)
    own_prob = (own_exp / total).astype(jnp.bfloat16)
    context_vector = jnp.einsum(
        "rgqt,rtgd->rgqd", probs, stored, preferred_element_type=jnp.float32
    )
    context_vector = (
        context_vector + own_prob.astype(jnp.float32)[..., None] * fresh_value[:, :, None, :]
    )
    context_vector = context_vector.reshape(rows, query_width).astype(jnp.bfloat16)
    slot_hits = slots[:, None] == jnp.arange(requests.shape[1])[None, :]
    adapter = jnp.sum(jnp.where(slot_hits, requests[0][None, :], 0), 1)
    adapter_selector = (adapter[:, None] == jnp.arange(ADAPTER_COUNT)[None, :]).astype(jnp.bfloat16)
    context_gathered, selector_gathered = (
        lax.all_gather(context_vector, "mp", axis=0, tiled=True),
        lax.all_gather(adapter_selector, "mp", axis=0, tiled=True),
    )
    shared_portion = adapter_down_matrices.shape[1]
    context_slice = lax.dynamic_slice_in_dim(
        context_gathered, lax.axis_index("mp") * shared_portion, shared_portion, 1
    )
    every_adapter = jnp.einsum(
        "gh,thy->gty", context_slice, adapter_down_matrices, preferred_element_type=jnp.float32
    )
    partial_down = jnp.sum(every_adapter * selector_gathered.astype(jnp.float32)[:, :, None], 1)
    down_gathered = lax.psum(partial_down, "mp").astype(jnp.bfloat16)
    projection_result = apply_up_matrix(
        context_gathered, selector_gathered, down_gathered, output_weight, adapter_up_matrices
    )
    returned = lax.all_to_all(projection_result, "mp", split_axis=0, concat_axis=1, tiled=True)
    return (widened + returned.astype(jnp.float32)).astype(jnp.bfloat16)


def fetch(block, axis, shift):
    size = lax.axis_size(axis)
    return lax.ppermute(block, axis, [((d + shift) % size, d) for d in range(size)])


def gather_ahead(block, axis):
    return [block] + [fetch(block, axis, k) for k in range(1, lax.axis_size(axis))]


def swap_ahead(blocks, axis):
    size = lax.axis_size(axis)
    return [blocks[0]] + [fetch(blocks[k], axis, size - k) for k in range(1, size)]


def absolute(blocks, axis, ahead):
    size = lax.axis_size(axis)
    if not ahead:
        blocks = [blocks[-k % size] for k in range(size)]
    twice = jnp.stack(blocks + blocks)
    return lax.dynamic_slice_in_dim(twice, size - lax.axis_index(axis), size, 0)


def fast_body(
    hidden,
    attention_norm_gain,
    query_key_value_weight,
    output_weight,
    key_cache,
    value_cache,
    lengths,
    slots,
    requests,
    adapter_down_matrices,
    adapter_up_matrices,
):
    widened = hidden.astype(jnp.float32)
    normed = (
        widened
        * lax.rsqrt(jnp.mean(widened * widened, -1, keepdims=True) + EPS)
        * attention_norm_gain.astype(jnp.float32)
    ).astype(jnp.bfloat16)
    rows = normed.shape[0]
    mp_size, batch_size = lax.axis_size("mp"), lax.axis_size("batch")
    slot_hits = slots[:, None] == jnp.arange(requests.shape[1])[None, :]
    adapter = jnp.sum(jnp.where(slot_hits, requests[0][None, :], 0), 1)
    adapter_gathered = jnp.concatenate(gather_ahead(adapter, "mp"))
    selector_gathered = (adapter_gathered[:, None] == jnp.arange(ADAPTER_COUNT)[None, :]).astype(
        jnp.bfloat16
    )
    own_core = jnp.concatenate(gather_ahead(normed, "mp"))
    normed_gathered = jnp.concatenate(gather_ahead(own_core, "batch"))
    width = query_key_value_weight.shape[1]
    columns = jnp.dot(
        normed_gathered, query_key_value_weight, preferred_element_type=jnp.float32
    ).astype(jnp.bfloat16)
    columns = columns.reshape(batch_size, mp_size, rows, width)
    cores = absolute(swap_ahead([columns[e] for e in range(batch_size)], "batch"), "batch", False)
    mixed = absolute(swap_ahead([cores[:, k] for k in range(mp_size)], "mp"), "mp", False)
    qkv = mixed.transpose(2, 0, 1, 3).reshape(rows, -1)
    query_width = HEADS * HEAD_DIM
    kv_width = KV_HEADS * HEAD_DIM
    group = HEADS // KV_HEADS
    scale = HEAD_DIM ** (-0.5)
    pos = lengths.astype(jnp.float32)
    query = rotate(
        qkv[:, :query_width].astype(jnp.float32).reshape(rows, HEADS, HEAD_DIM), pos
    ).astype(jnp.bfloat16)
    fresh_key = rotate(
        qkv[:, query_width : query_width + kv_width]
        .astype(jnp.float32)
        .reshape(rows, KV_HEADS, HEAD_DIM),
        pos,
    ).astype(jnp.bfloat16)
    fresh_value = (
        qkv[:, query_width + kv_width :].astype(jnp.float32).reshape(rows, KV_HEADS, HEAD_DIM)
    )
    grouped = query.reshape(rows, KV_HEADS, group, HEAD_DIM)
    cached = key_cache.reshape(rows, -1, KV_HEADS, HEAD_DIM)
    stored = value_cache.reshape(rows, -1, KV_HEADS, HEAD_DIM)
    scores = (
        jnp.einsum("rgqd,rtgd->rgqt", grouped, cached, preferred_element_type=jnp.float32) * scale
    )
    live = jnp.arange(cached.shape[1])[None, :] < lengths[:, None]
    scores = jnp.where(live[:, None, None, :], scores, -jnp.inf)
    own = (
        jnp.einsum("rgqd,rgd->rgq", grouped, fresh_key, preferred_element_type=jnp.float32) * scale
    )
    top = jnp.maximum(jnp.max(scores, -1), own)
    expo = jnp.exp(scores - top[..., None])
    own_exp = jnp.exp(own - top)
    total = jnp.sum(expo, -1) + own_exp
    probs = (expo / total[..., None]).astype(jnp.bfloat16)
    own_prob = (own_exp / total).astype(jnp.bfloat16)
    context_vector = jnp.einsum(
        "rgqt,rtgd->rgqd", probs, stored, preferred_element_type=jnp.float32
    )
    context_vector = (
        context_vector + own_prob.astype(jnp.float32)[..., None] * fresh_value[:, :, None, :]
    )
    context_vector = context_vector.reshape(rows, query_width).astype(jnp.bfloat16)
    context_gathered = jnp.concatenate(gather_ahead(context_vector, "mp"))
    shared_portion = adapter_down_matrices.shape[1]
    context_slice = lax.dynamic_slice_in_dim(
        context_gathered, lax.axis_index("mp") * shared_portion, shared_portion, 1
    )
    every_adapter = jnp.einsum(
        "gh,thy->gty", context_slice, adapter_down_matrices, preferred_element_type=jnp.float32
    )
    partial_down = jnp.sum(every_adapter * selector_gathered.astype(jnp.float32)[:, :, None], 1)
    mine = absolute(list(partial_down.reshape(mp_size, rows, -1)), "mp", True)
    total = sum(gather_ahead(mine, "mp"))
    twice = jnp.concatenate([total, total])
    down_gathered = (
        lax.dynamic_slice_in_dim(twice, lax.axis_index("mp"), mp_size, 0)
        .reshape(mp_size * rows, -1)
        .astype(jnp.bfloat16)
    )
    projection_result = apply_up_matrix(
        context_gathered, selector_gathered, down_gathered, output_weight, adapter_up_matrices
    )
    parts = swap_ahead(list(projection_result.reshape(mp_size, rows, -1)), "mp")
    returned = absolute(parts, "mp", False).transpose(1, 0, 2).reshape(rows, -1)
    return (widened + returned.astype(jnp.float32)).astype(jnp.bfloat16)


MOST_PEERS = 16


def body(*arguments):
    few = lax.axis_size("mp") <= MOST_PEERS
    whole_heads = arguments[2].shape[1] % HEAD_DIM == 0
    return (fast_body if few and whole_heads else general_body)(*arguments)


def solution(mesh):
    in_specs = (
        P(("groups", "mp", "batch"), None),
        P(),
        P(None, ("mp", "batch")),
        P(None, "mp"),
        P(("groups", "mp", "batch"), None, None),
        P(("groups", "mp", "batch"), None, None),
        P(("groups", "mp", "batch")),
        P(("groups", "mp", "batch")),
        P(("groups", "mp", "batch"), None),
        P(None, "mp", None),
        P(None, None, "mp"),
    )
    out_specs = P(("groups", "mp", "batch"), None)
    return jax.shard_map(body, mesh=mesh, in_specs=in_specs, out_specs=out_specs, check_vma=False)
```

```python
import jax
import jax.numpy as jnp
from jax import lax
from jax.sharding import PartitionSpec as P

HEADS = 64
KV_HEADS = 8
HEAD_DIM = 128
ADAPTER_COUNT = 64


EPS = 1e-05
THETA = 500000.0
ADAPTER_SCALE = 2.0


def rotate(vec, pos):
    width = vec.shape[-1]
    half = width // 2
    freq = THETA ** (-(jnp.arange(half, dtype=jnp.float32) * 2.0) / width)
    angle = pos[..., None, None] * freq
    cosine = jnp.concatenate([jnp.cos(angle), jnp.cos(angle)], -1)
    sine = jnp.concatenate([jnp.sin(angle), jnp.sin(angle)], -1)
    turned = jnp.concatenate([-vec[..., half:], vec[..., :half]], -1)
    return vec * cosine + turned * sine


def apply_up_matrix(
    context_vector, adapter_selector, down_result, output_weight, adapter_up_matrices
):
    base_output = jnp.dot(context_vector, output_weight, preferred_element_type=jnp.float32)
    spread = (adapter_selector[:, :, None] * down_result[:, None, :]).reshape(
        adapter_selector.shape[0], -1
    )
    adapter_table = adapter_up_matrices.reshape(-1, adapter_up_matrices.shape[2])
    adapter_delta = jnp.dot(spread, adapter_table, preferred_element_type=jnp.float32)
    return (base_output + ADAPTER_SCALE * adapter_delta).astype(jnp.bfloat16)


def general_body(
    hidden,
    attention_norm_gain,
    query_key_value_weight,
    output_weight,
    key_cache,
    value_cache,
    lengths,
    slots,
    requests,
    adapter_down_matrices,
    adapter_up_matrices,
):
    widened = hidden.astype(jnp.float32)
    normed = (
        widened
        * lax.rsqrt(jnp.mean(widened * widened, -1, keepdims=True) + EPS)
        * attention_norm_gain.astype(jnp.float32)
    ).astype(jnp.bfloat16)
    rows = normed.shape[0]
    columns = jnp.dot(
        lax.all_gather(normed, ("mp", "batch"), axis=0, tiled=True),
        query_key_value_weight,
        preferred_element_type=jnp.float32,
    ).astype(jnp.bfloat16)
    mixed = lax.all_to_all(
        lax.all_to_all(columns, "mp", split_axis=0, concat_axis=1, tiled=True),
        "batch",
        split_axis=0,
        concat_axis=1,
        tiled=True,
    )
    width = query_key_value_weight.shape[1]
    qkv = (
        mixed.reshape(rows, lax.axis_size("batch"), lax.axis_size("mp"), width)
        .transpose(0, 2, 1, 3)
        .reshape(rows, -1)
    )
    query_width = HEADS * HEAD_DIM
    kv_width = KV_HEADS * HEAD_DIM
    group = HEADS // KV_HEADS
    scale = HEAD_DIM ** (-0.5)
    pos = lengths.astype(jnp.float32)
    query = rotate(
        qkv[:, :query_width].astype(jnp.float32).reshape(rows, HEADS, HEAD_DIM), pos
    ).astype(jnp.bfloat16)
    fresh_key = rotate(
        qkv[:, query_width : query_width + kv_width]
        .astype(jnp.float32)
        .reshape(rows, KV_HEADS, HEAD_DIM),
        pos,
    ).astype(jnp.bfloat16)
    fresh_value = (
        qkv[:, query_width + kv_width :].astype(jnp.float32).reshape(rows, KV_HEADS, HEAD_DIM)
    )
    grouped = query.reshape(rows, KV_HEADS, group, HEAD_DIM)
    cached = key_cache.reshape(rows, -1, KV_HEADS, HEAD_DIM)
    stored = value_cache.reshape(rows, -1, KV_HEADS, HEAD_DIM)
    scores = (
        jnp.einsum("rgqd,rtgd->rgqt", grouped, cached, preferred_element_type=jnp.float32) * scale
    )
    live = jnp.arange(cached.shape[1])[None, :] < lengths[:, None]
    scores = jnp.where(live[:, None, None, :], scores, -jnp.inf)
    own = (
        jnp.einsum("rgqd,rgd->rgq", grouped, fresh_key, preferred_element_type=jnp.float32) * scale
    )
    top = jnp.maximum(jnp.max(scores, -1), own)
    expo = jnp.exp(scores - top[..., None])
    own_exp = jnp.exp(own - top)
    total = jnp.sum(expo, -1) + own_exp
    probs = (expo / total[..., None]).astype(jnp.bfloat16)
    own_prob = (own_exp / total).astype(jnp.bfloat16)
    context_vector = jnp.einsum(
        "rgqt,rtgd->rgqd", probs, stored, preferred_element_type=jnp.float32
    )
    context_vector = (
        context_vector + own_prob.astype(jnp.float32)[..., None] * fresh_value[:, :, None, :]
    )
    context_vector = context_vector.reshape(rows, query_width).astype(jnp.bfloat16)
    slot_hits = slots[:, None] == jnp.arange(requests.shape[1])[None, :]
    adapter = jnp.sum(jnp.where(slot_hits, requests[0][None, :], 0), 1)
    adapter_selector = (adapter[:, None] == jnp.arange(ADAPTER_COUNT)[None, :]).astype(jnp.bfloat16)
    context_gathered, selector_gathered = (
        lax.all_gather(context_vector, "mp", axis=0, tiled=True),
        lax.all_gather(adapter_selector, "mp", axis=0, tiled=True),
    )
    shared_portion = adapter_down_matrices.shape[1]
    context_slice = lax.dynamic_slice_in_dim(
        context_gathered, lax.axis_index("mp") * shared_portion, shared_portion, 1
    )
    every_adapter = jnp.einsum(
        "gh,thy->gty", context_slice, adapter_down_matrices, preferred_element_type=jnp.float32
    )
    partial_down = jnp.sum(every_adapter * selector_gathered.astype(jnp.float32)[:, :, None], 1)
    down_gathered = lax.psum(partial_down, "mp").astype(jnp.bfloat16)
    projection_result = apply_up_matrix(
        context_gathered, selector_gathered, down_gathered, output_weight, adapter_up_matrices
    )
    returned = lax.all_to_all(projection_result, "mp", split_axis=0, concat_axis=1, tiled=True)
    return (widened + returned.astype(jnp.float32)).astype(jnp.bfloat16)


def trade(block, axis, bit):
    return lax.ppermute(block, axis, [(d ^ bit, d) for d in range(lax.axis_size(axis))])


def bits_of(axis):
    size = lax.axis_size(axis)
    return [1 << b for b in reversed(range(size.bit_length() - 1))]


def gather_near(block, axis):
    held = block[None]
    for bit in reversed(bits_of(axis)):
        held = jnp.concatenate([held, trade(held, axis, bit)])
    return held


def gather_far(block, axis):
    held = block[None]
    for bit in bits_of(axis):
        held = jnp.stack([held, trade(held, axis, bit)], 1)
        held = held.reshape(-1, *block.shape)
    return held


def exchange(blocks, axis):
    size, shape = lax.axis_size(axis), blocks.shape[1:]
    for bit in bits_of(axis):
        split = blocks.reshape(size // (2 * bit), 2, bit, *shape)
        got = trade(split[:, 1], axis, bit)
        blocks = jnp.stack([split[:, 0], got], 1).reshape(size, *shape)
    return blocks


def absolute(blocks, axis):
    size, shape = lax.axis_size(axis), blocks.shape[1:]
    index = lax.axis_index(axis)
    for bit in bits_of(axis):
        split = blocks.reshape(size // (2 * bit), 2, bit, *shape)
        blocks = jnp.where((index & bit) > 0, split[:, ::-1], split).reshape(size, *shape)
    return blocks


def sum_all(block, axis):
    for bit in bits_of(axis):
        block = block + trade(block, axis, bit)
    return block


def fast_body(
    hidden,
    attention_norm_gain,
    query_key_value_weight,
    output_weight,
    key_cache,
    value_cache,
    lengths,
    slots,
    requests,
    adapter_down_matrices,
    adapter_up_matrices,
):
    widened = hidden.astype(jnp.float32)
    normed = (
        widened
        * lax.rsqrt(jnp.mean(widened * widened, -1, keepdims=True) + EPS)
        * attention_norm_gain.astype(jnp.float32)
    ).astype(jnp.bfloat16)
    rows = normed.shape[0]
    mp_size, batch_size = lax.axis_size("mp"), lax.axis_size("batch")
    slot_hits = slots[:, None] == jnp.arange(requests.shape[1])[None, :]
    adapter = jnp.sum(jnp.where(slot_hits, requests[0][None, :], 0), 1)
    adapter_gathered = gather_far(adapter, "mp").reshape(-1)
    selector_gathered = (adapter_gathered[:, None] == jnp.arange(ADAPTER_COUNT)[None, :]).astype(
        jnp.bfloat16
    )
    own_core = gather_far(normed, "mp")
    normed_gathered = gather_near(own_core, "batch").reshape(-1, normed.shape[1])
    width = query_key_value_weight.shape[1]
    columns = jnp.dot(
        normed_gathered, query_key_value_weight, preferred_element_type=jnp.float32
    ).astype(jnp.bfloat16)
    columns = columns.reshape(batch_size, mp_size, rows, width)
    cores = absolute(exchange(columns, "batch"), "batch")
    mixed = absolute(exchange(cores.transpose(1, 0, 2, 3), "mp"), "mp")
    qkv = mixed.transpose(2, 0, 1, 3).reshape(rows, -1)
    query_width = HEADS * HEAD_DIM
    kv_width = KV_HEADS * HEAD_DIM
    group = HEADS // KV_HEADS
    scale = HEAD_DIM ** (-0.5)
    pos = lengths.astype(jnp.float32)
    query = rotate(
        qkv[:, :query_width].astype(jnp.float32).reshape(rows, HEADS, HEAD_DIM), pos
    ).astype(jnp.bfloat16)
    fresh_key = rotate(
        qkv[:, query_width : query_width + kv_width]
        .astype(jnp.float32)
        .reshape(rows, KV_HEADS, HEAD_DIM),
        pos,
    ).astype(jnp.bfloat16)
    fresh_value = (
        qkv[:, query_width + kv_width :].astype(jnp.float32).reshape(rows, KV_HEADS, HEAD_DIM)
    )
    grouped = query.reshape(rows, KV_HEADS, group, HEAD_DIM)
    cached = key_cache.reshape(rows, -1, KV_HEADS, HEAD_DIM)
    stored = value_cache.reshape(rows, -1, KV_HEADS, HEAD_DIM)
    scores = (
        jnp.einsum("rgqd,rtgd->rgqt", grouped, cached, preferred_element_type=jnp.float32) * scale
    )
    live = jnp.arange(cached.shape[1])[None, :] < lengths[:, None]
    scores = jnp.where(live[:, None, None, :], scores, -jnp.inf)
    own = (
        jnp.einsum("rgqd,rgd->rgq", grouped, fresh_key, preferred_element_type=jnp.float32) * scale
    )
    top = jnp.maximum(jnp.max(scores, -1), own)
    expo = jnp.exp(scores - top[..., None])
    own_exp = jnp.exp(own - top)
    total = jnp.sum(expo, -1) + own_exp
    probs = (expo / total[..., None]).astype(jnp.bfloat16)
    own_prob = (own_exp / total).astype(jnp.bfloat16)
    context_vector = jnp.einsum(
        "rgqt,rtgd->rgqd", probs, stored, preferred_element_type=jnp.float32
    )
    context_vector = (
        context_vector + own_prob.astype(jnp.float32)[..., None] * fresh_value[:, :, None, :]
    )
    context_vector = context_vector.reshape(rows, query_width).astype(jnp.bfloat16)
    context_gathered = gather_far(context_vector, "mp").reshape(-1, query_width)
    shared_portion = adapter_down_matrices.shape[1]
    context_slice = lax.dynamic_slice_in_dim(
        context_gathered, lax.axis_index("mp") * shared_portion, shared_portion, 1
    )
    every_adapter = jnp.einsum(
        "gh,thy->gty", context_slice, adapter_down_matrices, preferred_element_type=jnp.float32
    )
    partial_down = jnp.sum(every_adapter * selector_gathered.astype(jnp.float32)[:, :, None], 1)
    mine = absolute(partial_down.reshape(mp_size, rows, -1), "mp")
    total = absolute(sum_all(mine, "mp"), "mp")
    down_gathered = total.reshape(mp_size * rows, -1).astype(jnp.bfloat16)
    projection_result = apply_up_matrix(
        context_gathered, selector_gathered, down_gathered, output_weight, adapter_up_matrices
    )
    parts = exchange(projection_result.reshape(mp_size, rows, -1), "mp")
    returned = absolute(parts, "mp").transpose(1, 0, 2).reshape(rows, -1)
    return (widened + returned.astype(jnp.float32)).astype(jnp.bfloat16)


def body(*arguments):
    size = lax.axis_size("mp")
    small = size <= 16 and size & (size - 1) == 0 and lax.axis_size("batch") == 2
    whole_heads = arguments[2].shape[1] % HEAD_DIM == 0
    return (fast_body if small and whole_heads else general_body)(*arguments)


def solution(mesh):
    in_specs = (
        P(("groups", "mp", "batch"), None),
        P(),
        P(None, ("mp", "batch")),
        P(None, "mp"),
        P(("groups", "mp", "batch"), None, None),
        P(("groups", "mp", "batch"), None, None),
        P(("groups", "mp", "batch")),
        P(("groups", "mp", "batch")),
        P(("groups", "mp", "batch"), None),
        P(None, "mp", None),
        P(None, None, "mp"),
    )
    out_specs = P(("groups", "mp", "batch"), None)
    return jax.shard_map(body, mesh=mesh, in_specs=in_specs, out_specs=out_specs, check_vma=False)
```

```python
import jax
import jax.numpy as jnp
from jax import lax
from jax.experimental import pallas as pl
from jax.experimental.pallas import tpu as pltpu
from jax.sharding import PartitionSpec as P

HEADS = 64
KV_HEADS = 8
HEAD_DIM = 128
ADAPTER_COUNT = 64


EPS = 1e-05
THETA = 500000.0
ADAPTER_SCALE = 2.0


def rotate(vec, pos):
    width = vec.shape[-1]
    half = width // 2
    freq = THETA ** (-(jnp.arange(half, dtype=jnp.float32) * 2.0) / width)
    angle = pos[..., None, None] * freq
    cosine = jnp.concatenate([jnp.cos(angle), jnp.cos(angle)], -1)
    sine = jnp.concatenate([jnp.sin(angle), jnp.sin(angle)], -1)
    turned = jnp.concatenate([-vec[..., half:], vec[..., :half]], -1)
    return vec * cosine + turned * sine


def apply_up_matrix(
    context_vector, adapter_selector, down_result, output_weight, adapter_up_matrices
):
    base_output = jnp.dot(context_vector, output_weight, preferred_element_type=jnp.float32)
    spread = (adapter_selector[:, :, None] * down_result[:, None, :]).reshape(
        adapter_selector.shape[0], -1
    )
    adapter_table = adapter_up_matrices.reshape(-1, adapter_up_matrices.shape[2])
    adapter_delta = jnp.dot(spread, adapter_table, preferred_element_type=jnp.float32)
    return (base_output + ADAPTER_SCALE * adapter_delta).astype(jnp.bfloat16)


def general_body(
    hidden,
    attention_norm_gain,
    query_key_value_weight,
    output_weight,
    key_cache,
    value_cache,
    lengths,
    slots,
    requests,
    adapter_down_matrices,
    adapter_up_matrices,
):
    widened = hidden.astype(jnp.float32)
    normed = (
        widened
        * lax.rsqrt(jnp.mean(widened * widened, -1, keepdims=True) + EPS)
        * attention_norm_gain.astype(jnp.float32)
    ).astype(jnp.bfloat16)
    rows = normed.shape[0]
    columns = jnp.dot(
        lax.all_gather(normed, ("mp", "batch"), axis=0, tiled=True),
        query_key_value_weight,
        preferred_element_type=jnp.float32,
    ).astype(jnp.bfloat16)
    mixed = lax.all_to_all(
        lax.all_to_all(columns, "mp", split_axis=0, concat_axis=1, tiled=True),
        "batch",
        split_axis=0,
        concat_axis=1,
        tiled=True,
    )
    width = query_key_value_weight.shape[1]
    qkv = (
        mixed.reshape(rows, lax.axis_size("batch"), lax.axis_size("mp"), width)
        .transpose(0, 2, 1, 3)
        .reshape(rows, -1)
    )
    query_width = HEADS * HEAD_DIM
    kv_width = KV_HEADS * HEAD_DIM
    group = HEADS // KV_HEADS
    scale = HEAD_DIM ** (-0.5)
    pos = lengths.astype(jnp.float32)
    query = rotate(
        qkv[:, :query_width].astype(jnp.float32).reshape(rows, HEADS, HEAD_DIM), pos
    ).astype(jnp.bfloat16)
    fresh_key = rotate(
        qkv[:, query_width : query_width + kv_width]
        .astype(jnp.float32)
        .reshape(rows, KV_HEADS, HEAD_DIM),
        pos,
    ).astype(jnp.bfloat16)
    fresh_value = (
        qkv[:, query_width + kv_width :].astype(jnp.float32).reshape(rows, KV_HEADS, HEAD_DIM)
    )
    grouped = query.reshape(rows, KV_HEADS, group, HEAD_DIM)
    cached = key_cache.reshape(rows, -1, KV_HEADS, HEAD_DIM)
    stored = value_cache.reshape(rows, -1, KV_HEADS, HEAD_DIM)
    scores = (
        jnp.einsum("rgqd,rtgd->rgqt", grouped, cached, preferred_element_type=jnp.float32) * scale
    )
    live = jnp.arange(cached.shape[1])[None, :] < lengths[:, None]
    scores = jnp.where(live[:, None, None, :], scores, -jnp.inf)
    own = (
        jnp.einsum("rgqd,rgd->rgq", grouped, fresh_key, preferred_element_type=jnp.float32) * scale
    )
    top = jnp.maximum(jnp.max(scores, -1), own)
    expo = jnp.exp(scores - top[..., None])
    own_exp = jnp.exp(own - top)
    total = jnp.sum(expo, -1) + own_exp
    probs = (expo / total[..., None]).astype(jnp.bfloat16)
    own_prob = (own_exp / total).astype(jnp.bfloat16)
    context_vector = jnp.einsum(
        "rgqt,rtgd->rgqd", probs, stored, preferred_element_type=jnp.float32
    )
    context_vector = (
        context_vector + own_prob.astype(jnp.float32)[..., None] * fresh_value[:, :, None, :]
    )
    context_vector = context_vector.reshape(rows, query_width).astype(jnp.bfloat16)
    slot_hits = slots[:, None] == jnp.arange(requests.shape[1])[None, :]
    adapter = jnp.sum(jnp.where(slot_hits, requests[0][None, :], 0), 1)
    adapter_selector = (adapter[:, None] == jnp.arange(ADAPTER_COUNT)[None, :]).astype(jnp.bfloat16)
    context_gathered, selector_gathered = (
        lax.all_gather(context_vector, "mp", axis=0, tiled=True),
        lax.all_gather(adapter_selector, "mp", axis=0, tiled=True),
    )
    shared_portion = adapter_down_matrices.shape[1]
    context_slice = lax.dynamic_slice_in_dim(
        context_gathered, lax.axis_index("mp") * shared_portion, shared_portion, 1
    )
    every_adapter = jnp.einsum(
        "gh,thy->gty", context_slice, adapter_down_matrices, preferred_element_type=jnp.float32
    )
    partial_down = jnp.sum(every_adapter * selector_gathered.astype(jnp.float32)[:, :, None], 1)
    down_gathered = lax.psum(partial_down, "mp").astype(jnp.bfloat16)
    projection_result = apply_up_matrix(
        context_gathered, selector_gathered, down_gathered, output_weight, adapter_up_matrices
    )
    returned = lax.all_to_all(projection_result, "mp", split_axis=0, concat_axis=1, tiled=True)
    return (widened + returned.astype(jnp.float32)).astype(jnp.bfloat16)


MIB = 1 << 20
LANES = 128
VMEM = pl.BlockSpec(memory_space=pltpu.VMEM)
SMEM = pl.BlockSpec(memory_space=pltpu.SMEM)
ANY = pl.BlockSpec(memory_space=pl.ANY)


def call(kernel, name, out_shape, in_specs, moved, limit=2 * MIB, flops=0, **options):
    return pl.pallas_call(
        kernel,
        out_shape=out_shape,
        in_specs=in_specs,
        out_specs=jax.tree.map(lambda _: VMEM, out_shape),
        compiler_params=pltpu.CompilerParams(vmem_limit_bytes=limit),
        cost_estimate=pl.CostEstimate(flops=flops, bytes_accessed=moved, transcendentals=0),
        name=name,
        **options,
    )


def norm_rows(hidden, gain, slots, requests, copies):
    rows, width = hidden.shape

    def kernel(hidden_ref, gain_ref, slots_ref, requests_ref, out_ref):
        wide = hidden_ref[...].astype(jnp.float32)
        inverse = lax.rsqrt(jnp.mean(wide * wide, -1, keepdims=True) + EPS)
        for k in range(width // LANES):
            part = pl.ds(k * LANES, LANES)
            normed = hidden_ref[:, part].astype(jnp.float32) * inverse
            normed = normed * gain_ref[k : k + 1, :].astype(jnp.float32)
            normed = normed.astype(jnp.bfloat16)
            for c in range(copies):
                out_ref[c, :, part] = normed
        row = lax.broadcasted_iota(jnp.int32, (rows, LANES), 0)
        adapter = jnp.zeros((rows, LANES), jnp.float32)
        for r in range(rows):
            chosen = requests_ref[0, slots_ref[r]].astype(jnp.float32)
            adapter = jnp.where(row == r, chosen, adapter)
        for c in range(copies):
            out_ref[c, :, pl.ds(width, LANES)] = adapter.astype(jnp.bfloat16)

    return call(
        kernel,
        "norm_rows",
        jax.ShapeDtypeStruct((copies, rows, width + LANES), jnp.bfloat16),
        [VMEM, VMEM, SMEM, SMEM],
        hidden.size * 2 * (copies + 1),
    )(hidden, gain.reshape(-1, LANES), slots, requests)


def hold(weight, after, *passed):
    def kernel(weight_ref, after_ref, *refs):
        del weight_ref, after_ref
        for source, target in zip(refs[: len(passed)], refs[len(passed) + 1 :]):
            target[...] = source[...]

    outs = call(
        kernel,
        "hold_weight",
        (pltpu.VMEM(weight.shape, weight.dtype),)
        + tuple(jax.ShapeDtypeStruct(p.shape, p.dtype) for p in passed),
        [VMEM, ANY] + [VMEM] * len(passed),
        weight.size * 2,
        limit=MIB,
        input_output_aliases={0: 0},
    )(weight, after, *passed)
    return outs if passed else outs[0]


def multiply(rows, weight, out_type, name, chunk=1024):
    count, depth = rows.shape[0], weight.shape[0]

    def kernel(rows_ref, weight_ref, out_ref):
        total = jnp.zeros((count, weight.shape[1]), jnp.float32)
        for k in range(depth // chunk):
            part = pl.ds(k * chunk, chunk)
            total = total + jnp.dot(
                rows_ref[:, part], weight_ref[part, :], preferred_element_type=jnp.float32
            )
        out_ref[...] = total.astype(out_type)

    return call(
        kernel,
        name,
        jax.ShapeDtypeStruct((count, weight.shape[1]), out_type),
        [VMEM, VMEM],
        weight.size,
        flops=2 * count * weight.size,
    )(rows, weight)


def pick_adapters(adapter, down, up, after):
    count, rank = adapter.shape[0], up.shape[1]
    down_shape, up_shape = (count,) + down.shape[1:], (count,) + up.shape[1:]

    def kernel(adapter_ref, down_ref, up_ref, after_ref, down_out, up_out, sems):
        del after_ref
        copies = []
        for r in range(count):
            chosen = adapter_ref[r]
            copies.append(
                pltpu.make_async_copy(down_ref.at[chosen], down_out.at[r], sems.at[0, r])
            )
            copies.append(pltpu.make_async_copy(up_ref.at[chosen], up_out.at[r], sems.at[1, r]))
        for copy in copies:
            copy.start()
        for copy in copies:
            copy.wait()

    return call(
        kernel,
        "pick_adapters",
        (pltpu.VMEM(down_shape, down.dtype), pltpu.VMEM(up_shape, up.dtype)),
        [SMEM, ANY, ANY, ANY],
        2 * count * rank * (down.shape[2] + up.shape[2]),
        limit=36 * MIB,
        scratch_shapes=[pltpu.SemaphoreType.DMA((2, count))],
    )(adapter, down, up, after)


def down_partials(rows, place, down, copies):
    count, rank, depth = down.shape

    def kernel(place_ref, rows_ref, down_ref, out_ref):
        start = pl.multiple_of(place_ref[0] * depth, depth)
        every = lax.dot_general(
            rows_ref[:, pl.ds(start, depth)],
            down_ref[...].reshape(count * rank, depth),
            (((1,), (1,)), ((), ())),
            preferred_element_type=jnp.float32,
        )
        row = lax.broadcasted_iota(jnp.int32, (count, LANES), 0)
        lane = lax.broadcasted_iota(jnp.int32, (count, LANES), 1)
        total = jnp.zeros((count, LANES), jnp.float32)
        for s in range(count * rank // LANES):
            mine = row == (lane + s * LANES) // rank
            total = total + jnp.where(mine, every[:, s * LANES : (s + 1) * LANES], 0.0)
        for c in range(copies):
            out_ref[c] = total

    return call(
        kernel,
        "down_partials",
        jax.ShapeDtypeStruct((copies, count, LANES), jnp.float32),
        [SMEM, VMEM, VMEM],
        down.size * 2,
        limit=4 * MIB,
        flops=2 * count * down.size,
    )(place, rows, down)


def add_up(base, partials, up):
    count, rank, width = up.shape

    def kernel(base_ref, partials_ref, up_ref, out_ref):
        total = partials_ref[0]
        for c in range(1, partials.shape[0]):
            total = total + partials_ref[c]
        down = total.astype(jnp.bfloat16).astype(jnp.float32)
        row = lax.broadcasted_iota(jnp.int32, (count, LANES), 0)
        lane = lax.broadcasted_iota(jnp.int32, (count, LANES), 1)
        spread = jnp.concatenate(
            [
                jnp.where(row == (lane + s * LANES) // rank, down, 0.0)
                for s in range(count * rank // LANES)
            ],
            1,
        ).astype(jnp.bfloat16)
        delta = jnp.dot(
            spread, up_ref[...].reshape(count * rank, width), preferred_element_type=jnp.float32
        )
        out_ref[...] = (base_ref[...] + ADAPTER_SCALE * delta).astype(jnp.bfloat16)

    return call(
        kernel,
        "add_up",
        jax.ShapeDtypeStruct((count, width), jnp.bfloat16),
        [VMEM, VMEM, VMEM],
        up.size * 2,
        limit=4 * MIB,
        flops=2 * count * up.size,
    )(base, partials, up)


def add_rows(hidden, parts):
    width = parts.shape[2]

    def kernel(hidden_ref, parts_ref, out_ref):
        for k in range(parts.shape[0]):
            part = pl.ds(k * width, width)
            total = hidden_ref[:, part].astype(jnp.float32) + parts_ref[k].astype(jnp.float32)
            out_ref[:, part] = total.astype(jnp.bfloat16)

    return call(
        kernel,
        "add_rows",
        jax.ShapeDtypeStruct(hidden.shape, hidden.dtype),
        [VMEM, VMEM],
        hidden.size * 6,
    )(hidden, parts)


def swap_cores(block):
    return lax.ppermute(block, "batch", [(0, 1), (1, 0)])


def exchange(blocks):
    return lax.all_to_all(blocks, "mp", split_axis=0, concat_axis=0, tiled=True)


def attend(qkv, cosine, sine, key_cache, value_cache, lengths):
    rows = qkv.shape[0]
    query_width = HEADS * HEAD_DIM
    kv_width = KV_HEADS * HEAD_DIM
    group = HEADS // KV_HEADS
    scale = HEAD_DIM ** (-0.5)

    def turn(part):
        vec = part.astype(jnp.float32).reshape(rows, -1, HEAD_DIM)
        half = HEAD_DIM // 2
        turned = jnp.concatenate([-vec[..., half:], vec[..., :half]], -1)
        return (vec * cosine[:, None] + turned * sine[:, None]).astype(jnp.bfloat16)

    query = turn(qkv[:, :query_width])
    fresh_key = turn(qkv[:, query_width : query_width + kv_width])
    fresh_value = (
        qkv[:, query_width + kv_width :].astype(jnp.float32).reshape(rows, KV_HEADS, HEAD_DIM)
    )
    grouped = query.reshape(rows, KV_HEADS, group, HEAD_DIM)
    cached = key_cache.reshape(rows, -1, KV_HEADS, HEAD_DIM)
    stored = value_cache.reshape(rows, -1, KV_HEADS, HEAD_DIM)
    scores = (
        jnp.einsum("rgqd,rtgd->rgqt", grouped, cached, preferred_element_type=jnp.float32) * scale
    )
    live = jnp.arange(cached.shape[1])[None, :] < lengths[:, None]
    scores = jnp.where(live[:, None, None, :], scores, -jnp.inf)
    own = (
        jnp.einsum("rgqd,rgd->rgq", grouped, fresh_key, preferred_element_type=jnp.float32) * scale
    )
    top = jnp.maximum(jnp.max(scores, -1), own)
    expo = jnp.exp(scores - top[..., None])
    own_exp = jnp.exp(own - top)
    total = jnp.sum(expo, -1) + own_exp
    probs = (expo / total[..., None]).astype(jnp.bfloat16)
    own_prob = (own_exp / total).astype(jnp.bfloat16)
    context_vector = jnp.einsum(
        "rgqt,rtgd->rgqd", probs, stored, preferred_element_type=jnp.float32
    )
    context_vector = (
        context_vector + own_prob.astype(jnp.float32)[..., None] * fresh_value[:, :, None, :]
    )
    return context_vector.reshape(rows, query_width).astype(jnp.bfloat16)


def angles(lengths):
    half = HEAD_DIM // 2
    freq = THETA ** (-(jnp.arange(half, dtype=jnp.float32) * 2.0) / HEAD_DIM)
    angle = lengths.astype(jnp.float32)[:, None] * freq
    cosine, sine = jnp.cos(angle), jnp.sin(angle)
    return jnp.concatenate([cosine, cosine], -1), jnp.concatenate([sine, sine], -1)


def fast_body(
    hidden,
    attention_norm_gain,
    query_key_value_weight,
    output_weight,
    key_cache,
    value_cache,
    lengths,
    slots,
    requests,
    adapter_down_matrices,
    adapter_up_matrices,
):
    rows, features = hidden.shape
    mp_size = lax.axis_size("mp")
    width = query_key_value_weight.shape[1]
    cosine, sine = angles(lengths)

    sent = norm_rows(hidden, attention_norm_gain, slots, requests, mp_size)
    near = exchange(sent)
    far = swap_cores(near)
    held_weight = hold(query_key_value_weight, sent)
    adapter = near[:, :, features].reshape(-1).astype(jnp.int32)
    normed = jnp.concatenate([near, far]).reshape(-1, features + LANES)
    columns = multiply(normed, held_weight, jnp.bfloat16, "project_qkv")

    split = columns.reshape(2, mp_size, rows, width)
    mixed = jnp.stack([split[0], swap_cores(split[1])], 1)
    mixed = exchange(mixed)
    held_weight, cosine, sine = hold(output_weight, columns, cosine, sine)
    mixed = jnp.where(lax.axis_index("batch") == 0, mixed, mixed[:, ::-1])
    qkv = mixed.transpose(2, 0, 1, 3).reshape(rows, -1)

    context = attend(qkv, cosine, sine, key_cache, value_cache, lengths)
    picked_down, picked_up = pick_adapters(
        adapter, adapter_down_matrices.swapaxes(1, 2), adapter_up_matrices, context
    )
    copies = jnp.broadcast_to(context[None], (mp_size, *context.shape))
    gathered = exchange(copies).reshape(-1, context.shape[1])

    place = lax.axis_index("mp").astype(jnp.int32).reshape(1)
    partials = exchange(down_partials(gathered, place, picked_down, mp_size))
    base = multiply(gathered, held_weight, jnp.float32, "project_out")
    projected = add_up(base, partials, picked_up)
    returned = exchange(projected.reshape(mp_size, rows, -1))
    return add_rows(hidden, returned)


def body(*arguments):
    small = lax.axis_size("mp") <= 16 and lax.axis_size("batch") == 2
    whole_heads = arguments[2].shape[1] % HEAD_DIM == 0
    return (fast_body if small and whole_heads else general_body)(*arguments)


def solution(mesh):
    in_specs = (
        P(("groups", "mp", "batch"), None),
        P(),
        P(None, ("mp", "batch")),
        P(None, "mp"),
        P(("groups", "mp", "batch"), None, None),
        P(("groups", "mp", "batch"), None, None),
        P(("groups", "mp", "batch")),
        P(("groups", "mp", "batch")),
        P(("groups", "mp", "batch"), None),
        P(None, "mp", None),
        P(None, None, "mp"),
    )
    out_specs = P(("groups", "mp", "batch"), None)
    return jax.shard_map(body, mesh=mesh, in_specs=in_specs, out_specs=out_specs, check_vma=False)
```

```python
import jax
import jax.numpy as jnp
from jax import lax
from jax.experimental import pallas as pl
from jax.experimental.pallas import tpu as pltpu
from jax.sharding import PartitionSpec as P

HEADS = 64
KV_HEADS = 8
HEAD_DIM = 128
ADAPTER_COUNT = 64


EPS = 1e-05
THETA = 500000.0
ADAPTER_SCALE = 2.0


def rotate(vec, pos):
    width = vec.shape[-1]
    half = width // 2
    freq = THETA ** (-(jnp.arange(half, dtype=jnp.float32) * 2.0) / width)
    angle = pos[..., None, None] * freq
    cosine = jnp.concatenate([jnp.cos(angle), jnp.cos(angle)], -1)
    sine = jnp.concatenate([jnp.sin(angle), jnp.sin(angle)], -1)
    turned = jnp.concatenate([-vec[..., half:], vec[..., :half]], -1)
    return vec * cosine + turned * sine


def apply_up_matrix(
    context_vector, adapter_selector, down_result, output_weight, adapter_up_matrices
):
    base_output = jnp.dot(context_vector, output_weight, preferred_element_type=jnp.float32)
    spread = (adapter_selector[:, :, None] * down_result[:, None, :]).reshape(
        adapter_selector.shape[0], -1
    )
    adapter_table = adapter_up_matrices.reshape(-1, adapter_up_matrices.shape[2])
    adapter_delta = jnp.dot(spread, adapter_table, preferred_element_type=jnp.float32)
    return (base_output + ADAPTER_SCALE * adapter_delta).astype(jnp.bfloat16)


def general_body(
    hidden,
    attention_norm_gain,
    query_key_value_weight,
    output_weight,
    key_cache,
    value_cache,
    lengths,
    slots,
    requests,
    adapter_down_matrices,
    adapter_up_matrices,
):
    widened = hidden.astype(jnp.float32)
    normed = (
        widened
        * lax.rsqrt(jnp.mean(widened * widened, -1, keepdims=True) + EPS)
        * attention_norm_gain.astype(jnp.float32)
    ).astype(jnp.bfloat16)
    rows = normed.shape[0]
    columns = jnp.dot(
        lax.all_gather(normed, ("mp", "batch"), axis=0, tiled=True),
        query_key_value_weight,
        preferred_element_type=jnp.float32,
    ).astype(jnp.bfloat16)
    mixed = lax.all_to_all(
        lax.all_to_all(columns, "mp", split_axis=0, concat_axis=1, tiled=True),
        "batch",
        split_axis=0,
        concat_axis=1,
        tiled=True,
    )
    width = query_key_value_weight.shape[1]
    qkv = (
        mixed.reshape(rows, lax.axis_size("batch"), lax.axis_size("mp"), width)
        .transpose(0, 2, 1, 3)
        .reshape(rows, -1)
    )
    query_width = HEADS * HEAD_DIM
    kv_width = KV_HEADS * HEAD_DIM
    group = HEADS // KV_HEADS
    scale = HEAD_DIM ** (-0.5)
    pos = lengths.astype(jnp.float32)
    query = rotate(
        qkv[:, :query_width].astype(jnp.float32).reshape(rows, HEADS, HEAD_DIM), pos
    ).astype(jnp.bfloat16)
    fresh_key = rotate(
        qkv[:, query_width : query_width + kv_width]
        .astype(jnp.float32)
        .reshape(rows, KV_HEADS, HEAD_DIM),
        pos,
    ).astype(jnp.bfloat16)
    fresh_value = (
        qkv[:, query_width + kv_width :].astype(jnp.float32).reshape(rows, KV_HEADS, HEAD_DIM)
    )
    grouped = query.reshape(rows, KV_HEADS, group, HEAD_DIM)
    cached = key_cache.reshape(rows, -1, KV_HEADS, HEAD_DIM)
    stored = value_cache.reshape(rows, -1, KV_HEADS, HEAD_DIM)
    scores = (
        jnp.einsum("rgqd,rtgd->rgqt", grouped, cached, preferred_element_type=jnp.float32) * scale
    )
    live = jnp.arange(cached.shape[1])[None, :] < lengths[:, None]
    scores = jnp.where(live[:, None, None, :], scores, -jnp.inf)
    own = (
        jnp.einsum("rgqd,rgd->rgq", grouped, fresh_key, preferred_element_type=jnp.float32) * scale
    )
    top = jnp.maximum(jnp.max(scores, -1), own)
    expo = jnp.exp(scores - top[..., None])
    own_exp = jnp.exp(own - top)
    total = jnp.sum(expo, -1) + own_exp
    probs = (expo / total[..., None]).astype(jnp.bfloat16)
    own_prob = (own_exp / total).astype(jnp.bfloat16)
    context_vector = jnp.einsum(
        "rgqt,rtgd->rgqd", probs, stored, preferred_element_type=jnp.float32
    )
    context_vector = (
        context_vector + own_prob.astype(jnp.float32)[..., None] * fresh_value[:, :, None, :]
    )
    context_vector = context_vector.reshape(rows, query_width).astype(jnp.bfloat16)
    slot_hits = slots[:, None] == jnp.arange(requests.shape[1])[None, :]
    adapter = jnp.sum(jnp.where(slot_hits, requests[0][None, :], 0), 1)
    adapter_selector = (adapter[:, None] == jnp.arange(ADAPTER_COUNT)[None, :]).astype(jnp.bfloat16)
    context_gathered, selector_gathered = (
        lax.all_gather(context_vector, "mp", axis=0, tiled=True),
        lax.all_gather(adapter_selector, "mp", axis=0, tiled=True),
    )
    shared_portion = adapter_down_matrices.shape[1]
    context_slice = lax.dynamic_slice_in_dim(
        context_gathered, lax.axis_index("mp") * shared_portion, shared_portion, 1
    )
    every_adapter = jnp.einsum(
        "gh,thy->gty", context_slice, adapter_down_matrices, preferred_element_type=jnp.float32
    )
    partial_down = jnp.sum(every_adapter * selector_gathered.astype(jnp.float32)[:, :, None], 1)
    down_gathered = lax.psum(partial_down, "mp").astype(jnp.bfloat16)
    projection_result = apply_up_matrix(
        context_gathered, selector_gathered, down_gathered, output_weight, adapter_up_matrices
    )
    returned = lax.all_to_all(projection_result, "mp", split_axis=0, concat_axis=1, tiled=True)
    return (widened + returned.astype(jnp.float32)).astype(jnp.bfloat16)


MIB = 1 << 20
LANES = 128
BATCH = 4
STREAM = 53 * MIB
VMEM = pl.BlockSpec(memory_space=pltpu.VMEM)
SMEM = pl.BlockSpec(memory_space=pltpu.SMEM)
ANY = pl.BlockSpec(memory_space=pl.ANY)


def call(kernel, name, out_shape, in_specs, moved, limit=2 * MIB, flops=0, **options):
    return pl.pallas_call(
        kernel,
        out_shape=out_shape,
        in_specs=in_specs,
        out_specs=jax.tree.map(lambda _: VMEM, out_shape),
        compiler_params=pltpu.CompilerParams(vmem_limit_bytes=limit),
        cost_estimate=pl.CostEstimate(flops=flops, bytes_accessed=moved, transcendentals=0),
        name=name,
        **options,
    )


def norm_rows(hidden, gain, slots, requests, lengths, copies):
    rows, width = hidden.shape

    def kernel(hidden_ref, gain_ref, slots_ref, requests_ref, lengths_ref, out_ref, pos_ref):
        wide = hidden_ref[...].astype(jnp.float32)
        inverse = lax.rsqrt(jnp.mean(wide * wide, -1, keepdims=True) + EPS)
        for k in range(width // LANES):
            part = pl.ds(k * LANES, LANES)
            normed = hidden_ref[:, part].astype(jnp.float32) * inverse
            normed = normed * gain_ref[k : k + 1, :].astype(jnp.float32)
            normed = normed.astype(jnp.bfloat16)
            for c in range(copies):
                out_ref[c, :, part] = normed
        row = lax.broadcasted_iota(jnp.int32, (rows, LANES), 0)
        adapter = jnp.zeros((rows, LANES), jnp.float32)
        for r in range(rows):
            chosen = requests_ref[0, slots_ref[r]].astype(jnp.float32)
            adapter = jnp.where(row == r, chosen, adapter)
        for c in range(copies):
            out_ref[c, :, pl.ds(width, LANES)] = adapter.astype(jnp.bfloat16)
        position = jnp.zeros((rows, LANES), jnp.float32)
        for r in range(rows):
            position = jnp.where(row == r, lengths_ref[r].astype(jnp.float32), position)
        pos_ref[...] = position

    return call(
        kernel,
        "norm_rows",
        (
            jax.ShapeDtypeStruct((copies, rows, width + LANES), jnp.bfloat16),
            jax.ShapeDtypeStruct((rows, LANES), jnp.float32),
        ),
        [VMEM, VMEM, SMEM, SMEM, SMEM],
        hidden.size * 2 * (copies + 1),
    )(hidden, gain.reshape(-1, LANES), slots, requests, lengths)


def stream(weight_ref, held_ref, sems, parts):
    depth = held_ref.shape[0] // parts
    copies = []
    for k in range(parts):
        rows = pl.ds(k * depth, depth)
        copies.append(
            pltpu.make_async_copy(weight_ref.at[rows], held_ref.at[rows], sems.at[k])
        )
        copies[-1].start()

    def part(k):
        copies[k].wait()
        return held_ref[pl.ds(k * depth, depth)]

    return part


def project_qkv(near, far, weight, core, parts=16):
    groups, rows, _ = near.shape
    depth, width = weight.shape
    count, step = 2 * groups * rows, weight.shape[0] // parts

    def kernel(core_ref, near_ref, far_ref, weight_ref, out_ref, rows_ref, held_ref, sems):
        part = stream(weight_ref, held_ref, sems, parts)
        for e, source in enumerate((near_ref, far_ref)):
            for j in range(groups):
                place = pl.ds((e * groups + j) * rows, rows)
                rows_ref[place] = source[j, :, pl.ds(0, depth)]
        total = jnp.zeros((count, width), jnp.float32)
        for k in range(parts):
            total = total + jnp.dot(
                rows_ref[:, pl.ds(k * step, step)], part(k), preferred_element_type=jnp.float32
            )
        for e in range(2):
            for j in range(groups):
                place = (e * groups + j) * rows
                out_ref[2 * j + (core_ref[0] ^ e)] = total[place : place + rows].astype(
                    jnp.bfloat16
                )

    return call(
        kernel,
        "project_qkv",
        jax.ShapeDtypeStruct((2 * groups, rows, width), jnp.bfloat16),
        [SMEM, VMEM, VMEM, ANY],
        weight.size * 2,
        limit=STREAM,
        flops=2 * count * weight.size,
        scratch_shapes=[
            pltpu.VMEM((count, depth), jnp.bfloat16),
            pltpu.VMEM(weight.shape, weight.dtype),
            pltpu.SemaphoreType.DMA((parts,)),
        ],
    )(core, near, far, weight)


def project_out(rows, weight, parts=16):
    count, step = rows.shape[0], weight.shape[0] // parts

    def kernel(rows_ref, weight_ref, out_ref, held_ref, sems):
        part = stream(weight_ref, held_ref, sems, parts)
        total = jnp.zeros(out_ref.shape, jnp.float32)
        for k in range(parts):
            total = total + jnp.dot(
                rows_ref[:, pl.ds(k * step, step)], part(k), preferred_element_type=jnp.float32
            )
        out_ref[...] = total

    return call(
        kernel,
        "project_out",
        jax.ShapeDtypeStruct((count, weight.shape[1]), jnp.float32),
        [VMEM, ANY],
        weight.size * 2,
        limit=STREAM,
        flops=2 * count * weight.size,
        scratch_shapes=[
            pltpu.VMEM(weight.shape, weight.dtype),
            pltpu.SemaphoreType.DMA((parts,)),
        ],
    )(rows, weight)


def pick(adapter_ref, store_ref, held_ref, sems):
    count, rank = adapter_ref.shape[0], store_ref.shape[1]
    copies = []
    for r in range(count):
        copies.append(
            pltpu.make_async_copy(
                store_ref.at[adapter_ref[r]], held_ref.at[pl.ds(r * rank, rank)], sems.at[r]
            )
        )
        copies[-1].start()

    def batch(k):
        for copy in copies[k * BATCH : (k + 1) * BATCH]:
            copy.wait()
        return held_ref[pl.ds(k * BATCH * rank, BATCH * rank)]

    return batch


def down_partials(rows, place, adapter, store, copies):
    count = adapter.shape[0]
    rank, depth = store.shape[1:]

    def kernel(place_ref, adapter_ref, rows_ref, store_ref, out_ref, held_ref, sems):
        batch = pick(adapter_ref, store_ref, held_ref, sems)
        slices = rows_ref[:, pl.ds(pl.multiple_of(place_ref[0] * depth, depth), depth)]
        row = lax.broadcasted_iota(jnp.int32, (count, LANES), 0)
        lane = lax.broadcasted_iota(jnp.int32, (count, LANES), 1)
        total = jnp.zeros((count, LANES), jnp.float32)
        for k in range(count // BATCH):
            every = lax.dot_general(
                slices,
                batch(k),
                (((1,), (1,)), ((), ())),
                preferred_element_type=jnp.float32,
            )
            for s in range(BATCH * rank // LANES):
                first = k * BATCH * rank + s * LANES
                mine = row == (lane + first) // rank
                total = total + jnp.where(mine, every[:, s * LANES : (s + 1) * LANES], 0.0)
        for c in range(copies):
            out_ref[c] = total

    return call(
        kernel,
        "down_partials",
        jax.ShapeDtypeStruct((copies, count, LANES), jnp.float32),
        [SMEM, SMEM, VMEM, ANY],
        2 * count * rank * depth,
        limit=STREAM,
        flops=2 * count * count * rank * depth,
        scratch_shapes=[
            pltpu.VMEM((count * rank, depth), store.dtype),
            pltpu.SemaphoreType.DMA((count,)),
        ],
    )(place, adapter, rows, store)


def add_up(base, partials, adapter, store):
    count = adapter.shape[0]
    rank, width = store.shape[1:]

    def kernel(adapter_ref, base_ref, partials_ref, store_ref, out_ref, held_ref, sems):
        batch = pick(adapter_ref, store_ref, held_ref, sems)
        total = partials_ref[0]
        for c in range(1, partials.shape[0]):
            total = total + partials_ref[c]
        down = total.astype(jnp.bfloat16).astype(jnp.float32)
        row = lax.broadcasted_iota(jnp.int32, (count, LANES), 0)
        lane = lax.broadcasted_iota(jnp.int32, (count, LANES), 1)
        delta = jnp.zeros((count, width), jnp.float32)
        for k in range(count // BATCH):
            spread = []
            for s in range(BATCH * rank // LANES):
                first = k * BATCH * rank + s * LANES
                spread.append(jnp.where(row == (lane + first) // rank, down, 0.0))
            spread = jnp.concatenate(spread, 1).astype(jnp.bfloat16)
            delta = delta + jnp.dot(spread, batch(k), preferred_element_type=jnp.float32)
        out_ref[...] = (base_ref[...] + ADAPTER_SCALE * delta).astype(jnp.bfloat16)

    return call(
        kernel,
        "add_up",
        jax.ShapeDtypeStruct((count, width), jnp.bfloat16),
        [SMEM, VMEM, VMEM, ANY],
        2 * count * rank * width,
        limit=STREAM,
        flops=2 * count * count * rank * width,
        scratch_shapes=[
            pltpu.VMEM((count * rank, width), store.dtype),
            pltpu.SemaphoreType.DMA((count,)),
        ],
    )(adapter, base, partials, store)


def widen(hidden, after):
    def kernel(hidden_ref, after_ref, out_ref):
        del after_ref
        out_ref[...] = hidden_ref[...].astype(jnp.float32)

    return call(
        kernel,
        "widen",
        jax.ShapeDtypeStruct(hidden.shape, jnp.float32),
        [VMEM, ANY],
        hidden.size * 64,
    )(hidden, after)


def add_rows(hidden, parts):
    width = parts.shape[2]

    def kernel(hidden_ref, parts_ref, out_ref):
        for k in range(parts.shape[0]):
            part = pl.ds(k * width, width)
            total = hidden_ref[:, part] + parts_ref[k].astype(jnp.float32)
            out_ref[:, part] = total.astype(jnp.bfloat16)

    return call(
        kernel,
        "add_rows",
        jax.ShapeDtypeStruct(hidden.shape, parts.dtype),
        [VMEM, VMEM],
        hidden.size * 6,
    )(hidden, parts)


def swap_cores(block):
    return lax.ppermute(block, "batch", [(0, 1), (1, 0)])


def exchange(blocks, axes="mp"):
    return lax.all_to_all(blocks, axes, split_axis=0, concat_axis=0, tiled=True)


def attend(qkv, cosine, sine, key_cache, value_cache, lengths):
    rows = qkv.shape[0]
    query_width = HEADS * HEAD_DIM
    kv_width = KV_HEADS * HEAD_DIM
    group = HEADS // KV_HEADS
    scale = HEAD_DIM ** (-0.5)

    def turn(part):
        vec = part.astype(jnp.float32).reshape(rows, -1, HEAD_DIM)
        half = HEAD_DIM // 2
        turned = jnp.concatenate([-vec[..., half:], vec[..., :half]], -1)
        return (vec * cosine[:, None] + turned * sine[:, None]).astype(jnp.bfloat16)

    query = turn(qkv[:, :query_width])
    fresh_key = turn(qkv[:, query_width : query_width + kv_width])
    fresh_value = (
        qkv[:, query_width + kv_width :].astype(jnp.float32).reshape(rows, KV_HEADS, HEAD_DIM)
    )
    grouped = query.reshape(rows, KV_HEADS, group, HEAD_DIM)
    cached = key_cache.reshape(rows, -1, KV_HEADS, HEAD_DIM)
    stored = value_cache.reshape(rows, -1, KV_HEADS, HEAD_DIM)
    scores = (
        jnp.einsum("rgqd,rtgd->rgqt", grouped, cached, preferred_element_type=jnp.float32) * scale
    )
    live = jnp.arange(cached.shape[1])[None, :] < lengths[:, None]
    scores = jnp.where(live[:, None, None, :], scores, -jnp.inf)
    own = (
        jnp.einsum("rgqd,rgd->rgq", grouped, fresh_key, preferred_element_type=jnp.float32) * scale
    )
    top = jnp.maximum(jnp.max(scores, -1), own)
    expo = jnp.exp(scores - top[..., None])
    own_exp = jnp.exp(own - top)
    total = jnp.sum(expo, -1) + own_exp
    probs = (expo / total[..., None]).astype(jnp.bfloat16)
    own_prob = (own_exp / total).astype(jnp.bfloat16)
    context_vector = jnp.einsum(
        "rgqt,rtgd->rgqd", probs, stored, preferred_element_type=jnp.float32
    )
    context_vector = (
        context_vector + own_prob.astype(jnp.float32)[..., None] * fresh_value[:, :, None, :]
    )
    return context_vector.reshape(rows, query_width).astype(jnp.bfloat16)


def angles(positions):
    half = HEAD_DIM // 2
    freq = THETA ** (-(jnp.arange(half, dtype=jnp.float32) * 2.0) / HEAD_DIM)
    angle = positions[:, :half] * freq
    cosine, sine = jnp.cos(angle), jnp.sin(angle)
    return jnp.concatenate([cosine, cosine], -1), jnp.concatenate([sine, sine], -1)


def fast_body(
    hidden,
    attention_norm_gain,
    query_key_value_weight,
    output_weight,
    key_cache,
    value_cache,
    lengths,
    slots,
    requests,
    adapter_down_matrices,
    adapter_up_matrices,
):
    rows, features = hidden.shape
    mp_size = lax.axis_size("mp")
    core = lax.axis_index("batch").astype(jnp.int32).reshape(1)
    place = lax.axis_index("mp").astype(jnp.int32).reshape(1)

    sent, positions = norm_rows(
        hidden, attention_norm_gain, slots, requests, lengths, mp_size
    )
    cosine, sine = angles(positions)
    near = exchange(sent)
    adapter = near[:, :, features].reshape(-1).astype(jnp.int32)
    mixed = exchange(
        project_qkv(near, swap_cores(near), query_key_value_weight, core), ("mp", "batch")
    )
    qkv = mixed.transpose(1, 0, 2).reshape(rows, -1)

    context = attend(qkv, cosine, sine, key_cache, value_cache, lengths)
    copies = jnp.broadcast_to(context[None], (mp_size, *context.shape))
    gathered = exchange(copies).reshape(-1, context.shape[1])

    partials = exchange(
        down_partials(gathered, place, adapter, adapter_down_matrices.swapaxes(1, 2), mp_size)
    )
    base = project_out(gathered, output_weight)
    projected = add_up(base, partials, adapter, adapter_up_matrices)
    returned = exchange(projected.reshape(mp_size, rows, -1))
    return add_rows(widen(hidden, projected), returned)


def body(*arguments):
    small = lax.axis_size("mp") <= 16 and lax.axis_size("batch") == 2
    whole_heads = arguments[2].shape[1] % HEAD_DIM == 0
    return (fast_body if small and whole_heads else general_body)(*arguments)


def solution(mesh):
    in_specs = (
        P(("groups", "mp", "batch"), None),
        P(),
        P(None, ("mp", "batch")),
        P(None, "mp"),
        P(("groups", "mp", "batch"), None, None),
        P(("groups", "mp", "batch"), None, None),
        P(("groups", "mp", "batch")),
        P(("groups", "mp", "batch")),
        P(("groups", "mp", "batch"), None),
        P(None, "mp", None),
        P(None, None, "mp"),
    )
    out_specs = P(("groups", "mp", "batch"), None)
    return jax.shard_map(body, mesh=mesh, in_specs=in_specs, out_specs=out_specs, check_vma=False)
```

```python
import jax
import jax.numpy as jnp
from jax import lax
from jax.experimental import pallas as pl
from jax.experimental.pallas import tpu as pltpu
from jax.sharding import PartitionSpec as P

HEADS = 64
KV_HEADS = 8
HEAD_DIM = 128
ADAPTER_COUNT = 64


EPS = 1e-05
THETA = 500000.0
ADAPTER_SCALE = 2.0


def rotate(vec, pos):
    width = vec.shape[-1]
    half = width // 2
    freq = THETA ** (-(jnp.arange(half, dtype=jnp.float32) * 2.0) / width)
    angle = pos[..., None, None] * freq
    cosine = jnp.concatenate([jnp.cos(angle), jnp.cos(angle)], -1)
    sine = jnp.concatenate([jnp.sin(angle), jnp.sin(angle)], -1)
    turned = jnp.concatenate([-vec[..., half:], vec[..., :half]], -1)
    return vec * cosine + turned * sine


def apply_up_matrix(
    context_vector, adapter_selector, down_result, output_weight, adapter_up_matrices
):
    base_output = jnp.dot(context_vector, output_weight, preferred_element_type=jnp.float32)
    spread = (adapter_selector[:, :, None] * down_result[:, None, :]).reshape(
        adapter_selector.shape[0], -1
    )
    adapter_table = adapter_up_matrices.reshape(-1, adapter_up_matrices.shape[2])
    adapter_delta = jnp.dot(spread, adapter_table, preferred_element_type=jnp.float32)
    return (base_output + ADAPTER_SCALE * adapter_delta).astype(jnp.bfloat16)


def general_body(
    hidden,
    attention_norm_gain,
    query_key_value_weight,
    output_weight,
    key_cache,
    value_cache,
    lengths,
    slots,
    requests,
    adapter_down_matrices,
    adapter_up_matrices,
):
    widened = hidden.astype(jnp.float32)
    normed = (
        widened
        * lax.rsqrt(jnp.mean(widened * widened, -1, keepdims=True) + EPS)
        * attention_norm_gain.astype(jnp.float32)
    ).astype(jnp.bfloat16)
    rows = normed.shape[0]
    columns = jnp.dot(
        lax.all_gather(normed, ("mp", "batch"), axis=0, tiled=True),
        query_key_value_weight,
        preferred_element_type=jnp.float32,
    ).astype(jnp.bfloat16)
    mixed = lax.all_to_all(
        lax.all_to_all(columns, "mp", split_axis=0, concat_axis=1, tiled=True),
        "batch",
        split_axis=0,
        concat_axis=1,
        tiled=True,
    )
    width = query_key_value_weight.shape[1]
    qkv = (
        mixed.reshape(rows, lax.axis_size("batch"), lax.axis_size("mp"), width)
        .transpose(0, 2, 1, 3)
        .reshape(rows, -1)
    )
    query_width = HEADS * HEAD_DIM
    kv_width = KV_HEADS * HEAD_DIM
    group = HEADS // KV_HEADS
    scale = HEAD_DIM ** (-0.5)
    pos = lengths.astype(jnp.float32)
    query = rotate(
        qkv[:, :query_width].astype(jnp.float32).reshape(rows, HEADS, HEAD_DIM), pos
    ).astype(jnp.bfloat16)
    fresh_key = rotate(
        qkv[:, query_width : query_width + kv_width]
        .astype(jnp.float32)
        .reshape(rows, KV_HEADS, HEAD_DIM),
        pos,
    ).astype(jnp.bfloat16)
    fresh_value = (
        qkv[:, query_width + kv_width :].astype(jnp.float32).reshape(rows, KV_HEADS, HEAD_DIM)
    )
    grouped = query.reshape(rows, KV_HEADS, group, HEAD_DIM)
    cached = key_cache.reshape(rows, -1, KV_HEADS, HEAD_DIM)
    stored = value_cache.reshape(rows, -1, KV_HEADS, HEAD_DIM)
    scores = (
        jnp.einsum("rgqd,rtgd->rgqt", grouped, cached, preferred_element_type=jnp.float32) * scale
    )
    live = jnp.arange(cached.shape[1])[None, :] < lengths[:, None]
    scores = jnp.where(live[:, None, None, :], scores, -jnp.inf)
    own = (
        jnp.einsum("rgqd,rgd->rgq", grouped, fresh_key, preferred_element_type=jnp.float32) * scale
    )
    top = jnp.maximum(jnp.max(scores, -1), own)
    expo = jnp.exp(scores - top[..., None])
    own_exp = jnp.exp(own - top)
    total = jnp.sum(expo, -1) + own_exp
    probs = (expo / total[..., None]).astype(jnp.bfloat16)
    own_prob = (own_exp / total).astype(jnp.bfloat16)
    context_vector = jnp.einsum(
        "rgqt,rtgd->rgqd", probs, stored, preferred_element_type=jnp.float32
    )
    context_vector = (
        context_vector + own_prob.astype(jnp.float32)[..., None] * fresh_value[:, :, None, :]
    )
    context_vector = context_vector.reshape(rows, query_width).astype(jnp.bfloat16)
    slot_hits = slots[:, None] == jnp.arange(requests.shape[1])[None, :]
    adapter = jnp.sum(jnp.where(slot_hits, requests[0][None, :], 0), 1)
    adapter_selector = (adapter[:, None] == jnp.arange(ADAPTER_COUNT)[None, :]).astype(jnp.bfloat16)
    context_gathered, selector_gathered = (
        lax.all_gather(context_vector, "mp", axis=0, tiled=True),
        lax.all_gather(adapter_selector, "mp", axis=0, tiled=True),
    )
    shared_portion = adapter_down_matrices.shape[1]
    context_slice = lax.dynamic_slice_in_dim(
        context_gathered, lax.axis_index("mp") * shared_portion, shared_portion, 1
    )
    every_adapter = jnp.einsum(
        "gh,thy->gty", context_slice, adapter_down_matrices, preferred_element_type=jnp.float32
    )
    partial_down = jnp.sum(every_adapter * selector_gathered.astype(jnp.float32)[:, :, None], 1)
    down_gathered = lax.psum(partial_down, "mp").astype(jnp.bfloat16)
    projection_result = apply_up_matrix(
        context_gathered, selector_gathered, down_gathered, output_weight, adapter_up_matrices
    )
    returned = lax.all_to_all(projection_result, "mp", split_axis=0, concat_axis=1, tiled=True)
    return (widened + returned.astype(jnp.float32)).astype(jnp.bfloat16)


MIB = 1 << 20
LANES = 128
BATCH = 4
VMEM = pl.BlockSpec(memory_space=pltpu.VMEM)
SMEM = pl.BlockSpec(memory_space=pltpu.SMEM)
ANY = pl.BlockSpec(memory_space=pl.ANY)


def call(kernel, name, out_shape, in_specs, moved, limit=2 * MIB, flops=0, **options):
    return pl.pallas_call(
        kernel,
        out_shape=out_shape,
        in_specs=in_specs,
        out_specs=jax.tree.map(lambda _: VMEM, out_shape),
        compiler_params=pltpu.CompilerParams(vmem_limit_bytes=limit),
        cost_estimate=pl.CostEstimate(flops=flops, bytes_accessed=moved, transcendentals=0),
        name=name,
        **options,
    )


def norm_rows(hidden, gain, copies):
    rows, width = hidden.shape

    def kernel(hidden_ref, gain_ref, out_ref):
        wide = hidden_ref[...].astype(jnp.float32)
        inverse = lax.rsqrt(jnp.mean(wide * wide, -1, keepdims=True) + EPS)
        for k in range(width // LANES):
            part = pl.ds(k * LANES, LANES)
            normed = hidden_ref[:, part].astype(jnp.float32) * inverse
            normed = normed * gain_ref[k : k + 1, :].astype(jnp.float32)
            normed = normed.astype(jnp.bfloat16)
            for c in range(copies):
                out_ref[c, :, part] = normed

    return call(
        kernel,
        "norm_rows",
        jax.ShapeDtypeStruct((copies, rows, width), jnp.bfloat16),
        [VMEM, VMEM],
        hidden.size * 2 * (copies + 1),
    )(hidden, gain.reshape(-1, LANES))


def project_qkv(near, far, weight, adapter, chunk=1024):
    groups, rows, _ = near.shape
    depth, width = weight.shape
    count = 2 * groups * rows

    def kernel(near_ref, far_ref, weight_ref, adapter_ref, out_ref, rows_ref):
        for e, source in enumerate((near_ref, far_ref)):
            for j in range(groups):
                rows_ref[pl.ds((e * groups + j) * rows, rows)] = source[j]
        total = jnp.zeros((count, width), jnp.float32)
        for k in range(depth // chunk):
            part = pl.ds(k * chunk, chunk)
            total = total + jnp.dot(
                rows_ref[:, part], weight_ref[part, :], preferred_element_type=jnp.float32
            )
        core = lax.axis_index("batch")
        for e in range(2):
            for j in range(groups):
                place = (e * groups + j) * rows
                device = 2 * j + (core ^ e)
                out_ref[device, :, pl.ds(0, width)] = total[place : place + rows].astype(
                    jnp.bfloat16
                )
                out_ref[device, :, pl.ds(width, LANES)] = adapter_ref[...]

    return call(
        kernel,
        "project_qkv",
        jax.ShapeDtypeStruct((2 * groups, rows, width + LANES), jnp.bfloat16),
        [VMEM, VMEM, VMEM, VMEM],
        weight.size * 2,
        flops=2 * count * weight.size,
        scratch_shapes=[pltpu.VMEM((count, depth), jnp.bfloat16)],
    )(near, far, weight, adapter)


def project_out(rows, weight, chunk=1024):
    count, depth = rows.shape

    def kernel(rows_ref, weight_ref, out_ref):
        total = jnp.zeros(out_ref.shape, jnp.float32)
        for k in range(depth // chunk):
            part = pl.ds(k * chunk, chunk)
            total = total + jnp.dot(
                rows_ref[:, part], weight_ref[part, :], preferred_element_type=jnp.float32
            )
        out_ref[...] = total

    return call(
        kernel,
        "project_out",
        jax.ShapeDtypeStruct((count, weight.shape[1]), jnp.float32),
        [VMEM, VMEM],
        weight.size * 2,
        flops=2 * count * weight.size,
    )(rows, weight)


def batch_of(store_ref, adapter_ref, k):
    return jnp.concatenate(
        [store_ref[adapter_ref[r]] for r in range(k * BATCH, (k + 1) * BATCH)]
    )


def down_partials(rows, adapter, store, copies):
    count = adapter.shape[0]
    rank, depth = store.shape[1:]

    def kernel(adapter_ref, rows_ref, store_ref, out_ref):
        start = pl.multiple_of(lax.axis_index("mp") * depth, depth)
        slices = rows_ref[:, pl.ds(start, depth)]
        row = lax.broadcasted_iota(jnp.int32, (count, LANES), 0)
        lane = lax.broadcasted_iota(jnp.int32, (count, LANES), 1)
        total = jnp.zeros((count, LANES), jnp.float32)
        for k in range(count // BATCH):
            every = lax.dot_general(
                slices,
                batch_of(store_ref, adapter_ref, k),
                (((1,), (1,)), ((), ())),
                preferred_element_type=jnp.float32,
            )
            for s in range(BATCH * rank // LANES):
                first = k * BATCH * rank + s * LANES
                mine = row == (lane + first) // rank
                total = total + jnp.where(mine, every[:, s * LANES : (s + 1) * LANES], 0.0)
        for c in range(copies):
            out_ref[c] = total

    return call(
        kernel,
        "down_partials",
        jax.ShapeDtypeStruct((copies, count, LANES), jnp.float32),
        [SMEM, VMEM, VMEM],
        2 * count * rank * depth,
        limit=4 * MIB,
        flops=2 * count * count * rank * depth,
    )(adapter, rows, store)


def add_up(base, partials, adapter, store):
    count = adapter.shape[0]
    rank, width = store.shape[1:]
    groups = partials.shape[0]

    def kernel(adapter_ref, base_ref, partials_ref, store_ref, out_ref):
        total = partials_ref[0]
        for c in range(1, groups):
            total = total + partials_ref[c]
        down = total.astype(jnp.bfloat16).astype(jnp.float32)
        row = lax.broadcasted_iota(jnp.int32, (count, LANES), 0)
        lane = lax.broadcasted_iota(jnp.int32, (count, LANES), 1)
        delta = jnp.zeros((count, width), jnp.float32)
        for k in range(count // BATCH):
            spread = []
            for s in range(BATCH * rank // LANES):
                first = k * BATCH * rank + s * LANES
                spread.append(jnp.where(row == (lane + first) // rank, down, 0.0))
            spread = jnp.concatenate(spread, 1).astype(jnp.bfloat16)
            delta = delta + jnp.dot(
                spread, batch_of(store_ref, adapter_ref, k), preferred_element_type=jnp.float32
            )
        result = (base_ref[...] + ADAPTER_SCALE * delta).astype(jnp.bfloat16)
        for j in range(groups):
            out_ref[j] = result[j * count // groups : (j + 1) * count // groups]

    return call(
        kernel,
        "add_up",
        jax.ShapeDtypeStruct((groups, count // groups, width), jnp.bfloat16),
        [SMEM, VMEM, VMEM, VMEM],
        2 * count * rank * width,
        limit=4 * MIB,
        flops=2 * count * count * rank * width,
    )(adapter, base, partials, store)


def widen(hidden, after):
    def kernel(hidden_ref, after_ref, out_ref):
        del after_ref
        out_ref[...] = hidden_ref[...].astype(jnp.float32)

    return call(
        kernel,
        "widen",
        jax.ShapeDtypeStruct(hidden.shape, jnp.float32),
        [VMEM, ANY],
        hidden.size * 64,
    )(hidden, after)


def add_rows(hidden, parts):
    width = parts.shape[2]

    def kernel(hidden_ref, parts_ref, out_ref):
        for k in range(parts.shape[0]):
            part = pl.ds(k * width, width)
            total = hidden_ref[:, part] + parts_ref[k].astype(jnp.float32)
            out_ref[:, part] = total.astype(jnp.bfloat16)

    return call(
        kernel,
        "add_rows",
        jax.ShapeDtypeStruct(hidden.shape, parts.dtype),
        [VMEM, VMEM],
        hidden.size * 6,
    )(hidden, parts)


def swap_cores(block):
    return lax.ppermute(block, "batch", [(0, 1), (1, 0)])


def exchange(blocks, axes="mp"):
    return lax.all_to_all(blocks, axes, split_axis=0, concat_axis=0, tiled=True)


def attend(qkv, cosine, sine, key_cache, value_cache, lengths):
    rows = qkv.shape[0]
    query_width = HEADS * HEAD_DIM
    kv_width = KV_HEADS * HEAD_DIM
    group = HEADS // KV_HEADS
    scale = HEAD_DIM ** (-0.5)

    def turn(part):
        vec = part.astype(jnp.float32).reshape(rows, -1, HEAD_DIM)
        half = HEAD_DIM // 2
        turned = jnp.concatenate([-vec[..., half:], vec[..., :half]], -1)
        return (vec * cosine[:, None] + turned * sine[:, None]).astype(jnp.bfloat16)

    query = turn(qkv[:, :query_width])
    fresh_key = turn(qkv[:, query_width : query_width + kv_width])
    fresh_value = (
        qkv[:, query_width + kv_width :].astype(jnp.float32).reshape(rows, KV_HEADS, HEAD_DIM)
    )
    grouped = query.reshape(rows, KV_HEADS, group, HEAD_DIM)
    cached = key_cache.reshape(rows, -1, KV_HEADS, HEAD_DIM)
    stored = value_cache.reshape(rows, -1, KV_HEADS, HEAD_DIM)
    scores = (
        jnp.einsum("rgqd,rtgd->rgqt", grouped, cached, preferred_element_type=jnp.float32) * scale
    )
    live = jnp.arange(cached.shape[1])[None, :] < lengths[:, None]
    scores = jnp.where(live[:, None, None, :], scores, -jnp.inf)
    own = (
        jnp.einsum("rgqd,rgd->rgq", grouped, fresh_key, preferred_element_type=jnp.float32) * scale
    )
    top = jnp.maximum(jnp.max(scores, -1), own)
    expo = jnp.exp(scores - top[..., None])
    own_exp = jnp.exp(own - top)
    total = jnp.sum(expo, -1) + own_exp
    probs = (expo / total[..., None]).astype(jnp.bfloat16)
    own_prob = (own_exp / total).astype(jnp.bfloat16)
    context_vector = jnp.einsum(
        "rgqt,rtgd->rgqd", probs, stored, preferred_element_type=jnp.float32
    )
    context_vector = (
        context_vector + own_prob.astype(jnp.float32)[..., None] * fresh_value[:, :, None, :]
    )
    return context_vector.reshape(rows, query_width).astype(jnp.bfloat16)


def angles(lengths):
    half = HEAD_DIM // 2
    freq = THETA ** (-(jnp.arange(half, dtype=jnp.float32) * 2.0) / HEAD_DIM)
    angle = lengths.astype(jnp.float32)[:, None] * freq
    cosine, sine = jnp.cos(angle), jnp.sin(angle)
    return jnp.concatenate([cosine, cosine], -1), jnp.concatenate([sine, sine], -1)


def fast_body(
    hidden,
    attention_norm_gain,
    query_key_value_weight,
    output_weight,
    key_cache,
    value_cache,
    lengths,
    slots,
    requests,
    adapter_down_matrices,
    adapter_up_matrices,
):
    rows = hidden.shape[0]
    mp_size = lax.axis_size("mp")
    width = query_key_value_weight.shape[1]

    slot_hits = slots[:, None] == jnp.arange(requests.shape[1])[None, :]
    adapter = jnp.sum(jnp.where(slot_hits, requests[0][None, :], 0), 1)
    adapter = jnp.broadcast_to(adapter[:, None], (rows, LANES)).astype(jnp.bfloat16)
    cosine, sine = angles(lengths)

    near = exchange(norm_rows(hidden, attention_norm_gain, mp_size))
    columns = project_qkv(near, swap_cores(near), query_key_value_weight, adapter)
    mixed = exchange(columns, ("mp", "batch"))
    adapter = mixed.reshape(mp_size, -1, rows, width + LANES)[:, :, :, width]
    adapter = lax.dynamic_index_in_dim(adapter, lax.axis_index("batch"), 1, keepdims=False)
    adapter = adapter.reshape(-1).astype(jnp.int32)
    qkv = mixed[:, :, :width].transpose(1, 0, 2).reshape(rows, -1)

    context = attend(qkv, cosine, sine, key_cache, value_cache, lengths)
    copies = jnp.broadcast_to(context[None], (mp_size, *context.shape))
    gathered = exchange(copies).reshape(-1, context.shape[1])

    partials = exchange(
        down_partials(gathered, adapter, adapter_down_matrices.swapaxes(1, 2), mp_size)
    )
    base = project_out(gathered, output_weight)
    projected = add_up(base, partials, adapter, adapter_up_matrices)
    returned = exchange(projected)
    return add_rows(widen(hidden, projected), returned)


def body(*arguments):
    small = lax.axis_size("mp") <= 16 and lax.axis_size("batch") == 2
    whole_heads = arguments[2].shape[1] % HEAD_DIM == 0
    return (fast_body if small and whole_heads else general_body)(*arguments)


def solution(mesh):
    in_specs = (
        P(("groups", "mp", "batch"), None),
        P(),
        P(None, ("mp", "batch")),
        P(None, "mp"),
        P(("groups", "mp", "batch"), None, None),
        P(("groups", "mp", "batch"), None, None),
        P(("groups", "mp", "batch")),
        P(("groups", "mp", "batch")),
        P(("groups", "mp", "batch"), None),
        P(None, "mp", None),
        P(None, None, "mp"),
    )
    out_specs = P(("groups", "mp", "batch"), None)
    return jax.shard_map(body, mesh=mesh, in_specs=in_specs, out_specs=out_specs, check_vma=False)
```

```python
import jax
import jax.numpy as jnp
from jax import lax
from jax.experimental import pallas as pl
from jax.experimental.pallas import tpu as pltpu
from jax.sharding import PartitionSpec as P

HEADS = 64
KV_HEADS = 8
HEAD_DIM = 128
ADAPTER_COUNT = 64


EPS = 1e-05
THETA = 500000.0
ADAPTER_SCALE = 2.0


def rotate(vec, pos):
    width = vec.shape[-1]
    half = width // 2
    freq = THETA ** (-(jnp.arange(half, dtype=jnp.float32) * 2.0) / width)
    angle = pos[..., None, None] * freq
    cosine = jnp.concatenate([jnp.cos(angle), jnp.cos(angle)], -1)
    sine = jnp.concatenate([jnp.sin(angle), jnp.sin(angle)], -1)
    turned = jnp.concatenate([-vec[..., half:], vec[..., :half]], -1)
    return vec * cosine + turned * sine


def apply_up_matrix(
    context_vector, adapter_selector, down_result, output_weight, adapter_up_matrices
):
    base_output = jnp.dot(context_vector, output_weight, preferred_element_type=jnp.float32)
    spread = (adapter_selector[:, :, None] * down_result[:, None, :]).reshape(
        adapter_selector.shape[0], -1
    )
    adapter_table = adapter_up_matrices.reshape(-1, adapter_up_matrices.shape[2])
    adapter_delta = jnp.dot(spread, adapter_table, preferred_element_type=jnp.float32)
    return (base_output + ADAPTER_SCALE * adapter_delta).astype(jnp.bfloat16)


def general_body(
    hidden,
    attention_norm_gain,
    query_key_value_weight,
    output_weight,
    key_cache,
    value_cache,
    lengths,
    slots,
    requests,
    adapter_down_matrices,
    adapter_up_matrices,
):
    widened = hidden.astype(jnp.float32)
    normed = (
        widened
        * lax.rsqrt(jnp.mean(widened * widened, -1, keepdims=True) + EPS)
        * attention_norm_gain.astype(jnp.float32)
    ).astype(jnp.bfloat16)
    rows = normed.shape[0]
    columns = jnp.dot(
        lax.all_gather(normed, ("mp", "batch"), axis=0, tiled=True),
        query_key_value_weight,
        preferred_element_type=jnp.float32,
    ).astype(jnp.bfloat16)
    mixed = lax.all_to_all(
        lax.all_to_all(columns, "mp", split_axis=0, concat_axis=1, tiled=True),
        "batch",
        split_axis=0,
        concat_axis=1,
        tiled=True,
    )
    width = query_key_value_weight.shape[1]
    qkv = (
        mixed.reshape(rows, lax.axis_size("batch"), lax.axis_size("mp"), width)
        .transpose(0, 2, 1, 3)
        .reshape(rows, -1)
    )
    query_width = HEADS * HEAD_DIM
    kv_width = KV_HEADS * HEAD_DIM
    group = HEADS // KV_HEADS
    scale = HEAD_DIM ** (-0.5)
    pos = lengths.astype(jnp.float32)
    query = rotate(
        qkv[:, :query_width].astype(jnp.float32).reshape(rows, HEADS, HEAD_DIM), pos
    ).astype(jnp.bfloat16)
    fresh_key = rotate(
        qkv[:, query_width : query_width + kv_width]
        .astype(jnp.float32)
        .reshape(rows, KV_HEADS, HEAD_DIM),
        pos,
    ).astype(jnp.bfloat16)
    fresh_value = (
        qkv[:, query_width + kv_width :].astype(jnp.float32).reshape(rows, KV_HEADS, HEAD_DIM)
    )
    grouped = query.reshape(rows, KV_HEADS, group, HEAD_DIM)
    cached = key_cache.reshape(rows, -1, KV_HEADS, HEAD_DIM)
    stored = value_cache.reshape(rows, -1, KV_HEADS, HEAD_DIM)
    scores = (
        jnp.einsum("rgqd,rtgd->rgqt", grouped, cached, preferred_element_type=jnp.float32) * scale
    )
    live = jnp.arange(cached.shape[1])[None, :] < lengths[:, None]
    scores = jnp.where(live[:, None, None, :], scores, -jnp.inf)
    own = (
        jnp.einsum("rgqd,rgd->rgq", grouped, fresh_key, preferred_element_type=jnp.float32) * scale
    )
    top = jnp.maximum(jnp.max(scores, -1), own)
    expo = jnp.exp(scores - top[..., None])
    own_exp = jnp.exp(own - top)
    total = jnp.sum(expo, -1) + own_exp
    probs = (expo / total[..., None]).astype(jnp.bfloat16)
    own_prob = (own_exp / total).astype(jnp.bfloat16)
    context_vector = jnp.einsum(
        "rgqt,rtgd->rgqd", probs, stored, preferred_element_type=jnp.float32
    )
    context_vector = (
        context_vector + own_prob.astype(jnp.float32)[..., None] * fresh_value[:, :, None, :]
    )
    context_vector = context_vector.reshape(rows, query_width).astype(jnp.bfloat16)
    slot_hits = slots[:, None] == jnp.arange(requests.shape[1])[None, :]
    adapter = jnp.sum(jnp.where(slot_hits, requests[0][None, :], 0), 1)
    adapter_selector = (adapter[:, None] == jnp.arange(ADAPTER_COUNT)[None, :]).astype(jnp.bfloat16)
    context_gathered, selector_gathered = (
        lax.all_gather(context_vector, "mp", axis=0, tiled=True),
        lax.all_gather(adapter_selector, "mp", axis=0, tiled=True),
    )
    shared_portion = adapter_down_matrices.shape[1]
    context_slice = lax.dynamic_slice_in_dim(
        context_gathered, lax.axis_index("mp") * shared_portion, shared_portion, 1
    )
    every_adapter = jnp.einsum(
        "gh,thy->gty", context_slice, adapter_down_matrices, preferred_element_type=jnp.float32
    )
    partial_down = jnp.sum(every_adapter * selector_gathered.astype(jnp.float32)[:, :, None], 1)
    down_gathered = lax.psum(partial_down, "mp").astype(jnp.bfloat16)
    projection_result = apply_up_matrix(
        context_gathered, selector_gathered, down_gathered, output_weight, adapter_up_matrices
    )
    returned = lax.all_to_all(projection_result, "mp", split_axis=0, concat_axis=1, tiled=True)
    return (widened + returned.astype(jnp.float32)).astype(jnp.bfloat16)


MIB = 1 << 20
LANES = 128
BATCH = 4
STREAM = 53 * MIB
VMEM = pl.BlockSpec(memory_space=pltpu.VMEM)
SMEM = pl.BlockSpec(memory_space=pltpu.SMEM)
ANY = pl.BlockSpec(memory_space=pl.ANY)


def call(kernel, name, out_shape, in_specs, moved, limit=2 * MIB, flops=0, **options):
    return pl.pallas_call(
        kernel,
        out_shape=out_shape,
        in_specs=in_specs,
        out_specs=jax.tree.map(lambda _: VMEM, out_shape),
        compiler_params=pltpu.CompilerParams(vmem_limit_bytes=limit),
        cost_estimate=pl.CostEstimate(flops=flops, bytes_accessed=moved, transcendentals=0),
        name=name,
        **options,
    )


def norm_rows(hidden, gain, copies):
    rows, width = hidden.shape

    def kernel(hidden_ref, gain_ref, out_ref):
        wide = hidden_ref[...].astype(jnp.float32)
        inverse = lax.rsqrt(jnp.mean(wide * wide, -1, keepdims=True) + EPS)
        for k in range(width // LANES):
            part = pl.ds(k * LANES, LANES)
            normed = hidden_ref[:, part].astype(jnp.float32) * inverse
            normed = normed * gain_ref[k : k + 1, :].astype(jnp.float32)
            normed = normed.astype(jnp.bfloat16)
            for c in range(copies):
                out_ref[c, :, part] = normed

    return call(
        kernel,
        "norm_rows",
        jax.ShapeDtypeStruct((copies, rows, width), jnp.bfloat16),
        [VMEM, VMEM],
        hidden.size * 2 * (copies + 1),
    )(hidden, gain.reshape(-1, LANES))


def project_qkv(near, far, weight, adapter, chunk=1024):
    groups, rows, _ = near.shape
    depth, width = weight.shape
    count = 2 * groups * rows

    def kernel(near_ref, far_ref, weight_ref, adapter_ref, out_ref, rows_ref):
        for e, source in enumerate((near_ref, far_ref)):
            for j in range(groups):
                rows_ref[pl.ds((e * groups + j) * rows, rows)] = source[j]
        total = jnp.zeros((count, width), jnp.float32)
        for k in range(depth // chunk):
            part = pl.ds(k * chunk, chunk)
            total = total + jnp.dot(
                rows_ref[:, part], weight_ref[part, :], preferred_element_type=jnp.float32
            )
        core = lax.axis_index("batch")
        for e in range(2):
            for j in range(groups):
                place = (e * groups + j) * rows
                device = 2 * j + (core ^ e)
                out_ref[device, :, pl.ds(0, width)] = total[place : place + rows].astype(
                    jnp.bfloat16
                )
                out_ref[device, :, pl.ds(width, LANES)] = (
                    adapter_ref[...] if e == 0 else jnp.zeros_like(adapter_ref)
                )

    return call(
        kernel,
        "project_qkv",
        jax.ShapeDtypeStruct((2 * groups, rows, width + LANES), jnp.bfloat16),
        [VMEM, VMEM, VMEM, VMEM],
        weight.size * 2,
        flops=2 * count * weight.size,
        scratch_shapes=[pltpu.VMEM((count, depth), jnp.bfloat16)],
    )(near, far, weight, adapter)


def stream(weight_ref, held_ref, sems, parts):
    depth = held_ref.shape[0] // parts
    copies = []
    for k in range(parts):
        rows = pl.ds(k * depth, depth)
        copies.append(
            pltpu.make_async_copy(weight_ref.at[rows], held_ref.at[rows], sems.at[k])
        )
        copies[-1].start()

    def part(k):
        copies[k].wait()
        return held_ref[pl.ds(k * depth, depth)]

    return part


def project_out(gathered, weight, parts=16):
    groups, rows, depth = gathered.shape
    count, step = groups * rows, depth // parts

    def kernel(gathered_ref, weight_ref, out_ref, rows_ref, held_ref, sems):
        part = stream(weight_ref, held_ref, sems, parts)
        for j in range(groups):
            rows_ref[pl.ds(j * rows, rows)] = gathered_ref[j]
        total = jnp.zeros(out_ref.shape, jnp.float32)
        for k in range(parts):
            total = total + jnp.dot(
                rows_ref[:, pl.ds(k * step, step)], part(k), preferred_element_type=jnp.float32
            )
        out_ref[...] = total

    return call(
        kernel,
        "project_out",
        jax.ShapeDtypeStruct((count, weight.shape[1]), jnp.float32),
        [VMEM, ANY],
        weight.size * 2,
        limit=STREAM,
        flops=2 * count * weight.size,
        scratch_shapes=[
            pltpu.VMEM((count, depth), gathered.dtype),
            pltpu.VMEM(weight.shape, weight.dtype),
            pltpu.SemaphoreType.DMA((parts,)),
        ],
    )(gathered, weight)


def down_partials(gathered, adapter, store):
    groups, rows, _ = gathered.shape
    count = groups * rows
    rank, depth = store.shape[1:]

    def kernel(adapter_ref, gathered_ref, store_ref, out_ref, rows_ref):
        start = pl.multiple_of(lax.axis_index("mp") * depth, depth)
        for j in range(groups):
            rows_ref[pl.ds(j * rows, rows)] = gathered_ref[j, :, pl.ds(start, depth)]
        row = lax.broadcasted_iota(jnp.int32, (count, LANES), 0)
        lane = lax.broadcasted_iota(jnp.int32, (count, LANES), 1)
        total = jnp.zeros((count, LANES), jnp.float32)
        for k in range(count // BATCH):
            chosen = [adapter_ref[r // rows, r % rows] for r in range(k * BATCH, (k + 1) * BATCH)]
            every = lax.dot_general(
                rows_ref[...],
                jnp.concatenate([store_ref[c] for c in chosen]),
                (((1,), (1,)), ((), ())),
                preferred_element_type=jnp.float32,
            )
            for s in range(BATCH * rank // LANES):
                first = k * BATCH * rank + s * LANES
                mine = row == (lane + first) // rank
                total = total + jnp.where(mine, every[:, s * LANES : (s + 1) * LANES], 0.0)
        for c in range(groups):
            out_ref[c] = total

    return call(
        kernel,
        "down_partials",
        jax.ShapeDtypeStruct((groups, count, LANES), jnp.float32),
        [SMEM, VMEM, VMEM],
        2 * count * rank * depth,
        limit=4 * MIB,
        flops=2 * count * count * rank * depth,
        scratch_shapes=[pltpu.VMEM((count, depth), gathered.dtype)],
    )(adapter, gathered, store)


def pick(adapter_ref, store_ref, held_ref, sems):
    groups, rows = adapter_ref.shape
    count, rank = groups * rows, store_ref.shape[1]
    copies = []
    for r in range(count):
        copies.append(
            pltpu.make_async_copy(
                store_ref.at[adapter_ref[r // rows, r % rows]], held_ref.at[pl.ds(r * rank, rank)], sems.at[r]
            )
        )
        copies[-1].start()

    def batch(k):
        for copy in copies[k * BATCH : (k + 1) * BATCH]:
            copy.wait()
        return held_ref[pl.ds(k * BATCH * rank, BATCH * rank)]

    return batch


def add_up(base, partials, adapter, store):
    count = adapter.size
    rank, width = store.shape[1:]
    groups = partials.shape[0]

    def kernel(adapter_ref, base_ref, partials_ref, store_ref, out_ref, held_ref, sems):
        batch = pick(adapter_ref, store_ref, held_ref, sems)
        total = partials_ref[0]
        for c in range(1, groups):
            total = total + partials_ref[c]
        down = total.astype(jnp.bfloat16).astype(jnp.float32)
        row = lax.broadcasted_iota(jnp.int32, (count, LANES), 0)
        lane = lax.broadcasted_iota(jnp.int32, (count, LANES), 1)
        delta = jnp.zeros((count, width), jnp.float32)
        for k in range(count // BATCH):
            spread = []
            for s in range(BATCH * rank // LANES):
                first = k * BATCH * rank + s * LANES
                spread.append(jnp.where(row == (lane + first) // rank, down, 0.0))
            spread = jnp.concatenate(spread, 1).astype(jnp.bfloat16)
            delta = delta + jnp.dot(
                spread, batch(k), preferred_element_type=jnp.float32
            )
        result = (base_ref[...] + ADAPTER_SCALE * delta).astype(jnp.bfloat16)
        for j in range(groups):
            out_ref[j] = result[j * count // groups : (j + 1) * count // groups]

    return call(
        kernel,
        "add_up",
        jax.ShapeDtypeStruct((groups, count // groups, width), jnp.bfloat16),
        [SMEM, VMEM, VMEM, ANY],
        2 * count * rank * width,
        limit=STREAM,
        flops=2 * count * count * rank * width,
        scratch_shapes=[
            pltpu.VMEM((count * rank, width), store.dtype),
            pltpu.SemaphoreType.DMA((count,)),
        ],
    )(adapter, base, partials, store)


def add_rows(hidden, parts):
    width = parts.shape[2]

    def kernel(hidden_ref, parts_ref, out_ref):
        for k in range(parts.shape[0]):
            part = pl.ds(k * width, width)
            total = hidden_ref[:, part].astype(jnp.float32) + parts_ref[k].astype(jnp.float32)
            out_ref[:, part] = total.astype(jnp.bfloat16)

    return call(
        kernel,
        "add_rows",
        jax.ShapeDtypeStruct(hidden.shape, parts.dtype),
        [VMEM, VMEM],
        hidden.size * 6,
    )(hidden, parts)


def swap_cores(block):
    return lax.ppermute(block, "batch", [(0, 1), (1, 0)])


def exchange(blocks, axes="mp"):
    return lax.all_to_all(blocks, axes, split_axis=0, concat_axis=0, tiled=True)


def attend(qkv, cosine, sine, key_cache, value_cache, live):
    rows = qkv.shape[0]
    query_width = HEADS * HEAD_DIM
    kv_width = KV_HEADS * HEAD_DIM
    group = HEADS // KV_HEADS
    scale = HEAD_DIM ** (-0.5)

    def turn(part):
        vec = part.astype(jnp.float32).reshape(rows, -1, HEAD_DIM)
        half = HEAD_DIM // 2
        turned = jnp.concatenate([-vec[..., half:], vec[..., :half]], -1)
        return (vec * cosine[:, None] + turned * sine[:, None]).astype(jnp.bfloat16)

    query = turn(qkv[:, :query_width])
    fresh_key = turn(qkv[:, query_width : query_width + kv_width])
    fresh_value = (
        qkv[:, query_width + kv_width :].astype(jnp.float32).reshape(rows, KV_HEADS, HEAD_DIM)
    )
    grouped = query.reshape(rows, KV_HEADS, group, HEAD_DIM)
    cached = key_cache.reshape(rows, -1, KV_HEADS, HEAD_DIM)
    stored = value_cache.reshape(rows, -1, KV_HEADS, HEAD_DIM)
    scores = (
        jnp.einsum("rgqd,rtgd->rgqt", grouped, cached, preferred_element_type=jnp.float32) * scale
    )
    scores = jnp.where(live[:, None, None, :], scores, -jnp.inf)
    own = (
        jnp.einsum("rgqd,rgd->rgq", grouped, fresh_key, preferred_element_type=jnp.float32) * scale
    )
    top = jnp.maximum(jnp.max(scores, -1), own)
    expo = jnp.exp(scores - top[..., None])
    own_exp = jnp.exp(own - top)
    total = jnp.sum(expo, -1) + own_exp
    probs = (expo / total[..., None]).astype(jnp.bfloat16)
    own_prob = (own_exp / total).astype(jnp.bfloat16)
    context_vector = jnp.einsum(
        "rgqt,rtgd->rgqd", probs, stored, preferred_element_type=jnp.float32
    )
    context_vector = (
        context_vector + own_prob.astype(jnp.float32)[..., None] * fresh_value[:, :, None, :]
    )
    return context_vector.reshape(rows, query_width).astype(jnp.bfloat16)


def angles(lengths):
    half = HEAD_DIM // 2
    freq = THETA ** (-(jnp.arange(half, dtype=jnp.float32) * 2.0) / HEAD_DIM)
    angle = lengths.astype(jnp.float32)[:, None] * freq
    cosine, sine = jnp.cos(angle), jnp.sin(angle)
    return jnp.concatenate([cosine, cosine], -1), jnp.concatenate([sine, sine], -1)


def fast_body(
    hidden,
    attention_norm_gain,
    query_key_value_weight,
    output_weight,
    key_cache,
    value_cache,
    lengths,
    slots,
    requests,
    adapter_down_matrices,
    adapter_up_matrices,
):
    rows = hidden.shape[0]
    mp_size = lax.axis_size("mp")
    width = query_key_value_weight.shape[1]

    near = exchange(norm_rows(hidden, attention_norm_gain, mp_size))
    far = swap_cores(near)

    near, lengths, slots, requests = lax.optimization_barrier((near, lengths, slots, requests))
    slot_hits = slots[:, None] == jnp.arange(requests.shape[1])[None, :]
    adapter = jnp.sum(jnp.where(slot_hits, requests[0][None, :], 0), 1)
    adapter = jnp.broadcast_to(adapter[:, None], (rows, LANES)).astype(jnp.bfloat16)
    cosine, sine = angles(lengths)
    live = jnp.arange(key_cache.shape[1])[None, :] < lengths[:, None]
    far, cosine, sine, live = lax.optimization_barrier((far, cosine, sine, live))

    columns = project_qkv(near, far, query_key_value_weight, adapter)
    mixed = exchange(columns, ("mp", "batch"))
    adapter = mixed.reshape(mp_size, -1, rows, width + LANES)[:, :, :, width]
    adapter = jnp.sum(adapter.astype(jnp.float32), 1).astype(jnp.int32)
    qkv = mixed[:, :, :width].transpose(1, 0, 2).reshape(rows, -1)

    context = attend(qkv, cosine, sine, key_cache, value_cache, live)
    context, adapter = lax.optimization_barrier((context, adapter))
    gathered = exchange(jnp.broadcast_to(context[None], (mp_size, *context.shape)))

    partials = exchange(
        down_partials(gathered, adapter, adapter_down_matrices.swapaxes(1, 2))
    )
    base = project_out(gathered, output_weight)
    projected = add_up(base, partials, adapter, adapter_up_matrices)
    return add_rows(hidden, exchange(projected))


def body(*arguments):
    small = lax.axis_size("mp") <= 16 and lax.axis_size("batch") == 2
    whole_heads = arguments[2].shape[1] % HEAD_DIM == 0
    return (fast_body if small and whole_heads else general_body)(*arguments)


def solution(mesh):
    in_specs = (
        P(("groups", "mp", "batch"), None),
        P(),
        P(None, ("mp", "batch")),
        P(None, "mp"),
        P(("groups", "mp", "batch"), None, None),
        P(("groups", "mp", "batch"), None, None),
        P(("groups", "mp", "batch")),
        P(("groups", "mp", "batch")),
        P(("groups", "mp", "batch"), None),
        P(None, "mp", None),
        P(None, None, "mp"),
    )
    out_specs = P(("groups", "mp", "batch"), None)
    return jax.shard_map(body, mesh=mesh, in_specs=in_specs, out_specs=out_specs, check_vma=False)
```

```python
import jax
import jax.numpy as jnp
from jax import lax
from jax.experimental import pallas as pl
from jax.experimental.pallas import tpu as pltpu
from jax.sharding import PartitionSpec as P

HEADS = 64
KV_HEADS = 8
HEAD_DIM = 128
ADAPTER_COUNT = 64


EPS = 1e-05
THETA = 500000.0
ADAPTER_SCALE = 2.0


def rotate(vec, pos):
    width = vec.shape[-1]
    half = width // 2
    freq = THETA ** (-(jnp.arange(half, dtype=jnp.float32) * 2.0) / width)
    angle = pos[..., None, None] * freq
    cosine = jnp.concatenate([jnp.cos(angle), jnp.cos(angle)], -1)
    sine = jnp.concatenate([jnp.sin(angle), jnp.sin(angle)], -1)
    turned = jnp.concatenate([-vec[..., half:], vec[..., :half]], -1)
    return vec * cosine + turned * sine


def apply_up_matrix(
    context_vector, adapter_selector, down_result, output_weight, adapter_up_matrices
):
    base_output = jnp.dot(context_vector, output_weight, preferred_element_type=jnp.float32)
    spread = (adapter_selector[:, :, None] * down_result[:, None, :]).reshape(
        adapter_selector.shape[0], -1
    )
    adapter_table = adapter_up_matrices.reshape(-1, adapter_up_matrices.shape[2])
    adapter_delta = jnp.dot(spread, adapter_table, preferred_element_type=jnp.float32)
    return (base_output + ADAPTER_SCALE * adapter_delta).astype(jnp.bfloat16)


def general_body(
    hidden,
    attention_norm_gain,
    query_key_value_weight,
    output_weight,
    key_cache,
    value_cache,
    lengths,
    slots,
    requests,
    adapter_down_matrices,
    adapter_up_matrices,
):
    widened = hidden.astype(jnp.float32)
    normed = (
        widened
        * lax.rsqrt(jnp.mean(widened * widened, -1, keepdims=True) + EPS)
        * attention_norm_gain.astype(jnp.float32)
    ).astype(jnp.bfloat16)
    rows = normed.shape[0]
    columns = jnp.dot(
        lax.all_gather(normed, ("mp", "batch"), axis=0, tiled=True),
        query_key_value_weight,
        preferred_element_type=jnp.float32,
    ).astype(jnp.bfloat16)
    mixed = lax.all_to_all(
        lax.all_to_all(columns, "mp", split_axis=0, concat_axis=1, tiled=True),
        "batch",
        split_axis=0,
        concat_axis=1,
        tiled=True,
    )
    width = query_key_value_weight.shape[1]
    qkv = (
        mixed.reshape(rows, lax.axis_size("batch"), lax.axis_size("mp"), width)
        .transpose(0, 2, 1, 3)
        .reshape(rows, -1)
    )
    query_width = HEADS * HEAD_DIM
    kv_width = KV_HEADS * HEAD_DIM
    group = HEADS // KV_HEADS
    scale = HEAD_DIM ** (-0.5)
    pos = lengths.astype(jnp.float32)
    query = rotate(
        qkv[:, :query_width].astype(jnp.float32).reshape(rows, HEADS, HEAD_DIM), pos
    ).astype(jnp.bfloat16)
    fresh_key = rotate(
        qkv[:, query_width : query_width + kv_width]
        .astype(jnp.float32)
        .reshape(rows, KV_HEADS, HEAD_DIM),
        pos,
    ).astype(jnp.bfloat16)
    fresh_value = (
        qkv[:, query_width + kv_width :].astype(jnp.float32).reshape(rows, KV_HEADS, HEAD_DIM)
    )
    grouped = query.reshape(rows, KV_HEADS, group, HEAD_DIM)
    cached = key_cache.reshape(rows, -1, KV_HEADS, HEAD_DIM)
    stored = value_cache.reshape(rows, -1, KV_HEADS, HEAD_DIM)
    scores = (
        jnp.einsum("rgqd,rtgd->rgqt", grouped, cached, preferred_element_type=jnp.float32) * scale
    )
    live = jnp.arange(cached.shape[1])[None, :] < lengths[:, None]
    scores = jnp.where(live[:, None, None, :], scores, -jnp.inf)
    own = (
        jnp.einsum("rgqd,rgd->rgq", grouped, fresh_key, preferred_element_type=jnp.float32) * scale
    )
    top = jnp.maximum(jnp.max(scores, -1), own)
    expo = jnp.exp(scores - top[..., None])
    own_exp = jnp.exp(own - top)
    total = jnp.sum(expo, -1) + own_exp
    probs = (expo / total[..., None]).astype(jnp.bfloat16)
    own_prob = (own_exp / total).astype(jnp.bfloat16)
    context_vector = jnp.einsum(
        "rgqt,rtgd->rgqd", probs, stored, preferred_element_type=jnp.float32
    )
    context_vector = (
        context_vector + own_prob.astype(jnp.float32)[..., None] * fresh_value[:, :, None, :]
    )
    context_vector = context_vector.reshape(rows, query_width).astype(jnp.bfloat16)
    slot_hits = slots[:, None] == jnp.arange(requests.shape[1])[None, :]
    adapter = jnp.sum(jnp.where(slot_hits, requests[0][None, :], 0), 1)
    adapter_selector = (adapter[:, None] == jnp.arange(ADAPTER_COUNT)[None, :]).astype(jnp.bfloat16)
    context_gathered, selector_gathered = (
        lax.all_gather(context_vector, "mp", axis=0, tiled=True),
        lax.all_gather(adapter_selector, "mp", axis=0, tiled=True),
    )
    shared_portion = adapter_down_matrices.shape[1]
    context_slice = lax.dynamic_slice_in_dim(
        context_gathered, lax.axis_index("mp") * shared_portion, shared_portion, 1
    )
    every_adapter = jnp.einsum(
        "gh,thy->gty", context_slice, adapter_down_matrices, preferred_element_type=jnp.float32
    )
    partial_down = jnp.sum(every_adapter * selector_gathered.astype(jnp.float32)[:, :, None], 1)
    down_gathered = lax.psum(partial_down, "mp").astype(jnp.bfloat16)
    projection_result = apply_up_matrix(
        context_gathered, selector_gathered, down_gathered, output_weight, adapter_up_matrices
    )
    returned = lax.all_to_all(projection_result, "mp", split_axis=0, concat_axis=1, tiled=True)
    return (widened + returned.astype(jnp.float32)).astype(jnp.bfloat16)


MIB = 1 << 20
LANES = 128
BATCH = 4
STREAM = 53 * MIB
VMEM = pl.BlockSpec(memory_space=pltpu.VMEM)
SMEM = pl.BlockSpec(memory_space=pltpu.SMEM)
ANY = pl.BlockSpec(memory_space=pl.ANY)


def call(kernel, name, out_shape, in_specs, moved, limit=2 * MIB, flops=0, **options):
    return pl.pallas_call(
        kernel,
        out_shape=out_shape,
        in_specs=in_specs,
        out_specs=jax.tree.map(lambda _: VMEM, out_shape),
        compiler_params=pltpu.CompilerParams(vmem_limit_bytes=limit),
        cost_estimate=pl.CostEstimate(flops=flops, bytes_accessed=moved, transcendentals=0),
        name=name,
        **options,
    )


def both_halves(frequency):
    def kernel(frequency_ref, out_ref):
        out_ref[...] = jnp.concatenate([frequency_ref[...], frequency_ref[...]], 1)

    return call(
        kernel,
        "both_halves",
        jax.ShapeDtypeStruct((1, 2 * frequency.shape[1]), frequency.dtype),
        [VMEM],
        16 * MIB,
    )(frequency)


def norm_rows(hidden, gain, frequency, lengths, slots, requests, copies):
    rows, width = hidden.shape
    numbers = (lengths, slots, requests)

    def kernel(hidden_ref, gain_ref, frequency_ref, *refs):
        sources, (out_ref, angle_ref, adapter_ref) = refs[:3], refs[3:6]
        held, sems = refs[6:9], refs[9]
        fetches = []
        for k in range(3):
            fetches.append(pltpu.make_async_copy(sources[k], held[k], sems.at[k]))
            fetches[-1].start()
        wide = hidden_ref[...].astype(jnp.float32)
        inverse = lax.rsqrt(jnp.mean(wide * wide, -1, keepdims=True) + EPS)
        for k in range(width // LANES):
            part = pl.ds(k * LANES, LANES)
            normed = hidden_ref[:, part].astype(jnp.float32) * inverse
            normed = normed * gain_ref[k : k + 1, :].astype(jnp.float32)
            normed = normed.astype(jnp.bfloat16)
            for c in range(copies):
                out_ref[c, :, part] = normed
        for fetch in fetches:
            fetch.wait()
        lengths_ref, slots_ref, requests_ref = held
        row = lax.broadcasted_iota(jnp.int32, (rows, LANES), 0)
        position = jnp.zeros((rows, LANES), jnp.float32)
        adapter = jnp.zeros((rows, LANES), jnp.float32)
        for r in range(rows):
            chosen = requests_ref[0, slots_ref[r]]
            position = jnp.where(row == r, lengths_ref[r].astype(jnp.float32), position)
            adapter = jnp.where(row == r, chosen.astype(jnp.float32), adapter)
        angle_ref[0] = position
        angle_ref[1] = position * frequency_ref[...]
        adapter_ref[...] = adapter.astype(jnp.bfloat16)

    return call(
        kernel,
        "norm_rows",
        (
            jax.ShapeDtypeStruct((copies, rows, width), jnp.bfloat16),
            jax.ShapeDtypeStruct((2, rows, LANES), jnp.float32),
            jax.ShapeDtypeStruct((rows, LANES), jnp.bfloat16),
        ),
        [VMEM] * 3 + [ANY] * 3,
        32 * MIB,
        scratch_shapes=[pltpu.SMEM(n.shape, n.dtype) for n in numbers]
        + [pltpu.SemaphoreType.DMA((3,))],
    )(hidden, gain.reshape(-1, LANES), frequency, *numbers)


def project_qkv(near, far, weight, adapter, chunk=1024):
    groups, rows, _ = near.shape
    depth, width = weight.shape
    count = 2 * groups * rows

    def kernel(near_ref, far_ref, weight_ref, adapter_ref, out_ref, rows_ref):
        for e, source in enumerate((near_ref, far_ref)):
            for j in range(groups):
                rows_ref[pl.ds((e * groups + j) * rows, rows)] = source[j]
        total = jnp.zeros((count, width), jnp.float32)
        for k in range(depth // chunk):
            part = pl.ds(k * chunk, chunk)
            total = total + jnp.dot(
                rows_ref[:, part], weight_ref[part, :], preferred_element_type=jnp.float32
            )
        core = lax.axis_index("batch")
        for e in range(2):
            for j in range(groups):
                place = (e * groups + j) * rows
                device = 2 * j + (core ^ e)
                out_ref[device, :, pl.ds(0, width)] = total[place : place + rows].astype(
                    jnp.bfloat16
                )
                out_ref[device, :, pl.ds(width, LANES)] = (
                    adapter_ref[...] if e == 0 else jnp.zeros_like(adapter_ref)
                )

    return call(
        kernel,
        "project_qkv",
        jax.ShapeDtypeStruct((2 * groups, rows, width + LANES), jnp.bfloat16),
        [VMEM, VMEM, VMEM, VMEM],
        weight.size * 2,
        flops=2 * count * weight.size,
        scratch_shapes=[pltpu.VMEM((count, depth), jnp.bfloat16)],
    )(near, far, weight, adapter)


def stream(weight_ref, held_ref, sems, parts):
    depth = held_ref.shape[0] // parts
    copies = []
    for k in range(parts):
        rows = pl.ds(k * depth, depth)
        copies.append(
            pltpu.make_async_copy(weight_ref.at[rows], held_ref.at[rows], sems.at[k])
        )
        copies[-1].start()

    def part(k):
        copies[k].wait()
        return held_ref[pl.ds(k * depth, depth)]

    return part


def project_out(gathered, weight, parts=16):
    groups, rows, depth = gathered.shape
    count, step = groups * rows, depth // parts

    def kernel(gathered_ref, weight_ref, out_ref, rows_ref, held_ref, sems):
        part = stream(weight_ref, held_ref, sems, parts)
        for j in range(groups):
            rows_ref[pl.ds(j * rows, rows)] = gathered_ref[j]
        total = jnp.zeros(out_ref.shape, jnp.float32)
        for k in range(parts):
            total = total + jnp.dot(
                rows_ref[:, pl.ds(k * step, step)], part(k), preferred_element_type=jnp.float32
            )
        out_ref[...] = total

    return call(
        kernel,
        "project_out",
        jax.ShapeDtypeStruct((count, weight.shape[1]), jnp.float32),
        [VMEM, ANY],
        weight.size * 2,
        limit=STREAM,
        flops=2 * count * weight.size,
        scratch_shapes=[
            pltpu.VMEM((count, depth), gathered.dtype),
            pltpu.VMEM(weight.shape, weight.dtype),
            pltpu.SemaphoreType.DMA((parts,)),
        ],
    )(gathered, weight)


def down_partials(gathered, adapter, store):
    groups, rows, _ = gathered.shape
    count = groups * rows
    rank, depth = store.shape[1:]

    def kernel(adapter_ref, gathered_ref, store_ref, out_ref, rows_ref):
        start = pl.multiple_of(lax.axis_index("mp") * depth, depth)
        for j in range(groups):
            rows_ref[pl.ds(j * rows, rows)] = gathered_ref[j, :, pl.ds(start, depth)]
        row = lax.broadcasted_iota(jnp.int32, (count, LANES), 0)
        lane = lax.broadcasted_iota(jnp.int32, (count, LANES), 1)
        total = jnp.zeros((count, LANES), jnp.float32)
        for k in range(count // BATCH):
            chosen = [adapter_ref[r // rows, r % rows] for r in range(k * BATCH, (k + 1) * BATCH)]
            every = lax.dot_general(
                rows_ref[...],
                jnp.concatenate([store_ref[c] for c in chosen]),
                (((1,), (1,)), ((), ())),
                preferred_element_type=jnp.float32,
            )
            for s in range(BATCH * rank // LANES):
                first = k * BATCH * rank + s * LANES
                mine = row == (lane + first) // rank
                total = total + jnp.where(mine, every[:, s * LANES : (s + 1) * LANES], 0.0)
        for c in range(groups):
            out_ref[c] = total

    return call(
        kernel,
        "down_partials",
        jax.ShapeDtypeStruct((groups, count, LANES), jnp.float32),
        [SMEM, VMEM, VMEM],
        2 * count * rank * depth,
        limit=4 * MIB,
        flops=2 * count * count * rank * depth,
        scratch_shapes=[pltpu.VMEM((count, depth), gathered.dtype)],
    )(adapter, gathered, store)


def pick(adapter_ref, store_ref, held_ref, sems):
    groups, rows = adapter_ref.shape
    count, rank = groups * rows, store_ref.shape[1]
    copies = []
    for r in range(count):
        copies.append(
            pltpu.make_async_copy(
                store_ref.at[adapter_ref[r // rows, r % rows]], held_ref.at[pl.ds(r * rank, rank)], sems.at[r]
            )
        )
        copies[-1].start()

    def batch(k):
        for copy in copies[k * BATCH : (k + 1) * BATCH]:
            copy.wait()
        return held_ref[pl.ds(k * BATCH * rank, BATCH * rank)]

    return batch


def add_up(base, partials, adapter, store):
    count = adapter.size
    rank, width = store.shape[1:]
    groups = partials.shape[0]

    def kernel(adapter_ref, base_ref, partials_ref, store_ref, out_ref, held_ref, sems):
        batch = pick(adapter_ref, store_ref, held_ref, sems)
        total = partials_ref[0]
        for c in range(1, groups):
            total = total + partials_ref[c]
        down = total.astype(jnp.bfloat16).astype(jnp.float32)
        row = lax.broadcasted_iota(jnp.int32, (count, LANES), 0)
        lane = lax.broadcasted_iota(jnp.int32, (count, LANES), 1)
        delta = jnp.zeros((count, width), jnp.float32)
        for k in range(count // BATCH):
            spread = []
            for s in range(BATCH * rank // LANES):
                first = k * BATCH * rank + s * LANES
                spread.append(jnp.where(row == (lane + first) // rank, down, 0.0))
            spread = jnp.concatenate(spread, 1).astype(jnp.bfloat16)
            delta = delta + jnp.dot(
                spread, batch(k), preferred_element_type=jnp.float32
            )
        result = (base_ref[...] + ADAPTER_SCALE * delta).astype(jnp.bfloat16)
        for j in range(groups):
            out_ref[j] = result[j * count // groups : (j + 1) * count // groups]

    return call(
        kernel,
        "add_up",
        jax.ShapeDtypeStruct((groups, count // groups, width), jnp.bfloat16),
        [SMEM, VMEM, VMEM, ANY],
        2 * count * rank * width,
        limit=STREAM,
        flops=2 * count * count * rank * width,
        scratch_shapes=[
            pltpu.VMEM((count * rank, width), store.dtype),
            pltpu.SemaphoreType.DMA((count,)),
        ],
    )(adapter, base, partials, store)


def add_rows(hidden, parts):
    width = parts.shape[2]

    def kernel(hidden_ref, parts_ref, out_ref):
        for k in range(parts.shape[0]):
            part = pl.ds(k * width, width)
            total = hidden_ref[:, part].astype(jnp.float32) + parts_ref[k].astype(jnp.float32)
            out_ref[:, part] = total.astype(jnp.bfloat16)

    return call(
        kernel,
        "add_rows",
        jax.ShapeDtypeStruct(hidden.shape, parts.dtype),
        [VMEM, VMEM],
        hidden.size * 6,
    )(hidden, parts)


def swap_cores(block):
    return lax.ppermute(block, "batch", [(0, 1), (1, 0)])


def exchange(blocks, axes="mp"):
    return lax.all_to_all(blocks, axes, split_axis=0, concat_axis=0, tiled=True)


def attend(qkv, cosine, sine, key_cache, value_cache, live):
    rows = qkv.shape[0]
    query_width = HEADS * HEAD_DIM
    kv_width = KV_HEADS * HEAD_DIM
    group = HEADS // KV_HEADS
    scale = HEAD_DIM ** (-0.5)

    def turn(part):
        vec = part.astype(jnp.float32).reshape(rows, -1, HEAD_DIM)
        half = HEAD_DIM // 2
        turned = jnp.concatenate([-vec[..., half:], vec[..., :half]], -1)
        return (vec * cosine[:, None] + turned * sine[:, None]).astype(jnp.bfloat16)

    query = turn(qkv[:, :query_width])
    fresh_key = turn(qkv[:, query_width : query_width + kv_width])
    fresh_value = (
        qkv[:, query_width + kv_width :].astype(jnp.float32).reshape(rows, KV_HEADS, HEAD_DIM)
    )
    grouped = query.reshape(rows, KV_HEADS, group, HEAD_DIM)
    cached = key_cache.reshape(rows, -1, KV_HEADS, HEAD_DIM)
    stored = value_cache.reshape(rows, -1, KV_HEADS, HEAD_DIM)
    scores = (
        jnp.einsum("rgqd,rtgd->rgqt", grouped, cached, preferred_element_type=jnp.float32) * scale
    )
    scores = jnp.where(live[:, None, None, :], scores, -jnp.inf)
    own = (
        jnp.einsum("rgqd,rgd->rgq", grouped, fresh_key, preferred_element_type=jnp.float32) * scale
    )
    top = jnp.maximum(jnp.max(scores, -1), own)
    expo = jnp.exp(scores - top[..., None])
    own_exp = jnp.exp(own - top)
    total = jnp.sum(expo, -1) + own_exp
    probs = (expo / total[..., None]).astype(jnp.bfloat16)
    own_prob = (own_exp / total).astype(jnp.bfloat16)
    context_vector = jnp.einsum(
        "rgqt,rtgd->rgqd", probs, stored, preferred_element_type=jnp.float32
    )
    context_vector = (
        context_vector + own_prob.astype(jnp.float32)[..., None] * fresh_value[:, :, None, :]
    )
    return context_vector.reshape(rows, query_width).astype(jnp.bfloat16)


def fast_body(
    hidden,
    attention_norm_gain,
    query_key_value_weight,
    output_weight,
    key_cache,
    value_cache,
    lengths,
    slots,
    requests,
    adapter_down_matrices,
    adapter_up_matrices,
):
    rows = hidden.shape[0]
    mp_size = lax.axis_size("mp")
    width = query_key_value_weight.shape[1]

    half = HEAD_DIM // 2
    frequency = THETA ** (-(jnp.arange(half, dtype=jnp.float32) * 2.0) / HEAD_DIM)
    frequency = both_halves(frequency[None])
    sent, angle, adapter = norm_rows(
        hidden, attention_norm_gain, frequency, lengths, slots, requests, mp_size
    )
    near = exchange(sent)
    far = swap_cores(near)

    near, angle, adapter = lax.optimization_barrier((near, angle, adapter))
    cosine, sine = jnp.cos(angle[1]), jnp.sin(angle[1])
    live = jnp.arange(key_cache.shape[1])[None, :] < angle[0, :, :1]
    far, cosine, sine, live = lax.optimization_barrier((far, cosine, sine, live))

    columns = project_qkv(near, far, query_key_value_weight, adapter)
    mixed = exchange(columns, ("mp", "batch"))
    adapter = mixed.reshape(mp_size, -1, rows, width + LANES)[:, :, :, width]
    adapter = jnp.sum(adapter.astype(jnp.float32), 1).astype(jnp.int32)
    qkv = mixed[:, :, :width].transpose(1, 0, 2).reshape(rows, -1)

    context = attend(qkv, cosine, sine, key_cache, value_cache, live)
    context, adapter = lax.optimization_barrier((context, adapter))
    gathered = exchange(jnp.broadcast_to(context[None], (mp_size, *context.shape)))

    partials = exchange(
        down_partials(gathered, adapter, adapter_down_matrices.swapaxes(1, 2))
    )
    base = project_out(gathered, output_weight)
    projected = add_up(base, partials, adapter, adapter_up_matrices)
    return add_rows(hidden, exchange(projected))


def body(*arguments):
    small = lax.axis_size("mp") <= 16 and lax.axis_size("batch") == 2
    whole_heads = arguments[2].shape[1] % HEAD_DIM == 0
    return (fast_body if small and whole_heads else general_body)(*arguments)


def solution(mesh):
    in_specs = (
        P(("groups", "mp", "batch"), None),
        P(),
        P(None, ("mp", "batch")),
        P(None, "mp"),
        P(("groups", "mp", "batch"), None, None),
        P(("groups", "mp", "batch"), None, None),
        P(("groups", "mp", "batch")),
        P(("groups", "mp", "batch")),
        P(("groups", "mp", "batch"), None),
        P(None, "mp", None),
        P(None, None, "mp"),
    )
    out_specs = P(("groups", "mp", "batch"), None)
    return jax.shard_map(body, mesh=mesh, in_specs=in_specs, out_specs=out_specs, check_vma=False)
```

```python
import math

import jax
import jax.numpy as jnp
from jax import lax
from jax.experimental import pallas as pl
from jax.experimental.pallas import tpu as pltpu
from jax.sharding import PartitionSpec as P

HEADS = 64
KV_HEADS = 8
HEAD_DIM = 128
ADAPTER_COUNT = 64


EPS = 1e-05
THETA = 500000.0
ADAPTER_SCALE = 2.0


def rotate(vec, pos):
    width = vec.shape[-1]
    half = width // 2
    freq = THETA ** (-(jnp.arange(half, dtype=jnp.float32) * 2.0) / width)
    angle = pos[..., None, None] * freq
    cosine = jnp.concatenate([jnp.cos(angle), jnp.cos(angle)], -1)
    sine = jnp.concatenate([jnp.sin(angle), jnp.sin(angle)], -1)
    turned = jnp.concatenate([-vec[..., half:], vec[..., :half]], -1)
    return vec * cosine + turned * sine


def apply_up_matrix(
    context_vector, adapter_selector, down_result, output_weight, adapter_up_matrices
):
    base_output = jnp.dot(context_vector, output_weight, preferred_element_type=jnp.float32)
    spread = (adapter_selector[:, :, None] * down_result[:, None, :]).reshape(
        adapter_selector.shape[0], -1
    )
    adapter_table = adapter_up_matrices.reshape(-1, adapter_up_matrices.shape[2])
    adapter_delta = jnp.dot(spread, adapter_table, preferred_element_type=jnp.float32)
    return (base_output + ADAPTER_SCALE * adapter_delta).astype(jnp.bfloat16)


def general_body(
    hidden,
    attention_norm_gain,
    query_key_value_weight,
    output_weight,
    key_cache,
    value_cache,
    lengths,
    slots,
    requests,
    adapter_down_matrices,
    adapter_up_matrices,
):
    widened = hidden.astype(jnp.float32)
    normed = (
        widened
        * lax.rsqrt(jnp.mean(widened * widened, -1, keepdims=True) + EPS)
        * attention_norm_gain.astype(jnp.float32)
    ).astype(jnp.bfloat16)
    rows = normed.shape[0]
    columns = jnp.dot(
        lax.all_gather(normed, ("mp", "batch"), axis=0, tiled=True),
        query_key_value_weight,
        preferred_element_type=jnp.float32,
    ).astype(jnp.bfloat16)
    mixed = lax.all_to_all(
        lax.all_to_all(columns, "mp", split_axis=0, concat_axis=1, tiled=True),
        "batch",
        split_axis=0,
        concat_axis=1,
        tiled=True,
    )
    width = query_key_value_weight.shape[1]
    qkv = (
        mixed.reshape(rows, lax.axis_size("batch"), lax.axis_size("mp"), width)
        .transpose(0, 2, 1, 3)
        .reshape(rows, -1)
    )
    query_width = HEADS * HEAD_DIM
    kv_width = KV_HEADS * HEAD_DIM
    group = HEADS // KV_HEADS
    scale = HEAD_DIM ** (-0.5)
    pos = lengths.astype(jnp.float32)
    query = rotate(
        qkv[:, :query_width].astype(jnp.float32).reshape(rows, HEADS, HEAD_DIM), pos
    ).astype(jnp.bfloat16)
    fresh_key = rotate(
        qkv[:, query_width : query_width + kv_width]
        .astype(jnp.float32)
        .reshape(rows, KV_HEADS, HEAD_DIM),
        pos,
    ).astype(jnp.bfloat16)
    fresh_value = (
        qkv[:, query_width + kv_width :].astype(jnp.float32).reshape(rows, KV_HEADS, HEAD_DIM)
    )
    grouped = query.reshape(rows, KV_HEADS, group, HEAD_DIM)
    cached = key_cache.reshape(rows, -1, KV_HEADS, HEAD_DIM)
    stored = value_cache.reshape(rows, -1, KV_HEADS, HEAD_DIM)
    scores = (
        jnp.einsum("rgqd,rtgd->rgqt", grouped, cached, preferred_element_type=jnp.float32) * scale
    )
    live = jnp.arange(cached.shape[1])[None, :] < lengths[:, None]
    scores = jnp.where(live[:, None, None, :], scores, -jnp.inf)
    own = (
        jnp.einsum("rgqd,rgd->rgq", grouped, fresh_key, preferred_element_type=jnp.float32) * scale
    )
    top = jnp.maximum(jnp.max(scores, -1), own)
    expo = jnp.exp(scores - top[..., None])
    own_exp = jnp.exp(own - top)
    total = jnp.sum(expo, -1) + own_exp
    probs = (expo / total[..., None]).astype(jnp.bfloat16)
    own_prob = (own_exp / total).astype(jnp.bfloat16)
    context_vector = jnp.einsum(
        "rgqt,rtgd->rgqd", probs, stored, preferred_element_type=jnp.float32
    )
    context_vector = (
        context_vector + own_prob.astype(jnp.float32)[..., None] * fresh_value[:, :, None, :]
    )
    context_vector = context_vector.reshape(rows, query_width).astype(jnp.bfloat16)
    slot_hits = slots[:, None] == jnp.arange(requests.shape[1])[None, :]
    adapter = jnp.sum(jnp.where(slot_hits, requests[0][None, :], 0), 1)
    adapter_selector = (adapter[:, None] == jnp.arange(ADAPTER_COUNT)[None, :]).astype(jnp.bfloat16)
    context_gathered, selector_gathered = (
        lax.all_gather(context_vector, "mp", axis=0, tiled=True),
        lax.all_gather(adapter_selector, "mp", axis=0, tiled=True),
    )
    shared_portion = adapter_down_matrices.shape[1]
    context_slice = lax.dynamic_slice_in_dim(
        context_gathered, lax.axis_index("mp") * shared_portion, shared_portion, 1
    )
    every_adapter = jnp.einsum(
        "gh,thy->gty", context_slice, adapter_down_matrices, preferred_element_type=jnp.float32
    )
    partial_down = jnp.sum(every_adapter * selector_gathered.astype(jnp.float32)[:, :, None], 1)
    down_gathered = lax.psum(partial_down, "mp").astype(jnp.bfloat16)
    projection_result = apply_up_matrix(
        context_gathered, selector_gathered, down_gathered, output_weight, adapter_up_matrices
    )
    returned = lax.all_to_all(projection_result, "mp", split_axis=0, concat_axis=1, tiled=True)
    return (widened + returned.astype(jnp.float32)).astype(jnp.bfloat16)


MIB = 1 << 20
LANES = 128
BATCH = 4
STREAM = 53 * MIB
VMEM = pl.BlockSpec(memory_space=pltpu.VMEM)
SMEM = pl.BlockSpec(memory_space=pltpu.SMEM)
ANY = pl.BlockSpec(memory_space=pl.ANY)


def call(kernel, name, out_shape, in_specs, moved, limit=2 * MIB, flops=0, **options):
    return pl.pallas_call(
        kernel,
        out_shape=out_shape,
        in_specs=in_specs,
        out_specs=jax.tree.map(lambda _: VMEM, out_shape),
        compiler_params=pltpu.CompilerParams(vmem_limit_bytes=limit),
        cost_estimate=pl.CostEstimate(flops=flops, bytes_accessed=moved, transcendentals=0),
        name=name,
        **options,
    )


def norm_rows(hidden, gain, copies):
    rows, width = hidden.shape

    def kernel(hidden_ref, gain_ref, out_ref):
        wide = hidden_ref[...].astype(jnp.float32)
        inverse = lax.rsqrt(jnp.mean(wide * wide, -1, keepdims=True) + EPS)
        normed = (wide * inverse * gain_ref[...].astype(jnp.float32)).astype(jnp.bfloat16)
        for c in range(copies):
            out_ref[c] = normed

    return call(
        kernel,
        "norm_rows",
        jax.ShapeDtypeStruct((copies, rows, width), jnp.bfloat16),
        [VMEM, VMEM],
        hidden.size * 2 * (copies + 1),
    )(hidden, gain[None])


def project_qkv(near, far, weight, lengths, slots, requests, chunk=1024):
    groups, rows, _ = near.shape
    depth, width = weight.shape
    count = 2 * groups * rows

    def kernel(
        lengths_ref, slots_ref, requests_ref, near_ref, far_ref, weight_ref, out_ref, turn_ref,
        rows_ref,
    ):
        for e, source in enumerate((near_ref, far_ref)):
            for j in range(groups):
                rows_ref[pl.ds((e * groups + j) * rows, rows)] = source[j]
        row = lax.broadcasted_iota(jnp.int32, (rows, LANES), 0)
        lane = lax.broadcasted_iota(jnp.int32, (rows, LANES), 1)
        position = jnp.zeros((rows, LANES), jnp.float32)
        adapter = jnp.zeros((rows, LANES), jnp.float32)
        for r in range(rows):
            chosen = requests_ref[0, slots_ref[r]]
            position = jnp.where(row == r, lengths_ref[r].astype(jnp.float32), position)
            adapter = jnp.where(row == r, chosen.astype(jnp.float32), adapter)
        exponent = (lane % (HEAD_DIM // 2)).astype(jnp.float32) * (2.0 / HEAD_DIM)
        angle = position * jnp.exp(exponent * -math.log(THETA))
        turn_ref[0] = jnp.cos(angle)
        turn_ref[1] = jnp.sin(angle)
        turn_ref[2] = position
        total = jnp.zeros((count, width), jnp.float32)
        for k in range(depth // chunk):
            part = pl.ds(k * chunk, chunk)
            total = total + jnp.dot(
                rows_ref[:, part], weight_ref[part, :], preferred_element_type=jnp.float32
            )
        core = lax.axis_index("batch")
        for e in range(2):
            for j in range(groups):
                place = (e * groups + j) * rows
                device = 2 * j + (core ^ e)
                out_ref[device, :, pl.ds(0, width)] = total[place : place + rows].astype(
                    jnp.bfloat16
                )
                out_ref[device, :, pl.ds(width, LANES)] = (
                    adapter if e == 0 else jnp.zeros_like(adapter)
                ).astype(jnp.bfloat16)

    return call(
        kernel,
        "project_qkv",
        (
            jax.ShapeDtypeStruct((2 * groups, rows, width + LANES), jnp.bfloat16),
            jax.ShapeDtypeStruct((3, rows, LANES), jnp.float32),
        ),
        [SMEM] * 3 + [VMEM] * 3,
        weight.size * 2,
        flops=2 * count * weight.size,
        scratch_shapes=[pltpu.VMEM((count, depth), jnp.bfloat16)],
    )(lengths, slots, requests, near, far, weight)


def stream(weight_ref, held_ref, sems, parts):
    depth = held_ref.shape[0] // parts
    copies = []
    for k in range(parts):
        rows = pl.ds(k * depth, depth)
        copies.append(
            pltpu.make_async_copy(weight_ref.at[rows], held_ref.at[rows], sems.at[k])
        )
        copies[-1].start()

    def part(k):
        copies[k].wait()
        return held_ref[pl.ds(k * depth, depth)]

    return part


def project_out(gathered, weight, parts=16):
    groups, rows, depth = gathered.shape
    count, step = groups * rows, depth // parts

    def kernel(gathered_ref, weight_ref, out_ref, rows_ref, held_ref, sems):
        part = stream(weight_ref, held_ref, sems, parts)
        for j in range(groups):
            rows_ref[pl.ds(j * rows, rows)] = gathered_ref[j]
        total = jnp.zeros(out_ref.shape, jnp.float32)
        for k in range(parts):
            total = total + jnp.dot(
                rows_ref[:, pl.ds(k * step, step)], part(k), preferred_element_type=jnp.float32
            )
        out_ref[...] = total

    return call(
        kernel,
        "project_out",
        jax.ShapeDtypeStruct((count, weight.shape[1]), jnp.float32),
        [VMEM, ANY],
        weight.size * 2,
        limit=STREAM,
        flops=2 * count * weight.size,
        scratch_shapes=[
            pltpu.VMEM((count, depth), gathered.dtype),
            pltpu.VMEM(weight.shape, weight.dtype),
            pltpu.SemaphoreType.DMA((parts,)),
        ],
    )(gathered, weight)


def down_partials(gathered, adapter, store):
    groups, rows, _ = gathered.shape
    count = groups * rows
    rank, depth = store.shape[1:]

    def kernel(adapter_ref, gathered_ref, store_ref, out_ref, rows_ref):
        start = pl.multiple_of(lax.axis_index("mp") * depth, depth)
        for j in range(groups):
            rows_ref[pl.ds(j * rows, rows)] = gathered_ref[j, :, pl.ds(start, depth)]
        row = lax.broadcasted_iota(jnp.int32, (count, LANES), 0)
        lane = lax.broadcasted_iota(jnp.int32, (count, LANES), 1)
        total = jnp.zeros((count, LANES), jnp.float32)
        for k in range(count // BATCH):
            chosen = [adapter_ref[r // rows, r % rows] for r in range(k * BATCH, (k + 1) * BATCH)]
            every = lax.dot_general(
                rows_ref[...],
                jnp.concatenate([store_ref[c] for c in chosen]),
                (((1,), (1,)), ((), ())),
                preferred_element_type=jnp.float32,
            )
            for s in range(BATCH * rank // LANES):
                first = k * BATCH * rank + s * LANES
                mine = row == (lane + first) // rank
                total = total + jnp.where(mine, every[:, s * LANES : (s + 1) * LANES], 0.0)
        for c in range(groups):
            out_ref[c] = total

    return call(
        kernel,
        "down_partials",
        jax.ShapeDtypeStruct((groups, count, LANES), jnp.float32),
        [SMEM, VMEM, VMEM],
        2 * count * rank * depth,
        limit=4 * MIB,
        flops=2 * count * count * rank * depth,
        scratch_shapes=[pltpu.VMEM((count, depth), gathered.dtype)],
    )(adapter, gathered, store)


def pick(adapter_ref, store_ref, held_ref, sems):
    groups, rows = adapter_ref.shape
    count, rank = groups * rows, store_ref.shape[1]
    copies = []
    for r in range(count):
        copies.append(
            pltpu.make_async_copy(
                store_ref.at[adapter_ref[r // rows, r % rows]], held_ref.at[pl.ds(r * rank, rank)], sems.at[r]
            )
        )
        copies[-1].start()

    def batch(k):
        for copy in copies[k * BATCH : (k + 1) * BATCH]:
            copy.wait()
        return held_ref[pl.ds(k * BATCH * rank, BATCH * rank)]

    return batch


def add_up(base, partials, adapter, store):
    count = adapter.size
    rank, width = store.shape[1:]
    groups = partials.shape[0]

    def kernel(adapter_ref, base_ref, partials_ref, store_ref, out_ref, held_ref, sems):
        batch = pick(adapter_ref, store_ref, held_ref, sems)
        total = partials_ref[0]
        for c in range(1, groups):
            total = total + partials_ref[c]
        down = total.astype(jnp.bfloat16).astype(jnp.float32)
        row = lax.broadcasted_iota(jnp.int32, (count, LANES), 0)
        lane = lax.broadcasted_iota(jnp.int32, (count, LANES), 1)
        delta = jnp.zeros((count, width), jnp.float32)
        for k in range(count // BATCH):
            spread = []
            for s in range(BATCH * rank // LANES):
                first = k * BATCH * rank + s * LANES
                spread.append(jnp.where(row == (lane + first) // rank, down, 0.0))
            spread = jnp.concatenate(spread, 1).astype(jnp.bfloat16)
            delta = delta + jnp.dot(
                spread, batch(k), preferred_element_type=jnp.float32
            )
        result = (base_ref[...] + ADAPTER_SCALE * delta).astype(jnp.bfloat16)
        for j in range(groups):
            out_ref[j] = result[j * count // groups : (j + 1) * count // groups]

    return call(
        kernel,
        "add_up",
        jax.ShapeDtypeStruct((groups, count // groups, width), jnp.bfloat16),
        [SMEM, VMEM, VMEM, ANY],
        2 * count * rank * width,
        limit=STREAM,
        flops=2 * count * count * rank * width,
        scratch_shapes=[
            pltpu.VMEM((count * rank, width), store.dtype),
            pltpu.SemaphoreType.DMA((count,)),
        ],
    )(adapter, base, partials, store)


def add_rows(hidden, parts):
    width = parts.shape[2]

    def kernel(hidden_ref, parts_ref, out_ref):
        for k in range(parts.shape[0]):
            part = pl.ds(k * width, width)
            total = hidden_ref[:, part].astype(jnp.float32) + parts_ref[k].astype(jnp.float32)
            out_ref[:, part] = total.astype(jnp.bfloat16)

    return call(
        kernel,
        "add_rows",
        jax.ShapeDtypeStruct(hidden.shape, parts.dtype),
        [VMEM, VMEM],
        hidden.size * 6,
    )(hidden, parts)


def swap_cores(block):
    return lax.ppermute(block, "batch", [(0, 1), (1, 0)])


def exchange(blocks, axes="mp"):
    return lax.all_to_all(blocks, axes, split_axis=0, concat_axis=0, tiled=True)


def attend(qkv, cosine, sine, key_cache, value_cache, live):
    rows = qkv.shape[0]
    query_width = HEADS * HEAD_DIM
    kv_width = KV_HEADS * HEAD_DIM
    group = HEADS // KV_HEADS
    scale = HEAD_DIM ** (-0.5)

    def turn(part):
        vec = part.astype(jnp.float32).reshape(rows, -1, HEAD_DIM)
        half = HEAD_DIM // 2
        turned = jnp.concatenate([-vec[..., half:], vec[..., :half]], -1)
        return (vec * cosine[:, None] + turned * sine[:, None]).astype(jnp.bfloat16)

    query = turn(qkv[:, :query_width])
    fresh_key = turn(qkv[:, query_width : query_width + kv_width])
    fresh_value = (
        qkv[:, query_width + kv_width :].astype(jnp.float32).reshape(rows, KV_HEADS, HEAD_DIM)
    )
    grouped = query.reshape(rows, KV_HEADS, group, HEAD_DIM)
    cached = key_cache.reshape(rows, -1, KV_HEADS, HEAD_DIM)
    stored = value_cache.reshape(rows, -1, KV_HEADS, HEAD_DIM)
    scores = (
        jnp.einsum("rgqd,rtgd->rgqt", grouped, cached, preferred_element_type=jnp.float32) * scale
    )
    scores = jnp.where(live[:, None, None, :], scores, -jnp.inf)
    own = (
        jnp.einsum("rgqd,rgd->rgq", grouped, fresh_key, preferred_element_type=jnp.float32) * scale
    )
    top = jnp.maximum(jnp.max(scores, -1), own)
    expo = jnp.exp(scores - top[..., None])
    own_exp = jnp.exp(own - top)
    total = jnp.sum(expo, -1) + own_exp
    probs = (expo / total[..., None]).astype(jnp.bfloat16)
    own_prob = (own_exp / total).astype(jnp.bfloat16)
    context_vector = jnp.einsum(
        "rgqt,rtgd->rgqd", probs, stored, preferred_element_type=jnp.float32
    )
    context_vector = (
        context_vector + own_prob.astype(jnp.float32)[..., None] * fresh_value[:, :, None, :]
    )
    return context_vector.reshape(rows, query_width).astype(jnp.bfloat16)


def fast_body(
    hidden,
    attention_norm_gain,
    query_key_value_weight,
    output_weight,
    key_cache,
    value_cache,
    lengths,
    slots,
    requests,
    adapter_down_matrices,
    adapter_up_matrices,
):
    rows = hidden.shape[0]
    mp_size = lax.axis_size("mp")
    width = query_key_value_weight.shape[1]

    near = exchange(norm_rows(hidden, attention_norm_gain, mp_size))
    columns, turn = project_qkv(
        near, swap_cores(near), query_key_value_weight, lengths, slots, requests
    )
    mixed = exchange(columns, ("mp", "batch"))
    mixed, turn = lax.optimization_barrier((mixed, turn))
    live = jnp.arange(key_cache.shape[1])[None, :] < turn[2, :, :1].astype(jnp.int32)
    adapter = mixed.reshape(mp_size, -1, rows, width + LANES)[:, :, :, width]
    adapter = jnp.sum(adapter.astype(jnp.float32), 1).astype(jnp.int32)
    qkv = mixed[:, :, :width].transpose(1, 0, 2).reshape(rows, -1)

    context = attend(qkv, turn[0], turn[1], key_cache, value_cache, live)
    context, adapter = lax.optimization_barrier((context, adapter))
    gathered = exchange(jnp.broadcast_to(context[None], (mp_size, *context.shape)))

    partials = exchange(
        down_partials(gathered, adapter, adapter_down_matrices.swapaxes(1, 2))
    )
    base = project_out(gathered, output_weight)
    projected = add_up(base, partials, adapter, adapter_up_matrices)
    return add_rows(hidden, exchange(projected))


def body(*arguments):
    small = lax.axis_size("mp") <= 16 and lax.axis_size("batch") == 2
    whole_heads = arguments[2].shape[1] % HEAD_DIM == 0
    return (fast_body if small and whole_heads else general_body)(*arguments)


def solution(mesh):
    in_specs = (
        P(("groups", "mp", "batch"), None),
        P(),
        P(None, ("mp", "batch")),
        P(None, "mp"),
        P(("groups", "mp", "batch"), None, None),
        P(("groups", "mp", "batch"), None, None),
        P(("groups", "mp", "batch")),
        P(("groups", "mp", "batch")),
        P(("groups", "mp", "batch"), None),
        P(None, "mp", None),
        P(None, None, "mp"),
    )
    out_specs = P(("groups", "mp", "batch"), None)
    return jax.shard_map(body, mesh=mesh, in_specs=in_specs, out_specs=out_specs, check_vma=False)
```

```python
import math

import jax
import jax.numpy as jnp
from jax import lax
from jax.experimental import pallas as pl
from jax.experimental.pallas import tpu as pltpu
from jax.sharding import PartitionSpec as P

HEADS = 64
KV_HEADS = 8
HEAD_DIM = 128
ADAPTER_COUNT = 64


EPS = 1e-05
THETA = 500000.0
ADAPTER_SCALE = 2.0


def rotate(vec, pos):
    width = vec.shape[-1]
    half = width // 2
    freq = THETA ** (-(jnp.arange(half, dtype=jnp.float32) * 2.0) / width)
    angle = pos[..., None, None] * freq
    cosine = jnp.concatenate([jnp.cos(angle), jnp.cos(angle)], -1)
    sine = jnp.concatenate([jnp.sin(angle), jnp.sin(angle)], -1)
    turned = jnp.concatenate([-vec[..., half:], vec[..., :half]], -1)
    return vec * cosine + turned * sine


def apply_up_matrix(
    context_vector, adapter_selector, down_result, output_weight, adapter_up_matrices
):
    base_output = jnp.dot(context_vector, output_weight, preferred_element_type=jnp.float32)
    spread = (adapter_selector[:, :, None] * down_result[:, None, :]).reshape(
        adapter_selector.shape[0], -1
    )
    adapter_table = adapter_up_matrices.reshape(-1, adapter_up_matrices.shape[2])
    adapter_delta = jnp.dot(spread, adapter_table, preferred_element_type=jnp.float32)
    return (base_output + ADAPTER_SCALE * adapter_delta).astype(jnp.bfloat16)


def general_body(
    hidden,
    attention_norm_gain,
    query_key_value_weight,
    output_weight,
    key_cache,
    value_cache,
    lengths,
    slots,
    requests,
    adapter_down_matrices,
    adapter_up_matrices,
):
    widened = hidden.astype(jnp.float32)
    normed = (
        widened
        * lax.rsqrt(jnp.mean(widened * widened, -1, keepdims=True) + EPS)
        * attention_norm_gain.astype(jnp.float32)
    ).astype(jnp.bfloat16)
    rows = normed.shape[0]
    columns = jnp.dot(
        lax.all_gather(normed, ("mp", "batch"), axis=0, tiled=True),
        query_key_value_weight,
        preferred_element_type=jnp.float32,
    ).astype(jnp.bfloat16)
    mixed = lax.all_to_all(
        lax.all_to_all(columns, "mp", split_axis=0, concat_axis=1, tiled=True),
        "batch",
        split_axis=0,
        concat_axis=1,
        tiled=True,
    )
    width = query_key_value_weight.shape[1]
    qkv = (
        mixed.reshape(rows, lax.axis_size("batch"), lax.axis_size("mp"), width)
        .transpose(0, 2, 1, 3)
        .reshape(rows, -1)
    )
    query_width = HEADS * HEAD_DIM
    kv_width = KV_HEADS * HEAD_DIM
    group = HEADS // KV_HEADS
    scale = HEAD_DIM ** (-0.5)
    pos = lengths.astype(jnp.float32)
    query = rotate(
        qkv[:, :query_width].astype(jnp.float32).reshape(rows, HEADS, HEAD_DIM), pos
    ).astype(jnp.bfloat16)
    fresh_key = rotate(
        qkv[:, query_width : query_width + kv_width]
        .astype(jnp.float32)
        .reshape(rows, KV_HEADS, HEAD_DIM),
        pos,
    ).astype(jnp.bfloat16)
    fresh_value = (
        qkv[:, query_width + kv_width :].astype(jnp.float32).reshape(rows, KV_HEADS, HEAD_DIM)
    )
    grouped = query.reshape(rows, KV_HEADS, group, HEAD_DIM)
    cached = key_cache.reshape(rows, -1, KV_HEADS, HEAD_DIM)
    stored = value_cache.reshape(rows, -1, KV_HEADS, HEAD_DIM)
    scores = (
        jnp.einsum("rgqd,rtgd->rgqt", grouped, cached, preferred_element_type=jnp.float32) * scale
    )
    live = jnp.arange(cached.shape[1])[None, :] < lengths[:, None]
    scores = jnp.where(live[:, None, None, :], scores, -jnp.inf)
    own = (
        jnp.einsum("rgqd,rgd->rgq", grouped, fresh_key, preferred_element_type=jnp.float32) * scale
    )
    top = jnp.maximum(jnp.max(scores, -1), own)
    expo = jnp.exp(scores - top[..., None])
    own_exp = jnp.exp(own - top)
    total = jnp.sum(expo, -1) + own_exp
    probs = (expo / total[..., None]).astype(jnp.bfloat16)
    own_prob = (own_exp / total).astype(jnp.bfloat16)
    context_vector = jnp.einsum(
        "rgqt,rtgd->rgqd", probs, stored, preferred_element_type=jnp.float32
    )
    context_vector = (
        context_vector + own_prob.astype(jnp.float32)[..., None] * fresh_value[:, :, None, :]
    )
    context_vector = context_vector.reshape(rows, query_width).astype(jnp.bfloat16)
    slot_hits = slots[:, None] == jnp.arange(requests.shape[1])[None, :]
    adapter = jnp.sum(jnp.where(slot_hits, requests[0][None, :], 0), 1)
    adapter_selector = (adapter[:, None] == jnp.arange(ADAPTER_COUNT)[None, :]).astype(jnp.bfloat16)
    context_gathered, selector_gathered = (
        lax.all_gather(context_vector, "mp", axis=0, tiled=True),
        lax.all_gather(adapter_selector, "mp", axis=0, tiled=True),
    )
    shared_portion = adapter_down_matrices.shape[1]
    context_slice = lax.dynamic_slice_in_dim(
        context_gathered, lax.axis_index("mp") * shared_portion, shared_portion, 1
    )
    every_adapter = jnp.einsum(
        "gh,thy->gty", context_slice, adapter_down_matrices, preferred_element_type=jnp.float32
    )
    partial_down = jnp.sum(every_adapter * selector_gathered.astype(jnp.float32)[:, :, None], 1)
    down_gathered = lax.psum(partial_down, "mp").astype(jnp.bfloat16)
    projection_result = apply_up_matrix(
        context_gathered, selector_gathered, down_gathered, output_weight, adapter_up_matrices
    )
    returned = lax.all_to_all(projection_result, "mp", split_axis=0, concat_axis=1, tiled=True)
    return (widened + returned.astype(jnp.float32)).astype(jnp.bfloat16)


MIB = 1 << 20
LANES = 128
BATCH = 4
LONG = 10**10
STREAM = 53 * MIB
VMEM = pl.BlockSpec(memory_space=pltpu.VMEM)
SMEM = pl.BlockSpec(memory_space=pltpu.SMEM)
ANY = pl.BlockSpec(memory_space=pl.ANY)


def call(kernel, name, out_shape, in_specs, moved, limit=2 * MIB, flops=0, **options):
    return pl.pallas_call(
        kernel,
        out_shape=out_shape,
        in_specs=in_specs,
        out_specs=jax.tree.map(lambda _: VMEM, out_shape),
        compiler_params=pltpu.CompilerParams(vmem_limit_bytes=limit),
        cost_estimate=pl.CostEstimate(flops=flops, bytes_accessed=moved, transcendentals=0),
        name=name,
        **options,
    )


def frequencies():
    def kernel(out_ref):
        lane = lax.broadcasted_iota(jnp.int32, (1, HEAD_DIM), 1)
        exponent = (lane % (HEAD_DIM // 2)).astype(jnp.float32) * (2.0 / HEAD_DIM)
        out_ref[...] = jnp.exp(exponent * -math.log(THETA))

    return call(
        kernel,
        "frequencies",
        jax.ShapeDtypeStruct((1, HEAD_DIM), jnp.float32),
        [],
        0,
        flops=LONG // 8,
    )()


def norm_rows(hidden, gain, after, copies):
    rows, width = hidden.shape

    def kernel(hidden_ref, gain_ref, after_ref, out_ref):
        del after_ref
        wide = hidden_ref[...].astype(jnp.float32)
        inverse = lax.rsqrt(jnp.mean(wide * wide, -1, keepdims=True) + EPS)
        normed = (wide * inverse * gain_ref[...].astype(jnp.float32)).astype(jnp.bfloat16)
        for c in range(copies):
            out_ref[c] = normed

    return call(
        kernel,
        "norm_rows",
        jax.ShapeDtypeStruct((copies, rows, width), jnp.bfloat16),
        [VMEM, VMEM, ANY],
        hidden.size * 2 * (copies + 1),
        flops=LONG,
    )(hidden, gain[None], after)


def turns(near, frequency, lengths, slots, requests, context):
    groups, rows, depth = near.shape

    def kernel(
        lengths_ref, slots_ref, requests_ref, near_ref, frequency_ref, lined_ref, cosine_ref,
        sine_ref, mask_ref, adapter_ref,
    ):
        for j in range(groups):
            lined_ref[pl.ds(j * rows, rows)] = near_ref[j]
        row = lax.broadcasted_iota(jnp.int32, (rows, LANES), 0)
        length = jnp.zeros((rows, LANES), jnp.int32)
        adapter = jnp.zeros((rows, LANES), jnp.int32)
        for r in range(rows):
            length = jnp.where(row == r, lengths_ref[r], length)
            adapter = jnp.where(row == r, requests_ref[0, slots_ref[r]], adapter)
        angle = length.astype(jnp.float32) * frequency_ref[...]
        cosine_ref[...] = jnp.cos(angle)
        sine_ref[...] = jnp.sin(angle)
        lane = lax.broadcasted_iota(jnp.int32, (rows, LANES), 1)
        for t in range(0, context, LANES):
            mask_ref[:, pl.ds(t, LANES)] = jnp.where(lane + t < length, 0.0, -jnp.inf)
        adapter_ref[...] = adapter.astype(jnp.float32).astype(jnp.bfloat16)

    return call(
        kernel,
        "turns",
        (
            jax.ShapeDtypeStruct((groups * rows, depth), near.dtype),
            jax.ShapeDtypeStruct((rows, HEAD_DIM), jnp.float32),
            jax.ShapeDtypeStruct((rows, HEAD_DIM), jnp.float32),
            jax.ShapeDtypeStruct((rows, context), jnp.float32),
            jax.ShapeDtypeStruct((rows, LANES), jnp.bfloat16),
        ),
        [SMEM] * 3 + [VMEM] * 2,
        near.size * 4,
    )(lengths, slots, requests, near, frequency)


def project_qkv(lined, far, weight, adapter, chunk=1024):
    groups, rows, _ = far.shape
    depth, width = weight.shape
    half = groups * rows

    def kernel(lined_ref, far_ref, weight_ref, adapter_ref, out_ref, far_lined_ref):
        for j in range(groups):
            far_lined_ref[pl.ds(j * rows, rows)] = far_ref[j]
        total = jnp.zeros((2 * half, width), jnp.float32)
        for k in range(depth // chunk):
            part = pl.ds(k * chunk, chunk)
            total = total + jnp.dot(
                jnp.concatenate([lined_ref[:, part], far_lined_ref[:, part]]),
                weight_ref[part, :],
                preferred_element_type=jnp.float32,
            )
        core = lax.axis_index("batch")
        adapter = adapter_ref[...]
        for e in range(2):
            for j in range(groups):
                place = e * half + j * rows
                device = 2 * j + (core ^ e)
                out_ref[device, :, pl.ds(0, width)] = total[place : place + rows].astype(
                    jnp.bfloat16
                )
                out_ref[device, :, pl.ds(width, LANES)] = (
                    adapter if e == 0 else jnp.zeros_like(adapter)
                )

    return call(
        kernel,
        "project_qkv",
        jax.ShapeDtypeStruct((2 * groups, rows, width + LANES), jnp.bfloat16),
        [VMEM] * 4,
        weight.size * 2,
        flops=LONG,
        scratch_shapes=[pltpu.VMEM((half, depth), jnp.bfloat16)],
    )(lined, far, weight, adapter)


def stream(weight_ref, held_ref, sems, parts):
    depth = held_ref.shape[0] // parts
    copies = []
    for k in range(parts):
        rows = pl.ds(k * depth, depth)
        copies.append(
            pltpu.make_async_copy(weight_ref.at[rows], held_ref.at[rows], sems.at[k])
        )
        copies[-1].start()

    def part(k):
        copies[k].wait()
        return held_ref[pl.ds(k * depth, depth)]

    return part


def project_out(gathered, weight, parts=16):
    groups, rows, depth = gathered.shape
    count, step = groups * rows, depth // parts

    def kernel(gathered_ref, weight_ref, out_ref, rows_ref, held_ref, sems):
        part = stream(weight_ref, held_ref, sems, parts)
        for j in range(groups):
            rows_ref[pl.ds(j * rows, rows)] = gathered_ref[j]
        total = jnp.zeros(out_ref.shape, jnp.float32)
        for k in range(parts):
            total = total + jnp.dot(
                rows_ref[:, pl.ds(k * step, step)], part(k), preferred_element_type=jnp.float32
            )
        out_ref[...] = total

    return call(
        kernel,
        "project_out",
        jax.ShapeDtypeStruct((count, weight.shape[1]), jnp.float32),
        [VMEM, ANY],
        weight.size * 2,
        limit=STREAM,
        flops=2 * count * weight.size,
        scratch_shapes=[
            pltpu.VMEM((count, depth), gathered.dtype),
            pltpu.VMEM(weight.shape, weight.dtype),
            pltpu.SemaphoreType.DMA((parts,)),
        ],
    )(gathered, weight)


def down_partials(gathered, adapter, store):
    groups, rows, _ = gathered.shape
    count = groups * rows
    rank, depth = store.shape[1:]

    def kernel(adapter_ref, gathered_ref, store_ref, out_ref, rows_ref):
        start = pl.multiple_of(lax.axis_index("mp") * depth, depth)
        for j in range(groups):
            rows_ref[pl.ds(j * rows, rows)] = gathered_ref[j, :, pl.ds(start, depth)]
        row = lax.broadcasted_iota(jnp.int32, (count, LANES), 0)
        lane = lax.broadcasted_iota(jnp.int32, (count, LANES), 1)
        total = jnp.zeros((count, LANES), jnp.float32)
        for k in range(count // BATCH):
            chosen = [adapter_ref[r // rows, r % rows] for r in range(k * BATCH, (k + 1) * BATCH)]
            every = lax.dot_general(
                rows_ref[...],
                jnp.concatenate([store_ref[c] for c in chosen]),
                (((1,), (1,)), ((), ())),
                preferred_element_type=jnp.float32,
            )
            for s in range(BATCH * rank // LANES):
                first = k * BATCH * rank + s * LANES
                mine = row == (lane + first) // rank
                total = total + jnp.where(mine, every[:, s * LANES : (s + 1) * LANES], 0.0)
        for c in range(groups):
            out_ref[c] = total

    return call(
        kernel,
        "down_partials",
        jax.ShapeDtypeStruct((groups, count, LANES), jnp.float32),
        [SMEM, VMEM, VMEM],
        2 * count * rank * depth,
        limit=4 * MIB,
        flops=2 * count * count * rank * depth,
        scratch_shapes=[pltpu.VMEM((count, depth), gathered.dtype)],
    )(adapter, gathered, store)


def pick(adapter_ref, store_ref, held_ref, sems):
    groups, rows = adapter_ref.shape
    count, rank = groups * rows, store_ref.shape[1]
    copies = []
    for r in range(count):
        copies.append(
            pltpu.make_async_copy(
                store_ref.at[adapter_ref[r // rows, r % rows]], held_ref.at[pl.ds(r * rank, rank)], sems.at[r]
            )
        )
        copies[-1].start()

    def batch(k):
        for copy in copies[k * BATCH : (k + 1) * BATCH]:
            copy.wait()
        return held_ref[pl.ds(k * BATCH * rank, BATCH * rank)]

    return batch


def add_up(base, partials, adapter, store):
    count = adapter.size
    rank, width = store.shape[1:]
    groups = partials.shape[0]

    def kernel(adapter_ref, base_ref, partials_ref, store_ref, out_ref, held_ref, sems):
        batch = pick(adapter_ref, store_ref, held_ref, sems)
        total = partials_ref[0]
        for c in range(1, groups):
            total = total + partials_ref[c]
        down = total.astype(jnp.bfloat16).astype(jnp.float32)
        row = lax.broadcasted_iota(jnp.int32, (count, LANES), 0)
        lane = lax.broadcasted_iota(jnp.int32, (count, LANES), 1)
        delta = jnp.zeros((count, width), jnp.float32)
        for k in range(count // BATCH):
            spread = []
            for s in range(BATCH * rank // LANES):
                first = k * BATCH * rank + s * LANES
                spread.append(jnp.where(row == (lane + first) // rank, down, 0.0))
            spread = jnp.concatenate(spread, 1).astype(jnp.bfloat16)
            delta = delta + jnp.dot(
                spread, batch(k), preferred_element_type=jnp.float32
            )
        result = (base_ref[...] + ADAPTER_SCALE * delta).astype(jnp.bfloat16)
        for j in range(groups):
            out_ref[j] = result[j * count // groups : (j + 1) * count // groups]

    return call(
        kernel,
        "add_up",
        jax.ShapeDtypeStruct((groups, count // groups, width), jnp.bfloat16),
        [SMEM, VMEM, VMEM, ANY],
        2 * count * rank * width,
        limit=STREAM,
        flops=2 * count * count * rank * width,
        scratch_shapes=[
            pltpu.VMEM((count * rank, width), store.dtype),
            pltpu.SemaphoreType.DMA((count,)),
        ],
    )(adapter, base, partials, store)


def add_rows(hidden, parts):
    width = parts.shape[2]

    def kernel(hidden_ref, parts_ref, out_ref):
        for k in range(parts.shape[0]):
            part = pl.ds(k * width, width)
            total = hidden_ref[:, part].astype(jnp.float32) + parts_ref[k].astype(jnp.float32)
            out_ref[:, part] = total.astype(jnp.bfloat16)

    return call(
        kernel,
        "add_rows",
        jax.ShapeDtypeStruct(hidden.shape, parts.dtype),
        [VMEM, VMEM],
        hidden.size * 6,
    )(hidden, parts)


def swap_cores(block):
    return lax.ppermute(block, "batch", [(0, 1), (1, 0)])


def exchange(blocks, axes="mp"):
    return lax.all_to_all(blocks, axes, split_axis=0, concat_axis=0, tiled=True)


def attend(qkv, cosine, sine, key_cache, value_cache, mask):
    rows = qkv.shape[0]
    query_width = HEADS * HEAD_DIM
    kv_width = KV_HEADS * HEAD_DIM
    group = HEADS // KV_HEADS
    scale = HEAD_DIM ** (-0.5)

    def turn(part):
        vec = part.astype(jnp.float32).reshape(rows, -1, HEAD_DIM)
        half = HEAD_DIM // 2
        turned = jnp.concatenate([-vec[..., half:], vec[..., :half]], -1)
        return (vec * cosine[:, None] + turned * sine[:, None]).astype(jnp.bfloat16)

    query = turn(qkv[:, :query_width])
    fresh_key = turn(qkv[:, query_width : query_width + kv_width])
    fresh_value = (
        qkv[:, query_width + kv_width :].astype(jnp.float32).reshape(rows, KV_HEADS, HEAD_DIM)
    )
    grouped = query.reshape(rows, KV_HEADS, group, HEAD_DIM)
    cached = key_cache.reshape(rows, -1, KV_HEADS, HEAD_DIM)
    stored = value_cache.reshape(rows, -1, KV_HEADS, HEAD_DIM)
    scores = (
        jnp.einsum("rgqd,rtgd->rgqt", grouped, cached, preferred_element_type=jnp.float32) * scale
    )
    scores = scores + mask[:, None, None, :]
    own = (
        jnp.einsum("rgqd,rgd->rgq", grouped, fresh_key, preferred_element_type=jnp.float32) * scale
    )
    top = jnp.maximum(jnp.max(scores, -1), own)
    expo = jnp.exp(scores - top[..., None])
    own_exp = jnp.exp(own - top)
    total = jnp.sum(expo, -1) + own_exp
    probs = (expo / total[..., None]).astype(jnp.bfloat16)
    own_prob = (own_exp / total).astype(jnp.bfloat16)
    context_vector = jnp.einsum(
        "rgqt,rtgd->rgqd", probs, stored, preferred_element_type=jnp.float32
    )
    context_vector = (
        context_vector + own_prob.astype(jnp.float32)[..., None] * fresh_value[:, :, None, :]
    )
    return context_vector.reshape(rows, query_width).astype(jnp.bfloat16)


def fast_body(
    hidden,
    attention_norm_gain,
    query_key_value_weight,
    output_weight,
    key_cache,
    value_cache,
    lengths,
    slots,
    requests,
    adapter_down_matrices,
    adapter_up_matrices,
):
    rows = hidden.shape[0]
    mp_size = lax.axis_size("mp")
    width = query_key_value_weight.shape[1]

    frequency = frequencies()
    near = exchange(norm_rows(hidden, attention_norm_gain, frequency, mp_size))
    lined, cosine, sine, mask, adapter = turns(
        near, frequency, lengths, slots, requests, key_cache.shape[1]
    )
    columns = project_qkv(lined, swap_cores(near), query_key_value_weight, adapter)
    mixed = exchange(columns, ("mp", "batch"))
    adapter = mixed.reshape(mp_size, -1, rows, width + LANES)[:, :, :, width]
    adapter = jnp.sum(adapter.astype(jnp.float32), 1).astype(jnp.int32)
    qkv = mixed[:, :, :width].transpose(1, 0, 2).reshape(rows, -1)

    context = attend(qkv, cosine, sine, key_cache, value_cache, mask)
    context, adapter = lax.optimization_barrier((context, adapter))
    gathered = exchange(jnp.broadcast_to(context[None], (mp_size, *context.shape)))

    partials = exchange(
        down_partials(gathered, adapter, adapter_down_matrices.swapaxes(1, 2))
    )
    base = project_out(gathered, output_weight)
    projected = add_up(base, partials, adapter, adapter_up_matrices)
    return add_rows(hidden, exchange(projected))


def body(*arguments):
    small = lax.axis_size("mp") <= 16 and lax.axis_size("batch") == 2
    whole_heads = arguments[2].shape[1] % HEAD_DIM == 0
    return (fast_body if small and whole_heads else general_body)(*arguments)


def solution(mesh):
    in_specs = (
        P(("groups", "mp", "batch"), None),
        P(),
        P(None, ("mp", "batch")),
        P(None, "mp"),
        P(("groups", "mp", "batch"), None, None),
        P(("groups", "mp", "batch"), None, None),
        P(("groups", "mp", "batch")),
        P(("groups", "mp", "batch")),
        P(("groups", "mp", "batch"), None),
        P(None, "mp", None),
        P(None, None, "mp"),
    )
    out_specs = P(("groups", "mp", "batch"), None)
    return jax.shard_map(body, mesh=mesh, in_specs=in_specs, out_specs=out_specs, check_vma=False)
```

```python
import math

import jax
import jax.numpy as jnp
from jax import lax
from jax.experimental import pallas as pl
from jax.experimental.pallas import tpu as pltpu
from jax.sharding import PartitionSpec as P

HEADS = 64
KV_HEADS = 8
HEAD_DIM = 128
ADAPTER_COUNT = 64


EPS = 1e-05
THETA = 500000.0
ADAPTER_SCALE = 2.0


def rotate(vec, pos):
    width = vec.shape[-1]
    half = width // 2
    freq = THETA ** (-(jnp.arange(half, dtype=jnp.float32) * 2.0) / width)
    angle = pos[..., None, None] * freq
    cosine = jnp.concatenate([jnp.cos(angle), jnp.cos(angle)], -1)
    sine = jnp.concatenate([jnp.sin(angle), jnp.sin(angle)], -1)
    turned = jnp.concatenate([-vec[..., half:], vec[..., :half]], -1)
    return vec * cosine + turned * sine


def apply_up_matrix(
    context_vector, adapter_selector, down_result, output_weight, adapter_up_matrices
):
    base_output = jnp.dot(context_vector, output_weight, preferred_element_type=jnp.float32)
    spread = (adapter_selector[:, :, None] * down_result[:, None, :]).reshape(
        adapter_selector.shape[0], -1
    )
    adapter_table = adapter_up_matrices.reshape(-1, adapter_up_matrices.shape[2])
    adapter_delta = jnp.dot(spread, adapter_table, preferred_element_type=jnp.float32)
    return (base_output + ADAPTER_SCALE * adapter_delta).astype(jnp.bfloat16)


def general_body(
    hidden,
    attention_norm_gain,
    query_key_value_weight,
    output_weight,
    key_cache,
    value_cache,
    lengths,
    slots,
    requests,
    adapter_down_matrices,
    adapter_up_matrices,
):
    widened = hidden.astype(jnp.float32)
    normed = (
        widened
        * lax.rsqrt(jnp.mean(widened * widened, -1, keepdims=True) + EPS)
        * attention_norm_gain.astype(jnp.float32)
    ).astype(jnp.bfloat16)
    rows = normed.shape[0]
    columns = jnp.dot(
        lax.all_gather(normed, ("mp", "batch"), axis=0, tiled=True),
        query_key_value_weight,
        preferred_element_type=jnp.float32,
    ).astype(jnp.bfloat16)
    mixed = lax.all_to_all(
        lax.all_to_all(columns, "mp", split_axis=0, concat_axis=1, tiled=True),
        "batch",
        split_axis=0,
        concat_axis=1,
        tiled=True,
    )
    width = query_key_value_weight.shape[1]
    qkv = (
        mixed.reshape(rows, lax.axis_size("batch"), lax.axis_size("mp"), width)
        .transpose(0, 2, 1, 3)
        .reshape(rows, -1)
    )
    query_width = HEADS * HEAD_DIM
    kv_width = KV_HEADS * HEAD_DIM
    group = HEADS // KV_HEADS
    scale = HEAD_DIM ** (-0.5)
    pos = lengths.astype(jnp.float32)
    query = rotate(
        qkv[:, :query_width].astype(jnp.float32).reshape(rows, HEADS, HEAD_DIM), pos
    ).astype(jnp.bfloat16)
    fresh_key = rotate(
        qkv[:, query_width : query_width + kv_width]
        .astype(jnp.float32)
        .reshape(rows, KV_HEADS, HEAD_DIM),
        pos,
    ).astype(jnp.bfloat16)
    fresh_value = (
        qkv[:, query_width + kv_width :].astype(jnp.float32).reshape(rows, KV_HEADS, HEAD_DIM)
    )
    grouped = query.reshape(rows, KV_HEADS, group, HEAD_DIM)
    cached = key_cache.reshape(rows, -1, KV_HEADS, HEAD_DIM)
    stored = value_cache.reshape(rows, -1, KV_HEADS, HEAD_DIM)
    scores = (
        jnp.einsum("rgqd,rtgd->rgqt", grouped, cached, preferred_element_type=jnp.float32) * scale
    )
    live = jnp.arange(cached.shape[1])[None, :] < lengths[:, None]
    scores = jnp.where(live[:, None, None, :], scores, -jnp.inf)
    own = (
        jnp.einsum("rgqd,rgd->rgq", grouped, fresh_key, preferred_element_type=jnp.float32) * scale
    )
    top = jnp.maximum(jnp.max(scores, -1), own)
    expo = jnp.exp(scores - top[..., None])
    own_exp = jnp.exp(own - top)
    total = jnp.sum(expo, -1) + own_exp
    probs = (expo / total[..., None]).astype(jnp.bfloat16)
    own_prob = (own_exp / total).astype(jnp.bfloat16)
    context_vector = jnp.einsum(
        "rgqt,rtgd->rgqd", probs, stored, preferred_element_type=jnp.float32
    )
    context_vector = (
        context_vector + own_prob.astype(jnp.float32)[..., None] * fresh_value[:, :, None, :]
    )
    context_vector = context_vector.reshape(rows, query_width).astype(jnp.bfloat16)
    slot_hits = slots[:, None] == jnp.arange(requests.shape[1])[None, :]
    adapter = jnp.sum(jnp.where(slot_hits, requests[0][None, :], 0), 1)
    adapter_selector = (adapter[:, None] == jnp.arange(ADAPTER_COUNT)[None, :]).astype(jnp.bfloat16)
    context_gathered, selector_gathered = (
        lax.all_gather(context_vector, "mp", axis=0, tiled=True),
        lax.all_gather(adapter_selector, "mp", axis=0, tiled=True),
    )
    shared_portion = adapter_down_matrices.shape[1]
    context_slice = lax.dynamic_slice_in_dim(
        context_gathered, lax.axis_index("mp") * shared_portion, shared_portion, 1
    )
    every_adapter = jnp.einsum(
        "gh,thy->gty", context_slice, adapter_down_matrices, preferred_element_type=jnp.float32
    )
    partial_down = jnp.sum(every_adapter * selector_gathered.astype(jnp.float32)[:, :, None], 1)
    down_gathered = lax.psum(partial_down, "mp").astype(jnp.bfloat16)
    projection_result = apply_up_matrix(
        context_gathered, selector_gathered, down_gathered, output_weight, adapter_up_matrices
    )
    returned = lax.all_to_all(projection_result, "mp", split_axis=0, concat_axis=1, tiled=True)
    return (widened + returned.astype(jnp.float32)).astype(jnp.bfloat16)


MIB = 1 << 20
LANES = 128
BATCH = 4
LONG = 10**10
STREAM = 53 * MIB
VMEM = pl.BlockSpec(memory_space=pltpu.VMEM)
SMEM = pl.BlockSpec(memory_space=pltpu.SMEM)
ANY = pl.BlockSpec(memory_space=pl.ANY)


def call(kernel, name, out_shape, in_specs, moved, limit=2 * MIB, flops=0, **options):
    return pl.pallas_call(
        kernel,
        out_shape=out_shape,
        in_specs=in_specs,
        out_specs=jax.tree.map(lambda _: VMEM, out_shape),
        compiler_params=pltpu.CompilerParams(vmem_limit_bytes=limit),
        cost_estimate=pl.CostEstimate(flops=flops, bytes_accessed=moved, transcendentals=0),
        name=name,
        **options,
    )


def exponents():
    def kernel(out_ref):
        lane = lax.broadcasted_iota(jnp.int32, (1, HEAD_DIM), 1)
        out_ref[...] = (lane % (HEAD_DIM // 2)).astype(jnp.float32) * (-2.0 / HEAD_DIM)

    shape = jax.ShapeDtypeStruct((1, HEAD_DIM), jnp.float32)
    return call(kernel, "exponents", shape, [], 0, flops=LONG // 8)()


def frequencies(exponent):
    def kernel(exponent_ref, out_ref):
        out_ref[...] = jnp.exp(exponent_ref[...] * math.log(THETA))

    shape = jax.ShapeDtypeStruct(exponent.shape, jnp.float32)
    return call(kernel, "frequencies", shape, [VMEM], 0, flops=LONG // 8)(exponent)


def norm_rows(hidden, gain, after, copies):
    rows, width = hidden.shape

    def kernel(hidden_ref, gain_ref, after_ref, out_ref):
        del after_ref
        wide = hidden_ref[...].astype(jnp.float32)
        inverse = lax.rsqrt(jnp.mean(wide * wide, -1, keepdims=True) + EPS)
        normed = (wide * inverse * gain_ref[...].astype(jnp.float32)).astype(jnp.bfloat16)
        for c in range(copies):
            out_ref[c] = normed

    return call(
        kernel,
        "norm_rows",
        jax.ShapeDtypeStruct((copies, rows, width), jnp.bfloat16),
        [VMEM, VMEM, ANY],
        hidden.size * 2 * (copies + 1),
        flops=LONG,
    )(hidden, gain[None], after)


def turns(near, frequency, lengths, slots, requests, context):
    groups, rows, depth = near.shape

    def kernel(
        lengths_ref, slots_ref, requests_ref, near_ref, frequency_ref, lined_ref, cosine_ref,
        sine_ref, mask_ref, adapter_ref,
    ):
        for j in range(groups):
            lined_ref[pl.ds(j * rows, rows)] = near_ref[j]
        row = lax.broadcasted_iota(jnp.int32, (rows, LANES), 0)
        length = jnp.zeros((rows, LANES), jnp.int32)
        adapter = jnp.zeros((rows, LANES), jnp.int32)
        for r in range(rows):
            length = jnp.where(row == r, lengths_ref[r], length)
            adapter = jnp.where(row == r, requests_ref[0, slots_ref[r]], adapter)
        angle = length.astype(jnp.float32) * frequency_ref[...]
        cosine_ref[...] = jnp.cos(angle)
        sine_ref[...] = jnp.sin(angle)
        lane = lax.broadcasted_iota(jnp.int32, (rows, LANES), 1)
        for t in range(0, context, LANES):
            mask_ref[:, pl.ds(t, LANES)] = jnp.where(lane + t < length, 0.0, -jnp.inf)
        adapter_ref[...] = adapter.astype(jnp.float32).astype(jnp.bfloat16)

    return call(
        kernel,
        "turns",
        (
            jax.ShapeDtypeStruct((groups * rows, depth), near.dtype),
            jax.ShapeDtypeStruct((rows, HEAD_DIM), jnp.float32),
            jax.ShapeDtypeStruct((rows, HEAD_DIM), jnp.float32),
            jax.ShapeDtypeStruct((rows, context), jnp.float32),
            jax.ShapeDtypeStruct((rows, LANES), jnp.bfloat16),
        ),
        [SMEM] * 3 + [VMEM] * 2,
        near.size * 4,
    )(lengths, slots, requests, near, frequency)


def project_qkv(lined, far, weight, adapter, chunk=1024):
    groups, rows, _ = far.shape
    depth, width = weight.shape
    half = groups * rows

    def kernel(lined_ref, far_ref, weight_ref, adapter_ref, out_ref, far_lined_ref):
        for j in range(groups):
            far_lined_ref[pl.ds(j * rows, rows)] = far_ref[j]
        total = jnp.zeros((2 * half, width), jnp.float32)
        for k in range(depth // chunk):
            part = pl.ds(k * chunk, chunk)
            total = total + jnp.dot(
                jnp.concatenate([lined_ref[:, part], far_lined_ref[:, part]]),
                weight_ref[part, :],
                preferred_element_type=jnp.float32,
            )
        core = lax.axis_index("batch")
        adapter = adapter_ref[...]
        for e in range(2):
            for j in range(groups):
                place = e * half + j * rows
                device = 2 * j + (core ^ e)
                out_ref[device, :, pl.ds(0, width)] = total[place : place + rows].astype(
                    jnp.bfloat16
                )
                out_ref[device, :, pl.ds(width, LANES)] = (
                    adapter if e == 0 else jnp.zeros_like(adapter)
                )

    return call(
        kernel,
        "project_qkv",
        jax.ShapeDtypeStruct((2 * groups, rows, width + LANES), jnp.bfloat16),
        [VMEM] * 4,
        weight.size * 2,
        flops=LONG,
        scratch_shapes=[pltpu.VMEM((half, depth), jnp.bfloat16)],
    )(lined, far, weight, adapter)


def stream(weight_ref, held_ref, sems, parts):
    depth = held_ref.shape[0] // parts
    copies = []
    for k in range(parts):
        rows = pl.ds(k * depth, depth)
        copies.append(
            pltpu.make_async_copy(weight_ref.at[rows], held_ref.at[rows], sems.at[k])
        )
        copies[-1].start()

    def part(k):
        copies[k].wait()
        return held_ref[pl.ds(k * depth, depth)]

    return part


def project_out(gathered, weight, adapter, store, parts=16):
    groups, rows, depth = gathered.shape
    count, step = groups * rows, depth // parts
    rank, width = store.shape[1:]

    def kernel(
        adapter_ref, gathered_ref, weight_ref, store_ref, out_ref, up_ref, rows_ref, held_ref, sems,
        up_sems,
    ):
        part = stream(weight_ref, held_ref, sems, parts)
        picks = []
        for r in range(count):
            chosen = adapter_ref[r // rows, r % rows]
            target = up_ref.at[pl.ds(r * rank, rank)]
            picks.append(pltpu.make_async_copy(store_ref.at[chosen], target, up_sems.at[r]))
            picks[-1].start()
        for j in range(groups):
            rows_ref[pl.ds(j * rows, rows)] = gathered_ref[j]
        total = jnp.zeros(out_ref.shape, jnp.float32)
        for k in range(parts):
            total = total + jnp.dot(
                rows_ref[:, pl.ds(k * step, step)], part(k), preferred_element_type=jnp.float32
            )
        out_ref[...] = total
        for pick in picks:
            pick.wait()

    return call(
        kernel,
        "project_out",
        (
            jax.ShapeDtypeStruct((count, weight.shape[1]), jnp.float32),
            pltpu.VMEM((count * rank, width), store.dtype),
        ),
        [SMEM, VMEM, ANY, ANY],
        weight.size * 2 + count * rank * width * 2,
        limit=STREAM,
        flops=2 * count * weight.size,
        scratch_shapes=[
            pltpu.VMEM((count, depth), gathered.dtype),
            pltpu.VMEM(weight.shape, weight.dtype),
            pltpu.SemaphoreType.DMA((parts,)),
            pltpu.SemaphoreType.DMA((count,)),
        ],
    )(adapter, gathered, weight, store)


def down_partials(gathered, adapter, store):
    groups, rows, _ = gathered.shape
    count = groups * rows
    rank, depth = store.shape[1:]

    def kernel(adapter_ref, gathered_ref, store_ref, out_ref, rows_ref):
        start = pl.multiple_of(lax.axis_index("mp") * depth, depth)
        for j in range(groups):
            rows_ref[pl.ds(j * rows, rows)] = gathered_ref[j, :, pl.ds(start, depth)]
        row = lax.broadcasted_iota(jnp.int32, (count, LANES), 0)
        lane = lax.broadcasted_iota(jnp.int32, (count, LANES), 1)
        total = jnp.zeros((count, LANES), jnp.float32)
        for k in range(count // BATCH):
            chosen = [adapter_ref[r // rows, r % rows] for r in range(k * BATCH, (k + 1) * BATCH)]
            every = lax.dot_general(
                rows_ref[...],
                jnp.concatenate([store_ref[c] for c in chosen]),
                (((1,), (1,)), ((), ())),
                preferred_element_type=jnp.float32,
            )
            for s in range(BATCH * rank // LANES):
                first = k * BATCH * rank + s * LANES
                mine = row == (lane + first) // rank
                total = total + jnp.where(mine, every[:, s * LANES : (s + 1) * LANES], 0.0)
        for c in range(groups):
            out_ref[c] = total

    return call(
        kernel,
        "down_partials",
        jax.ShapeDtypeStruct((groups, count, LANES), jnp.float32),
        [SMEM, VMEM, VMEM],
        2 * count * rank * depth,
        limit=4 * MIB,
        flops=2 * count * count * rank * depth,
        scratch_shapes=[pltpu.VMEM((count, depth), gathered.dtype)],
    )(adapter, gathered, store)


def add_up(base, partials, up):
    groups, count, _ = partials.shape
    depth, width = up.shape
    rank = depth // count

    def kernel(base_ref, partials_ref, up_ref, out_ref):
        total = partials_ref[0]
        for c in range(1, groups):
            total = total + partials_ref[c]
        down = total.astype(jnp.bfloat16).astype(jnp.float32)
        row = lax.broadcasted_iota(jnp.int32, (count, LANES), 0)
        lane = lax.broadcasted_iota(jnp.int32, (count, LANES), 1)
        spread = []
        for s in range(0, depth, LANES):
            spread.append(jnp.where(row == (lane + s) // rank, down, 0.0))
        spread = jnp.concatenate(spread, 1).astype(jnp.bfloat16)
        delta = jnp.dot(spread, up_ref[...], preferred_element_type=jnp.float32)
        result = (base_ref[...] + ADAPTER_SCALE * delta).astype(jnp.bfloat16)
        for j in range(groups):
            out_ref[j] = result[j * count // groups : (j + 1) * count // groups]

    return call(
        kernel,
        "add_up",
        jax.ShapeDtypeStruct((groups, count // groups, width), jnp.bfloat16),
        [VMEM] * 3,
        up.size * 2,
        limit=4 * MIB,
        flops=2 * count * up.size,
    )(base, partials, up)


def add_rows(hidden, parts):
    width = parts.shape[2]

    def kernel(hidden_ref, parts_ref, out_ref):
        for k in range(parts.shape[0]):
            part = pl.ds(k * width, width)
            total = hidden_ref[:, part].astype(jnp.float32) + parts_ref[k].astype(jnp.float32)
            out_ref[:, part] = total.astype(jnp.bfloat16)

    return call(
        kernel,
        "add_rows",
        jax.ShapeDtypeStruct(hidden.shape, parts.dtype),
        [VMEM, VMEM],
        hidden.size * 6,
    )(hidden, parts)


def swap_cores(block):
    return lax.ppermute(block, "batch", [(0, 1), (1, 0)])


def exchange(blocks, axes="mp"):
    return lax.all_to_all(blocks, axes, split_axis=0, concat_axis=0, tiled=True)


def attend(qkv, cosine, sine, key_cache, value_cache, mask):
    rows = qkv.shape[0]
    query_width = HEADS * HEAD_DIM
    kv_width = KV_HEADS * HEAD_DIM
    group = HEADS // KV_HEADS
    scale = HEAD_DIM ** (-0.5)

    def turn(part):
        vec = part.astype(jnp.float32).reshape(rows, -1, HEAD_DIM)
        half = HEAD_DIM // 2
        turned = jnp.concatenate([-vec[..., half:], vec[..., :half]], -1)
        return (vec * cosine[:, None] + turned * sine[:, None]).astype(jnp.bfloat16)

    query = turn(qkv[:, :query_width])
    fresh_key = turn(qkv[:, query_width : query_width + kv_width])
    fresh_value = (
        qkv[:, query_width + kv_width :].astype(jnp.float32).reshape(rows, KV_HEADS, HEAD_DIM)
    )
    grouped = query.reshape(rows, KV_HEADS, group, HEAD_DIM)
    cached = key_cache.reshape(rows, -1, KV_HEADS, HEAD_DIM)
    stored = value_cache.reshape(rows, -1, KV_HEADS, HEAD_DIM)
    scores = (
        jnp.einsum("rgqd,rtgd->rgqt", grouped, cached, preferred_element_type=jnp.float32) * scale
    )
    scores = scores + mask[:, None, None, :]
    own = (
        jnp.einsum("rgqd,rgd->rgq", grouped, fresh_key, preferred_element_type=jnp.float32) * scale
    )
    top = jnp.maximum(jnp.max(scores, -1), own)
    expo = jnp.exp(scores - top[..., None])
    own_exp = jnp.exp(own - top)
    total = jnp.sum(expo, -1) + own_exp
    probs = (expo / total[..., None]).astype(jnp.bfloat16)
    own_prob = (own_exp / total).astype(jnp.bfloat16)
    context_vector = jnp.einsum(
        "rgqt,rtgd->rgqd", probs, stored, preferred_element_type=jnp.float32
    )
    context_vector = (
        context_vector + own_prob.astype(jnp.float32)[..., None] * fresh_value[:, :, None, :]
    )
    return context_vector.reshape(rows, query_width).astype(jnp.bfloat16)


def fast_body(
    hidden,
    attention_norm_gain,
    query_key_value_weight,
    output_weight,
    key_cache,
    value_cache,
    lengths,
    slots,
    requests,
    adapter_down_matrices,
    adapter_up_matrices,
):
    rows = hidden.shape[0]
    mp_size = lax.axis_size("mp")
    width = query_key_value_weight.shape[1]

    frequency = frequencies(exponents())
    near = exchange(norm_rows(hidden, attention_norm_gain, frequency, mp_size))
    lined, cosine, sine, mask, adapter = turns(
        near, frequency, lengths, slots, requests, key_cache.shape[1]
    )
    columns = project_qkv(lined, swap_cores(near), query_key_value_weight, adapter)
    mixed = exchange(columns, ("mp", "batch"))
    adapter = mixed.reshape(mp_size, -1, rows, width + LANES)[:, :, :, width]
    adapter = jnp.sum(adapter.astype(jnp.float32), 1).astype(jnp.int32)
    qkv = mixed[:, :, :width].transpose(1, 0, 2).reshape(rows, -1)

    context = attend(qkv, cosine, sine, key_cache, value_cache, mask)
    context, adapter = lax.optimization_barrier((context, adapter))
    gathered = exchange(jnp.broadcast_to(context[None], (mp_size, *context.shape)))

    partials = exchange(
        down_partials(gathered, adapter, adapter_down_matrices.swapaxes(1, 2))
    )
    base, up = project_out(gathered, output_weight, adapter, adapter_up_matrices)
    projected = add_up(base, partials, up)
    return add_rows(hidden, exchange(projected))


def body(*arguments):
    small = lax.axis_size("mp") <= 16 and lax.axis_size("batch") == 2
    whole_heads = arguments[2].shape[1] % HEAD_DIM == 0
    return (fast_body if small and whole_heads else general_body)(*arguments)


def solution(mesh):
    in_specs = (
        P(("groups", "mp", "batch"), None),
        P(),
        P(None, ("mp", "batch")),
        P(None, "mp"),
        P(("groups", "mp", "batch"), None, None),
        P(("groups", "mp", "batch"), None, None),
        P(("groups", "mp", "batch")),
        P(("groups", "mp", "batch")),
        P(("groups", "mp", "batch"), None),
        P(None, "mp", None),
        P(None, None, "mp"),
    )
    out_specs = P(("groups", "mp", "batch"), None)
    return jax.shard_map(body, mesh=mesh, in_specs=in_specs, out_specs=out_specs, check_vma=False)
```

```python
import math

import jax
import jax.numpy as jnp
from jax import lax
from jax.experimental import pallas as pl
from jax.experimental.pallas import tpu as pltpu
from jax.sharding import PartitionSpec as P

HEADS = 64
KV_HEADS = 8
HEAD_DIM = 128
ADAPTER_COUNT = 64


EPS = 1e-05
THETA = 500000.0
ADAPTER_SCALE = 2.0


def rotate(vec, pos):
    width = vec.shape[-1]
    half = width // 2
    freq = THETA ** (-(jnp.arange(half, dtype=jnp.float32) * 2.0) / width)
    angle = pos[..., None, None] * freq
    cosine = jnp.concatenate([jnp.cos(angle), jnp.cos(angle)], -1)
    sine = jnp.concatenate([jnp.sin(angle), jnp.sin(angle)], -1)
    turned = jnp.concatenate([-vec[..., half:], vec[..., :half]], -1)
    return vec * cosine + turned * sine


def apply_up_matrix(
    context_vector, adapter_selector, down_result, output_weight, adapter_up_matrices
):
    base_output = jnp.dot(context_vector, output_weight, preferred_element_type=jnp.float32)
    spread = (adapter_selector[:, :, None] * down_result[:, None, :]).reshape(
        adapter_selector.shape[0], -1
    )
    adapter_table = adapter_up_matrices.reshape(-1, adapter_up_matrices.shape[2])
    adapter_delta = jnp.dot(spread, adapter_table, preferred_element_type=jnp.float32)
    return (base_output + ADAPTER_SCALE * adapter_delta).astype(jnp.bfloat16)


def general_body(
    hidden,
    attention_norm_gain,
    query_key_value_weight,
    output_weight,
    key_cache,
    value_cache,
    lengths,
    slots,
    requests,
    adapter_down_matrices,
    adapter_up_matrices,
):
    widened = hidden.astype(jnp.float32)
    normed = (
        widened
        * lax.rsqrt(jnp.mean(widened * widened, -1, keepdims=True) + EPS)
        * attention_norm_gain.astype(jnp.float32)
    ).astype(jnp.bfloat16)
    rows = normed.shape[0]
    columns = jnp.dot(
        lax.all_gather(normed, ("mp", "batch"), axis=0, tiled=True),
        query_key_value_weight,
        preferred_element_type=jnp.float32,
    ).astype(jnp.bfloat16)
    mixed = lax.all_to_all(
        lax.all_to_all(columns, "mp", split_axis=0, concat_axis=1, tiled=True),
        "batch",
        split_axis=0,
        concat_axis=1,
        tiled=True,
    )
    width = query_key_value_weight.shape[1]
    qkv = (
        mixed.reshape(rows, lax.axis_size("batch"), lax.axis_size("mp"), width)
        .transpose(0, 2, 1, 3)
        .reshape(rows, -1)
    )
    query_width = HEADS * HEAD_DIM
    kv_width = KV_HEADS * HEAD_DIM
    group = HEADS // KV_HEADS
    scale = HEAD_DIM ** (-0.5)
    pos = lengths.astype(jnp.float32)
    query = rotate(
        qkv[:, :query_width].astype(jnp.float32).reshape(rows, HEADS, HEAD_DIM), pos
    ).astype(jnp.bfloat16)
    fresh_key = rotate(
        qkv[:, query_width : query_width + kv_width]
        .astype(jnp.float32)
        .reshape(rows, KV_HEADS, HEAD_DIM),
        pos,
    ).astype(jnp.bfloat16)
    fresh_value = (
        qkv[:, query_width + kv_width :].astype(jnp.float32).reshape(rows, KV_HEADS, HEAD_DIM)
    )
    grouped = query.reshape(rows, KV_HEADS, group, HEAD_DIM)
    cached = key_cache.reshape(rows, -1, KV_HEADS, HEAD_DIM)
    stored = value_cache.reshape(rows, -1, KV_HEADS, HEAD_DIM)
    scores = (
        jnp.einsum("rgqd,rtgd->rgqt", grouped, cached, preferred_element_type=jnp.float32) * scale
    )
    live = jnp.arange(cached.shape[1])[None, :] < lengths[:, None]
    scores = jnp.where(live[:, None, None, :], scores, -jnp.inf)
    own = (
        jnp.einsum("rgqd,rgd->rgq", grouped, fresh_key, preferred_element_type=jnp.float32) * scale
    )
    top = jnp.maximum(jnp.max(scores, -1), own)
    expo = jnp.exp(scores - top[..., None])
    own_exp = jnp.exp(own - top)
    total = jnp.sum(expo, -1) + own_exp
    probs = (expo / total[..., None]).astype(jnp.bfloat16)
    own_prob = (own_exp / total).astype(jnp.bfloat16)
    context_vector = jnp.einsum(
        "rgqt,rtgd->rgqd", probs, stored, preferred_element_type=jnp.float32
    )
    context_vector = (
        context_vector + own_prob.astype(jnp.float32)[..., None] * fresh_value[:, :, None, :]
    )
    context_vector = context_vector.reshape(rows, query_width).astype(jnp.bfloat16)
    slot_hits = slots[:, None] == jnp.arange(requests.shape[1])[None, :]
    adapter = jnp.sum(jnp.where(slot_hits, requests[0][None, :], 0), 1)
    adapter_selector = (adapter[:, None] == jnp.arange(ADAPTER_COUNT)[None, :]).astype(jnp.bfloat16)
    context_gathered, selector_gathered = (
        lax.all_gather(context_vector, "mp", axis=0, tiled=True),
        lax.all_gather(adapter_selector, "mp", axis=0, tiled=True),
    )
    shared_portion = adapter_down_matrices.shape[1]
    context_slice = lax.dynamic_slice_in_dim(
        context_gathered, lax.axis_index("mp") * shared_portion, shared_portion, 1
    )
    every_adapter = jnp.einsum(
        "gh,thy->gty", context_slice, adapter_down_matrices, preferred_element_type=jnp.float32
    )
    partial_down = jnp.sum(every_adapter * selector_gathered.astype(jnp.float32)[:, :, None], 1)
    down_gathered = lax.psum(partial_down, "mp").astype(jnp.bfloat16)
    projection_result = apply_up_matrix(
        context_gathered, selector_gathered, down_gathered, output_weight, adapter_up_matrices
    )
    returned = lax.all_to_all(projection_result, "mp", split_axis=0, concat_axis=1, tiled=True)
    return (widened + returned.astype(jnp.float32)).astype(jnp.bfloat16)


MIB = 1 << 20
LANES = 128
BATCH = 4
LONG = 10**10
STREAM = 53 * MIB
VMEM = pl.BlockSpec(memory_space=pltpu.VMEM)
SMEM = pl.BlockSpec(memory_space=pltpu.SMEM)
ANY = pl.BlockSpec(memory_space=pl.ANY)


def call(kernel, name, out_shape, in_specs, moved, limit=2 * MIB, flops=0, **options):
    return pl.pallas_call(
        kernel,
        out_shape=out_shape,
        in_specs=in_specs,
        out_specs=jax.tree.map(lambda _: VMEM, out_shape),
        compiler_params=pltpu.CompilerParams(vmem_limit_bytes=limit),
        cost_estimate=pl.CostEstimate(flops=flops, bytes_accessed=moved, transcendentals=0),
        name=name,
        **options,
    )


def exponents():
    def kernel(out_ref):
        lane = lax.broadcasted_iota(jnp.int32, (1, HEAD_DIM), 1)
        out_ref[...] = (lane % (HEAD_DIM // 2)).astype(jnp.float32) * (-2.0 / HEAD_DIM)

    shape = jax.ShapeDtypeStruct((1, HEAD_DIM), jnp.float32)
    return call(kernel, "exponents", shape, [], 0, flops=LONG // 8)()


def frequencies(exponent):
    def kernel(exponent_ref, out_ref):
        out_ref[...] = jnp.exp(exponent_ref[...] * math.log(THETA))

    shape = jax.ShapeDtypeStruct(exponent.shape, jnp.float32)
    return call(kernel, "frequencies", shape, [VMEM], 0, flops=LONG // 8)(exponent)


def norm_rows(hidden, gain, after, copies):
    rows, width = hidden.shape

    def kernel(hidden_ref, gain_ref, after_ref, out_ref):
        del after_ref
        wide = hidden_ref[...].astype(jnp.float32)
        inverse = lax.rsqrt(jnp.mean(wide * wide, -1, keepdims=True) + EPS)
        normed = (wide * inverse * gain_ref[...].astype(jnp.float32)).astype(jnp.bfloat16)
        for c in range(copies):
            out_ref[c] = normed

    return call(
        kernel,
        "norm_rows",
        jax.ShapeDtypeStruct((copies, rows, width), jnp.bfloat16),
        [VMEM, VMEM, ANY],
        hidden.size * 2 * (copies + 1),
        flops=LONG,
    )(hidden, gain[None], after)


def turns(near, frequency, lengths, slots, requests, context):
    groups, rows, depth = near.shape

    def kernel(
        lengths_ref, slots_ref, requests_ref, near_ref, frequency_ref, lined_ref, cosine_ref,
        sine_ref, mask_ref, adapter_ref,
    ):
        for j in range(groups):
            lined_ref[pl.ds(j * rows, rows)] = near_ref[j]
        row = lax.broadcasted_iota(jnp.int32, (rows, LANES), 0)
        length = jnp.zeros((rows, LANES), jnp.int32)
        adapter = jnp.zeros((rows, LANES), jnp.int32)
        for r in range(rows):
            length = jnp.where(row == r, lengths_ref[r], length)
            adapter = jnp.where(row == r, requests_ref[0, slots_ref[r]], adapter)
        angle = length.astype(jnp.float32) * frequency_ref[...]
        cosine_ref[...] = jnp.cos(angle)
        sine_ref[...] = jnp.sin(angle)
        lane = lax.broadcasted_iota(jnp.int32, (rows, LANES), 1)
        for t in range(0, context, LANES):
            mask_ref[:, pl.ds(t, LANES)] = jnp.where(lane + t < length, 0.0, -jnp.inf)
        adapter_ref[...] = adapter.astype(jnp.float32).astype(jnp.bfloat16)

    return call(
        kernel,
        "turns",
        (
            jax.ShapeDtypeStruct((groups * rows, depth), near.dtype),
            jax.ShapeDtypeStruct((rows, HEAD_DIM), jnp.float32),
            jax.ShapeDtypeStruct((rows, HEAD_DIM), jnp.float32),
            jax.ShapeDtypeStruct((rows, context), jnp.float32),
            jax.ShapeDtypeStruct((rows, LANES), jnp.bfloat16),
        ),
        [SMEM] * 3 + [VMEM] * 2,
        near.size * 4,
    )(lengths, slots, requests, near, frequency)


def project_qkv(lined, far, weight, adapter, chunk=1024):
    groups, rows, _ = far.shape
    depth, width = weight.shape
    half = groups * rows

    def kernel(lined_ref, far_ref, weight_ref, adapter_ref, out_ref, far_lined_ref):
        for j in range(groups):
            far_lined_ref[pl.ds(j * rows, rows)] = far_ref[j]
        total = jnp.zeros((2 * half, width), jnp.float32)
        for k in range(depth // chunk):
            part = pl.ds(k * chunk, chunk)
            total = total + jnp.dot(
                jnp.concatenate([lined_ref[:, part], far_lined_ref[:, part]]),
                weight_ref[part, :],
                preferred_element_type=jnp.float32,
            )
        core = lax.axis_index("batch")
        adapter = adapter_ref[...]
        for e in range(2):
            for j in range(groups):
                place = e * half + j * rows
                device = 2 * j + (core ^ e)
                out_ref[device, :, pl.ds(0, width)] = total[place : place + rows].astype(
                    jnp.bfloat16
                )
                out_ref[device, :, pl.ds(width, LANES)] = (
                    adapter if e == 0 else jnp.zeros_like(adapter)
                )

    return call(
        kernel,
        "project_qkv",
        jax.ShapeDtypeStruct((2 * groups, rows, width + LANES), jnp.bfloat16),
        [VMEM] * 4,
        weight.size * 2,
        flops=LONG,
        scratch_shapes=[pltpu.VMEM((half, depth), jnp.bfloat16)],
    )(lined, far, weight, adapter)


def stream(weight_ref, held_ref, sems, parts):
    depth = held_ref.shape[0] // parts
    copies = []
    for k in range(parts):
        rows = pl.ds(k * depth, depth)
        copies.append(
            pltpu.make_async_copy(weight_ref.at[rows], held_ref.at[rows], sems.at[k])
        )
        copies[-1].start()

    def part(k):
        copies[k].wait()
        return held_ref[pl.ds(k * depth, depth)]

    return part


def project_out(gathered, weight, adapter, store, parts=16):
    groups, rows, depth = gathered.shape
    count, step = groups * rows, depth // parts
    rank, width = store.shape[1:]

    def kernel(
        adapter_ref, gathered_ref, weight_ref, store_ref, out_ref, up_ref, ids_ref, near_ref,
        rows_ref, held_ref, sems, up_sems, other_sems,
    ):
        ids = pltpu.make_async_copy(adapter_ref, ids_ref, other_sems.at[0])
        near = pltpu.make_async_copy(gathered_ref, near_ref, other_sems.at[1])
        ids.start()
        near.start()
        part = stream(weight_ref, held_ref, sems, parts)
        ids.wait()
        picks = []
        for r in range(count):
            chosen = ids_ref[r // rows, r % rows]
            target = up_ref.at[pl.ds(r * rank, rank)]
            picks.append(pltpu.make_async_copy(store_ref.at[chosen], target, up_sems.at[r]))
            picks[-1].start()
        near.wait()
        for j in range(groups):
            rows_ref[pl.ds(j * rows, rows)] = near_ref[j]
        total = jnp.zeros(out_ref.shape, jnp.float32)
        for k in range(parts):
            total = total + jnp.dot(
                rows_ref[:, pl.ds(k * step, step)], part(k), preferred_element_type=jnp.float32
            )
        out_ref[...] = total
        for pick in picks:
            pick.wait()

    return call(
        kernel,
        "project_out",
        (
            pltpu.VMEM((count, weight.shape[1]), jnp.float32),
            pltpu.VMEM((count * rank, width), store.dtype),
        ),
        [ANY] * 4,
        weight.size * 2 + count * rank * width * 2,
        limit=STREAM,
        flops=2 * count * weight.size,
        scratch_shapes=[
            pltpu.SMEM(adapter.shape, adapter.dtype),
            pltpu.VMEM(gathered.shape, gathered.dtype),
            pltpu.VMEM((count, depth), gathered.dtype),
            pltpu.VMEM(weight.shape, weight.dtype),
            pltpu.SemaphoreType.DMA((parts,)),
            pltpu.SemaphoreType.DMA((count,)),
            pltpu.SemaphoreType.DMA((2,)),
        ],
    )(adapter, gathered, weight, store)


def down_partials(gathered, adapter, store):
    groups, rows, _ = gathered.shape
    count = groups * rows
    rank, depth = store.shape[1:]

    def kernel(adapter_ref, gathered_ref, store_ref, out_ref, rows_ref):
        start = pl.multiple_of(lax.axis_index("mp") * depth, depth)
        rows_ref[...] = jnp.zeros_like(rows_ref)
        for j in range(groups):
            rows_ref[pl.ds(j * rows, rows)] = gathered_ref[j, :, pl.ds(start, depth)]
        lane = lax.broadcasted_iota(jnp.int32, (rank, LANES), 1)
        total = jnp.zeros((rank, LANES), jnp.float32)
        for k in range(0, count, BATCH):
            chosen = [adapter_ref[r // rows, r % rows] for r in range(k, k + BATCH)]
            every = lax.dot_general(
                jnp.concatenate([store_ref[c] for c in chosen]),
                rows_ref[...],
                (((1,), (1,)), ((), ())),
                preferred_element_type=jnp.float32,
            )
            for i in range(BATCH):
                mine = every[i * rank : (i + 1) * rank]
                total = total + jnp.where(lane == k + i, mine, 0.0)
        turned = total.T[:count]
        turned = jnp.concatenate([turned, turned], 1)
        for c in range(groups):
            out_ref[c] = turned

    return call(
        kernel,
        "down_partials",
        jax.ShapeDtypeStruct((groups, count, 2 * rank), jnp.float32),
        [SMEM, VMEM, VMEM],
        2 * count * rank * depth,
        limit=4 * MIB,
        flops=2 * count * count * rank * depth,
        scratch_shapes=[pltpu.VMEM((LANES, depth), gathered.dtype)],
    )(adapter, gathered, store)


def add_up(base, partials, up):
    groups, count, _ = partials.shape
    depth, width = up.shape
    rank = depth // count

    def kernel(base_ref, partials_ref, up_ref, out_ref):
        total = partials_ref[0]
        for c in range(1, groups):
            total = total + partials_ref[c]
        down = total.astype(jnp.bfloat16).astype(jnp.float32)
        row = lax.broadcasted_iota(jnp.int32, (count, LANES), 0)
        lane = lax.broadcasted_iota(jnp.int32, (count, LANES), 1)
        spread = []
        for s in range(0, depth, LANES):
            spread.append(jnp.where(row == (lane + s) // rank, down, 0.0))
        spread = jnp.concatenate(spread, 1).astype(jnp.bfloat16)
        delta = jnp.dot(spread, up_ref[...], preferred_element_type=jnp.float32)
        result = (base_ref[...] + ADAPTER_SCALE * delta).astype(jnp.bfloat16)
        for j in range(groups):
            out_ref[j] = result[j * count // groups : (j + 1) * count // groups]

    return call(
        kernel,
        "add_up",
        jax.ShapeDtypeStruct((groups, count // groups, width), jnp.bfloat16),
        [VMEM] * 3,
        up.size * 2,
        limit=4 * MIB,
        flops=2 * count * up.size,
    )(base, partials, up)


def add_rows(hidden, parts):
    width = parts.shape[2]

    def kernel(hidden_ref, parts_ref, out_ref):
        for k in range(parts.shape[0]):
            part = pl.ds(k * width, width)
            total = hidden_ref[:, part].astype(jnp.float32) + parts_ref[k].astype(jnp.float32)
            out_ref[:, part] = total.astype(jnp.bfloat16)

    return call(
        kernel,
        "add_rows",
        jax.ShapeDtypeStruct(hidden.shape, parts.dtype),
        [VMEM, VMEM],
        hidden.size * 6,
    )(hidden, parts)


def swap_cores(block):
    return lax.ppermute(block, "batch", [(0, 1), (1, 0)])


def exchange(blocks, axes="mp"):
    return lax.all_to_all(blocks, axes, split_axis=0, concat_axis=0, tiled=True)


def attend(qkv, cosine, sine, key_cache, value_cache, mask):
    rows = qkv.shape[0]
    query_width = HEADS * HEAD_DIM
    kv_width = KV_HEADS * HEAD_DIM
    group = HEADS // KV_HEADS
    scale = HEAD_DIM ** (-0.5)

    def turn(part):
        vec = part.astype(jnp.float32).reshape(rows, -1, HEAD_DIM)
        half = HEAD_DIM // 2
        turned = jnp.concatenate([-vec[..., half:], vec[..., :half]], -1)
        return (vec * cosine[:, None] + turned * sine[:, None]).astype(jnp.bfloat16)

    query = turn(qkv[:, :query_width])
    fresh_key = turn(qkv[:, query_width : query_width + kv_width])
    fresh_value = (
        qkv[:, query_width + kv_width :].astype(jnp.float32).reshape(rows, KV_HEADS, HEAD_DIM)
    )
    grouped = query.reshape(rows, KV_HEADS, group, HEAD_DIM)
    cached = key_cache.reshape(rows, -1, KV_HEADS, HEAD_DIM)
    stored = value_cache.reshape(rows, -1, KV_HEADS, HEAD_DIM)
    scores = (
        jnp.einsum("rgqd,rtgd->rgqt", grouped, cached, preferred_element_type=jnp.float32) * scale
    )
    scores = scores + mask[:, None, None, :]
    own = (
        jnp.einsum("rgqd,rgd->rgq", grouped, fresh_key, preferred_element_type=jnp.float32) * scale
    )
    top = jnp.maximum(jnp.max(scores, -1), own)
    expo = jnp.exp(scores - top[..., None])
    own_exp = jnp.exp(own - top)
    total = jnp.sum(expo, -1) + own_exp
    probs = (expo / total[..., None]).astype(jnp.bfloat16)
    own_prob = (own_exp / total).astype(jnp.bfloat16)
    context_vector = jnp.einsum(
        "rgqt,rtgd->rgqd", probs, stored, preferred_element_type=jnp.float32
    )
    context_vector = (
        context_vector + own_prob.astype(jnp.float32)[..., None] * fresh_value[:, :, None, :]
    )
    return context_vector.reshape(rows, query_width).astype(jnp.bfloat16)


def fast_body(
    hidden,
    attention_norm_gain,
    query_key_value_weight,
    output_weight,
    key_cache,
    value_cache,
    lengths,
    slots,
    requests,
    adapter_down_matrices,
    adapter_up_matrices,
):
    rows = hidden.shape[0]
    mp_size = lax.axis_size("mp")
    width = query_key_value_weight.shape[1]

    frequency = frequencies(exponents())
    near = exchange(norm_rows(hidden, attention_norm_gain, frequency, mp_size))
    lined, cosine, sine, mask, adapter = turns(
        near, frequency, lengths, slots, requests, key_cache.shape[1]
    )
    columns = project_qkv(lined, swap_cores(near), query_key_value_weight, adapter)
    mixed = exchange(columns, ("mp", "batch"))
    adapter = mixed.reshape(mp_size, -1, rows, width + LANES)[:, :, :, width]
    adapter = jnp.sum(adapter.astype(jnp.float32), 1).astype(jnp.int32)
    qkv = mixed[:, :, :width].transpose(1, 0, 2).reshape(rows, -1)

    context = attend(qkv, cosine, sine, key_cache, value_cache, mask)
    context, adapter = lax.optimization_barrier((context, adapter))
    gathered = exchange(jnp.broadcast_to(context[None], (mp_size, *context.shape)))

    partials = exchange(
        down_partials(gathered, adapter, adapter_down_matrices.swapaxes(1, 2))
    )
    base, up = project_out(gathered, output_weight, adapter, adapter_up_matrices)
    projected = add_up(base, partials, up)
    return add_rows(hidden, exchange(projected))


def body(*arguments):
    small = lax.axis_size("mp") <= 16 and lax.axis_size("batch") == 2
    whole_heads = arguments[2].shape[1] % HEAD_DIM == 0
    return (fast_body if small and whole_heads else general_body)(*arguments)


def solution(mesh):
    in_specs = (
        P(("groups", "mp", "batch"), None),
        P(),
        P(None, ("mp", "batch")),
        P(None, "mp"),
        P(("groups", "mp", "batch"), None, None),
        P(("groups", "mp", "batch"), None, None),
        P(("groups", "mp", "batch")),
        P(("groups", "mp", "batch")),
        P(("groups", "mp", "batch"), None),
        P(None, "mp", None),
        P(None, None, "mp"),
    )
    out_specs = P(("groups", "mp", "batch"), None)
    return jax.shard_map(body, mesh=mesh, in_specs=in_specs, out_specs=out_specs, check_vma=False)
```

```python
import math

import jax
import jax.numpy as jnp
from jax import lax
from jax.experimental import pallas as pl
from jax.experimental.pallas import tpu as pltpu
from jax.sharding import PartitionSpec as P

HEADS = 64
KV_HEADS = 8
HEAD_DIM = 128
ADAPTER_COUNT = 64


EPS = 1e-05
THETA = 500000.0
ADAPTER_SCALE = 2.0


def rotate(vec, pos):
    width = vec.shape[-1]
    half = width // 2
    freq = THETA ** (-(jnp.arange(half, dtype=jnp.float32) * 2.0) / width)
    angle = pos[..., None, None] * freq
    cosine = jnp.concatenate([jnp.cos(angle), jnp.cos(angle)], -1)
    sine = jnp.concatenate([jnp.sin(angle), jnp.sin(angle)], -1)
    turned = jnp.concatenate([-vec[..., half:], vec[..., :half]], -1)
    return vec * cosine + turned * sine


def apply_up_matrix(
    context_vector, adapter_selector, down_result, output_weight, adapter_up_matrices
):
    base_output = jnp.dot(context_vector, output_weight, preferred_element_type=jnp.float32)
    spread = (adapter_selector[:, :, None] * down_result[:, None, :]).reshape(
        adapter_selector.shape[0], -1
    )
    adapter_table = adapter_up_matrices.reshape(-1, adapter_up_matrices.shape[2])
    adapter_delta = jnp.dot(spread, adapter_table, preferred_element_type=jnp.float32)
    return (base_output + ADAPTER_SCALE * adapter_delta).astype(jnp.bfloat16)


def general_body(
    hidden,
    attention_norm_gain,
    query_key_value_weight,
    output_weight,
    key_cache,
    value_cache,
    lengths,
    slots,
    requests,
    adapter_down_matrices,
    adapter_up_matrices,
):
    widened = hidden.astype(jnp.float32)
    normed = (
        widened
        * lax.rsqrt(jnp.mean(widened * widened, -1, keepdims=True) + EPS)
        * attention_norm_gain.astype(jnp.float32)
    ).astype(jnp.bfloat16)
    rows = normed.shape[0]
    columns = jnp.dot(
        lax.all_gather(normed, ("mp", "batch"), axis=0, tiled=True),
        query_key_value_weight,
        preferred_element_type=jnp.float32,
    ).astype(jnp.bfloat16)
    mixed = lax.all_to_all(
        lax.all_to_all(columns, "mp", split_axis=0, concat_axis=1, tiled=True),
        "batch",
        split_axis=0,
        concat_axis=1,
        tiled=True,
    )
    width = query_key_value_weight.shape[1]
    qkv = (
        mixed.reshape(rows, lax.axis_size("batch"), lax.axis_size("mp"), width)
        .transpose(0, 2, 1, 3)
        .reshape(rows, -1)
    )
    query_width = HEADS * HEAD_DIM
    kv_width = KV_HEADS * HEAD_DIM
    group = HEADS // KV_HEADS
    scale = HEAD_DIM ** (-0.5)
    pos = lengths.astype(jnp.float32)
    query = rotate(
        qkv[:, :query_width].astype(jnp.float32).reshape(rows, HEADS, HEAD_DIM), pos
    ).astype(jnp.bfloat16)
    fresh_key = rotate(
        qkv[:, query_width : query_width + kv_width]
        .astype(jnp.float32)
        .reshape(rows, KV_HEADS, HEAD_DIM),
        pos,
    ).astype(jnp.bfloat16)
    fresh_value = (
        qkv[:, query_width + kv_width :].astype(jnp.float32).reshape(rows, KV_HEADS, HEAD_DIM)
    )
    grouped = query.reshape(rows, KV_HEADS, group, HEAD_DIM)
    cached = key_cache.reshape(rows, -1, KV_HEADS, HEAD_DIM)
    stored = value_cache.reshape(rows, -1, KV_HEADS, HEAD_DIM)
    scores = (
        jnp.einsum("rgqd,rtgd->rgqt", grouped, cached, preferred_element_type=jnp.float32) * scale
    )
    live = jnp.arange(cached.shape[1])[None, :] < lengths[:, None]
    scores = jnp.where(live[:, None, None, :], scores, -jnp.inf)
    own = (
        jnp.einsum("rgqd,rgd->rgq", grouped, fresh_key, preferred_element_type=jnp.float32) * scale
    )
    top = jnp.maximum(jnp.max(scores, -1), own)
    expo = jnp.exp(scores - top[..., None])
    own_exp = jnp.exp(own - top)
    total = jnp.sum(expo, -1) + own_exp
    probs = (expo / total[..., None]).astype(jnp.bfloat16)
    own_prob = (own_exp / total).astype(jnp.bfloat16)
    context_vector = jnp.einsum(
        "rgqt,rtgd->rgqd", probs, stored, preferred_element_type=jnp.float32
    )
    context_vector = (
        context_vector + own_prob.astype(jnp.float32)[..., None] * fresh_value[:, :, None, :]
    )
    context_vector = context_vector.reshape(rows, query_width).astype(jnp.bfloat16)
    slot_hits = slots[:, None] == jnp.arange(requests.shape[1])[None, :]
    adapter = jnp.sum(jnp.where(slot_hits, requests[0][None, :], 0), 1)
    adapter_selector = (adapter[:, None] == jnp.arange(ADAPTER_COUNT)[None, :]).astype(jnp.bfloat16)
    context_gathered, selector_gathered = (
        lax.all_gather(context_vector, "mp", axis=0, tiled=True),
        lax.all_gather(adapter_selector, "mp", axis=0, tiled=True),
    )
    shared_portion = adapter_down_matrices.shape[1]
    context_slice = lax.dynamic_slice_in_dim(
        context_gathered, lax.axis_index("mp") * shared_portion, shared_portion, 1
    )
    every_adapter = jnp.einsum(
        "gh,thy->gty", context_slice, adapter_down_matrices, preferred_element_type=jnp.float32
    )
    partial_down = jnp.sum(every_adapter * selector_gathered.astype(jnp.float32)[:, :, None], 1)
    down_gathered = lax.psum(partial_down, "mp").astype(jnp.bfloat16)
    projection_result = apply_up_matrix(
        context_gathered, selector_gathered, down_gathered, output_weight, adapter_up_matrices
    )
    returned = lax.all_to_all(projection_result, "mp", split_axis=0, concat_axis=1, tiled=True)
    return (widened + returned.astype(jnp.float32)).astype(jnp.bfloat16)


MIB = 1 << 20
LANES = 128
LONG = 10**10
STREAM = 53 * MIB
VMEM = pl.BlockSpec(memory_space=pltpu.VMEM)
SMEM = pl.BlockSpec(memory_space=pltpu.SMEM)
ANY = pl.BlockSpec(memory_space=pl.ANY)


def call(kernel, name, out_shape, in_specs, moved, limit=2 * MIB, flops=0, **options):
    return pl.pallas_call(
        kernel,
        out_shape=out_shape,
        in_specs=in_specs,
        out_specs=jax.tree.map(lambda _: VMEM, out_shape),
        compiler_params=pltpu.CompilerParams(vmem_limit_bytes=limit),
        cost_estimate=pl.CostEstimate(flops=flops, bytes_accessed=moved, transcendentals=0),
        name=name,
        **options,
    )


def exponents():
    def kernel(out_ref):
        lane = lax.broadcasted_iota(jnp.int32, (1, HEAD_DIM), 1)
        out_ref[...] = (lane % (HEAD_DIM // 2)).astype(jnp.float32) * (-2.0 / HEAD_DIM)

    shape = jax.ShapeDtypeStruct((1, HEAD_DIM), jnp.float32)
    return call(kernel, "exponents", shape, [], 0, flops=LONG // 8)()


def frequencies(exponent):
    def kernel(exponent_ref, out_ref):
        out_ref[...] = jnp.exp(exponent_ref[...] * math.log(THETA))

    shape = jax.ShapeDtypeStruct(exponent.shape, jnp.float32)
    return call(kernel, "frequencies", shape, [VMEM], 0, flops=LONG // 8)(exponent)


def norm_rows(hidden, gain, after, copies):
    rows, width = hidden.shape

    def kernel(hidden_ref, gain_ref, after_ref, out_ref):
        del after_ref
        wide = hidden_ref[...].astype(jnp.float32)
        inverse = lax.rsqrt(jnp.mean(wide * wide, -1, keepdims=True) + EPS)
        normed = (wide * inverse * gain_ref[...].astype(jnp.float32)).astype(jnp.bfloat16)
        for c in range(copies):
            out_ref[c] = normed

    return call(
        kernel,
        "norm_rows",
        jax.ShapeDtypeStruct((copies, rows, width), jnp.bfloat16),
        [VMEM, VMEM, ANY],
        hidden.size * 2 * (copies + 1),
        flops=LONG,
    )(hidden, gain[None], after)


def turns(near, frequency, lengths, slots, requests, context):
    groups, rows, depth = near.shape

    def kernel(
        lengths_ref, slots_ref, requests_ref, near_ref, frequency_ref, lined_ref, cosine_ref,
        sine_ref, mask_ref, adapter_ref,
    ):
        for j in range(groups):
            lined_ref[pl.ds(j * rows, rows)] = near_ref[j]
        row = lax.broadcasted_iota(jnp.int32, (rows, LANES), 0)
        length = jnp.zeros((rows, LANES), jnp.int32)
        adapter = jnp.zeros((rows, LANES), jnp.int32)
        for r in range(rows):
            length = jnp.where(row == r, lengths_ref[r], length)
            adapter = jnp.where(row == r, requests_ref[0, slots_ref[r]], adapter)
        angle = length.astype(jnp.float32) * frequency_ref[...]
        cosine_ref[...] = jnp.cos(angle)
        sine_ref[...] = jnp.sin(angle)
        lane = lax.broadcasted_iota(jnp.int32, (rows, LANES), 1)
        for t in range(0, context, LANES):
            mask_ref[:, pl.ds(t, LANES)] = jnp.where(lane + t < length, 0.0, -jnp.inf)
        adapter_ref[...] = adapter.astype(jnp.float32).astype(jnp.bfloat16)

    return call(
        kernel,
        "turns",
        (
            jax.ShapeDtypeStruct((groups * rows, depth), near.dtype),
            jax.ShapeDtypeStruct((rows, HEAD_DIM), jnp.float32),
            jax.ShapeDtypeStruct((rows, HEAD_DIM), jnp.float32),
            jax.ShapeDtypeStruct((rows, context), jnp.float32),
            jax.ShapeDtypeStruct((rows, LANES), jnp.bfloat16),
        ),
        [SMEM] * 3 + [VMEM] * 2,
        near.size * 4,
    )(lengths, slots, requests, near, frequency)


def project_qkv(lined, far, weight, adapter, chunk=1024):
    groups, rows, _ = far.shape
    depth, width = weight.shape
    half = groups * rows

    def kernel(lined_ref, far_ref, weight_ref, adapter_ref, out_ref, far_lined_ref):
        for j in range(groups):
            far_lined_ref[pl.ds(j * rows, rows)] = far_ref[j]
        total = jnp.zeros((2 * half, width), jnp.float32)
        for k in range(depth // chunk):
            part = pl.ds(k * chunk, chunk)
            total = total + jnp.dot(
                jnp.concatenate([lined_ref[:, part], far_lined_ref[:, part]]),
                weight_ref[part, :],
                preferred_element_type=jnp.float32,
            )
        core = lax.axis_index("batch")
        adapter = adapter_ref[...]
        for e in range(2):
            for j in range(groups):
                place = e * half + j * rows
                device = 2 * j + (core ^ e)
                out_ref[device, :, pl.ds(0, width)] = total[place : place + rows].astype(
                    jnp.bfloat16
                )
                out_ref[device, :, pl.ds(width, LANES)] = (
                    adapter if e == 0 else jnp.zeros_like(adapter)
                )

    return call(
        kernel,
        "project_qkv",
        jax.ShapeDtypeStruct((2 * groups, rows, width + LANES), jnp.bfloat16),
        [VMEM] * 4,
        weight.size * 2,
        flops=LONG,
        scratch_shapes=[pltpu.VMEM((half, depth), jnp.bfloat16)],
    )(lined, far, weight, adapter)


def stream(weight_ref, held_ref, sems, parts):
    depth = held_ref.shape[0] // parts
    copies = []
    for k in range(parts):
        rows = pl.ds(k * depth, depth)
        copies.append(
            pltpu.make_async_copy(weight_ref.at[rows], held_ref.at[rows], sems.at[k])
        )
        copies[-1].start()

    def part(k):
        copies[k].wait()
        return held_ref[pl.ds(k * depth, depth)]

    return part


def project_out(gathered, weight, parts=16):
    groups, rows, depth = gathered.shape
    count, step = groups * rows, depth // parts

    def kernel(gathered_ref, weight_ref, out_ref, near_ref, rows_ref, held_ref, sems, near_sem):
        near = pltpu.make_async_copy(gathered_ref, near_ref, near_sem)
        near.start()
        part = stream(weight_ref, held_ref, sems, parts)
        near.wait()
        for j in range(groups):
            rows_ref[pl.ds(j * rows, rows)] = near_ref[j]
        total = jnp.zeros(out_ref.shape, jnp.float32)
        for k in range(parts):
            total = total + jnp.dot(
                rows_ref[:, pl.ds(k * step, step)], part(k), preferred_element_type=jnp.float32
            )
        out_ref[...] = total

    return call(
        kernel,
        "project_out",
        pltpu.VMEM((count, weight.shape[1]), jnp.float32),
        [ANY] * 2,
        weight.size * 2,
        limit=STREAM,
        flops=2 * count * weight.size,
        scratch_shapes=[
            pltpu.VMEM(gathered.shape, gathered.dtype),
            pltpu.VMEM((count, depth), gathered.dtype),
            pltpu.VMEM(weight.shape, weight.dtype),
            pltpu.SemaphoreType.DMA((parts,)),
            pltpu.SemaphoreType.DMA,
        ],
    )(gathered, weight)


def down_partials(gathered, adapter, down_store, up_store):
    groups, rows, _ = gathered.shape
    count = groups * rows
    rank, depth = down_store.shape[1:]
    width = up_store.shape[2]

    def kernel(adapter_ref, gathered_ref, down_ref, up_ref, out_ref, picked_ref, held_ref, rows_ref):
        start = pl.multiple_of(lax.axis_index("mp") * depth, depth)
        for j in range(groups):
            rows_ref[pl.ds(j * rows, rows)] = gathered_ref[j, :, pl.ds(start, depth)]
        for r in range(count):
            chosen = adapter_ref[r // rows, r % rows]
            held_ref[pl.ds(r * rank, rank)] = down_ref[chosen]
            picked_ref[pl.ds(r * rank, rank)] = up_ref[chosen]
        every = lax.dot_general(
            rows_ref[...],
            held_ref[...],
            (((1,), (1,)), ((), ())),
            preferred_element_type=jnp.float32,
        )
        row = lax.broadcasted_iota(jnp.int32, (count, LANES), 0)
        lane = lax.broadcasted_iota(jnp.int32, (count, LANES), 1)
        total = jnp.zeros((count, LANES), jnp.float32)
        for s in range(0, count * rank, LANES):
            total = total + jnp.where(row == (lane + s) // rank, every[:, s : s + LANES], 0.0)
        for c in range(groups):
            out_ref[c] = total

    return call(
        kernel,
        "down_partials",
        (
            jax.ShapeDtypeStruct((groups, count, LANES), jnp.float32),
            pltpu.VMEM((count * rank, width), up_store.dtype),
        ),
        [SMEM] + [VMEM] * 3,
        2 * count * rank * (depth + width),
        limit=5 * MIB,
        flops=2 * count * count * rank * depth,
        scratch_shapes=[
            pltpu.VMEM((count * rank, depth), down_store.dtype),
            pltpu.VMEM((count, depth), gathered.dtype),
        ],
    )(adapter, gathered, down_store, up_store)


def add_up(base, partials, up):
    groups, count, _ = partials.shape
    depth, width = up.shape
    rank = depth // count

    def kernel(base_ref, partials_ref, up_ref, out_ref):
        total = partials_ref[0]
        for c in range(1, groups):
            total = total + partials_ref[c]
        down = total.astype(jnp.bfloat16).astype(jnp.float32)
        row = lax.broadcasted_iota(jnp.int32, (count, LANES), 0)
        lane = lax.broadcasted_iota(jnp.int32, (count, LANES), 1)
        spread = []
        for s in range(0, depth, LANES):
            spread.append(jnp.where(row == (lane + s) // rank, down, 0.0))
        spread = jnp.concatenate(spread, 1).astype(jnp.bfloat16)
        delta = jnp.dot(spread, up_ref[...], preferred_element_type=jnp.float32)
        result = (base_ref[...] + ADAPTER_SCALE * delta).astype(jnp.bfloat16)
        for j in range(groups):
            out_ref[j] = result[j * count // groups : (j + 1) * count // groups]

    return call(
        kernel,
        "add_up",
        jax.ShapeDtypeStruct((groups, count // groups, width), jnp.bfloat16),
        [VMEM] * 3,
        up.size * 2,
        limit=4 * MIB,
        flops=2 * count * up.size,
    )(base, partials, up)


def add_rows(hidden, parts):
    width = parts.shape[2]

    def kernel(hidden_ref, parts_ref, out_ref):
        for k in range(parts.shape[0]):
            part = pl.ds(k * width, width)
            total = hidden_ref[:, part].astype(jnp.float32) + parts_ref[k].astype(jnp.float32)
            out_ref[:, part] = total.astype(jnp.bfloat16)

    return call(
        kernel,
        "add_rows",
        jax.ShapeDtypeStruct(hidden.shape, parts.dtype),
        [VMEM, VMEM],
        hidden.size * 6,
    )(hidden, parts)


def swap_cores(block):
    return lax.ppermute(block, "batch", [(0, 1), (1, 0)])


def exchange(blocks, axes="mp"):
    return lax.all_to_all(blocks, axes, split_axis=0, concat_axis=0, tiled=True)


def attend(qkv, cosine, sine, key_cache, value_cache, mask):
    rows = qkv.shape[0]
    query_width = HEADS * HEAD_DIM
    kv_width = KV_HEADS * HEAD_DIM
    group = HEADS // KV_HEADS
    scale = HEAD_DIM ** (-0.5)

    def turn(part):
        vec = part.astype(jnp.float32).reshape(rows, -1, HEAD_DIM)
        half = HEAD_DIM // 2
        turned = jnp.concatenate([-vec[..., half:], vec[..., :half]], -1)
        return (vec * cosine[:, None] + turned * sine[:, None]).astype(jnp.bfloat16)

    query = turn(qkv[:, :query_width])
    fresh_key = turn(qkv[:, query_width : query_width + kv_width])
    fresh_value = (
        qkv[:, query_width + kv_width :].astype(jnp.float32).reshape(rows, KV_HEADS, HEAD_DIM)
    )
    grouped = query.reshape(rows, KV_HEADS, group, HEAD_DIM)
    cached = key_cache.reshape(rows, -1, KV_HEADS, HEAD_DIM)
    stored = value_cache.reshape(rows, -1, KV_HEADS, HEAD_DIM)
    scores = (
        jnp.einsum("rgqd,rtgd->rgqt", grouped, cached, preferred_element_type=jnp.float32) * scale
    )
    scores = scores + mask[:, None, None, :]
    own = (
        jnp.einsum("rgqd,rgd->rgq", grouped, fresh_key, preferred_element_type=jnp.float32) * scale
    )
    top = jnp.maximum(jnp.max(scores, -1), own)
    expo = jnp.exp(scores - top[..., None])
    own_exp = jnp.exp(own - top)
    total = jnp.sum(expo, -1) + own_exp
    probs = (expo / total[..., None]).astype(jnp.bfloat16)
    own_prob = (own_exp / total).astype(jnp.bfloat16)
    context_vector = jnp.einsum(
        "rgqt,rtgd->rgqd", probs, stored, preferred_element_type=jnp.float32
    )
    context_vector = (
        context_vector + own_prob.astype(jnp.float32)[..., None] * fresh_value[:, :, None, :]
    )
    return context_vector.reshape(rows, query_width).astype(jnp.bfloat16)


def fast_body(
    hidden,
    attention_norm_gain,
    query_key_value_weight,
    output_weight,
    key_cache,
    value_cache,
    lengths,
    slots,
    requests,
    adapter_down_matrices,
    adapter_up_matrices,
):
    rows = hidden.shape[0]
    mp_size = lax.axis_size("mp")
    width = query_key_value_weight.shape[1]

    frequency = frequencies(exponents())
    near = exchange(norm_rows(hidden, attention_norm_gain, frequency, mp_size))
    lined, cosine, sine, mask, adapter = turns(
        near, frequency, lengths, slots, requests, key_cache.shape[1]
    )
    columns = project_qkv(lined, swap_cores(near), query_key_value_weight, adapter)
    mixed = exchange(columns, ("mp", "batch"))
    adapter = mixed.reshape(mp_size, -1, rows, width + LANES)[:, :, :, width]
    adapter = jnp.sum(adapter.astype(jnp.float32), 1).astype(jnp.int32)
    qkv = mixed[:, :, :width].transpose(1, 0, 2).reshape(rows, -1)

    context = attend(qkv, cosine, sine, key_cache, value_cache, mask)
    context, adapter = lax.optimization_barrier((context, adapter))
    gathered = exchange(jnp.broadcast_to(context[None], (mp_size, *context.shape)))

    partials, up = down_partials(
        gathered, adapter, adapter_down_matrices.swapaxes(1, 2), adapter_up_matrices
    )
    partials = exchange(partials)
    projected = add_up(project_out(gathered, output_weight), partials, up)
    return add_rows(hidden, exchange(projected))


def body(*arguments):
    small = lax.axis_size("mp") <= 16 and lax.axis_size("batch") == 2
    whole_heads = arguments[2].shape[1] % HEAD_DIM == 0
    return (fast_body if small and whole_heads else general_body)(*arguments)


def solution(mesh):
    in_specs = (
        P(("groups", "mp", "batch"), None),
        P(),
        P(None, ("mp", "batch")),
        P(None, "mp"),
        P(("groups", "mp", "batch"), None, None),
        P(("groups", "mp", "batch"), None, None),
        P(("groups", "mp", "batch")),
        P(("groups", "mp", "batch")),
        P(("groups", "mp", "batch"), None),
        P(None, "mp", None),
        P(None, None, "mp"),
    )
    out_specs = P(("groups", "mp", "batch"), None)
    return jax.shard_map(body, mesh=mesh, in_specs=in_specs, out_specs=out_specs, check_vma=False)
```

```python
import math

import jax
import jax.numpy as jnp
from jax import lax
from jax.experimental import pallas as pl
from jax.experimental.pallas import tpu as pltpu
from jax.sharding import PartitionSpec as P

HEADS = 64
KV_HEADS = 8
HEAD_DIM = 128
ADAPTER_COUNT = 64


EPS = 1e-05
THETA = 500000.0
ADAPTER_SCALE = 2.0


def rotate(vec, pos):
    width = vec.shape[-1]
    half = width // 2
    freq = THETA ** (-(jnp.arange(half, dtype=jnp.float32) * 2.0) / width)
    angle = pos[..., None, None] * freq
    cosine = jnp.concatenate([jnp.cos(angle), jnp.cos(angle)], -1)
    sine = jnp.concatenate([jnp.sin(angle), jnp.sin(angle)], -1)
    turned = jnp.concatenate([-vec[..., half:], vec[..., :half]], -1)
    return vec * cosine + turned * sine


def apply_up_matrix(
    context_vector, adapter_selector, down_result, output_weight, adapter_up_matrices
):
    base_output = jnp.dot(context_vector, output_weight, preferred_element_type=jnp.float32)
    spread = (adapter_selector[:, :, None] * down_result[:, None, :]).reshape(
        adapter_selector.shape[0], -1
    )
    adapter_table = adapter_up_matrices.reshape(-1, adapter_up_matrices.shape[2])
    adapter_delta = jnp.dot(spread, adapter_table, preferred_element_type=jnp.float32)
    return (base_output + ADAPTER_SCALE * adapter_delta).astype(jnp.bfloat16)


def general_body(
    hidden,
    attention_norm_gain,
    query_key_value_weight,
    output_weight,
    key_cache,
    value_cache,
    lengths,
    slots,
    requests,
    adapter_down_matrices,
    adapter_up_matrices,
):
    widened = hidden.astype(jnp.float32)
    normed = (
        widened
        * lax.rsqrt(jnp.mean(widened * widened, -1, keepdims=True) + EPS)
        * attention_norm_gain.astype(jnp.float32)
    ).astype(jnp.bfloat16)
    rows = normed.shape[0]
    columns = jnp.dot(
        lax.all_gather(normed, ("mp", "batch"), axis=0, tiled=True),
        query_key_value_weight,
        preferred_element_type=jnp.float32,
    ).astype(jnp.bfloat16)
    mixed = lax.all_to_all(
        lax.all_to_all(columns, "mp", split_axis=0, concat_axis=1, tiled=True),
        "batch",
        split_axis=0,
        concat_axis=1,
        tiled=True,
    )
    width = query_key_value_weight.shape[1]
    qkv = (
        mixed.reshape(rows, lax.axis_size("batch"), lax.axis_size("mp"), width)
        .transpose(0, 2, 1, 3)
        .reshape(rows, -1)
    )
    query_width = HEADS * HEAD_DIM
    kv_width = KV_HEADS * HEAD_DIM
    group = HEADS // KV_HEADS
    scale = HEAD_DIM ** (-0.5)
    pos = lengths.astype(jnp.float32)
    query = rotate(
        qkv[:, :query_width].astype(jnp.float32).reshape(rows, HEADS, HEAD_DIM), pos
    ).astype(jnp.bfloat16)
    fresh_key = rotate(
        qkv[:, query_width : query_width + kv_width]
        .astype(jnp.float32)
        .reshape(rows, KV_HEADS, HEAD_DIM),
        pos,
    ).astype(jnp.bfloat16)
    fresh_value = (
        qkv[:, query_width + kv_width :].astype(jnp.float32).reshape(rows, KV_HEADS, HEAD_DIM)
    )
    grouped = query.reshape(rows, KV_HEADS, group, HEAD_DIM)
    cached = key_cache.reshape(rows, -1, KV_HEADS, HEAD_DIM)
    stored = value_cache.reshape(rows, -1, KV_HEADS, HEAD_DIM)
    scores = (
        jnp.einsum("rgqd,rtgd->rgqt", grouped, cached, preferred_element_type=jnp.float32) * scale
    )
    live = jnp.arange(cached.shape[1])[None, :] < lengths[:, None]
    scores = jnp.where(live[:, None, None, :], scores, -jnp.inf)
    own = (
        jnp.einsum("rgqd,rgd->rgq", grouped, fresh_key, preferred_element_type=jnp.float32) * scale
    )
    top = jnp.maximum(jnp.max(scores, -1), own)
    expo = jnp.exp(scores - top[..., None])
    own_exp = jnp.exp(own - top)
    total = jnp.sum(expo, -1) + own_exp
    probs = (expo / total[..., None]).astype(jnp.bfloat16)
    own_prob = (own_exp / total).astype(jnp.bfloat16)
    context_vector = jnp.einsum(
        "rgqt,rtgd->rgqd", probs, stored, preferred_element_type=jnp.float32
    )
    context_vector = (
        context_vector + own_prob.astype(jnp.float32)[..., None] * fresh_value[:, :, None, :]
    )
    context_vector = context_vector.reshape(rows, query_width).astype(jnp.bfloat16)
    slot_hits = slots[:, None] == jnp.arange(requests.shape[1])[None, :]
    adapter = jnp.sum(jnp.where(slot_hits, requests[0][None, :], 0), 1)
    adapter_selector = (adapter[:, None] == jnp.arange(ADAPTER_COUNT)[None, :]).astype(jnp.bfloat16)
    context_gathered, selector_gathered = (
        lax.all_gather(context_vector, "mp", axis=0, tiled=True),
        lax.all_gather(adapter_selector, "mp", axis=0, tiled=True),
    )
    shared_portion = adapter_down_matrices.shape[1]
    context_slice = lax.dynamic_slice_in_dim(
        context_gathered, lax.axis_index("mp") * shared_portion, shared_portion, 1
    )
    every_adapter = jnp.einsum(
        "gh,thy->gty", context_slice, adapter_down_matrices, preferred_element_type=jnp.float32
    )
    partial_down = jnp.sum(every_adapter * selector_gathered.astype(jnp.float32)[:, :, None], 1)
    down_gathered = lax.psum(partial_down, "mp").astype(jnp.bfloat16)
    projection_result = apply_up_matrix(
        context_gathered, selector_gathered, down_gathered, output_weight, adapter_up_matrices
    )
    returned = lax.all_to_all(projection_result, "mp", split_axis=0, concat_axis=1, tiled=True)
    return (widened + returned.astype(jnp.float32)).astype(jnp.bfloat16)


MIB = 1 << 20
LANES = 128
LONG = 10**10
STREAM = 53 * MIB
VMEM = pl.BlockSpec(memory_space=pltpu.VMEM)
SMEM = pl.BlockSpec(memory_space=pltpu.SMEM)
ANY = pl.BlockSpec(memory_space=pl.ANY)


def call(kernel, name, out_shape, in_specs, moved, limit=2 * MIB, flops=0, **options):
    return pl.pallas_call(
        kernel,
        out_shape=out_shape,
        in_specs=in_specs,
        out_specs=jax.tree.map(lambda _: VMEM, out_shape),
        compiler_params=pltpu.CompilerParams(vmem_limit_bytes=limit),
        cost_estimate=pl.CostEstimate(flops=flops, bytes_accessed=moved, transcendentals=0),
        name=name,
        **options,
    )


def exponents():
    def kernel(out_ref):
        lane = lax.broadcasted_iota(jnp.int32, (1, HEAD_DIM), 1)
        out_ref[...] = (lane % (HEAD_DIM // 2)).astype(jnp.float32) * (-2.0 / HEAD_DIM)

    shape = jax.ShapeDtypeStruct((1, HEAD_DIM), jnp.float32)
    return call(kernel, "exponents", shape, [], 0, flops=LONG // 8)()


def frequencies(exponent):
    def kernel(exponent_ref, out_ref):
        out_ref[...] = jnp.exp(exponent_ref[...] * math.log(THETA))

    shape = jax.ShapeDtypeStruct(exponent.shape, jnp.float32)
    return call(kernel, "frequencies", shape, [VMEM], 0, flops=LONG // 8)(exponent)


def norm_rows(hidden, gain, after, copies):
    rows, width = hidden.shape

    def kernel(hidden_ref, gain_ref, after_ref, out_ref):
        del after_ref
        wide = hidden_ref[...].astype(jnp.float32)
        inverse = lax.rsqrt(jnp.mean(wide * wide, -1, keepdims=True) + EPS)
        normed = (wide * inverse * gain_ref[...].astype(jnp.float32)).astype(jnp.bfloat16)
        for c in range(copies):
            out_ref[c] = normed

    return call(
        kernel,
        "norm_rows",
        jax.ShapeDtypeStruct((copies, rows, width), jnp.bfloat16),
        [VMEM, VMEM, ANY],
        hidden.size * 2 * (copies + 1),
        flops=LONG,
    )(hidden, gain[None], after)


def turns(near, frequency, lengths, slots, requests, context):
    groups, rows, depth = near.shape

    def kernel(
        lengths_ref, slots_ref, requests_ref, near_ref, frequency_ref, lined_ref, cosine_ref,
        sine_ref, mask_ref, adapter_ref,
    ):
        for j in range(groups):
            lined_ref[pl.ds(j * rows, rows)] = near_ref[j]
        row = lax.broadcasted_iota(jnp.int32, (rows, LANES), 0)
        length = jnp.zeros((rows, LANES), jnp.int32)
        adapter = jnp.zeros((rows, LANES), jnp.int32)
        for r in range(rows):
            length = jnp.where(row == r, lengths_ref[r], length)
            adapter = jnp.where(row == r, requests_ref[0, slots_ref[r]], adapter)
        angle = length.astype(jnp.float32) * frequency_ref[...]
        cosine_ref[...] = jnp.cos(angle)
        sine_ref[...] = jnp.sin(angle)
        lane = lax.broadcasted_iota(jnp.int32, (rows, LANES), 1)
        for t in range(0, context, LANES):
            mask_ref[:, pl.ds(t, LANES)] = jnp.where(lane + t < length, 0.0, -jnp.inf)
        adapter_ref[...] = adapter.astype(jnp.float32).astype(jnp.bfloat16)

    return call(
        kernel,
        "turns",
        (
            jax.ShapeDtypeStruct((groups * rows, depth), near.dtype),
            jax.ShapeDtypeStruct((rows, HEAD_DIM), jnp.float32),
            jax.ShapeDtypeStruct((rows, HEAD_DIM), jnp.float32),
            jax.ShapeDtypeStruct((rows, context), jnp.float32),
            jax.ShapeDtypeStruct((rows, LANES), jnp.bfloat16),
        ),
        [SMEM] * 3 + [VMEM] * 2,
        near.size * 4,
    )(lengths, slots, requests, near, frequency)


def project_qkv(lined, far, weight, adapter, chunk=1024):
    groups, rows, _ = far.shape
    depth, width = weight.shape
    half = groups * rows

    def kernel(lined_ref, far_ref, weight_ref, adapter_ref, out_ref, far_lined_ref):
        for j in range(groups):
            far_lined_ref[pl.ds(j * rows, rows)] = far_ref[j]
        total = jnp.zeros((2 * half, width), jnp.float32)
        for k in range(depth // chunk):
            part = pl.ds(k * chunk, chunk)
            total = total + jnp.dot(
                jnp.concatenate([lined_ref[:, part], far_lined_ref[:, part]]),
                weight_ref[part, :],
                preferred_element_type=jnp.float32,
            )
        core = lax.axis_index("batch")
        adapter = adapter_ref[...]
        for e in range(2):
            for j in range(groups):
                place = e * half + j * rows
                device = 2 * j + (core ^ e)
                out_ref[device, :, pl.ds(0, width)] = total[place : place + rows].astype(
                    jnp.bfloat16
                )
                out_ref[device, :, pl.ds(width, LANES)] = (
                    adapter if e == 0 else jnp.zeros_like(adapter)
                )

    return call(
        kernel,
        "project_qkv",
        jax.ShapeDtypeStruct((2 * groups, rows, width + LANES), jnp.bfloat16),
        [VMEM] * 4,
        weight.size * 2,
        flops=LONG,
        scratch_shapes=[pltpu.VMEM((half, depth), jnp.bfloat16)],
    )(lined, far, weight, adapter)


def stream(weight_ref, held_ref, sems, parts):
    depth = held_ref.shape[0] // parts
    copies = []
    for k in range(parts):
        rows = pl.ds(k * depth, depth)
        copies.append(
            pltpu.make_async_copy(weight_ref.at[rows], held_ref.at[rows], sems.at[k])
        )
        copies[-1].start()

    def part(k):
        copies[k].wait()
        return held_ref[pl.ds(k * depth, depth)]

    return part


def project_out(gathered, weight, parts=16):
    groups, rows, depth = gathered.shape
    count, step = groups * rows, depth // parts

    def kernel(gathered_ref, weight_ref, out_ref, near_ref, rows_ref, held_ref, sems, near_sem):
        near = pltpu.make_async_copy(gathered_ref, near_ref, near_sem)
        near.start()
        part = stream(weight_ref, held_ref, sems, parts)
        near.wait()
        for j in range(groups):
            rows_ref[pl.ds(j * rows, rows)] = near_ref[j]
        total = jnp.zeros(out_ref.shape, jnp.float32)
        for k in range(parts):
            total = total + jnp.dot(
                rows_ref[:, pl.ds(k * step, step)], part(k), preferred_element_type=jnp.float32
            )
        out_ref[...] = total

    return call(
        kernel,
        "project_out",
        pltpu.VMEM((count, weight.shape[1]), jnp.float32),
        [ANY] * 2,
        weight.size * 2,
        limit=STREAM,
        flops=2 * count * weight.size,
        scratch_shapes=[
            pltpu.VMEM(gathered.shape, gathered.dtype),
            pltpu.VMEM((count, depth), gathered.dtype),
            pltpu.VMEM(weight.shape, weight.dtype),
            pltpu.SemaphoreType.DMA((parts,)),
            pltpu.SemaphoreType.DMA,
        ],
    )(gathered, weight)


def down_partials(gathered, adapter, down_store, up_store):
    groups, rows, _ = gathered.shape
    count = groups * rows
    rank, depth = down_store.shape[1:]
    width = up_store.shape[2]

    def kernel(adapter_ref, gathered_ref, down_ref, up_ref, out_ref, picked_ref, held_ref, rows_ref):
        start = pl.multiple_of(lax.axis_index("mp") * depth, depth)
        for j in range(groups):
            rows_ref[pl.ds(j * rows, rows)] = gathered_ref[j, :, pl.ds(start, depth)]
        for r in range(count):
            chosen = adapter_ref[r // rows, r % rows]
            held_ref[pl.ds(r * rank, rank)] = down_ref[chosen]
            picked_ref[pl.ds(r * rank, rank)] = up_ref[chosen]
        every = lax.dot_general(
            rows_ref[...],
            held_ref[...],
            (((1,), (1,)), ((), ())),
            preferred_element_type=jnp.float32,
        )
        row = lax.broadcasted_iota(jnp.int32, (count, LANES), 0)
        lane = lax.broadcasted_iota(jnp.int32, (count, LANES), 1)
        total = jnp.zeros((count, LANES), jnp.float32)
        for s in range(0, count * rank, LANES):
            total = total + jnp.where(row == (lane + s) // rank, every[:, s : s + LANES], 0.0)
        for c in range(groups):
            out_ref[c] = total

    return call(
        kernel,
        "down_partials",
        (
            jax.ShapeDtypeStruct((groups, count, LANES), jnp.float32),
            pltpu.VMEM((count * rank, width), up_store.dtype),
        ),
        [SMEM] + [VMEM] * 3,
        2 * count * rank * (depth + width),
        limit=5 * MIB,
        flops=2 * count * count * rank * depth,
        scratch_shapes=[
            pltpu.VMEM((count * rank, depth), down_store.dtype),
            pltpu.VMEM((count, depth), gathered.dtype),
        ],
    )(adapter, gathered, down_store, up_store)


def add_up(base, partials, up):
    groups, count, _ = partials.shape
    depth, width = up.shape
    rank = depth // count

    def kernel(base_ref, partials_ref, up_ref, out_ref):
        total = partials_ref[0]
        for c in range(1, groups):
            total = total + partials_ref[c]
        down = total.astype(jnp.bfloat16).astype(jnp.float32)
        row = lax.broadcasted_iota(jnp.int32, (count, LANES), 0)
        lane = lax.broadcasted_iota(jnp.int32, (count, LANES), 1)
        spread = []
        for s in range(0, depth, LANES):
            spread.append(jnp.where(row == (lane + s) // rank, down, 0.0))
        spread = jnp.concatenate(spread, 1).astype(jnp.bfloat16)
        delta = jnp.dot(spread, up_ref[...], preferred_element_type=jnp.float32)
        result = (base_ref[...] + ADAPTER_SCALE * delta).astype(jnp.bfloat16)
        for j in range(groups):
            out_ref[j] = result[j * count // groups : (j + 1) * count // groups]

    return call(
        kernel,
        "add_up",
        jax.ShapeDtypeStruct((groups, count // groups, width), jnp.bfloat16),
        [VMEM] * 3,
        up.size * 2,
        limit=4 * MIB,
        flops=LONG,
    )(base, partials, up)


def add_rows(hidden, parts):
    width = parts.shape[2]

    def kernel(hidden_ref, parts_ref, out_ref):
        for k, place in enumerate(order(parts.shape[0])):
            part = pl.ds(place * width, width)
            total = hidden_ref[:, part].astype(jnp.float32) + parts_ref[k].astype(jnp.float32)
            out_ref[:, part] = total.astype(jnp.bfloat16)

    return call(
        kernel,
        "add_rows",
        jax.ShapeDtypeStruct(hidden.shape, parts.dtype),
        [VMEM, VMEM],
        hidden.size * 6,
    )(hidden, parts)


def swap_cores(block):
    return lax.ppermute(block, "batch", [(0, 1), (1, 0)])


def order(size):
    return [(k + size // 2) % size for k in range(size)]


def exchange(blocks):
    group = order(lax.axis_size("mp"))
    return lax.all_to_all(
        blocks, "mp", split_axis=0, concat_axis=0, tiled=True, axis_index_groups=[group]
    )


def exchange_all(blocks):
    group = [2 * j + core for j in order(lax.axis_size("mp")) for core in range(2)]
    return lax.all_to_all(
        blocks,
        ("mp", "batch"),
        split_axis=0,
        concat_axis=0,
        tiled=True,
        axis_index_groups=[group],
    )


def attend(qkv, cosine, sine, key_cache, value_cache, mask):
    rows = qkv.shape[0]
    query_width = HEADS * HEAD_DIM
    kv_width = KV_HEADS * HEAD_DIM
    group = HEADS // KV_HEADS
    scale = HEAD_DIM ** (-0.5)

    def turn(part):
        vec = part.astype(jnp.float32).reshape(rows, -1, HEAD_DIM)
        half = HEAD_DIM // 2
        turned = jnp.concatenate([-vec[..., half:], vec[..., :half]], -1)
        return (vec * cosine[:, None] + turned * sine[:, None]).astype(jnp.bfloat16)

    query = turn(qkv[:, :query_width])
    fresh_key = turn(qkv[:, query_width : query_width + kv_width])
    fresh_value = (
        qkv[:, query_width + kv_width :].astype(jnp.float32).reshape(rows, KV_HEADS, HEAD_DIM)
    )
    grouped = query.reshape(rows, KV_HEADS, group, HEAD_DIM)
    cached = key_cache.reshape(rows, -1, KV_HEADS, HEAD_DIM)
    stored = value_cache.reshape(rows, -1, KV_HEADS, HEAD_DIM)
    scores = (
        jnp.einsum("rgqd,rtgd->rgqt", grouped, cached, preferred_element_type=jnp.float32) * scale
    )
    scores = scores + mask[:, None, None, :]
    own = (
        jnp.einsum("rgqd,rgd->rgq", grouped, fresh_key, preferred_element_type=jnp.float32) * scale
    )
    top = jnp.maximum(jnp.max(scores, -1), own)
    expo = jnp.exp(scores - top[..., None])
    own_exp = jnp.exp(own - top)
    total = jnp.sum(expo, -1) + own_exp
    probs = (expo / total[..., None]).astype(jnp.bfloat16)
    own_prob = (own_exp / total).astype(jnp.bfloat16)
    context_vector = jnp.einsum(
        "rgqt,rtgd->rgqd", probs, stored, preferred_element_type=jnp.float32
    )
    context_vector = (
        context_vector + own_prob.astype(jnp.float32)[..., None] * fresh_value[:, :, None, :]
    )
    return context_vector.reshape(rows, query_width).astype(jnp.bfloat16)


def fast_body(
    hidden,
    attention_norm_gain,
    query_key_value_weight,
    output_weight,
    key_cache,
    value_cache,
    lengths,
    slots,
    requests,
    adapter_down_matrices,
    adapter_up_matrices,
):
    rows = hidden.shape[0]
    mp_size = lax.axis_size("mp")
    width = query_key_value_weight.shape[1]

    frequency = frequencies(exponents())
    near = exchange(norm_rows(hidden, attention_norm_gain, frequency, mp_size))
    lined, cosine, sine, mask, adapter = turns(
        near, frequency, lengths, slots, requests, key_cache.shape[1]
    )
    columns = project_qkv(lined, swap_cores(near), query_key_value_weight, adapter)
    mixed = exchange_all(columns)
    adapter = mixed.reshape(mp_size, -1, rows, width + LANES)[:, :, :, width]
    adapter = jnp.sum(adapter.astype(jnp.float32), 1).astype(jnp.int32)
    qkv = jnp.roll(mixed[:, :, :width], mp_size, 0).transpose(1, 0, 2).reshape(rows, -1)

    context = attend(qkv, cosine, sine, key_cache, value_cache, mask)
    context, adapter = lax.optimization_barrier((context, adapter))
    gathered = exchange(jnp.broadcast_to(context[None], (mp_size, *context.shape)))

    partials, up = down_partials(
        gathered, adapter, adapter_down_matrices.swapaxes(1, 2), adapter_up_matrices
    )
    partials = exchange(partials)
    projected = add_up(project_out(gathered, output_weight), partials, up)
    return add_rows(hidden, exchange(projected))


def body(*arguments):
    small = lax.axis_size("mp") <= 16 and lax.axis_size("batch") == 2
    whole_heads = arguments[2].shape[1] % HEAD_DIM == 0
    return (fast_body if small and whole_heads else general_body)(*arguments)


def solution(mesh):
    in_specs = (
        P(("groups", "mp", "batch"), None),
        P(),
        P(None, ("mp", "batch")),
        P(None, "mp"),
        P(("groups", "mp", "batch"), None, None),
        P(("groups", "mp", "batch"), None, None),
        P(("groups", "mp", "batch")),
        P(("groups", "mp", "batch")),
        P(("groups", "mp", "batch"), None),
        P(None, "mp", None),
        P(None, None, "mp"),
    )
    out_specs = P(("groups", "mp", "batch"), None)
    return jax.shard_map(body, mesh=mesh, in_specs=in_specs, out_specs=out_specs, check_vma=False)
```

```python
import math

import jax
import jax.numpy as jnp
from jax import lax
from jax.experimental import pallas as pl
from jax.experimental.pallas import tpu as pltpu
from jax.sharding import PartitionSpec as P

HEADS = 64
KV_HEADS = 8
HEAD_DIM = 128
ADAPTER_COUNT = 64


EPS = 1e-05
THETA = 500000.0
ADAPTER_SCALE = 2.0


def rotate(vec, pos):
    width = vec.shape[-1]
    half = width // 2
    freq = THETA ** (-(jnp.arange(half, dtype=jnp.float32) * 2.0) / width)
    angle = pos[..., None, None] * freq
    cosine = jnp.concatenate([jnp.cos(angle), jnp.cos(angle)], -1)
    sine = jnp.concatenate([jnp.sin(angle), jnp.sin(angle)], -1)
    turned = jnp.concatenate([-vec[..., half:], vec[..., :half]], -1)
    return vec * cosine + turned * sine


def apply_up_matrix(
    context_vector, adapter_selector, down_result, output_weight, adapter_up_matrices
):
    base_output = jnp.dot(context_vector, output_weight, preferred_element_type=jnp.float32)
    spread = (adapter_selector[:, :, None] * down_result[:, None, :]).reshape(
        adapter_selector.shape[0], -1
    )
    adapter_table = adapter_up_matrices.reshape(-1, adapter_up_matrices.shape[2])
    adapter_delta = jnp.dot(spread, adapter_table, preferred_element_type=jnp.float32)
    return (base_output + ADAPTER_SCALE * adapter_delta).astype(jnp.bfloat16)


def general_body(
    hidden,
    attention_norm_gain,
    query_key_value_weight,
    output_weight,
    key_cache,
    value_cache,
    lengths,
    slots,
    requests,
    adapter_down_matrices,
    adapter_up_matrices,
):
    widened = hidden.astype(jnp.float32)
    normed = (
        widened
        * lax.rsqrt(jnp.mean(widened * widened, -1, keepdims=True) + EPS)
        * attention_norm_gain.astype(jnp.float32)
    ).astype(jnp.bfloat16)
    rows = normed.shape[0]
    columns = jnp.dot(
        lax.all_gather(normed, ("mp", "batch"), axis=0, tiled=True),
        query_key_value_weight,
        preferred_element_type=jnp.float32,
    ).astype(jnp.bfloat16)
    mixed = lax.all_to_all(
        lax.all_to_all(columns, "mp", split_axis=0, concat_axis=1, tiled=True),
        "batch",
        split_axis=0,
        concat_axis=1,
        tiled=True,
    )
    width = query_key_value_weight.shape[1]
    qkv = (
        mixed.reshape(rows, lax.axis_size("batch"), lax.axis_size("mp"), width)
        .transpose(0, 2, 1, 3)
        .reshape(rows, -1)
    )
    query_width = HEADS * HEAD_DIM
    kv_width = KV_HEADS * HEAD_DIM
    group = HEADS // KV_HEADS
    scale = HEAD_DIM ** (-0.5)
    pos = lengths.astype(jnp.float32)
    query = rotate(
        qkv[:, :query_width].astype(jnp.float32).reshape(rows, HEADS, HEAD_DIM), pos
    ).astype(jnp.bfloat16)
    fresh_key = rotate(
        qkv[:, query_width : query_width + kv_width]
        .astype(jnp.float32)
        .reshape(rows, KV_HEADS, HEAD_DIM),
        pos,
    ).astype(jnp.bfloat16)
    fresh_value = (
        qkv[:, query_width + kv_width :].astype(jnp.float32).reshape(rows, KV_HEADS, HEAD_DIM)
    )
    grouped = query.reshape(rows, KV_HEADS, group, HEAD_DIM)
    cached = key_cache.reshape(rows, -1, KV_HEADS, HEAD_DIM)
    stored = value_cache.reshape(rows, -1, KV_HEADS, HEAD_DIM)
    scores = (
        jnp.einsum("rgqd,rtgd->rgqt", grouped, cached, preferred_element_type=jnp.float32) * scale
    )
    live = jnp.arange(cached.shape[1])[None, :] < lengths[:, None]
    scores = jnp.where(live[:, None, None, :], scores, -jnp.inf)
    own = (
        jnp.einsum("rgqd,rgd->rgq", grouped, fresh_key, preferred_element_type=jnp.float32) * scale
    )
    top = jnp.maximum(jnp.max(scores, -1), own)
    expo = jnp.exp(scores - top[..., None])
    own_exp = jnp.exp(own - top)
    total = jnp.sum(expo, -1) + own_exp
    probs = (expo / total[..., None]).astype(jnp.bfloat16)
    own_prob = (own_exp / total).astype(jnp.bfloat16)
    context_vector = jnp.einsum(
        "rgqt,rtgd->rgqd", probs, stored, preferred_element_type=jnp.float32
    )
    context_vector = (
        context_vector + own_prob.astype(jnp.float32)[..., None] * fresh_value[:, :, None, :]
    )
    context_vector = context_vector.reshape(rows, query_width).astype(jnp.bfloat16)
    slot_hits = slots[:, None] == jnp.arange(requests.shape[1])[None, :]
    adapter = jnp.sum(jnp.where(slot_hits, requests[0][None, :], 0), 1)
    adapter_selector = (adapter[:, None] == jnp.arange(ADAPTER_COUNT)[None, :]).astype(jnp.bfloat16)
    context_gathered, selector_gathered = (
        lax.all_gather(context_vector, "mp", axis=0, tiled=True),
        lax.all_gather(adapter_selector, "mp", axis=0, tiled=True),
    )
    shared_portion = adapter_down_matrices.shape[1]
    context_slice = lax.dynamic_slice_in_dim(
        context_gathered, lax.axis_index("mp") * shared_portion, shared_portion, 1
    )
    every_adapter = jnp.einsum(
        "gh,thy->gty", context_slice, adapter_down_matrices, preferred_element_type=jnp.float32
    )
    partial_down = jnp.sum(every_adapter * selector_gathered.astype(jnp.float32)[:, :, None], 1)
    down_gathered = lax.psum(partial_down, "mp").astype(jnp.bfloat16)
    projection_result = apply_up_matrix(
        context_gathered, selector_gathered, down_gathered, output_weight, adapter_up_matrices
    )
    returned = lax.all_to_all(projection_result, "mp", split_axis=0, concat_axis=1, tiled=True)
    return (widened + returned.astype(jnp.float32)).astype(jnp.bfloat16)


MIB = 1 << 20
LANES = 128
LONG = 10**10
STREAM = 53 * MIB
VMEM = pl.BlockSpec(memory_space=pltpu.VMEM)
SMEM = pl.BlockSpec(memory_space=pltpu.SMEM)
ANY = pl.BlockSpec(memory_space=pl.ANY)


def call(kernel, name, out_shape, in_specs, moved, limit=2 * MIB, flops=0, **options):
    return pl.pallas_call(
        kernel,
        out_shape=out_shape,
        in_specs=in_specs,
        out_specs=jax.tree.map(lambda _: VMEM, out_shape),
        compiler_params=pltpu.CompilerParams(vmem_limit_bytes=limit),
        cost_estimate=pl.CostEstimate(flops=flops, bytes_accessed=moved, transcendentals=0),
        name=name,
        **options,
    )


def exponents():
    def kernel(out_ref):
        lane = lax.broadcasted_iota(jnp.int32, (1, HEAD_DIM), 1)
        out_ref[...] = (lane % (HEAD_DIM // 2)).astype(jnp.float32) * (-2.0 / HEAD_DIM)

    shape = jax.ShapeDtypeStruct((1, HEAD_DIM), jnp.float32)
    return call(kernel, "exponents", shape, [], 0, flops=LONG // 8)()


def frequencies(exponent):
    def kernel(exponent_ref, out_ref):
        out_ref[...] = jnp.exp(exponent_ref[...] * math.log(THETA))

    shape = jax.ShapeDtypeStruct(exponent.shape, jnp.float32)
    return call(kernel, "frequencies", shape, [VMEM], 0, flops=LONG // 8)(exponent)


def norm_rows(hidden, gain, after, copies):
    rows, width = hidden.shape

    def kernel(hidden_ref, gain_ref, after_ref, out_ref):
        del after_ref
        wide = hidden_ref[...].astype(jnp.float32)
        inverse = lax.rsqrt(jnp.mean(wide * wide, -1, keepdims=True) + EPS)
        normed = (wide * inverse * gain_ref[...].astype(jnp.float32)).astype(jnp.bfloat16)
        for c in range(copies):
            out_ref[c] = normed

    return call(
        kernel,
        "norm_rows",
        jax.ShapeDtypeStruct((copies, rows, width), jnp.bfloat16),
        [VMEM, VMEM, ANY],
        hidden.size * 2 * (copies + 1),
        flops=LONG,
    )(hidden, gain[None], after)


def turns(near, frequency, lengths, slots, requests, context):
    groups, rows, depth = near.shape

    def kernel(
        lengths_ref, slots_ref, requests_ref, near_ref, frequency_ref, lined_ref, cosine_ref,
        sine_ref, mask_ref, adapter_ref,
    ):
        for j in range(groups):
            lined_ref[pl.ds(j * rows, rows)] = near_ref[j]
        row = lax.broadcasted_iota(jnp.int32, (rows, LANES), 0)
        length = jnp.zeros((rows, LANES), jnp.int32)
        adapter = jnp.zeros((rows, LANES), jnp.int32)
        for r in range(rows):
            length = jnp.where(row == r, lengths_ref[r], length)
            adapter = jnp.where(row == r, requests_ref[0, slots_ref[r]], adapter)
        angle = length.astype(jnp.float32) * frequency_ref[...]
        cosine_ref[...] = jnp.cos(angle)
        sine_ref[...] = jnp.sin(angle)
        lane = lax.broadcasted_iota(jnp.int32, (rows, LANES), 1)
        for t in range(0, context, LANES):
            mask_ref[:, pl.ds(t, LANES)] = jnp.where(lane + t < length, 0.0, -jnp.inf)
        adapter_ref[...] = adapter.astype(jnp.float32).astype(jnp.bfloat16)

    return call(
        kernel,
        "turns",
        (
            jax.ShapeDtypeStruct((groups * rows, depth), near.dtype),
            jax.ShapeDtypeStruct((rows, HEAD_DIM), jnp.float32),
            jax.ShapeDtypeStruct((rows, HEAD_DIM), jnp.float32),
            jax.ShapeDtypeStruct((rows, context), jnp.float32),
            jax.ShapeDtypeStruct((rows, LANES), jnp.bfloat16),
        ),
        [SMEM] * 3 + [VMEM] * 2,
        near.size * 4,
    )(lengths, slots, requests, near, frequency)


def project_qkv(lined, far, weight, adapter, chunk=1024):
    groups, rows, _ = far.shape
    depth, width = weight.shape
    half = groups * rows

    def kernel(lined_ref, far_ref, weight_ref, adapter_ref, out_ref, far_lined_ref):
        for j in range(groups):
            far_lined_ref[pl.ds(j * rows, rows)] = far_ref[j]
        total = jnp.zeros((2 * half, width), jnp.float32)
        for k in range(depth // chunk):
            part = pl.ds(k * chunk, chunk)
            total = total + jnp.dot(
                jnp.concatenate([lined_ref[:, part], far_lined_ref[:, part]]),
                weight_ref[part, :],
                preferred_element_type=jnp.float32,
            )
        core = lax.axis_index("batch")
        adapter = adapter_ref[...]
        for e in range(2):
            for j in range(groups):
                place = e * half + j * rows
                device = 2 * j + (core ^ e ^ 1)
                out_ref[device, :, pl.ds(0, width)] = total[place : place + rows].astype(
                    jnp.bfloat16
                )
                out_ref[device, :, pl.ds(width, LANES)] = (
                    adapter if e == 0 else jnp.zeros_like(adapter)
                )

    return call(
        kernel,
        "project_qkv",
        jax.ShapeDtypeStruct((2 * groups, rows, width + LANES), jnp.bfloat16),
        [VMEM] * 4,
        weight.size * 2,
        flops=LONG,
        scratch_shapes=[pltpu.VMEM((half, depth), jnp.bfloat16)],
    )(lined, far, weight, adapter)


def stream(weight_ref, held_ref, sems, parts):
    depth = held_ref.shape[0] // parts
    copies = []
    for k in range(parts):
        rows = pl.ds(k * depth, depth)
        copies.append(
            pltpu.make_async_copy(weight_ref.at[rows], held_ref.at[rows], sems.at[k])
        )
        copies[-1].start()

    def part(k):
        copies[k].wait()
        return held_ref[pl.ds(k * depth, depth)]

    return part


def project_out(gathered, weight, hidden, parts=16):
    groups, rows, depth = gathered.shape
    count, step = groups * rows, depth // parts

    def kernel(
        gathered_ref, weight_ref, hidden_ref, out_ref, kept_ref, near_ref, rows_ref, held_ref,
        sems, near_sem, kept_sem,
    ):
        near = pltpu.make_async_copy(gathered_ref, near_ref, near_sem)
        near.start()
        part = stream(weight_ref, held_ref, sems, parts)
        kept = pltpu.make_async_copy(hidden_ref, kept_ref, kept_sem)
        kept.start()
        near.wait()
        for j in range(groups):
            rows_ref[pl.ds(j * rows, rows)] = near_ref[j]
        total = jnp.zeros(out_ref.shape, jnp.float32)
        for k in range(parts):
            total = total + jnp.dot(
                rows_ref[:, pl.ds(k * step, step)], part(k), preferred_element_type=jnp.float32
            )
        out_ref[...] = total
        kept.wait()

    return call(
        kernel,
        "project_out",
        (
            pltpu.VMEM((count, weight.shape[1]), jnp.float32),
            pltpu.VMEM(hidden.shape, hidden.dtype),
        ),
        [ANY] * 3,
        weight.size * 2,
        limit=STREAM,
        flops=2 * count * weight.size,
        scratch_shapes=[
            pltpu.VMEM(gathered.shape, gathered.dtype),
            pltpu.VMEM((count, depth), gathered.dtype),
            pltpu.VMEM(weight.shape, weight.dtype),
            pltpu.SemaphoreType.DMA((parts,)),
            pltpu.SemaphoreType.DMA,
            pltpu.SemaphoreType.DMA,
        ],
    )(gathered, weight, hidden)


def down_partials(gathered, adapter, down_store, up_store):
    groups, rows, _ = gathered.shape
    count = groups * rows
    rank, depth = down_store.shape[1:]
    width = up_store.shape[2]

    def kernel(adapter_ref, gathered_ref, down_ref, up_ref, out_ref, picked_ref, held_ref, rows_ref):
        start = pl.multiple_of(lax.axis_index("mp") * depth, depth)
        for j in range(groups):
            rows_ref[pl.ds(j * rows, rows)] = gathered_ref[j, :, pl.ds(start, depth)]
        for r in range(count):
            chosen = adapter_ref[r // rows, r % rows]
            held_ref[pl.ds(r * rank, rank)] = down_ref[chosen]
            picked_ref[pl.ds(r * rank, rank)] = up_ref[chosen]
        every = lax.dot_general(
            rows_ref[...],
            held_ref[...],
            (((1,), (1,)), ((), ())),
            preferred_element_type=jnp.float32,
        )
        row = lax.broadcasted_iota(jnp.int32, (count, LANES), 0)
        lane = lax.broadcasted_iota(jnp.int32, (count, LANES), 1)
        total = jnp.zeros((count, LANES), jnp.float32)
        for s in range(0, count * rank, LANES):
            total = total + jnp.where(row == (lane + s) // rank, every[:, s : s + LANES], 0.0)
        for c in range(groups):
            out_ref[c] = total

    return call(
        kernel,
        "down_partials",
        (
            jax.ShapeDtypeStruct((groups, count, LANES), jnp.float32),
            pltpu.VMEM((count * rank, width), up_store.dtype),
        ),
        [SMEM] + [VMEM] * 3,
        2 * count * rank * (depth + width),
        limit=5 * MIB,
        flops=2 * count * count * rank * depth,
        scratch_shapes=[
            pltpu.VMEM((count * rank, depth), down_store.dtype),
            pltpu.VMEM((count, depth), gathered.dtype),
        ],
    )(adapter, gathered, down_store, up_store)


def add_up(base, partials, up):
    groups, count, _ = partials.shape
    depth, width = up.shape
    rank = depth // count

    def kernel(base_ref, partials_ref, up_ref, out_ref):
        total = partials_ref[0]
        for c in range(1, groups):
            total = total + partials_ref[c]
        down = total.astype(jnp.bfloat16).astype(jnp.float32)
        row = lax.broadcasted_iota(jnp.int32, (count, LANES), 0)
        lane = lax.broadcasted_iota(jnp.int32, (count, LANES), 1)
        spread = []
        for s in range(0, depth, LANES):
            spread.append(jnp.where(row == (lane + s) // rank, down, 0.0))
        spread = jnp.concatenate(spread, 1).astype(jnp.bfloat16)
        delta = jnp.dot(spread, up_ref[...], preferred_element_type=jnp.float32)
        result = (base_ref[...] + ADAPTER_SCALE * delta).astype(jnp.bfloat16)
        for j in range(groups):
            out_ref[j] = result[j * count // groups : (j + 1) * count // groups]

    return call(
        kernel,
        "add_up",
        jax.ShapeDtypeStruct((groups, count // groups, width), jnp.bfloat16),
        [VMEM] * 3,
        up.size * 2,
        limit=4 * MIB,
        flops=2 * count * up.size,
    )(base, partials, up)


def add_rows(hidden, parts):
    width = parts.shape[2]

    def kernel(hidden_ref, parts_ref, out_ref):
        for k, place in enumerate(order(parts.shape[0])):
            part = pl.ds(place * width, width)
            total = hidden_ref[:, part].astype(jnp.float32) + parts_ref[k].astype(jnp.float32)
            out_ref[:, part] = total.astype(jnp.bfloat16)

    return call(
        kernel,
        "add_rows",
        jax.ShapeDtypeStruct(hidden.shape, parts.dtype),
        [VMEM, VMEM],
        hidden.size * 6,
    )(hidden, parts)


def swap_cores(block):
    return lax.ppermute(block, "batch", [(0, 1), (1, 0)])


def order(size):
    return [(k + size // 2) % size for k in range(size)]


def exchange(blocks):
    group = order(lax.axis_size("mp"))
    return lax.all_to_all(
        blocks, "mp", split_axis=0, concat_axis=0, tiled=True, axis_index_groups=[group]
    )


def exchange_all(blocks):
    group = [2 * j + core for j in order(lax.axis_size("mp")) for core in (1, 0)]
    return lax.all_to_all(
        blocks,
        ("mp", "batch"),
        split_axis=0,
        concat_axis=0,
        tiled=True,
        axis_index_groups=[group],
    )


def attend(qkv, cosine, sine, key_cache, value_cache, mask):
    rows = qkv.shape[0]
    query_width = HEADS * HEAD_DIM
    kv_width = KV_HEADS * HEAD_DIM
    group = HEADS // KV_HEADS
    scale = HEAD_DIM ** (-0.5)

    def turn(part):
        vec = part.astype(jnp.float32).reshape(rows, -1, HEAD_DIM)
        half = HEAD_DIM // 2
        turned = jnp.concatenate([-vec[..., half:], vec[..., :half]], -1)
        return (vec * cosine[:, None] + turned * sine[:, None]).astype(jnp.bfloat16)

    query = turn(qkv[:, :query_width])
    fresh_key = turn(qkv[:, query_width : query_width + kv_width])
    fresh_value = (
        qkv[:, query_width + kv_width :].astype(jnp.float32).reshape(rows, KV_HEADS, HEAD_DIM)
    )
    grouped = query.reshape(rows, KV_HEADS, group, HEAD_DIM)
    cached = key_cache.reshape(rows, -1, KV_HEADS, HEAD_DIM)
    stored = value_cache.reshape(rows, -1, KV_HEADS, HEAD_DIM)
    scores = (
        jnp.einsum("rgqd,rtgd->rgqt", grouped, cached, preferred_element_type=jnp.float32) * scale
    )
    scores = scores + mask[:, None, None, :]
    own = (
        jnp.einsum("rgqd,rgd->rgq", grouped, fresh_key, preferred_element_type=jnp.float32) * scale
    )
    top = jnp.maximum(jnp.max(scores, -1), own)
    expo = jnp.exp(scores - top[..., None])
    own_exp = jnp.exp(own - top)
    total = jnp.sum(expo, -1) + own_exp
    probs = (expo / total[..., None]).astype(jnp.bfloat16)
    own_prob = (own_exp / total).astype(jnp.bfloat16)
    context_vector = jnp.einsum(
        "rgqt,rtgd->rgqd", probs, stored, preferred_element_type=jnp.float32
    )
    context_vector = (
        context_vector + own_prob.astype(jnp.float32)[..., None] * fresh_value[:, :, None, :]
    )
    return context_vector.reshape(rows, query_width).astype(jnp.bfloat16)


def fast_body(
    hidden,
    attention_norm_gain,
    query_key_value_weight,
    output_weight,
    key_cache,
    value_cache,
    lengths,
    slots,
    requests,
    adapter_down_matrices,
    adapter_up_matrices,
):
    rows = hidden.shape[0]
    mp_size = lax.axis_size("mp")
    width = query_key_value_weight.shape[1]

    frequency = frequencies(exponents())
    near = exchange(norm_rows(hidden, attention_norm_gain, frequency, mp_size))
    lined, cosine, sine, mask, adapter = turns(
        near, frequency, lengths, slots, requests, key_cache.shape[1]
    )
    columns = project_qkv(lined, swap_cores(near), query_key_value_weight, adapter)
    mixed = exchange_all(columns)
    adapter = mixed.reshape(mp_size, -1, rows, width + LANES)[:, :, :, width]
    adapter = jnp.sum(adapter.astype(jnp.float32), 1).astype(jnp.int32)
    qkv = mixed[:, :, :width].reshape(mp_size, 2, rows, width)
    qkv = jnp.roll(qkv[:, ::-1], mp_size // 2, 0).transpose(2, 0, 1, 3).reshape(rows, -1)

    context = attend(qkv, cosine, sine, key_cache, value_cache, mask)
    context, adapter = lax.optimization_barrier((context, adapter))
    gathered = exchange(jnp.broadcast_to(context[None], (mp_size, *context.shape)))

    partials, up = down_partials(
        gathered, adapter, adapter_down_matrices.swapaxes(1, 2), adapter_up_matrices
    )
    partials = exchange(partials)
    base, kept = project_out(gathered, output_weight, hidden)
    return add_rows(kept, exchange(add_up(base, partials, up)))


def body(*arguments):
    small = lax.axis_size("mp") <= 16 and lax.axis_size("batch") == 2
    whole_heads = arguments[2].shape[1] % HEAD_DIM == 0
    return (fast_body if small and whole_heads else general_body)(*arguments)


def solution(mesh):
    in_specs = (
        P(("groups", "mp", "batch"), None),
        P(),
        P(None, ("mp", "batch")),
        P(None, "mp"),
        P(("groups", "mp", "batch"), None, None),
        P(("groups", "mp", "batch"), None, None),
        P(("groups", "mp", "batch")),
        P(("groups", "mp", "batch")),
        P(("groups", "mp", "batch"), None),
        P(None, "mp", None),
        P(None, None, "mp"),
    )
    out_specs = P(("groups", "mp", "batch"), None)
    return jax.shard_map(body, mesh=mesh, in_specs=in_specs, out_specs=out_specs, check_vma=False)
```

```python
import math

import jax
import jax.numpy as jnp
from jax import lax
from jax.experimental import pallas as pl
from jax.experimental.pallas import tpu as pltpu
from jax.sharding import PartitionSpec as P

HEADS = 64
KV_HEADS = 8
HEAD_DIM = 128
ADAPTER_COUNT = 64


EPS = 1e-05
THETA = 500000.0
ADAPTER_SCALE = 2.0


def rotate(vec, pos):
    width = vec.shape[-1]
    half = width // 2
    freq = THETA ** (-(jnp.arange(half, dtype=jnp.float32) * 2.0) / width)
    angle = pos[..., None, None] * freq
    cosine = jnp.concatenate([jnp.cos(angle), jnp.cos(angle)], -1)
    sine = jnp.concatenate([jnp.sin(angle), jnp.sin(angle)], -1)
    turned = jnp.concatenate([-vec[..., half:], vec[..., :half]], -1)
    return vec * cosine + turned * sine


def apply_up_matrix(
    context_vector, adapter_selector, down_result, output_weight, adapter_up_matrices
):
    base_output = jnp.dot(context_vector, output_weight, preferred_element_type=jnp.float32)
    spread = (adapter_selector[:, :, None] * down_result[:, None, :]).reshape(
        adapter_selector.shape[0], -1
    )
    adapter_table = adapter_up_matrices.reshape(-1, adapter_up_matrices.shape[2])
    adapter_delta = jnp.dot(spread, adapter_table, preferred_element_type=jnp.float32)
    return (base_output + ADAPTER_SCALE * adapter_delta).astype(jnp.bfloat16)


def general_body(
    hidden,
    attention_norm_gain,
    query_key_value_weight,
    output_weight,
    key_cache,
    value_cache,
    lengths,
    slots,
    requests,
    adapter_down_matrices,
    adapter_up_matrices,
):
    widened = hidden.astype(jnp.float32)
    normed = (
        widened
        * lax.rsqrt(jnp.mean(widened * widened, -1, keepdims=True) + EPS)
        * attention_norm_gain.astype(jnp.float32)
    ).astype(jnp.bfloat16)
    rows = normed.shape[0]
    columns = jnp.dot(
        lax.all_gather(normed, ("mp", "batch"), axis=0, tiled=True),
        query_key_value_weight,
        preferred_element_type=jnp.float32,
    ).astype(jnp.bfloat16)
    mixed = lax.all_to_all(
        lax.all_to_all(columns, "mp", split_axis=0, concat_axis=1, tiled=True),
        "batch",
        split_axis=0,
        concat_axis=1,
        tiled=True,
    )
    width = query_key_value_weight.shape[1]
    qkv = (
        mixed.reshape(rows, lax.axis_size("batch"), lax.axis_size("mp"), width)
        .transpose(0, 2, 1, 3)
        .reshape(rows, -1)
    )
    query_width = HEADS * HEAD_DIM
    kv_width = KV_HEADS * HEAD_DIM
    group = HEADS // KV_HEADS
    scale = HEAD_DIM ** (-0.5)
    pos = lengths.astype(jnp.float32)
    query = rotate(
        qkv[:, :query_width].astype(jnp.float32).reshape(rows, HEADS, HEAD_DIM), pos
    ).astype(jnp.bfloat16)
    fresh_key = rotate(
        qkv[:, query_width : query_width + kv_width]
        .astype(jnp.float32)
        .reshape(rows, KV_HEADS, HEAD_DIM),
        pos,
    ).astype(jnp.bfloat16)
    fresh_value = (
        qkv[:, query_width + kv_width :].astype(jnp.float32).reshape(rows, KV_HEADS, HEAD_DIM)
    )
    grouped = query.reshape(rows, KV_HEADS, group, HEAD_DIM)
    cached = key_cache.reshape(rows, -1, KV_HEADS, HEAD_DIM)
    stored = value_cache.reshape(rows, -1, KV_HEADS, HEAD_DIM)
    scores = (
        jnp.einsum("rgqd,rtgd->rgqt", grouped, cached, preferred_element_type=jnp.float32) * scale
    )
    live = jnp.arange(cached.shape[1])[None, :] < lengths[:, None]
    scores = jnp.where(live[:, None, None, :], scores, -jnp.inf)
    own = (
        jnp.einsum("rgqd,rgd->rgq", grouped, fresh_key, preferred_element_type=jnp.float32) * scale
    )
    top = jnp.maximum(jnp.max(scores, -1), own)
    expo = jnp.exp(scores - top[..., None])
    own_exp = jnp.exp(own - top)
    total = jnp.sum(expo, -1) + own_exp
    probs = (expo / total[..., None]).astype(jnp.bfloat16)
    own_prob = (own_exp / total).astype(jnp.bfloat16)
    context_vector = jnp.einsum(
        "rgqt,rtgd->rgqd", probs, stored, preferred_element_type=jnp.float32
    )
    context_vector = (
        context_vector + own_prob.astype(jnp.float32)[..., None] * fresh_value[:, :, None, :]
    )
    context_vector = context_vector.reshape(rows, query_width).astype(jnp.bfloat16)
    slot_hits = slots[:, None] == jnp.arange(requests.shape[1])[None, :]
    adapter = jnp.sum(jnp.where(slot_hits, requests[0][None, :], 0), 1)
    adapter_selector = (adapter[:, None] == jnp.arange(ADAPTER_COUNT)[None, :]).astype(jnp.bfloat16)
    context_gathered, selector_gathered = (
        lax.all_gather(context_vector, "mp", axis=0, tiled=True),
        lax.all_gather(adapter_selector, "mp", axis=0, tiled=True),
    )
    shared_portion = adapter_down_matrices.shape[1]
    context_slice = lax.dynamic_slice_in_dim(
        context_gathered, lax.axis_index("mp") * shared_portion, shared_portion, 1
    )
    every_adapter = jnp.einsum(
        "gh,thy->gty", context_slice, adapter_down_matrices, preferred_element_type=jnp.float32
    )
    partial_down = jnp.sum(every_adapter * selector_gathered.astype(jnp.float32)[:, :, None], 1)
    down_gathered = lax.psum(partial_down, "mp").astype(jnp.bfloat16)
    projection_result = apply_up_matrix(
        context_gathered, selector_gathered, down_gathered, output_weight, adapter_up_matrices
    )
    returned = lax.all_to_all(projection_result, "mp", split_axis=0, concat_axis=1, tiled=True)
    return (widened + returned.astype(jnp.float32)).astype(jnp.bfloat16)


MIB = 1 << 20
LANES = 128
LONG = 10**10
STREAM = 53 * MIB
VMEM = pl.BlockSpec(memory_space=pltpu.VMEM)
SMEM = pl.BlockSpec(memory_space=pltpu.SMEM)
ANY = pl.BlockSpec(memory_space=pl.ANY)


def call(kernel, name, out_shape, in_specs, moved, limit=2 * MIB, flops=0, **options):
    return pl.pallas_call(
        kernel,
        out_shape=out_shape,
        in_specs=in_specs,
        out_specs=jax.tree.map(lambda _: VMEM, out_shape),
        compiler_params=pltpu.CompilerParams(vmem_limit_bytes=limit),
        cost_estimate=pl.CostEstimate(flops=flops, bytes_accessed=moved, transcendentals=0),
        name=name,
        **options,
    )


def exponents():
    def kernel(out_ref):
        lane = lax.broadcasted_iota(jnp.int32, (1, HEAD_DIM), 1)
        out_ref[...] = (lane % (HEAD_DIM // 2)).astype(jnp.float32) * (-2.0 / HEAD_DIM)

    shape = jax.ShapeDtypeStruct((1, HEAD_DIM), jnp.float32)
    return call(kernel, "exponents", shape, [], 0, flops=LONG // 8)()


def frequencies(exponent):
    def kernel(exponent_ref, out_ref):
        out_ref[...] = jnp.exp(exponent_ref[...] * math.log(THETA))

    shape = jax.ShapeDtypeStruct(exponent.shape, jnp.float32)
    return call(kernel, "frequencies", shape, [VMEM], 0, flops=LONG // 8)(exponent)


def norm_rows(hidden, gain, after, copies):
    rows, width = hidden.shape

    def kernel(hidden_ref, gain_ref, after_ref, out_ref):
        del after_ref
        wide = hidden_ref[...].astype(jnp.float32)
        inverse = lax.rsqrt(jnp.mean(wide * wide, -1, keepdims=True) + EPS)
        normed = (wide * inverse * gain_ref[...].astype(jnp.float32)).astype(jnp.bfloat16)
        for c in range(copies):
            out_ref[c] = normed

    return call(
        kernel,
        "norm_rows",
        jax.ShapeDtypeStruct((copies, rows, width), jnp.bfloat16),
        [VMEM, VMEM, ANY],
        hidden.size * 2 * (copies + 1),
        flops=LONG,
    )(hidden, gain[None], after)


def turns(near, frequency, lengths, slots, requests, context):
    groups, rows, depth = near.shape

    def kernel(
        lengths_ref, slots_ref, requests_ref, near_ref, frequency_ref, lined_ref, cosine_ref,
        sine_ref, mask_ref, adapter_ref,
    ):
        for j in range(groups):
            lined_ref[pl.ds(j * rows, rows)] = near_ref[j]
        row = lax.broadcasted_iota(jnp.int32, (rows, LANES), 0)
        length = jnp.zeros((rows, LANES), jnp.int32)
        adapter = jnp.zeros((rows, LANES), jnp.int32)
        for r in range(rows):
            length = jnp.where(row == r, lengths_ref[r], length)
            adapter = jnp.where(row == r, requests_ref[0, slots_ref[r]], adapter)
        angle = length.astype(jnp.float32) * frequency_ref[...]
        cosine_ref[...] = jnp.cos(angle)
        sine_ref[...] = jnp.sin(angle)
        lane = lax.broadcasted_iota(jnp.int32, (rows, LANES), 1)
        for t in range(0, context, LANES):
            mask_ref[:, pl.ds(t, LANES)] = jnp.where(lane + t < length, 0.0, -jnp.inf)
        adapter_ref[...] = adapter.astype(jnp.float32).astype(jnp.bfloat16)

    return call(
        kernel,
        "turns",
        (
            jax.ShapeDtypeStruct((groups * rows, depth), near.dtype),
            jax.ShapeDtypeStruct((rows, HEAD_DIM), jnp.float32),
            jax.ShapeDtypeStruct((rows, HEAD_DIM), jnp.float32),
            jax.ShapeDtypeStruct((rows, context), jnp.float32),
            jax.ShapeDtypeStruct((rows, LANES), jnp.bfloat16),
        ),
        [SMEM] * 3 + [VMEM] * 2,
        near.size * 4,
    )(lengths, slots, requests, near, frequency)


def project_qkv(lined, far, weight, adapter, chunk=1024):
    groups, rows, _ = far.shape
    depth, width = weight.shape
    half = groups * rows

    def kernel(lined_ref, far_ref, weight_ref, adapter_ref, out_ref, far_lined_ref):
        for j in range(groups):
            far_lined_ref[pl.ds(j * rows, rows)] = far_ref[j]
        total = jnp.zeros((2 * half, width), jnp.float32)
        for k in range(depth // chunk):
            part = pl.ds(k * chunk, chunk)
            total = total + jnp.dot(
                jnp.concatenate([lined_ref[:, part], far_lined_ref[:, part]]),
                weight_ref[part, :],
                preferred_element_type=jnp.float32,
            )
        core = lax.axis_index("batch")
        adapter = adapter_ref[...]
        for e in range(2):
            for j in range(groups):
                place = e * half + j * rows
                device = 2 * j + (core ^ e ^ 1)
                out_ref[device, :, pl.ds(0, width)] = total[place : place + rows].astype(
                    jnp.bfloat16
                )
                out_ref[device, :, pl.ds(width, LANES)] = (
                    adapter if e == 0 else jnp.zeros_like(adapter)
                )

    return call(
        kernel,
        "project_qkv",
        jax.ShapeDtypeStruct((2 * groups, rows, width + LANES), jnp.bfloat16),
        [VMEM] * 4,
        weight.size * 2,
        flops=LONG,
        scratch_shapes=[pltpu.VMEM((half, depth), jnp.bfloat16)],
    )(lined, far, weight, adapter)


def stream(weight_ref, held_ref, sems, parts):
    depth = held_ref.shape[0] // parts
    copies = []
    for k in range(parts):
        rows = pl.ds(k * depth, depth)
        copies.append(
            pltpu.make_async_copy(weight_ref.at[rows], held_ref.at[rows], sems.at[k])
        )
        copies[-1].start()

    def part(k):
        copies[k].wait()
        return held_ref[pl.ds(k * depth, depth)]

    return part


def project_out(gathered, weight, parts=16):
    groups, rows, depth = gathered.shape
    count, step = groups * rows, depth // parts

    def kernel(gathered_ref, weight_ref, out_ref, near_ref, rows_ref, held_ref, sems, near_sem):
        near = pltpu.make_async_copy(gathered_ref, near_ref, near_sem)
        near.start()
        part = stream(weight_ref, held_ref, sems, parts)
        near.wait()
        for j in range(groups):
            rows_ref[pl.ds(j * rows, rows)] = near_ref[j]
        total = jnp.zeros(out_ref.shape, jnp.float32)
        for k in range(parts):
            total = total + jnp.dot(
                rows_ref[:, pl.ds(k * step, step)], part(k), preferred_element_type=jnp.float32
            )
        out_ref[...] = total

    return call(
        kernel,
        "project_out",
        pltpu.VMEM((count, weight.shape[1]), jnp.float32),
        [ANY] * 2,
        weight.size * 2,
        limit=STREAM,
        flops=2 * count * weight.size,
        scratch_shapes=[
            pltpu.VMEM(gathered.shape, gathered.dtype),
            pltpu.VMEM((count, depth), gathered.dtype),
            pltpu.VMEM(weight.shape, weight.dtype),
            pltpu.SemaphoreType.DMA((parts,)),
            pltpu.SemaphoreType.DMA,
        ],
    )(gathered, weight)


def down_partials(gathered, adapter, down_store, up_store):
    groups, rows, _ = gathered.shape
    count = groups * rows
    rank, depth = down_store.shape[1:]
    width = up_store.shape[2]

    def kernel(adapter_ref, gathered_ref, down_ref, up_ref, out_ref, picked_ref, held_ref, rows_ref):
        start = pl.multiple_of(lax.axis_index("mp") * depth, depth)
        for j in range(groups):
            rows_ref[pl.ds(j * rows, rows)] = gathered_ref[j, :, pl.ds(start, depth)]
        for r in range(count):
            chosen = adapter_ref[r, 0]
            held_ref[pl.ds(r * rank, rank)] = down_ref[chosen]
            picked_ref[pl.ds(r * rank, rank)] = up_ref[chosen]
        every = lax.dot_general(
            rows_ref[...],
            held_ref[...],
            (((1,), (1,)), ((), ())),
            preferred_element_type=jnp.float32,
        )
        row = lax.broadcasted_iota(jnp.int32, (count, LANES), 0)
        lane = lax.broadcasted_iota(jnp.int32, (count, LANES), 1)
        total = jnp.zeros((count, LANES), jnp.float32)
        for s in range(0, count * rank, LANES):
            total = total + jnp.where(row == (lane + s) // rank, every[:, s : s + LANES], 0.0)
        for c in range(groups):
            out_ref[c] = total

    return call(
        kernel,
        "down_partials",
        (
            jax.ShapeDtypeStruct((groups, count, LANES), jnp.float32),
            pltpu.VMEM((count * rank, width), up_store.dtype),
        ),
        [SMEM] + [VMEM] * 3,
        2 * count * rank * (depth + width),
        limit=5 * MIB,
        flops=2 * count * count * rank * depth,
        scratch_shapes=[
            pltpu.VMEM((count * rank, depth), down_store.dtype),
            pltpu.VMEM((count, depth), gathered.dtype),
        ],
    )(adapter, gathered, down_store, up_store)


def add_up(base, partials, up):
    groups, count, _ = partials.shape
    depth, width = up.shape
    rank = depth // count

    def kernel(base_ref, partials_ref, up_ref, out_ref):
        total = partials_ref[0]
        for c in range(1, groups):
            total = total + partials_ref[c]
        down = total.astype(jnp.bfloat16).astype(jnp.float32)
        row = lax.broadcasted_iota(jnp.int32, (count, LANES), 0)
        lane = lax.broadcasted_iota(jnp.int32, (count, LANES), 1)
        spread = []
        for s in range(0, depth, LANES):
            spread.append(jnp.where(row == (lane + s) // rank, down, 0.0))
        spread = jnp.concatenate(spread, 1).astype(jnp.bfloat16)
        delta = jnp.dot(spread, up_ref[...], preferred_element_type=jnp.float32)
        result = (base_ref[...] + ADAPTER_SCALE * delta).astype(jnp.bfloat16)
        for j in range(groups):
            out_ref[j] = result[j * count // groups : (j + 1) * count // groups]

    return call(
        kernel,
        "add_up",
        jax.ShapeDtypeStruct((groups, count // groups, width), jnp.bfloat16),
        [VMEM] * 3,
        up.size * 2,
        limit=4 * MIB,
        flops=2 * count * up.size,
    )(base, partials, up)


def add_rows(hidden, parts):
    width = parts.shape[2]

    def kernel(hidden_ref, parts_ref, out_ref):
        for k, place in enumerate(order(parts.shape[0])):
            part = pl.ds(place * width, width)
            total = hidden_ref[:, part].astype(jnp.float32) + parts_ref[k].astype(jnp.float32)
            out_ref[:, part] = total.astype(jnp.bfloat16)

    return call(
        kernel,
        "add_rows",
        jax.ShapeDtypeStruct(hidden.shape, parts.dtype),
        [VMEM, VMEM],
        hidden.size * 6,
    )(hidden, parts)


def swap_cores(block):
    return lax.ppermute(block, "batch", [(0, 1), (1, 0)])


def order(size):
    return [(k + size // 2) % size for k in range(size)]


def exchange(blocks):
    group = order(lax.axis_size("mp"))
    return lax.all_to_all(
        blocks, "mp", split_axis=0, concat_axis=0, tiled=True, axis_index_groups=[group]
    )


def exchange_all(blocks):
    group = [2 * j + core for j in order(lax.axis_size("mp")) for core in (1, 0)]
    return lax.all_to_all(
        blocks,
        ("mp", "batch"),
        split_axis=0,
        concat_axis=0,
        tiled=True,
        axis_index_groups=[group],
    )


def attend(mixed, cosine, sine, mask, key_cache, value_cache, copies):
    rows, context = key_cache.shape[:2]
    group = HEADS // KV_HEADS
    heads = HEADS + 2 * KV_HEADS
    width = mixed.shape[2] - LANES
    per_device = width // HEAD_DIM
    devices = order(mixed.shape[0] // 2)

    def kernel(
        mixed_ref, cosine_ref, sine_ref, mask_ref, key_ref, value_ref, out_ref, adapter_ref,
        vec_ref, context_ref,
    ):
        for k, j in enumerate(devices):
            for core in range(2):
                block = mixed_ref[2 * k + 1 - core].astype(jnp.float32)
                for c in range(per_device):
                    head = (2 * j + core) * per_device + c
                    vec_ref[pl.ds(head * rows, rows)] = block[:, c * HEAD_DIM : (c + 1) * HEAD_DIM]
            both = mixed_ref[2 * k, :, pl.ds(width, LANES)].astype(jnp.float32)
            both = both + mixed_ref[2 * k + 1, :, pl.ds(width, LANES)].astype(jnp.float32)
            adapter_ref[pl.ds(k * rows, rows)] = both.astype(jnp.int32)

        def tiled(pair, count):
            return jnp.concatenate([pair] * count)

        keyed = (HEADS + KV_HEADS) * rows
        vec = vec_ref[pl.ds(0, keyed)]
        turned = pltpu.roll(vec, HEAD_DIM // 2, 1)
        lane = lax.broadcasted_iota(jnp.int32, (rows, HEAD_DIM), 1)
        signed = jnp.where(lane < HEAD_DIM // 2, -sine_ref[...], sine_ref[...])
        pairs = keyed // rows
        vec = vec * tiled(cosine_ref[...], pairs) + turned * tiled(signed, pairs)
        vec = vec.astype(jnp.bfloat16)
        query = vec[: HEADS * rows]
        fresh_key = vec[HEADS * rows :].astype(jnp.float32)
        fresh_value = vec_ref[pl.ds(keyed, KV_HEADS * rows)]
        size = group * rows
        owner = lax.broadcasted_iota(jnp.int32, (size, 1), 0) % rows

        def of_owner(products):
            result = products[0]
            for r in range(1, rows):
                result = jnp.where(owner == r, products[r], result)
            return result

        scores, own_key, own_value = [], [], []
        for g in range(KV_HEADS):
            lanes = pl.ds(g * HEAD_DIM, HEAD_DIM)
            part = query[g * size : (g + 1) * size]
            products = [
                lax.dot_general(
                    part,
                    key_ref[r, :, lanes],
                    (((1,), (1,)), ((), ())),
                    preferred_element_type=jnp.float32,
                )
                for r in range(rows)
            ]
            scores.append(of_owner(products))
            own_key.append(tiled(fresh_key[g * rows : (g + 1) * rows], group))
            own_value.append(tiled(fresh_value[g * rows : (g + 1) * rows], group))
        scale = HEAD_DIM ** (-0.5)
        scores = jnp.concatenate(scores) * scale + tiled(mask_ref[...], HEADS)
        own = jnp.sum(query.astype(jnp.float32) * jnp.concatenate(own_key), 1, keepdims=True)
        own = own * scale
        top = jnp.maximum(jnp.max(scores, 1, keepdims=True), own)
        expo = jnp.exp(scores - top)
        own_exp = jnp.exp(own - top)
        total = jnp.sum(expo, 1, keepdims=True) + own_exp
        probs = (expo / total).astype(jnp.bfloat16)
        own_prob = (own_exp / total).astype(jnp.bfloat16).astype(jnp.float32)
        for g in range(KV_HEADS):
            lanes = pl.ds(g * HEAD_DIM, HEAD_DIM)
            part = probs[g * size : (g + 1) * size]
            products = [
                jnp.dot(part, value_ref[r, :, lanes], preferred_element_type=jnp.float32)
                for r in range(rows)
            ]
            result = of_owner(products) + own_prob[g * size : (g + 1) * size] * own_value[g]
            for h in range(group):
                place = pl.ds((g * group + h) * HEAD_DIM, HEAD_DIM)
                context_ref[:, place] = result[h * rows : (h + 1) * rows]
        rounded = context_ref[...].astype(jnp.bfloat16)
        for c in range(copies):
            out_ref[c] = rounded

    return call(
        kernel,
        "attend",
        (
            jax.ShapeDtypeStruct((copies, rows, HEADS * HEAD_DIM), jnp.bfloat16),
            jax.ShapeDtypeStruct((copies * rows, LANES), jnp.int32),
        ),
        [VMEM] * 6,
        key_cache.size * 4,
        limit=4 * MIB,
        flops=LONG,
        scratch_shapes=[
            pltpu.VMEM((heads * rows, HEAD_DIM), jnp.float32),
            pltpu.VMEM((rows, HEADS * HEAD_DIM), jnp.float32),
        ],
    )(mixed, cosine, sine, mask, key_cache, value_cache)


def fast_body(
    hidden,
    attention_norm_gain,
    query_key_value_weight,
    output_weight,
    key_cache,
    value_cache,
    lengths,
    slots,
    requests,
    adapter_down_matrices,
    adapter_up_matrices,
):
    mp_size = lax.axis_size("mp")
    frequency = frequencies(exponents())
    near = exchange(norm_rows(hidden, attention_norm_gain, frequency, mp_size))
    lined, cosine, sine, mask, adapter = turns(
        near, frequency, lengths, slots, requests, key_cache.shape[1]
    )
    columns = project_qkv(lined, swap_cores(near), query_key_value_weight, adapter)
    mixed = exchange_all(columns)
    context, adapter = attend(mixed, cosine, sine, mask, key_cache, value_cache, mp_size)
    gathered = exchange(context)

    partials, up = down_partials(
        gathered, adapter, adapter_down_matrices.swapaxes(1, 2), adapter_up_matrices
    )
    partials = exchange(partials)
    projected = add_up(project_out(gathered, output_weight), partials, up)
    return add_rows(hidden, exchange(projected))


def body(*arguments):
    small = lax.axis_size("mp") <= 16 and lax.axis_size("batch") == 2
    whole_heads = arguments[2].shape[1] % HEAD_DIM == 0
    return (fast_body if small and whole_heads else general_body)(*arguments)


def solution(mesh):
    in_specs = (
        P(("groups", "mp", "batch"), None),
        P(),
        P(None, ("mp", "batch")),
        P(None, "mp"),
        P(("groups", "mp", "batch"), None, None),
        P(("groups", "mp", "batch"), None, None),
        P(("groups", "mp", "batch")),
        P(("groups", "mp", "batch")),
        P(("groups", "mp", "batch"), None),
        P(None, "mp", None),
        P(None, None, "mp"),
    )
    out_specs = P(("groups", "mp", "batch"), None)
    return jax.shard_map(body, mesh=mesh, in_specs=in_specs, out_specs=out_specs, check_vma=False)
```

```python
import math

import jax
import jax.numpy as jnp
from jax import lax
from jax.experimental import pallas as pl
from jax.experimental.pallas import tpu as pltpu
from jax.sharding import PartitionSpec as P

HEADS = 64
KV_HEADS = 8
HEAD_DIM = 128
ADAPTER_COUNT = 64


EPS = 1e-05
THETA = 500000.0
ADAPTER_SCALE = 2.0


def rotate(vec, pos):
    width = vec.shape[-1]
    half = width // 2
    freq = THETA ** (-(jnp.arange(half, dtype=jnp.float32) * 2.0) / width)
    angle = pos[..., None, None] * freq
    cosine = jnp.concatenate([jnp.cos(angle), jnp.cos(angle)], -1)
    sine = jnp.concatenate([jnp.sin(angle), jnp.sin(angle)], -1)
    turned = jnp.concatenate([-vec[..., half:], vec[..., :half]], -1)
    return vec * cosine + turned * sine


def apply_up_matrix(
    context_vector, adapter_selector, down_result, output_weight, adapter_up_matrices
):
    base_output = jnp.dot(context_vector, output_weight, preferred_element_type=jnp.float32)
    spread = (adapter_selector[:, :, None] * down_result[:, None, :]).reshape(
        adapter_selector.shape[0], -1
    )
    adapter_table = adapter_up_matrices.reshape(-1, adapter_up_matrices.shape[2])
    adapter_delta = jnp.dot(spread, adapter_table, preferred_element_type=jnp.float32)
    return (base_output + ADAPTER_SCALE * adapter_delta).astype(jnp.bfloat16)


def general_body(
    hidden,
    attention_norm_gain,
    query_key_value_weight,
    output_weight,
    key_cache,
    value_cache,
    lengths,
    slots,
    requests,
    adapter_down_matrices,
    adapter_up_matrices,
):
    widened = hidden.astype(jnp.float32)
    normed = (
        widened
        * lax.rsqrt(jnp.mean(widened * widened, -1, keepdims=True) + EPS)
        * attention_norm_gain.astype(jnp.float32)
    ).astype(jnp.bfloat16)
    rows = normed.shape[0]
    columns = jnp.dot(
        lax.all_gather(normed, ("mp", "batch"), axis=0, tiled=True),
        query_key_value_weight,
        preferred_element_type=jnp.float32,
    ).astype(jnp.bfloat16)
    mixed = lax.all_to_all(
        lax.all_to_all(columns, "mp", split_axis=0, concat_axis=1, tiled=True),
        "batch",
        split_axis=0,
        concat_axis=1,
        tiled=True,
    )
    width = query_key_value_weight.shape[1]
    qkv = (
        mixed.reshape(rows, lax.axis_size("batch"), lax.axis_size("mp"), width)
        .transpose(0, 2, 1, 3)
        .reshape(rows, -1)
    )
    query_width = HEADS * HEAD_DIM
    kv_width = KV_HEADS * HEAD_DIM
    group = HEADS // KV_HEADS
    scale = HEAD_DIM ** (-0.5)
    pos = lengths.astype(jnp.float32)
    query = rotate(
        qkv[:, :query_width].astype(jnp.float32).reshape(rows, HEADS, HEAD_DIM), pos
    ).astype(jnp.bfloat16)
    fresh_key = rotate(
        qkv[:, query_width : query_width + kv_width]
        .astype(jnp.float32)
        .reshape(rows, KV_HEADS, HEAD_DIM),
        pos,
    ).astype(jnp.bfloat16)
    fresh_value = (
        qkv[:, query_width + kv_width :].astype(jnp.float32).reshape(rows, KV_HEADS, HEAD_DIM)
    )
    grouped = query.reshape(rows, KV_HEADS, group, HEAD_DIM)
    cached = key_cache.reshape(rows, -1, KV_HEADS, HEAD_DIM)
    stored = value_cache.reshape(rows, -1, KV_HEADS, HEAD_DIM)
    scores = (
        jnp.einsum("rgqd,rtgd->rgqt", grouped, cached, preferred_element_type=jnp.float32) * scale
    )
    live = jnp.arange(cached.shape[1])[None, :] < lengths[:, None]
    scores = jnp.where(live[:, None, None, :], scores, -jnp.inf)
    own = (
        jnp.einsum("rgqd,rgd->rgq", grouped, fresh_key, preferred_element_type=jnp.float32) * scale
    )
    top = jnp.maximum(jnp.max(scores, -1), own)
    expo = jnp.exp(scores - top[..., None])
    own_exp = jnp.exp(own - top)
    total = jnp.sum(expo, -1) + own_exp
    probs = (expo / total[..., None]).astype(jnp.bfloat16)
    own_prob = (own_exp / total).astype(jnp.bfloat16)
    context_vector = jnp.einsum(
        "rgqt,rtgd->rgqd", probs, stored, preferred_element_type=jnp.float32
    )
    context_vector = (
        context_vector + own_prob.astype(jnp.float32)[..., None] * fresh_value[:, :, None, :]
    )
    context_vector = context_vector.reshape(rows, query_width).astype(jnp.bfloat16)
    slot_hits = slots[:, None] == jnp.arange(requests.shape[1])[None, :]
    adapter = jnp.sum(jnp.where(slot_hits, requests[0][None, :], 0), 1)
    adapter_selector = (adapter[:, None] == jnp.arange(ADAPTER_COUNT)[None, :]).astype(jnp.bfloat16)
    context_gathered, selector_gathered = (
        lax.all_gather(context_vector, "mp", axis=0, tiled=True),
        lax.all_gather(adapter_selector, "mp", axis=0, tiled=True),
    )
    shared_portion = adapter_down_matrices.shape[1]
    context_slice = lax.dynamic_slice_in_dim(
        context_gathered, lax.axis_index("mp") * shared_portion, shared_portion, 1
    )
    every_adapter = jnp.einsum(
        "gh,thy->gty", context_slice, adapter_down_matrices, preferred_element_type=jnp.float32
    )
    partial_down = jnp.sum(every_adapter * selector_gathered.astype(jnp.float32)[:, :, None], 1)
    down_gathered = lax.psum(partial_down, "mp").astype(jnp.bfloat16)
    projection_result = apply_up_matrix(
        context_gathered, selector_gathered, down_gathered, output_weight, adapter_up_matrices
    )
    returned = lax.all_to_all(projection_result, "mp", split_axis=0, concat_axis=1, tiled=True)
    return (widened + returned.astype(jnp.float32)).astype(jnp.bfloat16)


MIB = 1 << 20
LANES = 128
LONG = 10**10
STREAM = 53 * MIB
VMEM = pl.BlockSpec(memory_space=pltpu.VMEM)
SMEM = pl.BlockSpec(memory_space=pltpu.SMEM)
ANY = pl.BlockSpec(memory_space=pl.ANY)


def call(kernel, name, out_shape, in_specs, moved, limit=2 * MIB, flops=0, **options):
    return pl.pallas_call(
        kernel,
        out_shape=out_shape,
        in_specs=in_specs,
        out_specs=jax.tree.map(lambda _: VMEM, out_shape),
        compiler_params=pltpu.CompilerParams(vmem_limit_bytes=limit),
        cost_estimate=pl.CostEstimate(flops=flops, bytes_accessed=moved, transcendentals=0),
        name=name,
        **options,
    )


def exponents():
    def kernel(out_ref):
        lane = lax.broadcasted_iota(jnp.int32, (1, HEAD_DIM), 1)
        out_ref[...] = (lane % (HEAD_DIM // 2)).astype(jnp.float32) * (-2.0 / HEAD_DIM)

    shape = jax.ShapeDtypeStruct((1, HEAD_DIM), jnp.float32)
    return call(kernel, "exponents", shape, [], 0, flops=LONG // 8)()


def frequencies(exponent):
    def kernel(exponent_ref, out_ref):
        out_ref[...] = jnp.exp(exponent_ref[...] * math.log(THETA))

    shape = jax.ShapeDtypeStruct(exponent.shape, jnp.float32)
    return call(kernel, "frequencies", shape, [VMEM], 0, flops=LONG // 8)(exponent)


def norm_rows(hidden, gain, after, copies):
    rows, width = hidden.shape

    def kernel(hidden_ref, gain_ref, after_ref, out_ref):
        del after_ref
        wide = hidden_ref[...].astype(jnp.float32)
        inverse = lax.rsqrt(jnp.mean(wide * wide, -1, keepdims=True) + EPS)
        normed = (wide * inverse * gain_ref[...].astype(jnp.float32)).astype(jnp.bfloat16)
        for c in range(copies):
            out_ref[c] = normed

    return call(
        kernel,
        "norm_rows",
        jax.ShapeDtypeStruct((copies, rows, width), jnp.bfloat16),
        [VMEM, VMEM, ANY],
        hidden.size * 2 * (copies + 1),
        flops=LONG,
    )(hidden, gain[None], after)


def turns(near, frequency, lengths, slots, requests, context):
    groups, rows, depth = near.shape

    def kernel(
        lengths_ref, slots_ref, requests_ref, near_ref, frequency_ref, lined_ref, cosine_ref,
        sine_ref, mask_ref, adapter_ref,
    ):
        for j in range(groups):
            lined_ref[pl.ds(j * rows, rows)] = near_ref[j]
        row = lax.broadcasted_iota(jnp.int32, (rows, LANES), 0)
        length = jnp.zeros((rows, LANES), jnp.int32)
        adapter = jnp.zeros((rows, LANES), jnp.int32)
        for r in range(rows):
            length = jnp.where(row == r, lengths_ref[r], length)
            adapter = jnp.where(row == r, requests_ref[0, slots_ref[r]], adapter)
        angle = length.astype(jnp.float32) * frequency_ref[...]
        cosine_ref[...] = jnp.cos(angle)
        sine_ref[...] = jnp.sin(angle)
        lane = lax.broadcasted_iota(jnp.int32, (rows, LANES), 1)
        for t in range(0, context, LANES):
            mask_ref[:, pl.ds(t, LANES)] = jnp.where(lane + t < length, 0.0, -jnp.inf)
        adapter_ref[...] = adapter.astype(jnp.float32).astype(jnp.bfloat16)

    return call(
        kernel,
        "turns",
        (
            jax.ShapeDtypeStruct((groups * rows, depth), near.dtype),
            jax.ShapeDtypeStruct((rows, HEAD_DIM), jnp.float32),
            jax.ShapeDtypeStruct((rows, HEAD_DIM), jnp.float32),
            jax.ShapeDtypeStruct((rows, context), jnp.float32),
            jax.ShapeDtypeStruct((rows, LANES), jnp.bfloat16),
        ),
        [SMEM] * 3 + [VMEM] * 2,
        near.size * 4,
    )(lengths, slots, requests, near, frequency)


def project_qkv(lined, far, weight, adapter, chunk=1024):
    groups, rows, _ = far.shape
    depth, width = weight.shape
    half = groups * rows

    def kernel(lined_ref, far_ref, weight_ref, adapter_ref, out_ref, far_lined_ref):
        for j in range(groups):
            far_lined_ref[pl.ds(j * rows, rows)] = far_ref[j]
        total = jnp.zeros((2 * half, width), jnp.float32)
        for k in range(depth // chunk):
            part = pl.ds(k * chunk, chunk)
            total = total + jnp.dot(
                jnp.concatenate([lined_ref[:, part], far_lined_ref[:, part]]),
                weight_ref[part, :],
                preferred_element_type=jnp.float32,
            )
        core = lax.axis_index("batch")
        adapter = adapter_ref[...]
        for e in range(2):
            for j in range(groups):
                place = e * half + j * rows
                device = 2 * j + (core ^ e ^ 1)
                out_ref[device, :, pl.ds(0, width)] = total[place : place + rows].astype(
                    jnp.bfloat16
                )
                out_ref[device, :, pl.ds(width, LANES)] = (
                    adapter if e == 0 else jnp.zeros_like(adapter)
                )

    return call(
        kernel,
        "project_qkv",
        jax.ShapeDtypeStruct((2 * groups, rows, width + LANES), jnp.bfloat16),
        [VMEM] * 4,
        weight.size * 2,
        flops=LONG,
        scratch_shapes=[pltpu.VMEM((half, depth), jnp.bfloat16)],
    )(lined, far, weight, adapter)


def stream(weight_ref, held_ref, sems, parts):
    depth = held_ref.shape[0] // parts
    copies = []
    for k in range(parts):
        rows = pl.ds(k * depth, depth)
        copies.append(
            pltpu.make_async_copy(weight_ref.at[rows], held_ref.at[rows], sems.at[k])
        )
        copies[-1].start()

    def part(k):
        copies[k].wait()
        return held_ref[pl.ds(k * depth, depth)]

    return part


def project_out(gathered, weight, parts=16):
    groups, rows, depth = gathered.shape
    count, step = groups * rows, depth // parts

    def kernel(gathered_ref, weight_ref, out_ref, near_ref, rows_ref, held_ref, sems, near_sem):
        near = pltpu.make_async_copy(gathered_ref, near_ref, near_sem)
        near.start()
        part = stream(weight_ref, held_ref, sems, parts)
        near.wait()
        for j in range(groups):
            rows_ref[pl.ds(j * rows, rows)] = near_ref[j]
        total = jnp.zeros(out_ref.shape, jnp.float32)
        for k in range(parts):
            total = total + jnp.dot(
                rows_ref[:, pl.ds(k * step, step)], part(k), preferred_element_type=jnp.float32
            )
        out_ref[...] = total

    return call(
        kernel,
        "project_out",
        pltpu.VMEM((count, weight.shape[1]), jnp.float32),
        [ANY] * 2,
        weight.size * 2,
        limit=STREAM,
        flops=2 * count * weight.size,
        scratch_shapes=[
            pltpu.VMEM(gathered.shape, gathered.dtype),
            pltpu.VMEM((count, depth), gathered.dtype),
            pltpu.VMEM(weight.shape, weight.dtype),
            pltpu.SemaphoreType.DMA((parts,)),
            pltpu.SemaphoreType.DMA,
        ],
    )(gathered, weight)


def down_partials(gathered, adapter, down_store, up_store):
    groups, rows, _ = gathered.shape
    count = groups * rows
    rank, depth = down_store.shape[1:]
    width = up_store.shape[2]

    def kernel(adapter_ref, gathered_ref, down_ref, up_ref, out_ref, picked_ref, held_ref, rows_ref):
        start = pl.multiple_of(lax.axis_index("mp") * depth, depth)
        for j in range(groups):
            rows_ref[pl.ds(j * rows, rows)] = gathered_ref[j, :, pl.ds(start, depth)]
        for r in range(count):
            chosen = adapter_ref[r, 0]
            held_ref[pl.ds(r * rank, rank)] = down_ref[chosen]
            picked_ref[pl.ds(r * rank, rank)] = up_ref[chosen]
        every = lax.dot_general(
            rows_ref[...],
            held_ref[...],
            (((1,), (1,)), ((), ())),
            preferred_element_type=jnp.float32,
        )
        row = lax.broadcasted_iota(jnp.int32, (count, LANES), 0)
        lane = lax.broadcasted_iota(jnp.int32, (count, LANES), 1)
        total = jnp.zeros((count, LANES), jnp.float32)
        for s in range(0, count * rank, LANES):
            total = total + jnp.where(row == (lane + s) // rank, every[:, s : s + LANES], 0.0)
        for c in range(groups):
            out_ref[c] = total

    return call(
        kernel,
        "down_partials",
        (
            jax.ShapeDtypeStruct((groups, count, LANES), jnp.float32),
            pltpu.VMEM((count * rank, width), up_store.dtype),
        ),
        [SMEM] + [VMEM] * 3,
        2 * count * rank * (depth + width),
        limit=5 * MIB,
        flops=2 * count * count * rank * depth,
        scratch_shapes=[
            pltpu.VMEM((count * rank, depth), down_store.dtype),
            pltpu.VMEM((count, depth), gathered.dtype),
        ],
    )(adapter, gathered, down_store, up_store)


def add_up(base, partials, up):
    groups, count, _ = partials.shape
    depth, width = up.shape
    rank = depth // count

    def kernel(base_ref, partials_ref, up_ref, out_ref):
        total = partials_ref[0]
        for c in range(1, groups):
            total = total + partials_ref[c]
        down = total.astype(jnp.bfloat16).astype(jnp.float32)
        row = lax.broadcasted_iota(jnp.int32, (count, LANES), 0)
        lane = lax.broadcasted_iota(jnp.int32, (count, LANES), 1)
        spread = []
        for s in range(0, depth, LANES):
            spread.append(jnp.where(row == (lane + s) // rank, down, 0.0))
        spread = jnp.concatenate(spread, 1).astype(jnp.bfloat16)
        delta = jnp.dot(spread, up_ref[...], preferred_element_type=jnp.float32)
        result = (base_ref[...] + ADAPTER_SCALE * delta).astype(jnp.bfloat16)
        for j in range(groups):
            out_ref[j] = result[j * count // groups : (j + 1) * count // groups]

    return call(
        kernel,
        "add_up",
        jax.ShapeDtypeStruct((groups, count // groups, width), jnp.bfloat16),
        [VMEM] * 3,
        up.size * 2,
        limit=4 * MIB,
        flops=2 * count * up.size,
    )(base, partials, up)


def add_rows(hidden, parts):
    width = parts.shape[2]

    def kernel(hidden_ref, parts_ref, out_ref):
        for k, place in enumerate(order(parts.shape[0])):
            part = pl.ds(place * width, width)
            total = hidden_ref[:, part].astype(jnp.float32) + parts_ref[k].astype(jnp.float32)
            out_ref[:, part] = total.astype(jnp.bfloat16)

    return call(
        kernel,
        "add_rows",
        jax.ShapeDtypeStruct(hidden.shape, parts.dtype),
        [VMEM, VMEM],
        hidden.size * 6,
    )(hidden, parts)


def swap_cores(block):
    return lax.ppermute(block, "batch", [(0, 1), (1, 0)])


def order(size):
    return [(k + size // 2 + 1) % size for k in range(size)]


def exchange(blocks):
    group = order(lax.axis_size("mp"))
    return lax.all_to_all(
        blocks, "mp", split_axis=0, concat_axis=0, tiled=True, axis_index_groups=[group]
    )


def exchange_all(blocks):
    group = [2 * j + core for j in order(lax.axis_size("mp")) for core in (1, 0)]
    return lax.all_to_all(
        blocks,
        ("mp", "batch"),
        split_axis=0,
        concat_axis=0,
        tiled=True,
        axis_index_groups=[group],
    )


def attend(mixed, cosine, sine, mask, key_cache, value_cache, copies):
    rows, context = key_cache.shape[:2]
    group = HEADS // KV_HEADS
    heads = HEADS + 2 * KV_HEADS
    width = mixed.shape[2] - LANES
    per_device = width // HEAD_DIM
    devices = order(mixed.shape[0] // 2)

    def kernel(
        mixed_ref, cosine_ref, sine_ref, mask_ref, key_ref, value_ref, out_ref, adapter_ref,
        vec_ref, context_ref,
    ):
        for k, j in enumerate(devices):
            for core in range(2):
                block = mixed_ref[2 * k + 1 - core].astype(jnp.float32)
                for c in range(per_device):
                    head = (2 * j + core) * per_device + c
                    vec_ref[pl.ds(head * rows, rows)] = block[:, c * HEAD_DIM : (c + 1) * HEAD_DIM]
            both = mixed_ref[2 * k, :, pl.ds(width, LANES)].astype(jnp.float32)
            both = both + mixed_ref[2 * k + 1, :, pl.ds(width, LANES)].astype(jnp.float32)
            adapter_ref[pl.ds(k * rows, rows)] = both.astype(jnp.int32)

        def tiled(pair, count):
            return jnp.concatenate([pair] * count)

        keyed = (HEADS + KV_HEADS) * rows
        vec = vec_ref[pl.ds(0, keyed)]
        turned = pltpu.roll(vec, HEAD_DIM // 2, 1)
        lane = lax.broadcasted_iota(jnp.int32, (rows, HEAD_DIM), 1)
        signed = jnp.where(lane < HEAD_DIM // 2, -sine_ref[...], sine_ref[...])
        pairs = keyed // rows
        vec = vec * tiled(cosine_ref[...], pairs) + turned * tiled(signed, pairs)
        vec = vec.astype(jnp.bfloat16)
        query = vec[: HEADS * rows]
        fresh_key = vec[HEADS * rows :].astype(jnp.float32)
        fresh_value = vec_ref[pl.ds(keyed, KV_HEADS * rows)]
        size = group * rows
        owner = lax.broadcasted_iota(jnp.int32, (size, 1), 0) % rows

        def of_owner(products):
            result = products[0]
            for r in range(1, rows):
                result = jnp.where(owner == r, products[r], result)
            return result

        scores, own_key, own_value = [], [], []
        for g in range(KV_HEADS):
            lanes = pl.ds(g * HEAD_DIM, HEAD_DIM)
            part = query[g * size : (g + 1) * size]
            products = [
                lax.dot_general(
                    part,
                    key_ref[r, :, lanes],
                    (((1,), (1,)), ((), ())),
                    preferred_element_type=jnp.float32,
                )
                for r in range(rows)
            ]
            scores.append(of_owner(products))
            own_key.append(tiled(fresh_key[g * rows : (g + 1) * rows], group))
            own_value.append(tiled(fresh_value[g * rows : (g + 1) * rows], group))
        scale = HEAD_DIM ** (-0.5)
        scores = jnp.concatenate(scores) * scale + tiled(mask_ref[...], HEADS)
        own = jnp.sum(query.astype(jnp.float32) * jnp.concatenate(own_key), 1, keepdims=True)
        own = own * scale
        top = jnp.maximum(jnp.max(scores, 1, keepdims=True), own)
        expo = jnp.exp(scores - top)
        own_exp = jnp.exp(own - top)
        total = jnp.sum(expo, 1, keepdims=True) + own_exp
        probs = (expo / total).astype(jnp.bfloat16)
        own_prob = (own_exp / total).astype(jnp.bfloat16).astype(jnp.float32)
        for g in range(KV_HEADS):
            lanes = pl.ds(g * HEAD_DIM, HEAD_DIM)
            part = probs[g * size : (g + 1) * size]
            products = [
                jnp.dot(part, value_ref[r, :, lanes], preferred_element_type=jnp.float32)
                for r in range(rows)
            ]
            result = of_owner(products) + own_prob[g * size : (g + 1) * size] * own_value[g]
            for h in range(group):
                place = pl.ds((g * group + h) * HEAD_DIM, HEAD_DIM)
                context_ref[:, place] = result[h * rows : (h + 1) * rows]
        rounded = context_ref[...].astype(jnp.bfloat16)
        for c in range(copies):
            out_ref[c] = rounded

    return call(
        kernel,
        "attend",
        (
            jax.ShapeDtypeStruct((copies, rows, HEADS * HEAD_DIM), jnp.bfloat16),
            jax.ShapeDtypeStruct((copies * rows, LANES), jnp.int32),
        ),
        [VMEM] * 6,
        key_cache.size * 4,
        limit=4 * MIB,
        flops=LONG,
        scratch_shapes=[
            pltpu.VMEM((heads * rows, HEAD_DIM), jnp.float32),
            pltpu.VMEM((rows, HEADS * HEAD_DIM), jnp.float32),
        ],
    )(mixed, cosine, sine, mask, key_cache, value_cache)


def fast_body(
    hidden,
    attention_norm_gain,
    query_key_value_weight,
    output_weight,
    key_cache,
    value_cache,
    lengths,
    slots,
    requests,
    adapter_down_matrices,
    adapter_up_matrices,
):
    mp_size = lax.axis_size("mp")
    frequency = frequencies(exponents())
    near = exchange(norm_rows(hidden, attention_norm_gain, frequency, mp_size))
    lined, cosine, sine, mask, adapter = turns(
        near, frequency, lengths, slots, requests, key_cache.shape[1]
    )
    columns = project_qkv(lined, swap_cores(near), query_key_value_weight, adapter)
    mixed = exchange_all(columns)
    context, adapter = attend(mixed, cosine, sine, mask, key_cache, value_cache, mp_size)
    gathered = exchange(context)

    partials, up = down_partials(
        gathered, adapter, adapter_down_matrices.swapaxes(1, 2), adapter_up_matrices
    )
    partials = exchange(partials)
    projected = add_up(project_out(gathered, output_weight), partials, up)
    return add_rows(hidden, exchange(projected))


def body(*arguments):
    small = lax.axis_size("mp") <= 16 and lax.axis_size("batch") == 2
    whole_heads = arguments[2].shape[1] % HEAD_DIM == 0
    return (fast_body if small and whole_heads else general_body)(*arguments)


def solution(mesh):
    in_specs = (
        P(("groups", "mp", "batch"), None),
        P(),
        P(None, ("mp", "batch")),
        P(None, "mp"),
        P(("groups", "mp", "batch"), None, None),
        P(("groups", "mp", "batch"), None, None),
        P(("groups", "mp", "batch")),
        P(("groups", "mp", "batch")),
        P(("groups", "mp", "batch"), None),
        P(None, "mp", None),
        P(None, None, "mp"),
    )
    out_specs = P(("groups", "mp", "batch"), None)
    return jax.shard_map(body, mesh=mesh, in_specs=in_specs, out_specs=out_specs, check_vma=False)
```

```python
import math

import jax
import jax.numpy as jnp
from jax import lax
from jax.experimental import pallas as pl
from jax.experimental.pallas import tpu as pltpu
from jax.sharding import PartitionSpec as P

HEADS = 64
KV_HEADS = 8
HEAD_DIM = 128
ADAPTER_COUNT = 64


EPS = 1e-05
THETA = 500000.0
ADAPTER_SCALE = 2.0


def rotate(vec, pos):
    width = vec.shape[-1]
    half = width // 2
    freq = THETA ** (-(jnp.arange(half, dtype=jnp.float32) * 2.0) / width)
    angle = pos[..., None, None] * freq
    cosine = jnp.concatenate([jnp.cos(angle), jnp.cos(angle)], -1)
    sine = jnp.concatenate([jnp.sin(angle), jnp.sin(angle)], -1)
    turned = jnp.concatenate([-vec[..., half:], vec[..., :half]], -1)
    return vec * cosine + turned * sine


def apply_up_matrix(
    context_vector, adapter_selector, down_result, output_weight, adapter_up_matrices
):
    base_output = jnp.dot(context_vector, output_weight, preferred_element_type=jnp.float32)
    spread = (adapter_selector[:, :, None] * down_result[:, None, :]).reshape(
        adapter_selector.shape[0], -1
    )
    adapter_table = adapter_up_matrices.reshape(-1, adapter_up_matrices.shape[2])
    adapter_delta = jnp.dot(spread, adapter_table, preferred_element_type=jnp.float32)
    return (base_output + ADAPTER_SCALE * adapter_delta).astype(jnp.bfloat16)


def general_body(
    hidden,
    attention_norm_gain,
    query_key_value_weight,
    output_weight,
    key_cache,
    value_cache,
    lengths,
    slots,
    requests,
    adapter_down_matrices,
    adapter_up_matrices,
):
    widened = hidden.astype(jnp.float32)
    normed = (
        widened
        * lax.rsqrt(jnp.mean(widened * widened, -1, keepdims=True) + EPS)
        * attention_norm_gain.astype(jnp.float32)
    ).astype(jnp.bfloat16)
    rows = normed.shape[0]
    columns = jnp.dot(
        lax.all_gather(normed, ("mp", "batch"), axis=0, tiled=True),
        query_key_value_weight,
        preferred_element_type=jnp.float32,
    ).astype(jnp.bfloat16)
    mixed = lax.all_to_all(
        lax.all_to_all(columns, "mp", split_axis=0, concat_axis=1, tiled=True),
        "batch",
        split_axis=0,
        concat_axis=1,
        tiled=True,
    )
    width = query_key_value_weight.shape[1]
    qkv = (
        mixed.reshape(rows, lax.axis_size("batch"), lax.axis_size("mp"), width)
        .transpose(0, 2, 1, 3)
        .reshape(rows, -1)
    )
    query_width = HEADS * HEAD_DIM
    kv_width = KV_HEADS * HEAD_DIM
    group = HEADS // KV_HEADS
    scale = HEAD_DIM ** (-0.5)
    pos = lengths.astype(jnp.float32)
    query = rotate(
        qkv[:, :query_width].astype(jnp.float32).reshape(rows, HEADS, HEAD_DIM), pos
    ).astype(jnp.bfloat16)
    fresh_key = rotate(
        qkv[:, query_width : query_width + kv_width]
        .astype(jnp.float32)
        .reshape(rows, KV_HEADS, HEAD_DIM),
        pos,
    ).astype(jnp.bfloat16)
    fresh_value = (
        qkv[:, query_width + kv_width :].astype(jnp.float32).reshape(rows, KV_HEADS, HEAD_DIM)
    )
    grouped = query.reshape(rows, KV_HEADS, group, HEAD_DIM)
    cached = key_cache.reshape(rows, -1, KV_HEADS, HEAD_DIM)
    stored = value_cache.reshape(rows, -1, KV_HEADS, HEAD_DIM)
    scores = (
        jnp.einsum("rgqd,rtgd->rgqt", grouped, cached, preferred_element_type=jnp.float32) * scale
    )
    live = jnp.arange(cached.shape[1])[None, :] < lengths[:, None]
    scores = jnp.where(live[:, None, None, :], scores, -jnp.inf)
    own = (
        jnp.einsum("rgqd,rgd->rgq", grouped, fresh_key, preferred_element_type=jnp.float32) * scale
    )
    top = jnp.maximum(jnp.max(scores, -1), own)
    expo = jnp.exp(scores - top[..., None])
    own_exp = jnp.exp(own - top)
    total = jnp.sum(expo, -1) + own_exp
    probs = (expo / total[..., None]).astype(jnp.bfloat16)
    own_prob = (own_exp / total).astype(jnp.bfloat16)
    context_vector = jnp.einsum(
        "rgqt,rtgd->rgqd", probs, stored, preferred_element_type=jnp.float32
    )
    context_vector = (
        context_vector + own_prob.astype(jnp.float32)[..., None] * fresh_value[:, :, None, :]
    )
    context_vector = context_vector.reshape(rows, query_width).astype(jnp.bfloat16)
    slot_hits = slots[:, None] == jnp.arange(requests.shape[1])[None, :]
    adapter = jnp.sum(jnp.where(slot_hits, requests[0][None, :], 0), 1)
    adapter_selector = (adapter[:, None] == jnp.arange(ADAPTER_COUNT)[None, :]).astype(jnp.bfloat16)
    context_gathered, selector_gathered = (
        lax.all_gather(context_vector, "mp", axis=0, tiled=True),
        lax.all_gather(adapter_selector, "mp", axis=0, tiled=True),
    )
    shared_portion = adapter_down_matrices.shape[1]
    context_slice = lax.dynamic_slice_in_dim(
        context_gathered, lax.axis_index("mp") * shared_portion, shared_portion, 1
    )
    every_adapter = jnp.einsum(
        "gh,thy->gty", context_slice, adapter_down_matrices, preferred_element_type=jnp.float32
    )
    partial_down = jnp.sum(every_adapter * selector_gathered.astype(jnp.float32)[:, :, None], 1)
    down_gathered = lax.psum(partial_down, "mp").astype(jnp.bfloat16)
    projection_result = apply_up_matrix(
        context_gathered, selector_gathered, down_gathered, output_weight, adapter_up_matrices
    )
    returned = lax.all_to_all(projection_result, "mp", split_axis=0, concat_axis=1, tiled=True)
    return (widened + returned.astype(jnp.float32)).astype(jnp.bfloat16)


MIB = 1 << 20
LANES = 128
LONG = 10**10
VMEM = pl.BlockSpec(memory_space=pltpu.VMEM)
SMEM = pl.BlockSpec(memory_space=pltpu.SMEM)
ANY = pl.BlockSpec(memory_space=pl.ANY)


def call(kernel, name, out_shape, in_specs, moved, limit=2 * MIB, flops=0, **options):
    return pl.pallas_call(
        kernel,
        out_shape=out_shape,
        in_specs=in_specs,
        out_specs=jax.tree.map(lambda _: VMEM, out_shape),
        compiler_params=pltpu.CompilerParams(vmem_limit_bytes=limit),
        cost_estimate=pl.CostEstimate(flops=flops, bytes_accessed=moved, transcendentals=0),
        name=name,
        **options,
    )


def exponents():
    def kernel(out_ref):
        lane = lax.broadcasted_iota(jnp.int32, (1, HEAD_DIM), 1)
        out_ref[...] = (lane % (HEAD_DIM // 2)).astype(jnp.float32) * (-2.0 / HEAD_DIM)

    shape = jax.ShapeDtypeStruct((1, HEAD_DIM), jnp.float32)
    return call(kernel, "exponents", shape, [], 0, flops=LONG // 8)()


def frequencies(exponent):
    def kernel(exponent_ref, out_ref):
        out_ref[...] = jnp.exp(exponent_ref[...] * math.log(THETA))

    shape = jax.ShapeDtypeStruct(exponent.shape, jnp.float32)
    return call(kernel, "frequencies", shape, [VMEM], 0, flops=LONG // 8)(exponent)


def norm_rows(hidden, gain, after, copies):
    rows, width = hidden.shape

    def kernel(hidden_ref, gain_ref, after_ref, out_ref):
        del after_ref
        wide = hidden_ref[...].astype(jnp.float32)
        inverse = lax.rsqrt(jnp.mean(wide * wide, -1, keepdims=True) + EPS)
        normed = (wide * inverse * gain_ref[...].astype(jnp.float32)).astype(jnp.bfloat16)
        for c in range(copies):
            out_ref[c] = normed

    return call(
        kernel,
        "norm_rows",
        jax.ShapeDtypeStruct((copies, rows, width), jnp.bfloat16),
        [VMEM, VMEM, ANY],
        hidden.size * 2 * (copies + 1),
        flops=LONG,
    )(hidden, gain[None], after)


def turns(near, frequency, lengths, slots, requests, context):
    groups, rows, depth = near.shape

    def kernel(
        lengths_ref, slots_ref, requests_ref, near_ref, frequency_ref, lined_ref, cosine_ref,
        sine_ref, mask_ref, adapter_ref,
    ):
        for j in range(groups):
            lined_ref[pl.ds(j * rows, rows)] = near_ref[j]
        row = lax.broadcasted_iota(jnp.int32, (rows, LANES), 0)
        length = jnp.zeros((rows, LANES), jnp.int32)
        adapter = jnp.zeros((rows, LANES), jnp.int32)
        for r in range(rows):
            length = jnp.where(row == r, lengths_ref[r], length)
            adapter = jnp.where(row == r, requests_ref[0, slots_ref[r]], adapter)
        angle = length.astype(jnp.float32) * frequency_ref[...]
        cosine_ref[...] = jnp.cos(angle)
        sine_ref[...] = jnp.sin(angle)
        lane = lax.broadcasted_iota(jnp.int32, (rows, LANES), 1)
        for t in range(0, context, LANES):
            mask_ref[:, pl.ds(t, LANES)] = jnp.where(lane + t < length, 0.0, -jnp.inf)
        adapter_ref[...] = adapter.astype(jnp.float32).astype(jnp.bfloat16)

    return call(
        kernel,
        "turns",
        (
            jax.ShapeDtypeStruct((groups * rows, depth), near.dtype),
            jax.ShapeDtypeStruct((rows, HEAD_DIM), jnp.float32),
            jax.ShapeDtypeStruct((rows, HEAD_DIM), jnp.float32),
            jax.ShapeDtypeStruct((rows, context), jnp.float32),
            jax.ShapeDtypeStruct((rows, LANES), jnp.bfloat16),
        ),
        [SMEM] * 3 + [VMEM] * 2,
        near.size * 4,
    )(lengths, slots, requests, near, frequency)


def project_qkv(lined, far, weight, adapter, chunk=1024):
    groups, rows, _ = far.shape
    depth, width = weight.shape
    half = groups * rows

    def kernel(lined_ref, far_ref, weight_ref, adapter_ref, out_ref, far_lined_ref):
        for j in range(groups):
            far_lined_ref[pl.ds(j * rows, rows)] = far_ref[j]
        total = jnp.zeros((2 * half, width), jnp.float32)
        for k in range(depth // chunk):
            part = pl.ds(k * chunk, chunk)
            total = total + jnp.dot(
                jnp.concatenate([lined_ref[:, part], far_lined_ref[:, part]]),
                weight_ref[part, :],
                preferred_element_type=jnp.float32,
            )
        core = lax.axis_index("batch")
        adapter = adapter_ref[...]
        for e in range(2):
            for j in range(groups):
                place = e * half + j * rows
                device = 2 * j + (core ^ e ^ 1)
                out_ref[device, :, pl.ds(0, width)] = total[place : place + rows].astype(
                    jnp.bfloat16
                )
                out_ref[device, :, pl.ds(width, LANES)] = (
                    adapter if e == 0 else jnp.zeros_like(adapter)
                )

    return call(
        kernel,
        "project_qkv",
        jax.ShapeDtypeStruct((2 * groups, rows, width + LANES), jnp.bfloat16),
        [VMEM] * 4,
        weight.size * 2,
        flops=LONG,
        scratch_shapes=[pltpu.VMEM((half, depth), jnp.bfloat16)],
    )(lined, far, weight, adapter)


def project_out(gathered, adapter, weight, down_store, up_store, chunk=1024):
    groups, rows, features = gathered.shape
    count = groups * rows
    rank, depth = down_store.shape[1:]
    columns = weight.shape[1]

    def kernel(
        adapter_ref, gathered_ref, weight_ref, down_ref, up_ref, partial_ref, base_ref, picked_ref,
        rows_ref, held_ref,
    ):
        for j in range(groups):
            rows_ref[pl.ds(j * rows, rows)] = gathered_ref[j]
        for r in range(count):
            chosen = adapter_ref[r, 0]
            held_ref[pl.ds(r * rank, rank)] = down_ref[chosen]
            picked_ref[pl.ds(r * rank, rank)] = up_ref[chosen]
        start = pl.multiple_of(lax.axis_index("mp") * depth, depth)
        every = lax.dot_general(
            rows_ref[:, pl.ds(start, depth)],
            held_ref[...],
            (((1,), (1,)), ((), ())),
            preferred_element_type=jnp.float32,
        )
        row = lax.broadcasted_iota(jnp.int32, (count, LANES), 0)
        lane = lax.broadcasted_iota(jnp.int32, (count, LANES), 1)
        total = jnp.zeros((count, LANES), jnp.float32)
        for s in range(0, count * rank, LANES):
            total = total + jnp.where(row == (lane + s) // rank, every[:, s : s + LANES], 0.0)
        for c in range(groups):
            partial_ref[c] = total
        total = jnp.zeros((count, columns), jnp.float32)
        for k in range(features // chunk):
            part = pl.ds(k * chunk, chunk)
            total = total + jnp.dot(
                rows_ref[:, part], weight_ref[part, :], preferred_element_type=jnp.float32
            )
        base_ref[...] = total

    return call(
        kernel,
        "project_out",
        (
            jax.ShapeDtypeStruct((groups, count, LANES), jnp.float32),
            jax.ShapeDtypeStruct((count, columns), jnp.float32),
            pltpu.VMEM((count * rank, columns), up_store.dtype),
        ),
        [SMEM] + [VMEM] * 4,
        weight.size * 2,
        limit=5 * MIB,
        flops=LONG,
        scratch_shapes=[
            pltpu.VMEM((count, features), gathered.dtype),
            pltpu.VMEM((count * rank, depth), down_store.dtype),
        ],
    )(adapter, gathered, weight, down_store, up_store)


def add_up(base, partials, up):
    groups, count, _ = partials.shape
    depth, width = up.shape
    rank = depth // count

    def kernel(base_ref, partials_ref, up_ref, out_ref):
        total = partials_ref[0]
        for c in range(1, groups):
            total = total + partials_ref[c]
        down = total.astype(jnp.bfloat16).astype(jnp.float32)
        row = lax.broadcasted_iota(jnp.int32, (count, LANES), 0)
        lane = lax.broadcasted_iota(jnp.int32, (count, LANES), 1)
        spread = []
        for s in range(0, depth, LANES):
            spread.append(jnp.where(row == (lane + s) // rank, down, 0.0))
        spread = jnp.concatenate(spread, 1).astype(jnp.bfloat16)
        delta = jnp.dot(spread, up_ref[...], preferred_element_type=jnp.float32)
        result = (base_ref[...] + ADAPTER_SCALE * delta).astype(jnp.bfloat16)
        for j in range(groups):
            out_ref[j] = result[j * count // groups : (j + 1) * count // groups]

    return call(
        kernel,
        "add_up",
        jax.ShapeDtypeStruct((groups, count // groups, width), jnp.bfloat16),
        [VMEM] * 3,
        up.size * 2,
        limit=4 * MIB,
        flops=2 * count * up.size,
    )(base, partials, up)


def add_rows(hidden, parts):
    width = parts.shape[2]

    def kernel(hidden_ref, parts_ref, out_ref):
        for k, place in enumerate(order(parts.shape[0])):
            part = pl.ds(place * width, width)
            total = hidden_ref[:, part].astype(jnp.float32) + parts_ref[k].astype(jnp.float32)
            out_ref[:, part] = total.astype(jnp.bfloat16)

    return call(
        kernel,
        "add_rows",
        jax.ShapeDtypeStruct(hidden.shape, parts.dtype),
        [VMEM, VMEM],
        hidden.size * 6,
    )(hidden, parts)


def swap_cores(block):
    return lax.ppermute(block, "batch", [(0, 1), (1, 0)])


def order(size):
    return [(k + size - 1) % size for k in range(size)]


def exchange(blocks):
    group = order(lax.axis_size("mp"))
    return lax.all_to_all(
        blocks, "mp", split_axis=0, concat_axis=0, tiled=True, axis_index_groups=[group]
    )


def exchange_all(blocks):
    group = [2 * j + core for j in order(lax.axis_size("mp")) for core in (1, 0)]
    return lax.all_to_all(
        blocks,
        ("mp", "batch"),
        split_axis=0,
        concat_axis=0,
        tiled=True,
        axis_index_groups=[group],
    )


def attend(mixed, cosine, sine, mask, key_cache, value_cache, copies):
    rows, context = key_cache.shape[:2]
    group = HEADS // KV_HEADS
    heads = HEADS + 2 * KV_HEADS
    width = mixed.shape[2] - LANES
    per_device = width // HEAD_DIM
    devices = order(mixed.shape[0] // 2)

    def kernel(
        mixed_ref, cosine_ref, sine_ref, mask_ref, key_ref, value_ref, out_ref, adapter_ref,
        vec_ref, context_ref,
    ):
        for k, j in enumerate(devices):
            for core in range(2):
                block = mixed_ref[2 * k + 1 - core].astype(jnp.float32)
                for c in range(per_device):
                    head = (2 * j + core) * per_device + c
                    vec_ref[pl.ds(head * rows, rows)] = block[:, c * HEAD_DIM : (c + 1) * HEAD_DIM]
            both = mixed_ref[2 * k, :, pl.ds(width, LANES)].astype(jnp.float32)
            both = both + mixed_ref[2 * k + 1, :, pl.ds(width, LANES)].astype(jnp.float32)
            adapter_ref[pl.ds(k * rows, rows)] = both.astype(jnp.int32)

        def tiled(pair, count):
            return jnp.concatenate([pair] * count)

        keyed = (HEADS + KV_HEADS) * rows
        vec = vec_ref[pl.ds(0, keyed)]
        turned = pltpu.roll(vec, HEAD_DIM // 2, 1)
        lane = lax.broadcasted_iota(jnp.int32, (rows, HEAD_DIM), 1)
        signed = jnp.where(lane < HEAD_DIM // 2, -sine_ref[...], sine_ref[...])
        pairs = keyed // rows
        vec = vec * tiled(cosine_ref[...], pairs) + turned * tiled(signed, pairs)
        vec = vec.astype(jnp.bfloat16)
        query = vec[: HEADS * rows]
        fresh_key = vec[HEADS * rows :].astype(jnp.float32)
        fresh_value = vec_ref[pl.ds(keyed, KV_HEADS * rows)]
        size = group * rows
        owner = lax.broadcasted_iota(jnp.int32, (size, 1), 0) % rows

        def of_owner(products):
            result = products[0]
            for r in range(1, rows):
                result = jnp.where(owner == r, products[r], result)
            return result

        scores, own_key, own_value = [], [], []
        for g in range(KV_HEADS):
            lanes = pl.ds(g * HEAD_DIM, HEAD_DIM)
            part = query[g * size : (g + 1) * size]
            products = [
                lax.dot_general(
                    part,
                    key_ref[r, :, lanes],
                    (((1,), (1,)), ((), ())),
                    preferred_element_type=jnp.float32,
                )
                for r in range(rows)
            ]
            scores.append(of_owner(products))
            own_key.append(tiled(fresh_key[g * rows : (g + 1) * rows], group))
            own_value.append(tiled(fresh_value[g * rows : (g + 1) * rows], group))
        scale = HEAD_DIM ** (-0.5)
        scores = jnp.concatenate(scores) * scale + tiled(mask_ref[...], HEADS)
        own = jnp.sum(query.astype(jnp.float32) * jnp.concatenate(own_key), 1, keepdims=True)
        own = own * scale
        top = jnp.maximum(jnp.max(scores, 1, keepdims=True), own)
        expo = jnp.exp(scores - top)
        own_exp = jnp.exp(own - top)
        total = jnp.sum(expo, 1, keepdims=True) + own_exp
        probs = (expo / total).astype(jnp.bfloat16)
        own_prob = (own_exp / total).astype(jnp.bfloat16).astype(jnp.float32)
        for g in range(KV_HEADS):
            lanes = pl.ds(g * HEAD_DIM, HEAD_DIM)
            part = probs[g * size : (g + 1) * size]
            products = [
                jnp.dot(part, value_ref[r, :, lanes], preferred_element_type=jnp.float32)
                for r in range(rows)
            ]
            result = of_owner(products) + own_prob[g * size : (g + 1) * size] * own_value[g]
            for h in range(group):
                place = pl.ds((g * group + h) * HEAD_DIM, HEAD_DIM)
                context_ref[:, place] = result[h * rows : (h + 1) * rows]
        rounded = context_ref[...].astype(jnp.bfloat16)
        for c in range(copies):
            out_ref[c] = rounded

    return call(
        kernel,
        "attend",
        (
            jax.ShapeDtypeStruct((copies, rows, HEADS * HEAD_DIM), jnp.bfloat16),
            jax.ShapeDtypeStruct((copies * rows, LANES), jnp.int32),
        ),
        [VMEM] * 6,
        key_cache.size * 4,
        limit=4 * MIB,
        flops=LONG,
        scratch_shapes=[
            pltpu.VMEM((heads * rows, HEAD_DIM), jnp.float32),
            pltpu.VMEM((rows, HEADS * HEAD_DIM), jnp.float32),
        ],
    )(mixed, cosine, sine, mask, key_cache, value_cache)


def fast_body(
    hidden,
    attention_norm_gain,
    query_key_value_weight,
    output_weight,
    key_cache,
    value_cache,
    lengths,
    slots,
    requests,
    adapter_down_matrices,
    adapter_up_matrices,
):
    mp_size = lax.axis_size("mp")
    frequency = frequencies(exponents())
    near = exchange(norm_rows(hidden, attention_norm_gain, frequency, mp_size))
    lined, cosine, sine, mask, adapter = turns(
        near, frequency, lengths, slots, requests, key_cache.shape[1]
    )
    columns = project_qkv(lined, swap_cores(near), query_key_value_weight, adapter)
    mixed = exchange_all(columns)
    context, adapter = attend(mixed, cosine, sine, mask, key_cache, value_cache, mp_size)
    gathered = exchange(context)

    partials, base, up = project_out(
        gathered,
        adapter,
        output_weight,
        adapter_down_matrices.swapaxes(1, 2),
        adapter_up_matrices,
    )
    projected = add_up(base, exchange(partials), up)
    return add_rows(hidden, exchange(projected))


def body(*arguments):
    small = lax.axis_size("mp") <= 16 and lax.axis_size("batch") == 2
    whole_heads = arguments[2].shape[1] % HEAD_DIM == 0
    return (fast_body if small and whole_heads else general_body)(*arguments)


def solution(mesh):
    in_specs = (
        P(("groups", "mp", "batch"), None),
        P(),
        P(None, ("mp", "batch")),
        P(None, "mp"),
        P(("groups", "mp", "batch"), None, None),
        P(("groups", "mp", "batch"), None, None),
        P(("groups", "mp", "batch")),
        P(("groups", "mp", "batch")),
        P(("groups", "mp", "batch"), None),
        P(None, "mp", None),
        P(None, None, "mp"),
    )
    out_specs = P(("groups", "mp", "batch"), None)
    return jax.shard_map(body, mesh=mesh, in_specs=in_specs, out_specs=out_specs, check_vma=False)
```

```python
import math

import jax
import jax.numpy as jnp
from jax import lax
from jax.experimental import pallas as pl
from jax.experimental.pallas import tpu as pltpu
from jax.sharding import PartitionSpec as P

HEADS = 64
KV_HEADS = 8
HEAD_DIM = 128
ADAPTER_COUNT = 64


EPS = 1e-05
THETA = 500000.0
ADAPTER_SCALE = 2.0


def rotate(vec, pos):
    width = vec.shape[-1]
    half = width // 2
    freq = THETA ** (-(jnp.arange(half, dtype=jnp.float32) * 2.0) / width)
    angle = pos[..., None, None] * freq
    cosine = jnp.concatenate([jnp.cos(angle), jnp.cos(angle)], -1)
    sine = jnp.concatenate([jnp.sin(angle), jnp.sin(angle)], -1)
    turned = jnp.concatenate([-vec[..., half:], vec[..., :half]], -1)
    return vec * cosine + turned * sine


def apply_up_matrix(
    context_vector, adapter_selector, down_result, output_weight, adapter_up_matrices
):
    base_output = jnp.dot(context_vector, output_weight, preferred_element_type=jnp.float32)
    spread = (adapter_selector[:, :, None] * down_result[:, None, :]).reshape(
        adapter_selector.shape[0], -1
    )
    adapter_table = adapter_up_matrices.reshape(-1, adapter_up_matrices.shape[2])
    adapter_delta = jnp.dot(spread, adapter_table, preferred_element_type=jnp.float32)
    return (base_output + ADAPTER_SCALE * adapter_delta).astype(jnp.bfloat16)


def general_body(
    hidden,
    attention_norm_gain,
    query_key_value_weight,
    output_weight,
    key_cache,
    value_cache,
    lengths,
    slots,
    requests,
    adapter_down_matrices,
    adapter_up_matrices,
):
    widened = hidden.astype(jnp.float32)
    normed = (
        widened
        * lax.rsqrt(jnp.mean(widened * widened, -1, keepdims=True) + EPS)
        * attention_norm_gain.astype(jnp.float32)
    ).astype(jnp.bfloat16)
    rows = normed.shape[0]
    columns = jnp.dot(
        lax.all_gather(normed, ("mp", "batch"), axis=0, tiled=True),
        query_key_value_weight,
        preferred_element_type=jnp.float32,
    ).astype(jnp.bfloat16)
    mixed = lax.all_to_all(
        lax.all_to_all(columns, "mp", split_axis=0, concat_axis=1, tiled=True),
        "batch",
        split_axis=0,
        concat_axis=1,
        tiled=True,
    )
    width = query_key_value_weight.shape[1]
    qkv = (
        mixed.reshape(rows, lax.axis_size("batch"), lax.axis_size("mp"), width)
        .transpose(0, 2, 1, 3)
        .reshape(rows, -1)
    )
    query_width = HEADS * HEAD_DIM
    kv_width = KV_HEADS * HEAD_DIM
    group = HEADS // KV_HEADS
    scale = HEAD_DIM ** (-0.5)
    pos = lengths.astype(jnp.float32)
    query = rotate(
        qkv[:, :query_width].astype(jnp.float32).reshape(rows, HEADS, HEAD_DIM), pos
    ).astype(jnp.bfloat16)
    fresh_key = rotate(
        qkv[:, query_width : query_width + kv_width]
        .astype(jnp.float32)
        .reshape(rows, KV_HEADS, HEAD_DIM),
        pos,
    ).astype(jnp.bfloat16)
    fresh_value = (
        qkv[:, query_width + kv_width :].astype(jnp.float32).reshape(rows, KV_HEADS, HEAD_DIM)
    )
    grouped = query.reshape(rows, KV_HEADS, group, HEAD_DIM)
    cached = key_cache.reshape(rows, -1, KV_HEADS, HEAD_DIM)
    stored = value_cache.reshape(rows, -1, KV_HEADS, HEAD_DIM)
    scores = (
        jnp.einsum("rgqd,rtgd->rgqt", grouped, cached, preferred_element_type=jnp.float32) * scale
    )
    live = jnp.arange(cached.shape[1])[None, :] < lengths[:, None]
    scores = jnp.where(live[:, None, None, :], scores, -jnp.inf)
    own = (
        jnp.einsum("rgqd,rgd->rgq", grouped, fresh_key, preferred_element_type=jnp.float32) * scale
    )
    top = jnp.maximum(jnp.max(scores, -1), own)
    expo = jnp.exp(scores - top[..., None])
    own_exp = jnp.exp(own - top)
    total = jnp.sum(expo, -1) + own_exp
    probs = (expo / total[..., None]).astype(jnp.bfloat16)
    own_prob = (own_exp / total).astype(jnp.bfloat16)
    context_vector = jnp.einsum(
        "rgqt,rtgd->rgqd", probs, stored, preferred_element_type=jnp.float32
    )
    context_vector = (
        context_vector + own_prob.astype(jnp.float32)[..., None] * fresh_value[:, :, None, :]
    )
    context_vector = context_vector.reshape(rows, query_width).astype(jnp.bfloat16)
    slot_hits = slots[:, None] == jnp.arange(requests.shape[1])[None, :]
    adapter = jnp.sum(jnp.where(slot_hits, requests[0][None, :], 0), 1)
    adapter_selector = (adapter[:, None] == jnp.arange(ADAPTER_COUNT)[None, :]).astype(jnp.bfloat16)
    context_gathered, selector_gathered = (
        lax.all_gather(context_vector, "mp", axis=0, tiled=True),
        lax.all_gather(adapter_selector, "mp", axis=0, tiled=True),
    )
    shared_portion = adapter_down_matrices.shape[1]
    context_slice = lax.dynamic_slice_in_dim(
        context_gathered, lax.axis_index("mp") * shared_portion, shared_portion, 1
    )
    every_adapter = jnp.einsum(
        "gh,thy->gty", context_slice, adapter_down_matrices, preferred_element_type=jnp.float32
    )
    partial_down = jnp.sum(every_adapter * selector_gathered.astype(jnp.float32)[:, :, None], 1)
    down_gathered = lax.psum(partial_down, "mp").astype(jnp.bfloat16)
    projection_result = apply_up_matrix(
        context_gathered, selector_gathered, down_gathered, output_weight, adapter_up_matrices
    )
    returned = lax.all_to_all(projection_result, "mp", split_axis=0, concat_axis=1, tiled=True)
    return (widened + returned.astype(jnp.float32)).astype(jnp.bfloat16)


MIB = 1 << 20
LANES = 128
LONG = 10**10
VMEM = pl.BlockSpec(memory_space=pltpu.VMEM)
SMEM = pl.BlockSpec(memory_space=pltpu.SMEM)
ANY = pl.BlockSpec(memory_space=pl.ANY)


def call(kernel, name, out_shape, in_specs, moved, limit=2 * MIB, flops=0, **options):
    return pl.pallas_call(
        kernel,
        out_shape=out_shape,
        in_specs=in_specs,
        out_specs=jax.tree.map(lambda _: VMEM, out_shape),
        compiler_params=pltpu.CompilerParams(vmem_limit_bytes=limit),
        cost_estimate=pl.CostEstimate(flops=flops, bytes_accessed=moved, transcendentals=0),
        name=name,
        **options,
    )


def exponents():
    def kernel(out_ref):
        lane = lax.broadcasted_iota(jnp.int32, (1, HEAD_DIM), 1)
        out_ref[...] = (lane % (HEAD_DIM // 2)).astype(jnp.float32) * (-2.0 / HEAD_DIM)

    shape = jax.ShapeDtypeStruct((1, HEAD_DIM), jnp.float32)
    return call(kernel, "exponents", shape, [], 0, flops=LONG // 8)()


def frequencies(exponent):
    def kernel(exponent_ref, out_ref):
        out_ref[...] = jnp.exp(exponent_ref[...] * math.log(THETA))

    shape = jax.ShapeDtypeStruct(exponent.shape, jnp.float32)
    return call(kernel, "frequencies", shape, [VMEM], 0, flops=LONG // 8)(exponent)


def norm_rows(hidden, gain, after, copies):
    rows, width = hidden.shape

    def kernel(hidden_ref, gain_ref, after_ref, out_ref):
        del after_ref
        wide = hidden_ref[...].astype(jnp.float32)
        inverse = lax.rsqrt(jnp.mean(wide * wide, -1, keepdims=True) + EPS)
        normed = (wide * inverse * gain_ref[...].astype(jnp.float32)).astype(jnp.bfloat16)
        for c in range(copies):
            out_ref[c] = normed

    return call(
        kernel,
        "norm_rows",
        jax.ShapeDtypeStruct((copies, rows, width), jnp.bfloat16),
        [VMEM, VMEM, ANY],
        hidden.size * 2 * (copies + 1),
        flops=LONG,
    )(hidden, gain[None], after)


def turns(near, frequency, lengths, slots, requests, context):
    groups, rows, depth = near.shape

    def kernel(
        lengths_ref, slots_ref, requests_ref, near_ref, frequency_ref, lined_ref, cosine_ref,
        sine_ref, mask_ref, adapter_ref,
    ):
        for j in range(groups):
            lined_ref[pl.ds(j * rows, rows)] = near_ref[j]
        row = lax.broadcasted_iota(jnp.int32, (rows, LANES), 0)
        length = jnp.zeros((rows, LANES), jnp.int32)
        adapter = jnp.zeros((rows, LANES), jnp.int32)
        for r in range(rows):
            length = jnp.where(row == r, lengths_ref[r], length)
            adapter = jnp.where(row == r, requests_ref[0, slots_ref[r]], adapter)
        angle = length.astype(jnp.float32) * frequency_ref[...]
        cosine_ref[...] = jnp.cos(angle)
        sine_ref[...] = jnp.sin(angle)
        lane = lax.broadcasted_iota(jnp.int32, (rows, LANES), 1)
        for t in range(0, context, LANES):
            mask_ref[:, pl.ds(t, LANES)] = jnp.where(lane + t < length, 0.0, -jnp.inf)
        adapter_ref[...] = adapter.astype(jnp.float32).astype(jnp.bfloat16)

    return call(
        kernel,
        "turns",
        (
            jax.ShapeDtypeStruct((groups * rows, depth), near.dtype),
            jax.ShapeDtypeStruct((rows, HEAD_DIM), jnp.float32),
            jax.ShapeDtypeStruct((rows, HEAD_DIM), jnp.float32),
            jax.ShapeDtypeStruct((rows, context), jnp.float32),
            jax.ShapeDtypeStruct((rows, LANES), jnp.bfloat16),
        ),
        [SMEM] * 3 + [VMEM] * 2,
        near.size * 4,
    )(lengths, slots, requests, near, frequency)


def project_qkv(lined, far, weight, adapter, chunk=1024):
    groups, rows, _ = far.shape
    depth, width = weight.shape
    half = groups * rows

    def kernel(lined_ref, far_ref, weight_ref, adapter_ref, out_ref, far_lined_ref):
        for j in range(groups):
            far_lined_ref[pl.ds(j * rows, rows)] = far_ref[j]
        total = jnp.zeros((2 * half, width), jnp.float32)
        for k in range(depth // chunk):
            part = pl.ds(k * chunk, chunk)
            total = total + jnp.dot(
                jnp.concatenate([lined_ref[:, part], far_lined_ref[:, part]]),
                weight_ref[part, :],
                preferred_element_type=jnp.float32,
            )
        core = lax.axis_index("batch")
        adapter = adapter_ref[...]
        for e in range(2):
            for j in range(groups):
                place = e * half + j * rows
                device = 2 * j + (core ^ e ^ 1)
                out_ref[device, :, pl.ds(0, width)] = total[place : place + rows].astype(
                    jnp.bfloat16
                )
                out_ref[device, :, pl.ds(width, LANES)] = (
                    adapter if e == 0 else jnp.zeros_like(adapter)
                )

    return call(
        kernel,
        "project_qkv",
        jax.ShapeDtypeStruct((2 * groups, rows, width + LANES), jnp.bfloat16),
        [VMEM] * 4,
        weight.size * 2,
        flops=LONG,
        scratch_shapes=[pltpu.VMEM((half, depth), jnp.bfloat16)],
    )(lined, far, weight, adapter)


def project_out(gathered, adapter, weight, down_store, up_store, chunk=1024):
    groups, rows, features = gathered.shape
    count = groups * rows
    rank, depth = down_store.shape[1:]
    columns = weight.shape[1]

    def kernel(
        adapter_ref, gathered_ref, weight_ref, down_ref, up_ref, partial_ref, base_ref, picked_ref,
        rows_ref, held_ref,
    ):
        for j in range(groups):
            rows_ref[pl.ds(j * rows, rows)] = gathered_ref[j]
        for r in range(count):
            chosen = adapter_ref[r, 0]
            held_ref[pl.ds(r * rank, rank)] = down_ref[chosen]
            picked_ref[pl.ds(r * rank, rank)] = up_ref[chosen]
        start = pl.multiple_of(lax.axis_index("mp") * depth, depth)
        every = lax.dot_general(
            rows_ref[:, pl.ds(start, depth)],
            held_ref[...],
            (((1,), (1,)), ((), ())),
            preferred_element_type=jnp.float32,
        )
        row = lax.broadcasted_iota(jnp.int32, (count, LANES), 0)
        lane = lax.broadcasted_iota(jnp.int32, (count, LANES), 1)
        total = jnp.zeros((count, LANES), jnp.float32)
        for s in range(0, count * rank, LANES):
            total = total + jnp.where(row == (lane + s) // rank, every[:, s : s + LANES], 0.0)
        for c in range(groups):
            partial_ref[c] = total
        total = jnp.zeros((count, columns), jnp.float32)
        for k in range(features // chunk):
            part = pl.ds(k * chunk, chunk)
            total = total + jnp.dot(
                rows_ref[:, part], weight_ref[part, :], preferred_element_type=jnp.float32
            )
        base_ref[...] = total

    return call(
        kernel,
        "project_out",
        (
            jax.ShapeDtypeStruct((groups, count, LANES), jnp.float32),
            jax.ShapeDtypeStruct((count, columns), jnp.float32),
            pltpu.VMEM((count * rank, columns), up_store.dtype),
        ),
        [SMEM] + [VMEM] * 4,
        weight.size * 2,
        limit=5 * MIB,
        flops=LONG,
        scratch_shapes=[
            pltpu.VMEM((count, features), gathered.dtype),
            pltpu.VMEM((count * rank, depth), down_store.dtype),
        ],
    )(adapter, gathered, weight, down_store, up_store)


def add_up(base, partials, up):
    groups, count, _ = partials.shape
    depth, width = up.shape
    rank = depth // count

    def kernel(base_ref, partials_ref, up_ref, out_ref):
        total = partials_ref[0]
        for c in range(1, groups):
            total = total + partials_ref[c]
        down = total.astype(jnp.bfloat16).astype(jnp.float32)
        row = lax.broadcasted_iota(jnp.int32, (count, LANES), 0)
        lane = lax.broadcasted_iota(jnp.int32, (count, LANES), 1)
        spread = []
        for s in range(0, depth, LANES):
            spread.append(jnp.where(row == (lane + s) // rank, down, 0.0))
        spread = jnp.concatenate(spread, 1).astype(jnp.bfloat16)
        delta = jnp.dot(spread, up_ref[...], preferred_element_type=jnp.float32)
        result = (base_ref[...] + ADAPTER_SCALE * delta).astype(jnp.bfloat16)
        for j in range(groups):
            out_ref[j] = result[j * count // groups : (j + 1) * count // groups]

    return call(
        kernel,
        "add_up",
        jax.ShapeDtypeStruct((groups, count // groups, width), jnp.bfloat16),
        [VMEM] * 3,
        up.size * 2,
        limit=4 * MIB,
        flops=2 * count * up.size,
    )(base, partials, up)


def add_rows(hidden, parts):
    width = parts.shape[2]

    def kernel(hidden_ref, parts_ref, out_ref):
        for k, place in enumerate(order(parts.shape[0])):
            part = pl.ds(place * width, width)
            total = hidden_ref[:, part].astype(jnp.float32) + parts_ref[k].astype(jnp.float32)
            out_ref[:, part] = total.astype(jnp.bfloat16)

    return call(
        kernel,
        "add_rows",
        jax.ShapeDtypeStruct(hidden.shape, parts.dtype),
        [VMEM, VMEM],
        hidden.size * 6,
    )(hidden, parts)


def swap_cores(block):
    return lax.ppermute(block, "batch", [(0, 1), (1, 0)])


def order(size):
    return [(k + size // 2 + 1) % size for k in range(size)]


def exchange(blocks):
    group = order(lax.axis_size("mp"))
    return lax.all_to_all(
        blocks, "mp", split_axis=0, concat_axis=0, tiled=True, axis_index_groups=[group]
    )


def exchange_all(blocks):
    group = [2 * j + core for j in order(lax.axis_size("mp")) for core in (1, 0)]
    return lax.all_to_all(
        blocks,
        ("mp", "batch"),
        split_axis=0,
        concat_axis=0,
        tiled=True,
        axis_index_groups=[group],
    )


def attend(mixed, cosine, sine, mask, key_cache, value_cache, copies):
    rows, context = key_cache.shape[:2]
    group = HEADS // KV_HEADS
    heads = HEADS + 2 * KV_HEADS
    width = mixed.shape[2] - LANES
    per_device = width // HEAD_DIM
    devices = order(mixed.shape[0] // 2)

    def kernel(
        mixed_ref, cosine_ref, sine_ref, mask_ref, key_ref, value_ref, out_ref, adapter_ref,
        vec_ref, context_ref,
    ):
        for k, j in enumerate(devices):
            for core in range(2):
                block = mixed_ref[2 * k + 1 - core].astype(jnp.float32)
                for c in range(per_device):
                    head = (2 * j + core) * per_device + c
                    vec_ref[pl.ds(head * rows, rows)] = block[:, c * HEAD_DIM : (c + 1) * HEAD_DIM]
            both = mixed_ref[2 * k, :, pl.ds(width, LANES)].astype(jnp.float32)
            both = both + mixed_ref[2 * k + 1, :, pl.ds(width, LANES)].astype(jnp.float32)
            adapter_ref[pl.ds(k * rows, rows)] = both.astype(jnp.int32)

        def tiled(pair, count):
            return jnp.concatenate([pair] * count)

        keyed = (HEADS + KV_HEADS) * rows
        vec = vec_ref[pl.ds(0, keyed)]
        turned = pltpu.roll(vec, HEAD_DIM // 2, 1)
        lane = lax.broadcasted_iota(jnp.int32, (rows, HEAD_DIM), 1)
        signed = jnp.where(lane < HEAD_DIM // 2, -sine_ref[...], sine_ref[...])
        pairs = keyed // rows
        vec = vec * tiled(cosine_ref[...], pairs) + turned * tiled(signed, pairs)
        vec = vec.astype(jnp.bfloat16)
        query = vec[: HEADS * rows]
        fresh_key = vec[HEADS * rows :].astype(jnp.float32)
        fresh_value = vec_ref[pl.ds(keyed, KV_HEADS * rows)]
        size = group * rows
        owner = lax.broadcasted_iota(jnp.int32, (size, 1), 0) % rows

        def of_owner(products):
            result = products[0]
            for r in range(1, rows):
                result = jnp.where(owner == r, products[r], result)
            return result

        scores, own_key, own_value = [], [], []
        for g in range(KV_HEADS):
            lanes = pl.ds(g * HEAD_DIM, HEAD_DIM)
            part = query[g * size : (g + 1) * size]
            products = [
                lax.dot_general(
                    part,
                    key_ref[r, :, lanes],
                    (((1,), (1,)), ((), ())),
                    preferred_element_type=jnp.float32,
                )
                for r in range(rows)
            ]
            scores.append(of_owner(products))
            own_key.append(tiled(fresh_key[g * rows : (g + 1) * rows], group))
            own_value.append(tiled(fresh_value[g * rows : (g + 1) * rows], group))
        scale = HEAD_DIM ** (-0.5)
        scores = jnp.concatenate(scores) * scale + tiled(mask_ref[...], HEADS)
        own = jnp.sum(query.astype(jnp.float32) * jnp.concatenate(own_key), 1, keepdims=True)
        own = own * scale
        top = jnp.maximum(jnp.max(scores, 1, keepdims=True), own)
        expo = jnp.exp(scores - top)
        own_exp = jnp.exp(own - top)
        total = jnp.sum(expo, 1, keepdims=True) + own_exp
        probs = (expo / total).astype(jnp.bfloat16)
        own_prob = (own_exp / total).astype(jnp.bfloat16).astype(jnp.float32)
        for g in range(KV_HEADS):
            lanes = pl.ds(g * HEAD_DIM, HEAD_DIM)
            part = probs[g * size : (g + 1) * size]
            products = [
                jnp.dot(part, value_ref[r, :, lanes], preferred_element_type=jnp.float32)
                for r in range(rows)
            ]
            result = of_owner(products) + own_prob[g * size : (g + 1) * size] * own_value[g]
            for h in range(group):
                place = pl.ds((g * group + h) * HEAD_DIM, HEAD_DIM)
                context_ref[:, place] = result[h * rows : (h + 1) * rows]
        rounded = context_ref[...].astype(jnp.bfloat16)
        for c in range(copies):
            out_ref[c] = rounded

    return call(
        kernel,
        "attend",
        (
            jax.ShapeDtypeStruct((copies, rows, HEADS * HEAD_DIM), jnp.bfloat16),
            jax.ShapeDtypeStruct((copies * rows, LANES), jnp.int32),
        ),
        [VMEM] * 6,
        key_cache.size * 4,
        limit=4 * MIB,
        flops=LONG,
        scratch_shapes=[
            pltpu.VMEM((heads * rows, HEAD_DIM), jnp.float32),
            pltpu.VMEM((rows, HEADS * HEAD_DIM), jnp.float32),
        ],
    )(mixed, cosine, sine, mask, key_cache, value_cache)


def fast_body(
    hidden,
    attention_norm_gain,
    query_key_value_weight,
    output_weight,
    key_cache,
    value_cache,
    lengths,
    slots,
    requests,
    adapter_down_matrices,
    adapter_up_matrices,
):
    mp_size = lax.axis_size("mp")
    frequency = frequencies(exponents())
    near = exchange(norm_rows(hidden, attention_norm_gain, frequency, mp_size))
    lined, cosine, sine, mask, adapter = turns(
        near, frequency, lengths, slots, requests, key_cache.shape[1]
    )
    columns = project_qkv(lined, swap_cores(near), query_key_value_weight, adapter)
    mixed = exchange_all(columns)
    context, adapter = attend(mixed, cosine, sine, mask, key_cache, value_cache, mp_size)
    gathered = exchange(context)

    partials, base, up = project_out(
        gathered,
        adapter,
        output_weight,
        adapter_down_matrices.swapaxes(1, 2),
        adapter_up_matrices,
    )
    projected = add_up(base, exchange(partials), up)
    return add_rows(hidden, exchange(projected))


def body(*arguments):
    small = lax.axis_size("mp") <= 16 and lax.axis_size("batch") == 2
    whole_heads = arguments[2].shape[1] % HEAD_DIM == 0
    return (fast_body if small and whole_heads else general_body)(*arguments)


def solution(mesh):
    in_specs = (
        P(("groups", "mp", "batch"), None),
        P(),
        P(None, ("mp", "batch")),
        P(None, "mp"),
        P(("groups", "mp", "batch"), None, None),
        P(("groups", "mp", "batch"), None, None),
        P(("groups", "mp", "batch")),
        P(("groups", "mp", "batch")),
        P(("groups", "mp", "batch"), None),
        P(None, "mp", None),
        P(None, None, "mp"),
    )
    out_specs = P(("groups", "mp", "batch"), None)
    return jax.shard_map(body, mesh=mesh, in_specs=in_specs, out_specs=out_specs, check_vma=False)
```

```python
import math

import jax
import jax.numpy as jnp
from jax import lax
from jax.experimental import pallas as pl
from jax.experimental.pallas import tpu as pltpu
from jax.sharding import PartitionSpec as P

HEADS = 64
KV_HEADS = 8
HEAD_DIM = 128
ADAPTER_COUNT = 64


EPS = 1e-05
THETA = 500000.0
ADAPTER_SCALE = 2.0


def rotate(vec, pos):
    width = vec.shape[-1]
    half = width // 2
    freq = THETA ** (-(jnp.arange(half, dtype=jnp.float32) * 2.0) / width)
    angle = pos[..., None, None] * freq
    cosine = jnp.concatenate([jnp.cos(angle), jnp.cos(angle)], -1)
    sine = jnp.concatenate([jnp.sin(angle), jnp.sin(angle)], -1)
    turned = jnp.concatenate([-vec[..., half:], vec[..., :half]], -1)
    return vec * cosine + turned * sine


def apply_up_matrix(
    context_vector, adapter_selector, down_result, output_weight, adapter_up_matrices
):
    base_output = jnp.dot(context_vector, output_weight, preferred_element_type=jnp.float32)
    spread = (adapter_selector[:, :, None] * down_result[:, None, :]).reshape(
        adapter_selector.shape[0], -1
    )
    adapter_table = adapter_up_matrices.reshape(-1, adapter_up_matrices.shape[2])
    adapter_delta = jnp.dot(spread, adapter_table, preferred_element_type=jnp.float32)
    return (base_output + ADAPTER_SCALE * adapter_delta).astype(jnp.bfloat16)


def general_body(
    hidden,
    attention_norm_gain,
    query_key_value_weight,
    output_weight,
    key_cache,
    value_cache,
    lengths,
    slots,
    requests,
    adapter_down_matrices,
    adapter_up_matrices,
):
    widened = hidden.astype(jnp.float32)
    normed = (
        widened
        * lax.rsqrt(jnp.mean(widened * widened, -1, keepdims=True) + EPS)
        * attention_norm_gain.astype(jnp.float32)
    ).astype(jnp.bfloat16)
    rows = normed.shape[0]
    columns = jnp.dot(
        lax.all_gather(normed, ("mp", "batch"), axis=0, tiled=True),
        query_key_value_weight,
        preferred_element_type=jnp.float32,
    ).astype(jnp.bfloat16)
    mixed = lax.all_to_all(
        lax.all_to_all(columns, "mp", split_axis=0, concat_axis=1, tiled=True),
        "batch",
        split_axis=0,
        concat_axis=1,
        tiled=True,
    )
    width = query_key_value_weight.shape[1]
    qkv = (
        mixed.reshape(rows, lax.axis_size("batch"), lax.axis_size("mp"), width)
        .transpose(0, 2, 1, 3)
        .reshape(rows, -1)
    )
    query_width = HEADS * HEAD_DIM
    kv_width = KV_HEADS * HEAD_DIM
    group = HEADS // KV_HEADS
    scale = HEAD_DIM ** (-0.5)
    pos = lengths.astype(jnp.float32)
    query = rotate(
        qkv[:, :query_width].astype(jnp.float32).reshape(rows, HEADS, HEAD_DIM), pos
    ).astype(jnp.bfloat16)
    fresh_key = rotate(
        qkv[:, query_width : query_width + kv_width]
        .astype(jnp.float32)
        .reshape(rows, KV_HEADS, HEAD_DIM),
        pos,
    ).astype(jnp.bfloat16)
    fresh_value = (
        qkv[:, query_width + kv_width :].astype(jnp.float32).reshape(rows, KV_HEADS, HEAD_DIM)
    )
    grouped = query.reshape(rows, KV_HEADS, group, HEAD_DIM)
    cached = key_cache.reshape(rows, -1, KV_HEADS, HEAD_DIM)
    stored = value_cache.reshape(rows, -1, KV_HEADS, HEAD_DIM)
    scores = (
        jnp.einsum("rgqd,rtgd->rgqt", grouped, cached, preferred_element_type=jnp.float32) * scale
    )
    live = jnp.arange(cached.shape[1])[None, :] < lengths[:, None]
    scores = jnp.where(live[:, None, None, :], scores, -jnp.inf)
    own = (
        jnp.einsum("rgqd,rgd->rgq", grouped, fresh_key, preferred_element_type=jnp.float32) * scale
    )
    top = jnp.maximum(jnp.max(scores, -1), own)
    expo = jnp.exp(scores - top[..., None])
    own_exp = jnp.exp(own - top)
    total = jnp.sum(expo, -1) + own_exp
    probs = (expo / total[..., None]).astype(jnp.bfloat16)
    own_prob = (own_exp / total).astype(jnp.bfloat16)
    context_vector = jnp.einsum(
        "rgqt,rtgd->rgqd", probs, stored, preferred_element_type=jnp.float32
    )
    context_vector = (
        context_vector + own_prob.astype(jnp.float32)[..., None] * fresh_value[:, :, None, :]
    )
    context_vector = context_vector.reshape(rows, query_width).astype(jnp.bfloat16)
    slot_hits = slots[:, None] == jnp.arange(requests.shape[1])[None, :]
    adapter = jnp.sum(jnp.where(slot_hits, requests[0][None, :], 0), 1)
    adapter_selector = (adapter[:, None] == jnp.arange(ADAPTER_COUNT)[None, :]).astype(jnp.bfloat16)
    context_gathered, selector_gathered = (
        lax.all_gather(context_vector, "mp", axis=0, tiled=True),
        lax.all_gather(adapter_selector, "mp", axis=0, tiled=True),
    )
    shared_portion = adapter_down_matrices.shape[1]
    context_slice = lax.dynamic_slice_in_dim(
        context_gathered, lax.axis_index("mp") * shared_portion, shared_portion, 1
    )
    every_adapter = jnp.einsum(
        "gh,thy->gty", context_slice, adapter_down_matrices, preferred_element_type=jnp.float32
    )
    partial_down = jnp.sum(every_adapter * selector_gathered.astype(jnp.float32)[:, :, None], 1)
    down_gathered = lax.psum(partial_down, "mp").astype(jnp.bfloat16)
    projection_result = apply_up_matrix(
        context_gathered, selector_gathered, down_gathered, output_weight, adapter_up_matrices
    )
    returned = lax.all_to_all(projection_result, "mp", split_axis=0, concat_axis=1, tiled=True)
    return (widened + returned.astype(jnp.float32)).astype(jnp.bfloat16)


MIB = 1 << 20
LANES = 128
LONG = 10**10
VMEM = pl.BlockSpec(memory_space=pltpu.VMEM)
SMEM = pl.BlockSpec(memory_space=pltpu.SMEM)
ANY = pl.BlockSpec(memory_space=pl.ANY)


def call(kernel, name, out_shape, in_specs, moved, limit=2 * MIB, flops=0, **options):
    return pl.pallas_call(
        kernel,
        out_shape=out_shape,
        in_specs=in_specs,
        out_specs=jax.tree.map(lambda _: VMEM, out_shape),
        compiler_params=pltpu.CompilerParams(vmem_limit_bytes=limit),
        cost_estimate=pl.CostEstimate(flops=flops, bytes_accessed=moved, transcendentals=0),
        name=name,
        **options,
    )


def exponents():
    def kernel(out_ref):
        lane = lax.broadcasted_iota(jnp.int32, (1, HEAD_DIM), 1)
        out_ref[...] = (lane % (HEAD_DIM // 2)).astype(jnp.float32) * (-2.0 / HEAD_DIM)

    shape = jax.ShapeDtypeStruct((1, HEAD_DIM), jnp.float32)
    return call(kernel, "exponents", shape, [], 0, flops=LONG // 8)()


def frequencies(exponent):
    def kernel(exponent_ref, out_ref):
        out_ref[...] = jnp.exp(exponent_ref[...] * math.log(THETA))

    shape = jax.ShapeDtypeStruct(exponent.shape, jnp.float32)
    return call(kernel, "frequencies", shape, [VMEM], 0, flops=LONG // 8)(exponent)


def norm_rows(hidden, gain, after, copies):
    rows, width = hidden.shape

    def kernel(hidden_ref, gain_ref, after_ref, out_ref):
        del after_ref
        wide = hidden_ref[...].astype(jnp.float32)
        inverse = lax.rsqrt(jnp.mean(wide * wide, -1, keepdims=True) + EPS)
        normed = (wide * inverse * gain_ref[...].astype(jnp.float32)).astype(jnp.bfloat16)
        for c in range(copies):
            out_ref[c] = normed

    return call(
        kernel,
        "norm_rows",
        jax.ShapeDtypeStruct((copies, rows, width), jnp.bfloat16),
        [VMEM, VMEM, ANY],
        hidden.size * 2 * (copies + 1),
        flops=LONG,
    )(hidden, gain[None], after)


def turns(near, frequency, lengths, slots, requests, context):
    groups, rows, depth = near.shape

    def kernel(
        lengths_ref, slots_ref, requests_ref, near_ref, frequency_ref, lined_ref, cosine_ref,
        sine_ref, mask_ref, adapter_ref,
    ):
        for j in range(groups):
            lined_ref[pl.ds(j * rows, rows)] = near_ref[j]
        row = lax.broadcasted_iota(jnp.int32, (rows, LANES), 0)
        length = jnp.zeros((rows, LANES), jnp.int32)
        adapter = jnp.zeros((rows, LANES), jnp.int32)
        for r in range(rows):
            length = jnp.where(row == r, lengths_ref[r], length)
            adapter = jnp.where(row == r, requests_ref[0, slots_ref[r]], adapter)
        angle = length.astype(jnp.float32) * frequency_ref[...]
        cosine_ref[...] = jnp.cos(angle)
        sine_ref[...] = jnp.sin(angle)
        lane = lax.broadcasted_iota(jnp.int32, (rows, LANES), 1)
        for t in range(0, context, LANES):
            mask_ref[:, pl.ds(t, LANES)] = jnp.where(lane + t < length, 0.0, -jnp.inf)
        adapter_ref[...] = adapter.astype(jnp.float32).astype(jnp.bfloat16)

    return call(
        kernel,
        "turns",
        (
            jax.ShapeDtypeStruct((groups * rows, depth), near.dtype),
            jax.ShapeDtypeStruct((rows, HEAD_DIM), jnp.float32),
            jax.ShapeDtypeStruct((rows, HEAD_DIM), jnp.float32),
            jax.ShapeDtypeStruct((rows, context), jnp.float32),
            jax.ShapeDtypeStruct((rows, LANES), jnp.bfloat16),
        ),
        [SMEM] * 3 + [VMEM] * 2,
        near.size * 4,
    )(lengths, slots, requests, near, frequency)


def project_qkv(lined, far, weight, adapter, chunk=1024):
    groups, rows, _ = far.shape
    depth, width = weight.shape
    half = groups * rows

    def kernel(lined_ref, far_ref, weight_ref, adapter_ref, out_ref, far_lined_ref):
        for j in range(groups):
            far_lined_ref[pl.ds(j * rows, rows)] = far_ref[j]
        total = jnp.zeros((2 * half, width), jnp.float32)
        for k in range(depth // chunk):
            part = pl.ds(k * chunk, chunk)
            total = total + jnp.dot(
                jnp.concatenate([lined_ref[:, part], far_lined_ref[:, part]]),
                weight_ref[part, :],
                preferred_element_type=jnp.float32,
            )
        core = lax.axis_index("batch")
        adapter = adapter_ref[...]
        for e in range(2):
            for j in range(groups):
                place = e * half + j * rows
                device = 2 * j + (core ^ e ^ 1)
                out_ref[device, :, pl.ds(0, width)] = total[place : place + rows].astype(
                    jnp.bfloat16
                )
                out_ref[device, :, pl.ds(width, LANES)] = (
                    adapter if e == 0 else jnp.zeros_like(adapter)
                )

    return call(
        kernel,
        "project_qkv",
        jax.ShapeDtypeStruct((2 * groups, rows, width + LANES), jnp.bfloat16),
        [VMEM] * 4,
        weight.size * 2,
        flops=LONG,
        scratch_shapes=[pltpu.VMEM((half, depth), jnp.bfloat16)],
    )(lined, far, weight, adapter)


def project_out(gathered, adapter, weight, down_store, up_store, chunk=1024):
    groups, rows, features = gathered.shape
    count = groups * rows
    rank, depth = down_store.shape[1:]
    columns = weight.shape[1]

    def kernel(
        adapter_ref, gathered_ref, weight_ref, down_ref, up_ref, partial_ref, base_ref, picked_ref,
        rows_ref, held_ref,
    ):
        for j in range(groups):
            rows_ref[pl.ds(j * rows, rows)] = gathered_ref[j]
        for r in range(count):
            chosen = adapter_ref[r, 0]
            held_ref[pl.ds(r * rank, rank)] = down_ref[chosen]
            picked_ref[pl.ds(r * rank, rank)] = up_ref[chosen]
        start = pl.multiple_of(lax.axis_index("mp") * depth, depth)
        every = lax.dot_general(
            rows_ref[:, pl.ds(start, depth)],
            held_ref[...],
            (((1,), (1,)), ((), ())),
            preferred_element_type=jnp.float32,
        )
        row = lax.broadcasted_iota(jnp.int32, (count, LANES), 0)
        lane = lax.broadcasted_iota(jnp.int32, (count, LANES), 1)
        total = jnp.zeros((count, LANES), jnp.float32)
        for s in range(0, count * rank, LANES):
            total = total + jnp.where(row == (lane + s) // rank, every[:, s : s + LANES], 0.0)
        for c in range(groups):
            partial_ref[c] = total
        total = jnp.zeros((count, columns), jnp.float32)
        for k in range(features // chunk):
            part = pl.ds(k * chunk, chunk)
            total = total + jnp.dot(
                rows_ref[:, part], weight_ref[part, :], preferred_element_type=jnp.float32
            )
        base_ref[...] = total

    return call(
        kernel,
        "project_out",
        (
            jax.ShapeDtypeStruct((groups, count, LANES), jnp.float32),
            jax.ShapeDtypeStruct((count, columns), jnp.float32),
            pltpu.VMEM((count * rank, columns), up_store.dtype),
        ),
        [SMEM] + [VMEM] * 4,
        weight.size * 2,
        limit=5 * MIB,
        flops=LONG,
        scratch_shapes=[
            pltpu.VMEM((count, features), gathered.dtype),
            pltpu.VMEM((count * rank, depth), down_store.dtype),
        ],
    )(adapter, gathered, weight, down_store, up_store)


def add_up(base, partials, up):
    groups, count, _ = partials.shape
    depth, width = up.shape
    rank = depth // count

    def kernel(base_ref, partials_ref, up_ref, out_ref):
        total = partials_ref[0]
        for c in range(1, groups):
            total = total + partials_ref[c]
        down = total.astype(jnp.bfloat16).astype(jnp.float32)
        row = lax.broadcasted_iota(jnp.int32, (count, LANES), 0)
        lane = lax.broadcasted_iota(jnp.int32, (count, LANES), 1)
        spread = []
        for s in range(0, depth, LANES):
            spread.append(jnp.where(row == (lane + s) // rank, down, 0.0))
        spread = jnp.concatenate(spread, 1).astype(jnp.bfloat16)
        delta = jnp.dot(spread, up_ref[...], preferred_element_type=jnp.float32)
        result = (base_ref[...] + ADAPTER_SCALE * delta).astype(jnp.bfloat16)
        for j in range(groups):
            out_ref[j] = result[j * count // groups : (j + 1) * count // groups]

    return call(
        kernel,
        "add_up",
        jax.ShapeDtypeStruct((groups, count // groups, width), jnp.bfloat16),
        [VMEM] * 3,
        up.size * 2,
        limit=4 * MIB,
        flops=2 * count * up.size,
    )(base, partials, up)


def add_rows(hidden, parts):
    width = parts.shape[2]

    def kernel(hidden_ref, parts_ref, out_ref):
        for k, place in enumerate(order(parts.shape[0])):
            part = pl.ds(place * width, width)
            total = hidden_ref[:, part].astype(jnp.float32) + parts_ref[k].astype(jnp.float32)
            out_ref[:, part] = total.astype(jnp.bfloat16)

    return call(
        kernel,
        "add_rows",
        jax.ShapeDtypeStruct(hidden.shape, parts.dtype),
        [VMEM, VMEM],
        hidden.size * 6,
    )(hidden, parts)


def swap_cores(block):
    return lax.ppermute(block, "batch", [(0, 1), (1, 0)])


def order(size):
    half = size // 2
    return [(k + 1) % half + start for k in range(half) for start in (half, 0)]


def exchange(blocks):
    group = order(lax.axis_size("mp"))
    return lax.all_to_all(
        blocks, "mp", split_axis=0, concat_axis=0, tiled=True, axis_index_groups=[group]
    )


def exchange_all(blocks):
    group = [2 * j + core for j in order(lax.axis_size("mp")) for core in (1, 0)]
    return lax.all_to_all(
        blocks,
        ("mp", "batch"),
        split_axis=0,
        concat_axis=0,
        tiled=True,
        axis_index_groups=[group],
    )


def attend(mixed, cosine, sine, mask, key_cache, value_cache, copies):
    rows, context = key_cache.shape[:2]
    group = HEADS // KV_HEADS
    heads = HEADS + 2 * KV_HEADS
    width = mixed.shape[2] - LANES
    per_device = width // HEAD_DIM
    devices = order(mixed.shape[0] // 2)

    def kernel(
        mixed_ref, cosine_ref, sine_ref, mask_ref, key_ref, value_ref, out_ref, adapter_ref,
        vec_ref, context_ref,
    ):
        for k, j in enumerate(devices):
            for core in range(2):
                block = mixed_ref[2 * k + 1 - core].astype(jnp.float32)
                for c in range(per_device):
                    head = (2 * j + core) * per_device + c
                    vec_ref[pl.ds(head * rows, rows)] = block[:, c * HEAD_DIM : (c + 1) * HEAD_DIM]
            both = mixed_ref[2 * k, :, pl.ds(width, LANES)].astype(jnp.float32)
            both = both + mixed_ref[2 * k + 1, :, pl.ds(width, LANES)].astype(jnp.float32)
            adapter_ref[pl.ds(k * rows, rows)] = both.astype(jnp.int32)

        def tiled(pair, count):
            return jnp.concatenate([pair] * count)

        keyed = (HEADS + KV_HEADS) * rows
        vec = vec_ref[pl.ds(0, keyed)]
        turned = pltpu.roll(vec, HEAD_DIM // 2, 1)
        lane = lax.broadcasted_iota(jnp.int32, (rows, HEAD_DIM), 1)
        signed = jnp.where(lane < HEAD_DIM // 2, -sine_ref[...], sine_ref[...])
        pairs = keyed // rows
        vec = vec * tiled(cosine_ref[...], pairs) + turned * tiled(signed, pairs)
        vec = vec.astype(jnp.bfloat16)
        query = vec[: HEADS * rows]
        fresh_key = vec[HEADS * rows :].astype(jnp.float32)
        fresh_value = vec_ref[pl.ds(keyed, KV_HEADS * rows)]
        size = group * rows
        owner = lax.broadcasted_iota(jnp.int32, (size, 1), 0) % rows

        def of_owner(products):
            result = products[0]
            for r in range(1, rows):
                result = jnp.where(owner == r, products[r], result)
            return result

        scores, own_key, own_value = [], [], []
        for g in range(KV_HEADS):
            lanes = pl.ds(g * HEAD_DIM, HEAD_DIM)
            part = query[g * size : (g + 1) * size]
            products = [
                lax.dot_general(
                    part,
                    key_ref[r, :, lanes],
                    (((1,), (1,)), ((), ())),
                    preferred_element_type=jnp.float32,
                )
                for r in range(rows)
            ]
            scores.append(of_owner(products))
            own_key.append(tiled(fresh_key[g * rows : (g + 1) * rows], group))
            own_value.append(tiled(fresh_value[g * rows : (g + 1) * rows], group))
        scale = HEAD_DIM ** (-0.5)
        scores = jnp.concatenate(scores) * scale + tiled(mask_ref[...], HEADS)
        own = jnp.sum(query.astype(jnp.float32) * jnp.concatenate(own_key), 1, keepdims=True)
        own = own * scale
        top = jnp.maximum(jnp.max(scores, 1, keepdims=True), own)
        expo = jnp.exp(scores - top)
        own_exp = jnp.exp(own - top)
        total = jnp.sum(expo, 1, keepdims=True) + own_exp
        probs = (expo / total).astype(jnp.bfloat16)
        own_prob = (own_exp / total).astype(jnp.bfloat16).astype(jnp.float32)
        for g in range(KV_HEADS):
            lanes = pl.ds(g * HEAD_DIM, HEAD_DIM)
            part = probs[g * size : (g + 1) * size]
            products = [
                jnp.dot(part, value_ref[r, :, lanes], preferred_element_type=jnp.float32)
                for r in range(rows)
            ]
            result = of_owner(products) + own_prob[g * size : (g + 1) * size] * own_value[g]
            for h in range(group):
                place = pl.ds((g * group + h) * HEAD_DIM, HEAD_DIM)
                context_ref[:, place] = result[h * rows : (h + 1) * rows]
        rounded = context_ref[...].astype(jnp.bfloat16)
        for c in range(copies):
            out_ref[c] = rounded

    return call(
        kernel,
        "attend",
        (
            jax.ShapeDtypeStruct((copies, rows, HEADS * HEAD_DIM), jnp.bfloat16),
            jax.ShapeDtypeStruct((copies * rows, LANES), jnp.int32),
        ),
        [VMEM] * 6,
        key_cache.size * 4,
        limit=4 * MIB,
        flops=LONG,
        scratch_shapes=[
            pltpu.VMEM((heads * rows, HEAD_DIM), jnp.float32),
            pltpu.VMEM((rows, HEADS * HEAD_DIM), jnp.float32),
        ],
    )(mixed, cosine, sine, mask, key_cache, value_cache)


def fast_body(
    hidden,
    attention_norm_gain,
    query_key_value_weight,
    output_weight,
    key_cache,
    value_cache,
    lengths,
    slots,
    requests,
    adapter_down_matrices,
    adapter_up_matrices,
):
    mp_size = lax.axis_size("mp")
    frequency = frequencies(exponents())
    near = exchange(norm_rows(hidden, attention_norm_gain, frequency, mp_size))
    lined, cosine, sine, mask, adapter = turns(
        near, frequency, lengths, slots, requests, key_cache.shape[1]
    )
    columns = project_qkv(lined, swap_cores(near), query_key_value_weight, adapter)
    mixed = exchange_all(columns)
    context, adapter = attend(mixed, cosine, sine, mask, key_cache, value_cache, mp_size)
    gathered = exchange(context)

    partials, base, up = project_out(
        gathered,
        adapter,
        output_weight,
        adapter_down_matrices.swapaxes(1, 2),
        adapter_up_matrices,
    )
    projected = add_up(base, exchange(partials), up)
    return add_rows(hidden, exchange(projected))


def body(*arguments):
    small = lax.axis_size("mp") <= 16 and lax.axis_size("batch") == 2
    whole_heads = arguments[2].shape[1] % HEAD_DIM == 0
    return (fast_body if small and whole_heads else general_body)(*arguments)


def solution(mesh):
    in_specs = (
        P(("groups", "mp", "batch"), None),
        P(),
        P(None, ("mp", "batch")),
        P(None, "mp"),
        P(("groups", "mp", "batch"), None, None),
        P(("groups", "mp", "batch"), None, None),
        P(("groups", "mp", "batch")),
        P(("groups", "mp", "batch")),
        P(("groups", "mp", "batch"), None),
        P(None, "mp", None),
        P(None, None, "mp"),
    )
    out_specs = P(("groups", "mp", "batch"), None)
    return jax.shard_map(body, mesh=mesh, in_specs=in_specs, out_specs=out_specs, check_vma=False)
```

```python
import math

import jax
import jax.numpy as jnp
from jax import lax
from jax.experimental import pallas as pl
from jax.experimental.pallas import tpu as pltpu
from jax.sharding import PartitionSpec as P

HEADS = 64
KV_HEADS = 8
HEAD_DIM = 128
ADAPTER_COUNT = 64


EPS = 1e-05
THETA = 500000.0
ADAPTER_SCALE = 2.0


def rotate(vec, pos):
    width = vec.shape[-1]
    half = width // 2
    freq = THETA ** (-(jnp.arange(half, dtype=jnp.float32) * 2.0) / width)
    angle = pos[..., None, None] * freq
    cosine = jnp.concatenate([jnp.cos(angle), jnp.cos(angle)], -1)
    sine = jnp.concatenate([jnp.sin(angle), jnp.sin(angle)], -1)
    turned = jnp.concatenate([-vec[..., half:], vec[..., :half]], -1)
    return vec * cosine + turned * sine


def apply_up_matrix(
    context_vector, adapter_selector, down_result, output_weight, adapter_up_matrices
):
    base_output = jnp.dot(context_vector, output_weight, preferred_element_type=jnp.float32)
    spread = (adapter_selector[:, :, None] * down_result[:, None, :]).reshape(
        adapter_selector.shape[0], -1
    )
    adapter_table = adapter_up_matrices.reshape(-1, adapter_up_matrices.shape[2])
    adapter_delta = jnp.dot(spread, adapter_table, preferred_element_type=jnp.float32)
    return (base_output + ADAPTER_SCALE * adapter_delta).astype(jnp.bfloat16)


def general_body(
    hidden,
    attention_norm_gain,
    query_key_value_weight,
    output_weight,
    key_cache,
    value_cache,
    lengths,
    slots,
    requests,
    adapter_down_matrices,
    adapter_up_matrices,
):
    widened = hidden.astype(jnp.float32)
    normed = (
        widened
        * lax.rsqrt(jnp.mean(widened * widened, -1, keepdims=True) + EPS)
        * attention_norm_gain.astype(jnp.float32)
    ).astype(jnp.bfloat16)
    rows = normed.shape[0]
    columns = jnp.dot(
        lax.all_gather(normed, ("mp", "batch"), axis=0, tiled=True),
        query_key_value_weight,
        preferred_element_type=jnp.float32,
    ).astype(jnp.bfloat16)
    mixed = lax.all_to_all(
        lax.all_to_all(columns, "mp", split_axis=0, concat_axis=1, tiled=True),
        "batch",
        split_axis=0,
        concat_axis=1,
        tiled=True,
    )
    width = query_key_value_weight.shape[1]
    qkv = (
        mixed.reshape(rows, lax.axis_size("batch"), lax.axis_size("mp"), width)
        .transpose(0, 2, 1, 3)
        .reshape(rows, -1)
    )
    query_width = HEADS * HEAD_DIM
    kv_width = KV_HEADS * HEAD_DIM
    group = HEADS // KV_HEADS
    scale = HEAD_DIM ** (-0.5)
    pos = lengths.astype(jnp.float32)
    query = rotate(
        qkv[:, :query_width].astype(jnp.float32).reshape(rows, HEADS, HEAD_DIM), pos
    ).astype(jnp.bfloat16)
    fresh_key = rotate(
        qkv[:, query_width : query_width + kv_width]
        .astype(jnp.float32)
        .reshape(rows, KV_HEADS, HEAD_DIM),
        pos,
    ).astype(jnp.bfloat16)
    fresh_value = (
        qkv[:, query_width + kv_width :].astype(jnp.float32).reshape(rows, KV_HEADS, HEAD_DIM)
    )
    grouped = query.reshape(rows, KV_HEADS, group, HEAD_DIM)
    cached = key_cache.reshape(rows, -1, KV_HEADS, HEAD_DIM)
    stored = value_cache.reshape(rows, -1, KV_HEADS, HEAD_DIM)
    scores = (
        jnp.einsum("rgqd,rtgd->rgqt", grouped, cached, preferred_element_type=jnp.float32) * scale
    )
    live = jnp.arange(cached.shape[1])[None, :] < lengths[:, None]
    scores = jnp.where(live[:, None, None, :], scores, -jnp.inf)
    own = (
        jnp.einsum("rgqd,rgd->rgq", grouped, fresh_key, preferred_element_type=jnp.float32) * scale
    )
    top = jnp.maximum(jnp.max(scores, -1), own)
    expo = jnp.exp(scores - top[..., None])
    own_exp = jnp.exp(own - top)
    total = jnp.sum(expo, -1) + own_exp
    probs = (expo / total[..., None]).astype(jnp.bfloat16)
    own_prob = (own_exp / total).astype(jnp.bfloat16)
    context_vector = jnp.einsum(
        "rgqt,rtgd->rgqd", probs, stored, preferred_element_type=jnp.float32
    )
    context_vector = (
        context_vector + own_prob.astype(jnp.float32)[..., None] * fresh_value[:, :, None, :]
    )
    context_vector = context_vector.reshape(rows, query_width).astype(jnp.bfloat16)
    slot_hits = slots[:, None] == jnp.arange(requests.shape[1])[None, :]
    adapter = jnp.sum(jnp.where(slot_hits, requests[0][None, :], 0), 1)
    adapter_selector = (adapter[:, None] == jnp.arange(ADAPTER_COUNT)[None, :]).astype(jnp.bfloat16)
    context_gathered, selector_gathered = (
        lax.all_gather(context_vector, "mp", axis=0, tiled=True),
        lax.all_gather(adapter_selector, "mp", axis=0, tiled=True),
    )
    shared_portion = adapter_down_matrices.shape[1]
    context_slice = lax.dynamic_slice_in_dim(
        context_gathered, lax.axis_index("mp") * shared_portion, shared_portion, 1
    )
    every_adapter = jnp.einsum(
        "gh,thy->gty", context_slice, adapter_down_matrices, preferred_element_type=jnp.float32
    )
    partial_down = jnp.sum(every_adapter * selector_gathered.astype(jnp.float32)[:, :, None], 1)
    down_gathered = lax.psum(partial_down, "mp").astype(jnp.bfloat16)
    projection_result = apply_up_matrix(
        context_gathered, selector_gathered, down_gathered, output_weight, adapter_up_matrices
    )
    returned = lax.all_to_all(projection_result, "mp", split_axis=0, concat_axis=1, tiled=True)
    return (widened + returned.astype(jnp.float32)).astype(jnp.bfloat16)


MIB = 1 << 20
LANES = 128
LONG = 10**10
VMEM = pl.BlockSpec(memory_space=pltpu.VMEM)
SMEM = pl.BlockSpec(memory_space=pltpu.SMEM)
ANY = pl.BlockSpec(memory_space=pl.ANY)


def call(kernel, name, out_shape, in_specs, moved, limit=2 * MIB, flops=0, **options):
    return pl.pallas_call(
        kernel,
        out_shape=out_shape,
        in_specs=in_specs,
        out_specs=jax.tree.map(lambda _: VMEM, out_shape),
        compiler_params=pltpu.CompilerParams(vmem_limit_bytes=limit),
        cost_estimate=pl.CostEstimate(flops=flops, bytes_accessed=moved, transcendentals=0),
        name=name,
        **options,
    )


def exponents():
    def kernel(out_ref):
        lane = lax.broadcasted_iota(jnp.int32, (1, HEAD_DIM), 1)
        out_ref[...] = (lane % (HEAD_DIM // 2)).astype(jnp.float32) * (-2.0 / HEAD_DIM)

    shape = jax.ShapeDtypeStruct((1, HEAD_DIM), jnp.float32)
    return call(kernel, "exponents", shape, [], 0, flops=LONG // 8)()


def frequencies(exponent):
    def kernel(exponent_ref, out_ref):
        out_ref[...] = jnp.exp(exponent_ref[...] * math.log(THETA))

    shape = jax.ShapeDtypeStruct(exponent.shape, jnp.float32)
    return call(kernel, "frequencies", shape, [VMEM], 0, flops=LONG // 8)(exponent)


def norm_rows(hidden, gain, after, copies):
    rows, width = hidden.shape

    def kernel(hidden_ref, gain_ref, after_ref, out_ref):
        del after_ref
        wide = hidden_ref[...].astype(jnp.float32)
        inverse = lax.rsqrt(jnp.mean(wide * wide, -1, keepdims=True) + EPS)
        normed = (wide * inverse * gain_ref[...].astype(jnp.float32)).astype(jnp.bfloat16)
        for c in range(copies):
            out_ref[c] = normed

    return call(
        kernel,
        "norm_rows",
        jax.ShapeDtypeStruct((copies, rows, width), jnp.bfloat16),
        [VMEM, VMEM, ANY],
        hidden.size * 2 * (copies + 1),
        flops=LONG,
    )(hidden, gain[None], after)


def turns(near, frequency, lengths, slots, requests, context):
    groups, rows, depth = near.shape

    def kernel(
        lengths_ref, slots_ref, requests_ref, near_ref, frequency_ref, lined_ref, cosine_ref,
        sine_ref, mask_ref, adapter_ref,
    ):
        for j in range(groups):
            lined_ref[pl.ds(j * rows, rows)] = near_ref[j]
        row = lax.broadcasted_iota(jnp.int32, (rows, LANES), 0)
        length = jnp.zeros((rows, LANES), jnp.int32)
        adapter = jnp.zeros((rows, LANES), jnp.int32)
        for r in range(rows):
            length = jnp.where(row == r, lengths_ref[r], length)
            adapter = jnp.where(row == r, requests_ref[0, slots_ref[r]], adapter)
        angle = length.astype(jnp.float32) * frequency_ref[...]
        cosine_ref[...] = jnp.cos(angle)
        sine_ref[...] = jnp.sin(angle)
        lane = lax.broadcasted_iota(jnp.int32, (rows, LANES), 1)
        for t in range(0, context, LANES):
            mask_ref[:, pl.ds(t, LANES)] = jnp.where(lane + t < length, 0.0, -jnp.inf)
        adapter_ref[...] = adapter.astype(jnp.float32).astype(jnp.bfloat16)

    return call(
        kernel,
        "turns",
        (
            jax.ShapeDtypeStruct((groups * rows, depth), near.dtype),
            jax.ShapeDtypeStruct((rows, HEAD_DIM), jnp.float32),
            jax.ShapeDtypeStruct((rows, HEAD_DIM), jnp.float32),
            jax.ShapeDtypeStruct((rows, context), jnp.float32),
            jax.ShapeDtypeStruct((rows, LANES), jnp.bfloat16),
        ),
        [SMEM] * 3 + [VMEM] * 2,
        near.size * 4,
    )(lengths, slots, requests, near, frequency)


def project_qkv(lined, far, weight, adapter, chunk=1024):
    groups, rows, _ = far.shape
    depth, width = weight.shape
    half = groups * rows

    def kernel(lined_ref, far_ref, weight_ref, adapter_ref, out_ref, far_lined_ref):
        total = jnp.zeros((2 * half, width), jnp.float32)
        for k in range(depth // chunk):
            part = pl.ds(k * chunk, chunk)
            for j in range(groups):
                far_lined_ref[pl.ds(j * rows, rows), part] = far_ref[j, :, part]
            total = total + jnp.dot(
                jnp.concatenate([lined_ref[:, part], far_lined_ref[:, part]]),
                weight_ref[part, :],
                preferred_element_type=jnp.float32,
            )
        core = lax.axis_index("batch")
        adapter = adapter_ref[...]
        for e in range(2):
            for j in range(groups):
                place = e * half + j * rows
                device = 2 * j + (core ^ e ^ 1)
                out_ref[device, :, pl.ds(0, width)] = total[place : place + rows].astype(
                    jnp.bfloat16
                )
                out_ref[device, :, pl.ds(width, LANES)] = (
                    adapter if e == 0 else jnp.zeros_like(adapter)
                )

    return call(
        kernel,
        "project_qkv",
        jax.ShapeDtypeStruct((2 * groups, rows, width + LANES), jnp.bfloat16),
        [VMEM] * 4,
        weight.size * 2,
        flops=LONG,
        scratch_shapes=[pltpu.VMEM((half, depth), jnp.bfloat16)],
    )(lined, far, weight, adapter)


def project_out(gathered, adapter, weight, down_store, up_store, chunk=1024):
    groups, rows, features = gathered.shape
    count = groups * rows
    rank, depth = down_store.shape[1:]
    columns = weight.shape[1]

    def kernel(
        adapter_ref, gathered_ref, weight_ref, down_ref, up_ref, partial_ref, base_ref, picked_ref,
        rows_ref, held_ref,
    ):
        base = jnp.zeros((count, columns), jnp.float32)
        chunks = features // chunk
        for k in range(chunks):
            part = pl.ds(k * chunk, chunk)
            for j in range(groups):
                rows_ref[pl.ds(j * rows, rows), part] = gathered_ref[j, :, part]
            base = base + jnp.dot(
                rows_ref[:, part], weight_ref[part, :], preferred_element_type=jnp.float32
            )
            for r in range(k * count // chunks, (k + 1) * count // chunks):
                chosen = adapter_ref[0, r]
                held_ref[pl.ds(r * rank, rank)] = down_ref[chosen]
                picked_ref[pl.ds(r * rank, rank)] = up_ref[chosen]
        base_ref[...] = base
        start = pl.multiple_of(lax.axis_index("mp") * depth, depth)
        every = lax.dot_general(
            rows_ref[:, pl.ds(start, depth)],
            held_ref[...],
            (((1,), (1,)), ((), ())),
            preferred_element_type=jnp.float32,
        )
        row = lax.broadcasted_iota(jnp.int32, (count, LANES), 0)
        lane = lax.broadcasted_iota(jnp.int32, (count, LANES), 1)
        total = jnp.zeros((count, LANES), jnp.float32)
        for s in range(0, count * rank, LANES):
            total = total + jnp.where(row == (lane + s) // rank, every[:, s : s + LANES], 0.0)
        for c in range(groups):
            partial_ref[c] = total

    return call(
        kernel,
        "project_out",
        (
            jax.ShapeDtypeStruct((groups, count, LANES), jnp.float32),
            jax.ShapeDtypeStruct((count, columns), jnp.float32),
            pltpu.VMEM((count * rank, columns), up_store.dtype),
        ),
        [SMEM] + [VMEM] * 4,
        weight.size * 2,
        limit=5 * MIB,
        flops=LONG,
        scratch_shapes=[
            pltpu.VMEM((count, features), gathered.dtype),
            pltpu.VMEM((count * rank, depth), down_store.dtype),
        ],
    )(adapter, gathered, weight, down_store, up_store)


def add_up(base, partials, up):
    groups, count, _ = partials.shape
    depth, width = up.shape
    rank = depth // count

    def kernel(base_ref, partials_ref, up_ref, out_ref):
        total = partials_ref[0]
        for c in range(1, groups):
            total = total + partials_ref[c]
        down = total.astype(jnp.bfloat16).astype(jnp.float32)
        row = lax.broadcasted_iota(jnp.int32, (count, LANES), 0)
        lane = lax.broadcasted_iota(jnp.int32, (count, LANES), 1)
        spread = []
        for s in range(0, depth, LANES):
            spread.append(jnp.where(row == (lane + s) // rank, down, 0.0))
        spread = jnp.concatenate(spread, 1).astype(jnp.bfloat16)
        delta = jnp.dot(spread, up_ref[...], preferred_element_type=jnp.float32)
        result = (base_ref[...] + ADAPTER_SCALE * delta).astype(jnp.bfloat16)
        for j in range(groups):
            out_ref[j] = result[j * count // groups : (j + 1) * count // groups]

    return call(
        kernel,
        "add_up",
        jax.ShapeDtypeStruct((groups, count // groups, width), jnp.bfloat16),
        [VMEM] * 3,
        up.size * 2,
        limit=4 * MIB,
        flops=2 * count * up.size,
    )(base, partials, up)


def add_rows(hidden, parts):
    width = parts.shape[2]

    def kernel(hidden_ref, parts_ref, out_ref):
        for k, place in enumerate(order(parts.shape[0])):
            part = pl.ds(place * width, width)
            total = hidden_ref[:, part].astype(jnp.float32) + parts_ref[k].astype(jnp.float32)
            out_ref[:, part] = total.astype(jnp.bfloat16)

    return call(
        kernel,
        "add_rows",
        jax.ShapeDtypeStruct(hidden.shape, parts.dtype),
        [VMEM, VMEM],
        hidden.size * 6,
    )(hidden, parts)


def swap_cores(block):
    return lax.ppermute(block, "batch", [(0, 1), (1, 0)])


def order(size):
    half = size // 2
    return [(k + 1) % half + start for k in range(half) for start in (half, 0)]


def exchange(blocks):
    group = order(lax.axis_size("mp"))
    return lax.all_to_all(
        blocks, "mp", split_axis=0, concat_axis=0, tiled=True, axis_index_groups=[group]
    )


def exchange_all(blocks):
    group = [2 * j + core for j in order(lax.axis_size("mp")) for core in (1, 0)]
    return lax.all_to_all(
        blocks,
        ("mp", "batch"),
        split_axis=0,
        concat_axis=0,
        tiled=True,
        axis_index_groups=[group],
    )


def attend(mixed, cosine, sine, mask, key_cache, value_cache, copies):
    rows, context = key_cache.shape[:2]
    group = HEADS // KV_HEADS
    heads = HEADS + 2 * KV_HEADS
    width = mixed.shape[2] - LANES
    per_device = width // HEAD_DIM
    devices = order(mixed.shape[0] // 2)

    def kernel(
        mixed_ref, cosine_ref, sine_ref, mask_ref, key_ref, value_ref, out_ref, adapter_ref,
        vec_ref, context_ref,
    ):
        place = lax.broadcasted_iota(jnp.int32, (1, LANES), 1)
        adapter = jnp.zeros((1, LANES), jnp.float32)
        for k, j in enumerate(devices):
            for core in range(2):
                block = mixed_ref[2 * k + 1 - core].astype(jnp.float32)
                for c in range(per_device):
                    head = (2 * j + core) * per_device + c
                    vec_ref[pl.ds(head * rows, rows)] = block[:, c * HEAD_DIM : (c + 1) * HEAD_DIM]
            both = mixed_ref[2 * k, :, pl.ds(width, LANES)].astype(jnp.float32)
            both = both + mixed_ref[2 * k + 1, :, pl.ds(width, LANES)].astype(jnp.float32)
            for r in range(rows):
                adapter = jnp.where(place == k * rows + r, both[r : r + 1], adapter)
        adapter_ref[...] = adapter.astype(jnp.int32)

        def tiled(pair, count):
            return jnp.concatenate([pair] * count)

        keyed = (HEADS + KV_HEADS) * rows
        vec = vec_ref[pl.ds(0, keyed)]
        turned = pltpu.roll(vec, HEAD_DIM // 2, 1)
        lane = lax.broadcasted_iota(jnp.int32, (rows, HEAD_DIM), 1)
        signed = jnp.where(lane < HEAD_DIM // 2, -sine_ref[...], sine_ref[...])
        pairs = keyed // rows
        vec = vec * tiled(cosine_ref[...], pairs) + turned * tiled(signed, pairs)
        vec = vec.astype(jnp.bfloat16)
        query = vec[: HEADS * rows]
        fresh_key = vec[HEADS * rows :].astype(jnp.float32)
        fresh_value = vec_ref[pl.ds(keyed, KV_HEADS * rows)]
        size = group * rows
        owner = lax.broadcasted_iota(jnp.int32, (size, 1), 0) % rows

        def of_owner(products):
            result = products[0]
            for r in range(1, rows):
                result = jnp.where(owner == r, products[r], result)
            return result

        scores, own_key, own_value = [], [], []
        for g in range(KV_HEADS):
            lanes = pl.ds(g * HEAD_DIM, HEAD_DIM)
            part = query[g * size : (g + 1) * size]
            products = [
                lax.dot_general(
                    part,
                    key_ref[r, :, lanes],
                    (((1,), (1,)), ((), ())),
                    preferred_element_type=jnp.float32,
                )
                for r in range(rows)
            ]
            scores.append(of_owner(products))
            own_key.append(tiled(fresh_key[g * rows : (g + 1) * rows], group))
            own_value.append(tiled(fresh_value[g * rows : (g + 1) * rows], group))
        scale = HEAD_DIM ** (-0.5)
        scores = jnp.concatenate(scores) * scale + tiled(mask_ref[...], HEADS)
        own = jnp.sum(query.astype(jnp.float32) * jnp.concatenate(own_key), 1, keepdims=True)
        own = own * scale
        top = jnp.maximum(jnp.max(scores, 1, keepdims=True), own)
        expo = jnp.exp(scores - top)
        own_exp = jnp.exp(own - top)
        total = jnp.sum(expo, 1, keepdims=True) + own_exp
        probs = (expo / total).astype(jnp.bfloat16)
        own_prob = (own_exp / total).astype(jnp.bfloat16).astype(jnp.float32)
        for g in range(KV_HEADS):
            lanes = pl.ds(g * HEAD_DIM, HEAD_DIM)
            part = probs[g * size : (g + 1) * size]
            products = [
                jnp.dot(part, value_ref[r, :, lanes], preferred_element_type=jnp.float32)
                for r in range(rows)
            ]
            result = of_owner(products) + own_prob[g * size : (g + 1) * size] * own_value[g]
            for h in range(group):
                place = pl.ds((g * group + h) * HEAD_DIM, HEAD_DIM)
                context_ref[:, place] = result[h * rows : (h + 1) * rows]
        rounded = context_ref[...].astype(jnp.bfloat16)
        for c in range(copies):
            out_ref[c] = rounded

    return call(
        kernel,
        "attend",
        (
            jax.ShapeDtypeStruct((copies, rows, HEADS * HEAD_DIM), jnp.bfloat16),
            jax.ShapeDtypeStruct((1, LANES), jnp.int32),
        ),
        [VMEM] * 6,
        key_cache.size * 4,
        limit=4 * MIB,
        flops=LONG,
        scratch_shapes=[
            pltpu.VMEM((heads * rows, HEAD_DIM), jnp.float32),
            pltpu.VMEM((rows, HEADS * HEAD_DIM), jnp.float32),
        ],
    )(mixed, cosine, sine, mask, key_cache, value_cache)


def fast_body(
    hidden,
    attention_norm_gain,
    query_key_value_weight,
    output_weight,
    key_cache,
    value_cache,
    lengths,
    slots,
    requests,
    adapter_down_matrices,
    adapter_up_matrices,
):
    mp_size = lax.axis_size("mp")
    frequency = frequencies(exponents())
    near = exchange(norm_rows(hidden, attention_norm_gain, frequency, mp_size))
    lined, cosine, sine, mask, adapter = turns(
        near, frequency, lengths, slots, requests, key_cache.shape[1]
    )
    columns = project_qkv(lined, swap_cores(near), query_key_value_weight, adapter)
    mixed = exchange_all(columns)
    context, adapter = attend(mixed, cosine, sine, mask, key_cache, value_cache, mp_size)
    gathered = exchange(context)

    partials, base, up = project_out(
        gathered,
        adapter,
        output_weight,
        adapter_down_matrices.swapaxes(1, 2),
        adapter_up_matrices,
    )
    projected = add_up(base, exchange(partials), up)
    return add_rows(hidden, exchange(projected))


def body(*arguments):
    small = lax.axis_size("mp") <= 16 and lax.axis_size("batch") == 2
    whole_heads = arguments[2].shape[1] % HEAD_DIM == 0
    return (fast_body if small and whole_heads else general_body)(*arguments)


def solution(mesh):
    in_specs = (
        P(("groups", "mp", "batch"), None),
        P(),
        P(None, ("mp", "batch")),
        P(None, "mp"),
        P(("groups", "mp", "batch"), None, None),
        P(("groups", "mp", "batch"), None, None),
        P(("groups", "mp", "batch")),
        P(("groups", "mp", "batch")),
        P(("groups", "mp", "batch"), None),
        P(None, "mp", None),
        P(None, None, "mp"),
    )
    out_specs = P(("groups", "mp", "batch"), None)
    return jax.shard_map(body, mesh=mesh, in_specs=in_specs, out_specs=out_specs, check_vma=False)
```

```python
import math

import jax
import jax.numpy as jnp
from jax import lax
from jax.experimental import pallas as pl
from jax.experimental.pallas import tpu as pltpu
from jax.sharding import PartitionSpec as P

HEADS = 64
KV_HEADS = 8
HEAD_DIM = 128
ADAPTER_COUNT = 64


EPS = 1e-05
THETA = 500000.0
ADAPTER_SCALE = 2.0


def rotate(vec, pos):
    width = vec.shape[-1]
    half = width // 2
    freq = THETA ** (-(jnp.arange(half, dtype=jnp.float32) * 2.0) / width)
    angle = pos[..., None, None] * freq
    cosine = jnp.concatenate([jnp.cos(angle), jnp.cos(angle)], -1)
    sine = jnp.concatenate([jnp.sin(angle), jnp.sin(angle)], -1)
    turned = jnp.concatenate([-vec[..., half:], vec[..., :half]], -1)
    return vec * cosine + turned * sine


def apply_up_matrix(
    context_vector, adapter_selector, down_result, output_weight, adapter_up_matrices
):
    base_output = jnp.dot(context_vector, output_weight, preferred_element_type=jnp.float32)
    spread = (adapter_selector[:, :, None] * down_result[:, None, :]).reshape(
        adapter_selector.shape[0], -1
    )
    adapter_table = adapter_up_matrices.reshape(-1, adapter_up_matrices.shape[2])
    adapter_delta = jnp.dot(spread, adapter_table, preferred_element_type=jnp.float32)
    return (base_output + ADAPTER_SCALE * adapter_delta).astype(jnp.bfloat16)


def general_body(
    hidden,
    attention_norm_gain,
    query_key_value_weight,
    output_weight,
    key_cache,
    value_cache,
    lengths,
    slots,
    requests,
    adapter_down_matrices,
    adapter_up_matrices,
):
    widened = hidden.astype(jnp.float32)
    normed = (
        widened
        * lax.rsqrt(jnp.mean(widened * widened, -1, keepdims=True) + EPS)
        * attention_norm_gain.astype(jnp.float32)
    ).astype(jnp.bfloat16)
    rows = normed.shape[0]
    columns = jnp.dot(
        lax.all_gather(normed, ("mp", "batch"), axis=0, tiled=True),
        query_key_value_weight,
        preferred_element_type=jnp.float32,
    ).astype(jnp.bfloat16)
    mixed = lax.all_to_all(
        lax.all_to_all(columns, "mp", split_axis=0, concat_axis=1, tiled=True),
        "batch",
        split_axis=0,
        concat_axis=1,
        tiled=True,
    )
    width = query_key_value_weight.shape[1]
    qkv = (
        mixed.reshape(rows, lax.axis_size("batch"), lax.axis_size("mp"), width)
        .transpose(0, 2, 1, 3)
        .reshape(rows, -1)
    )
    query_width = HEADS * HEAD_DIM
    kv_width = KV_HEADS * HEAD_DIM
    group = HEADS // KV_HEADS
    scale = HEAD_DIM ** (-0.5)
    pos = lengths.astype(jnp.float32)
    query = rotate(
        qkv[:, :query_width].astype(jnp.float32).reshape(rows, HEADS, HEAD_DIM), pos
    ).astype(jnp.bfloat16)
    fresh_key = rotate(
        qkv[:, query_width : query_width + kv_width]
        .astype(jnp.float32)
        .reshape(rows, KV_HEADS, HEAD_DIM),
        pos,
    ).astype(jnp.bfloat16)
    fresh_value = (
        qkv[:, query_width + kv_width :].astype(jnp.float32).reshape(rows, KV_HEADS, HEAD_DIM)
    )
    grouped = query.reshape(rows, KV_HEADS, group, HEAD_DIM)
    cached = key_cache.reshape(rows, -1, KV_HEADS, HEAD_DIM)
    stored = value_cache.reshape(rows, -1, KV_HEADS, HEAD_DIM)
    scores = (
        jnp.einsum("rgqd,rtgd->rgqt", grouped, cached, preferred_element_type=jnp.float32) * scale
    )
    live = jnp.arange(cached.shape[1])[None, :] < lengths[:, None]
    scores = jnp.where(live[:, None, None, :], scores, -jnp.inf)
    own = (
        jnp.einsum("rgqd,rgd->rgq", grouped, fresh_key, preferred_element_type=jnp.float32) * scale
    )
    top = jnp.maximum(jnp.max(scores, -1), own)
    expo = jnp.exp(scores - top[..., None])
    own_exp = jnp.exp(own - top)
    total = jnp.sum(expo, -1) + own_exp
    probs = (expo / total[..., None]).astype(jnp.bfloat16)
    own_prob = (own_exp / total).astype(jnp.bfloat16)
    context_vector = jnp.einsum(
        "rgqt,rtgd->rgqd", probs, stored, preferred_element_type=jnp.float32
    )
    context_vector = (
        context_vector + own_prob.astype(jnp.float32)[..., None] * fresh_value[:, :, None, :]
    )
    context_vector = context_vector.reshape(rows, query_width).astype(jnp.bfloat16)
    slot_hits = slots[:, None] == jnp.arange(requests.shape[1])[None, :]
    adapter = jnp.sum(jnp.where(slot_hits, requests[0][None, :], 0), 1)
    adapter_selector = (adapter[:, None] == jnp.arange(ADAPTER_COUNT)[None, :]).astype(jnp.bfloat16)
    context_gathered, selector_gathered = (
        lax.all_gather(context_vector, "mp", axis=0, tiled=True),
        lax.all_gather(adapter_selector, "mp", axis=0, tiled=True),
    )
    shared_portion = adapter_down_matrices.shape[1]
    context_slice = lax.dynamic_slice_in_dim(
        context_gathered, lax.axis_index("mp") * shared_portion, shared_portion, 1
    )
    every_adapter = jnp.einsum(
        "gh,thy->gty", context_slice, adapter_down_matrices, preferred_element_type=jnp.float32
    )
    partial_down = jnp.sum(every_adapter * selector_gathered.astype(jnp.float32)[:, :, None], 1)
    down_gathered = lax.psum(partial_down, "mp").astype(jnp.bfloat16)
    projection_result = apply_up_matrix(
        context_gathered, selector_gathered, down_gathered, output_weight, adapter_up_matrices
    )
    returned = lax.all_to_all(projection_result, "mp", split_axis=0, concat_axis=1, tiled=True)
    return (widened + returned.astype(jnp.float32)).astype(jnp.bfloat16)


MIB = 1 << 20
LANES = 128
LONG = 10**10
VMEM = pl.BlockSpec(memory_space=pltpu.VMEM)
SMEM = pl.BlockSpec(memory_space=pltpu.SMEM)
ANY = pl.BlockSpec(memory_space=pl.ANY)


def call(kernel, name, out_shape, in_specs, moved, limit=2 * MIB, flops=0, **options):
    return pl.pallas_call(
        kernel,
        out_shape=out_shape,
        in_specs=in_specs,
        out_specs=jax.tree.map(lambda _: VMEM, out_shape),
        compiler_params=pltpu.CompilerParams(vmem_limit_bytes=limit),
        cost_estimate=pl.CostEstimate(flops=flops, bytes_accessed=moved, transcendentals=0),
        name=name,
        **options,
    )


def exponents():
    def kernel(out_ref):
        lane = lax.broadcasted_iota(jnp.int32, (1, HEAD_DIM), 1)
        out_ref[...] = (lane % (HEAD_DIM // 2)).astype(jnp.float32) * (-2.0 / HEAD_DIM)

    shape = jax.ShapeDtypeStruct((1, HEAD_DIM), jnp.float32)
    return call(kernel, "exponents", shape, [], 0, flops=LONG // 8)()


def frequencies(exponent):
    def kernel(exponent_ref, out_ref):
        out_ref[...] = jnp.exp(exponent_ref[...] * math.log(THETA))

    shape = jax.ShapeDtypeStruct(exponent.shape, jnp.float32)
    return call(kernel, "frequencies", shape, [VMEM], 0, flops=LONG // 8)(exponent)


def norm_rows(hidden, gain, after, copies):
    rows, width = hidden.shape

    def kernel(hidden_ref, gain_ref, after_ref, out_ref):
        del after_ref
        wide = hidden_ref[...].astype(jnp.float32)
        inverse = lax.rsqrt(jnp.mean(wide * wide, -1, keepdims=True) + EPS)
        normed = (wide * inverse * gain_ref[...].astype(jnp.float32)).astype(jnp.bfloat16)
        for c in range(copies):
            out_ref[c] = normed

    return call(
        kernel,
        "norm_rows",
        jax.ShapeDtypeStruct((copies, rows, width), jnp.bfloat16),
        [VMEM, VMEM, ANY],
        hidden.size * 2 * (copies + 1),
        flops=LONG,
    )(hidden, gain[None], after)


def turns(near, frequency, lengths, slots, requests, context):
    groups, rows, depth = near.shape

    def kernel(
        lengths_ref, slots_ref, requests_ref, near_ref, frequency_ref, lined_ref, cosine_ref,
        sine_ref, mask_ref, adapter_ref,
    ):
        for j in range(groups):
            lined_ref[pl.ds(j * rows, rows)] = near_ref[j]
        row = lax.broadcasted_iota(jnp.int32, (rows, LANES), 0)
        length = jnp.zeros((rows, LANES), jnp.int32)
        adapter = jnp.zeros((rows, LANES), jnp.int32)
        for r in range(rows):
            length = jnp.where(row == r, lengths_ref[r], length)
            adapter = jnp.where(row == r, requests_ref[0, slots_ref[r]], adapter)
        angle = length.astype(jnp.float32) * frequency_ref[...]
        cosine_ref[...] = jnp.cos(angle)
        sine_ref[...] = jnp.sin(angle)
        lane = lax.broadcasted_iota(jnp.int32, (rows, LANES), 1)
        for t in range(0, context, LANES):
            mask_ref[:, pl.ds(t, LANES)] = jnp.where(lane + t < length, 0.0, -jnp.inf)
        adapter_ref[...] = adapter.astype(jnp.float32).astype(jnp.bfloat16)

    return call(
        kernel,
        "turns",
        (
            jax.ShapeDtypeStruct((groups * rows, depth), near.dtype),
            jax.ShapeDtypeStruct((rows, HEAD_DIM), jnp.float32),
            jax.ShapeDtypeStruct((rows, HEAD_DIM), jnp.float32),
            jax.ShapeDtypeStruct((rows, context), jnp.float32),
            jax.ShapeDtypeStruct((rows, LANES), jnp.bfloat16),
        ),
        [SMEM] * 3 + [VMEM] * 2,
        near.size * 4,
    )(lengths, slots, requests, near, frequency)


def project_qkv(lined, far, weight, adapter, chunk=1024):
    groups, rows, _ = far.shape
    depth, width = weight.shape
    half = groups * rows

    def kernel(lined_ref, far_ref, weight_ref, adapter_ref, out_ref, far_lined_ref):
        total = jnp.zeros((2 * half, width), jnp.float32)
        for k in range(depth // chunk):
            part = pl.ds(k * chunk, chunk)
            for j in range(groups):
                far_lined_ref[pl.ds(j * rows, rows), part] = far_ref[j, :, part]
            total = total + jnp.dot(
                jnp.concatenate([lined_ref[:, part], far_lined_ref[:, part]]),
                weight_ref[part, :],
                preferred_element_type=jnp.float32,
            )
        core = lax.axis_index("batch")
        adapter = adapter_ref[...]
        for e in range(2):
            for j in range(groups):
                place = e * half + j * rows
                device = 2 * j + (core ^ e ^ 1)
                out_ref[device, :, pl.ds(0, width)] = total[place : place + rows].astype(
                    jnp.bfloat16
                )
                out_ref[device, :, pl.ds(width, LANES)] = adapter

    return call(
        kernel,
        "project_qkv",
        jax.ShapeDtypeStruct((2 * groups, rows, width + LANES), jnp.bfloat16),
        [VMEM] * 4,
        weight.size * 2,
        flops=LONG,
        scratch_shapes=[pltpu.VMEM((half, depth), jnp.bfloat16)],
    )(lined, far, weight, adapter)


def project_out(gathered, adapter, weight, down_store, up_store):
    blocks, rows, features = gathered.shape
    groups, count = blocks // 2, blocks * rows // 2
    rank, depth = down_store.shape[1:]
    columns, half = weight.shape[1], depth // 2

    def kernel(
        adapter_ref, gathered_ref, weight_ref, down_ref, up_ref, partial_ref, mine_ref, theirs_ref,
        picked_ref, rows_ref, held_ref,
    ):
        core = lax.axis_index("batch")
        start = pl.multiple_of(core * half, half)
        base = jnp.zeros((2 * count, columns), jnp.float32)
        for k in range(groups):
            part = pl.ds(k * half, half)
            for p in range(blocks):
                place = pl.ds((p % 2 * groups + p // 2) * rows, rows)
                rows_ref[place, part] = gathered_ref[p, :, part]
            base = base + jnp.dot(
                rows_ref[:, part],
                weight_ref[pl.ds(pl.multiple_of(start + k * depth, half), half), :],
                preferred_element_type=jnp.float32,
            )
            for r in range(k * 2 * count // groups, (k + 1) * 2 * count // groups):
                chosen = adapter_ref[0, r]
                held_ref[pl.ds(r * rank, rank)] = down_ref[chosen, :, pl.ds(start, half)]
            for r in range(k * count // groups, (k + 1) * count // groups):
                chosen = adapter_ref[0, (1 - core) * count + r]
                picked_ref[pl.ds(r * rank, rank)] = up_ref[chosen]
        first, second = base[count:], base[:count]
        mine_ref[...] = jnp.where(core == 0, first, second)
        theirs_ref[...] = jnp.where(core == 0, second, first)
        every = lax.dot_general(
            rows_ref[:, pl.ds(pl.multiple_of(lax.axis_index("mp") * half, half), half)],
            held_ref[...],
            (((1,), (1,)), ((), ())),
            preferred_element_type=jnp.float32,
        )
        row = lax.broadcasted_iota(jnp.int32, (2 * count, LANES), 0)
        lane = lax.broadcasted_iota(jnp.int32, (2 * count, LANES), 1)
        total = jnp.zeros((2 * count, LANES), jnp.float32)
        for s in range(0, 2 * count * rank, LANES):
            total = total + jnp.where(row == (lane + s) // rank, every[:, s : s + LANES], 0.0)
        for p in range(blocks):
            partial_ref[p] = total[p % 2 * count : (p % 2 + 1) * count]

    sums = jax.ShapeDtypeStruct((count, columns), jnp.float32)
    return call(
        kernel,
        "project_out",
        (
            jax.ShapeDtypeStruct((blocks, count, LANES), jnp.float32),
            sums,
            sums,
            pltpu.VMEM((count * rank, columns), up_store.dtype),
        ),
        [SMEM] + [VMEM] * 4,
        weight.size * 2,
        limit=6 * MIB,
        flops=LONG,
        scratch_shapes=[
            pltpu.VMEM((2 * count, features), gathered.dtype),
            pltpu.VMEM((2 * count * rank, half), down_store.dtype),
        ],
    )(adapter, gathered, weight, down_store, up_store)


def add_up(mine, other, partials, up):
    blocks, count, _ = partials.shape
    groups = blocks // 2
    depth, width = up.shape
    rank = depth // count

    def kernel(mine_ref, other_ref, partials_ref, up_ref, out_ref):
        total = partials_ref[0]
        for p in range(1, blocks):
            total = total + partials_ref[p]
        down = total.astype(jnp.bfloat16).astype(jnp.float32)
        row = lax.broadcasted_iota(jnp.int32, (count, LANES), 0)
        lane = lax.broadcasted_iota(jnp.int32, (count, LANES), 1)
        spread = []
        for s in range(0, depth, LANES):
            spread.append(jnp.where(row == (lane + s) // rank, down, 0.0))
        spread = jnp.concatenate(spread, 1).astype(jnp.bfloat16)
        delta = jnp.dot(spread, up_ref[...], preferred_element_type=jnp.float32)
        base = mine_ref[...] + other_ref[...]
        result = (base + ADAPTER_SCALE * delta).astype(jnp.bfloat16)
        for j in range(groups):
            out_ref[j] = result[j * count // groups : (j + 1) * count // groups]

    return call(
        kernel,
        "add_up",
        jax.ShapeDtypeStruct((groups, count // groups, width), jnp.bfloat16),
        [VMEM] * 4,
        up.size * 2,
        limit=4 * MIB,
        flops=2 * count * up.size,
    )(mine, other, partials, up)


def add_rows(hidden, parts):
    width = parts.shape[2]

    def kernel(hidden_ref, parts_ref, out_ref):
        for k, place in enumerate(order(parts.shape[0])):
            part = pl.ds(place * width, width)
            total = hidden_ref[:, part].astype(jnp.float32) + parts_ref[k].astype(jnp.float32)
            out_ref[:, part] = total.astype(jnp.bfloat16)

    return call(
        kernel,
        "add_rows",
        jax.ShapeDtypeStruct(hidden.shape, parts.dtype),
        [VMEM, VMEM],
        hidden.size * 6,
    )(hidden, parts)


def swap_cores(block):
    return lax.ppermute(block, "batch", [(0, 1), (1, 0)])


def order(size):
    half = size // 2
    return [(k + 1) % half + start for k in range(half) for start in (half, 0)]


def exchange(blocks):
    group = order(lax.axis_size("mp"))
    return lax.all_to_all(
        blocks, "mp", split_axis=0, concat_axis=0, tiled=True, axis_index_groups=[group]
    )


def exchange_all(blocks):
    group = [2 * j + core for j in order(lax.axis_size("mp")) for core in (1, 0)]
    return lax.all_to_all(
        blocks,
        ("mp", "batch"),
        split_axis=0,
        concat_axis=0,
        tiled=True,
        axis_index_groups=[group],
    )


def attend(mixed, cosine, sine, mask, key_cache, value_cache, copies):
    rows, context = key_cache.shape[:2]
    group = HEADS // KV_HEADS
    heads = HEADS + 2 * KV_HEADS
    width = mixed.shape[2] - LANES
    per_device = width // HEAD_DIM
    devices = order(mixed.shape[0] // 2)
    part_width = HEADS * HEAD_DIM // (2 * copies)

    def kernel(
        mixed_ref, cosine_ref, sine_ref, mask_ref, key_ref, value_ref, out_ref, adapter_ref,
        vec_ref, context_ref,
    ):
        place = lax.broadcasted_iota(jnp.int32, (1, LANES), 1)
        adapter = jnp.zeros((1, LANES), jnp.float32)
        for k, j in enumerate(devices):
            for core in range(2):
                block = mixed_ref[2 * k + 1 - core].astype(jnp.float32)
                for c in range(per_device):
                    head = (2 * j + core) * per_device + c
                    vec_ref[pl.ds(head * rows, rows)] = block[:, c * HEAD_DIM : (c + 1) * HEAD_DIM]
                ids = mixed_ref[2 * k + 1 - core, :, pl.ds(width, LANES)].astype(jnp.float32)
                first = ((1 - core) * len(devices) + k) * rows
                for r in range(rows):
                    adapter = jnp.where(place == first + r, ids[r : r + 1], adapter)
        adapter_ref[...] = adapter.astype(jnp.int32)

        def tiled(pair, count):
            return jnp.concatenate([pair] * count)

        keyed = (HEADS + KV_HEADS) * rows
        vec = vec_ref[pl.ds(0, keyed)]
        turned = pltpu.roll(vec, HEAD_DIM // 2, 1)
        lane = lax.broadcasted_iota(jnp.int32, (rows, HEAD_DIM), 1)
        signed = jnp.where(lane < HEAD_DIM // 2, -sine_ref[...], sine_ref[...])
        pairs = keyed // rows
        vec = vec * tiled(cosine_ref[...], pairs) + turned * tiled(signed, pairs)
        vec = vec.astype(jnp.bfloat16)
        query = vec[: HEADS * rows]
        fresh_key = vec[HEADS * rows :].astype(jnp.float32)
        fresh_value = vec_ref[pl.ds(keyed, KV_HEADS * rows)]
        size = group * rows
        owner = lax.broadcasted_iota(jnp.int32, (size, 1), 0) % rows

        def of_owner(products):
            result = products[0]
            for r in range(1, rows):
                result = jnp.where(owner == r, products[r], result)
            return result

        scores, own_key, own_value = [], [], []
        for g in range(KV_HEADS):
            lanes = pl.ds(g * HEAD_DIM, HEAD_DIM)
            part = query[g * size : (g + 1) * size]
            products = [
                lax.dot_general(
                    part,
                    key_ref[r, :, lanes],
                    (((1,), (1,)), ((), ())),
                    preferred_element_type=jnp.float32,
                )
                for r in range(rows)
            ]
            scores.append(of_owner(products))
            own_key.append(tiled(fresh_key[g * rows : (g + 1) * rows], group))
            own_value.append(tiled(fresh_value[g * rows : (g + 1) * rows], group))
        scale = HEAD_DIM ** (-0.5)
        scores = jnp.concatenate(scores) * scale + tiled(mask_ref[...], HEADS)
        own = jnp.sum(query.astype(jnp.float32) * jnp.concatenate(own_key), 1, keepdims=True)
        own = own * scale
        top = jnp.maximum(jnp.max(scores, 1, keepdims=True), own)
        expo = jnp.exp(scores - top)
        own_exp = jnp.exp(own - top)
        total = jnp.sum(expo, 1, keepdims=True) + own_exp
        probs = (expo / total).astype(jnp.bfloat16)
        own_prob = (own_exp / total).astype(jnp.bfloat16).astype(jnp.float32)
        for g in range(KV_HEADS):
            lanes = pl.ds(g * HEAD_DIM, HEAD_DIM)
            part = probs[g * size : (g + 1) * size]
            products = [
                jnp.dot(part, value_ref[r, :, lanes], preferred_element_type=jnp.float32)
                for r in range(rows)
            ]
            result = of_owner(products) + own_prob[g * size : (g + 1) * size] * own_value[g]
            for h in range(group):
                first = (g * group + h) * HEAD_DIM
                core, first = first // part_width % 2, first // part_width // 2 * part_width + (
                    first % part_width
                )
                context_ref[core, :, pl.ds(first, HEAD_DIM)] = result[h * rows : (h + 1) * rows]
        for core in range(2):
            rounded = context_ref[core].astype(jnp.bfloat16)
            for k in range(copies):
                out_ref[2 * k + 1 - core] = rounded

    return call(
        kernel,
        "attend",
        (
            jax.ShapeDtypeStruct((2 * copies, rows, HEADS * HEAD_DIM // 2), jnp.bfloat16),
            jax.ShapeDtypeStruct((1, LANES), jnp.int32),
        ),
        [VMEM] * 6,
        key_cache.size * 4,
        limit=4 * MIB,
        flops=LONG,
        scratch_shapes=[
            pltpu.VMEM((heads * rows, HEAD_DIM), jnp.float32),
            pltpu.VMEM((2, rows, HEADS * HEAD_DIM // 2), jnp.float32),
        ],
    )(mixed, cosine, sine, mask, key_cache, value_cache)


def fast_body(
    hidden,
    attention_norm_gain,
    query_key_value_weight,
    output_weight,
    key_cache,
    value_cache,
    lengths,
    slots,
    requests,
    adapter_down_matrices,
    adapter_up_matrices,
):
    mp_size = lax.axis_size("mp")
    frequency = frequencies(exponents())
    near = exchange(norm_rows(hidden, attention_norm_gain, frequency, mp_size))
    lined, cosine, sine, mask, adapter = turns(
        near, frequency, lengths, slots, requests, key_cache.shape[1]
    )
    columns = project_qkv(lined, swap_cores(near), query_key_value_weight, adapter)
    mixed = exchange_all(columns)
    context, adapter = attend(mixed, cosine, sine, mask, key_cache, value_cache, mp_size)
    gathered = exchange_all(context)

    partials, mine, theirs, up = project_out(
        gathered,
        adapter,
        output_weight,
        adapter_down_matrices.swapaxes(1, 2),
        adapter_up_matrices,
    )
    projected = add_up(mine, swap_cores(theirs), exchange_all(partials), up)
    return add_rows(hidden, exchange(projected))


def body(*arguments):
    small = lax.axis_size("mp") <= 16 and lax.axis_size("batch") == 2
    whole_heads = arguments[2].shape[1] % HEAD_DIM == 0
    return (fast_body if small and whole_heads else general_body)(*arguments)


def solution(mesh):
    in_specs = (
        P(("groups", "mp", "batch"), None),
        P(),
        P(None, ("mp", "batch")),
        P(None, "mp"),
        P(("groups", "mp", "batch"), None, None),
        P(("groups", "mp", "batch"), None, None),
        P(("groups", "mp", "batch")),
        P(("groups", "mp", "batch")),
        P(("groups", "mp", "batch"), None),
        P(None, "mp", None),
        P(None, None, "mp"),
    )
    out_specs = P(("groups", "mp", "batch"), None)
    return jax.shard_map(body, mesh=mesh, in_specs=in_specs, out_specs=out_specs, check_vma=False)
```

```python
import math

import jax
import jax.numpy as jnp
from jax import lax
from jax.experimental import pallas as pl
from jax.experimental.pallas import tpu as pltpu
from jax.sharding import PartitionSpec as P

HEADS = 64
KV_HEADS = 8
HEAD_DIM = 128
ADAPTER_COUNT = 64


EPS = 1e-05
THETA = 500000.0
ADAPTER_SCALE = 2.0


def rotate(vec, pos):
    width = vec.shape[-1]
    half = width // 2
    freq = THETA ** (-(jnp.arange(half, dtype=jnp.float32) * 2.0) / width)
    angle = pos[..., None, None] * freq
    cosine = jnp.concatenate([jnp.cos(angle), jnp.cos(angle)], -1)
    sine = jnp.concatenate([jnp.sin(angle), jnp.sin(angle)], -1)
    turned = jnp.concatenate([-vec[..., half:], vec[..., :half]], -1)
    return vec * cosine + turned * sine


def apply_up_matrix(
    context_vector, adapter_selector, down_result, output_weight, adapter_up_matrices
):
    base_output = jnp.dot(context_vector, output_weight, preferred_element_type=jnp.float32)
    spread = (adapter_selector[:, :, None] * down_result[:, None, :]).reshape(
        adapter_selector.shape[0], -1
    )
    adapter_table = adapter_up_matrices.reshape(-1, adapter_up_matrices.shape[2])
    adapter_delta = jnp.dot(spread, adapter_table, preferred_element_type=jnp.float32)
    return (base_output + ADAPTER_SCALE * adapter_delta).astype(jnp.bfloat16)


def general_body(
    hidden,
    attention_norm_gain,
    query_key_value_weight,
    output_weight,
    key_cache,
    value_cache,
    lengths,
    slots,
    requests,
    adapter_down_matrices,
    adapter_up_matrices,
):
    widened = hidden.astype(jnp.float32)
    normed = (
        widened
        * lax.rsqrt(jnp.mean(widened * widened, -1, keepdims=True) + EPS)
        * attention_norm_gain.astype(jnp.float32)
    ).astype(jnp.bfloat16)
    rows = normed.shape[0]
    columns = jnp.dot(
        lax.all_gather(normed, ("mp", "batch"), axis=0, tiled=True),
        query_key_value_weight,
        preferred_element_type=jnp.float32,
    ).astype(jnp.bfloat16)
    mixed = lax.all_to_all(
        lax.all_to_all(columns, "mp", split_axis=0, concat_axis=1, tiled=True),
        "batch",
        split_axis=0,
        concat_axis=1,
        tiled=True,
    )
    width = query_key_value_weight.shape[1]
    qkv = (
        mixed.reshape(rows, lax.axis_size("batch"), lax.axis_size("mp"), width)
        .transpose(0, 2, 1, 3)
        .reshape(rows, -1)
    )
    query_width = HEADS * HEAD_DIM
    kv_width = KV_HEADS * HEAD_DIM
    group = HEADS // KV_HEADS
    scale = HEAD_DIM ** (-0.5)
    pos = lengths.astype(jnp.float32)
    query = rotate(
        qkv[:, :query_width].astype(jnp.float32).reshape(rows, HEADS, HEAD_DIM), pos
    ).astype(jnp.bfloat16)
    fresh_key = rotate(
        qkv[:, query_width : query_width + kv_width]
        .astype(jnp.float32)
        .reshape(rows, KV_HEADS, HEAD_DIM),
        pos,
    ).astype(jnp.bfloat16)
    fresh_value = (
        qkv[:, query_width + kv_width :].astype(jnp.float32).reshape(rows, KV_HEADS, HEAD_DIM)
    )
    grouped = query.reshape(rows, KV_HEADS, group, HEAD_DIM)
    cached = key_cache.reshape(rows, -1, KV_HEADS, HEAD_DIM)
    stored = value_cache.reshape(rows, -1, KV_HEADS, HEAD_DIM)
    scores = (
        jnp.einsum("rgqd,rtgd->rgqt", grouped, cached, preferred_element_type=jnp.float32) * scale
    )
    live = jnp.arange(cached.shape[1])[None, :] < lengths[:, None]
    scores = jnp.where(live[:, None, None, :], scores, -jnp.inf)
    own = (
        jnp.einsum("rgqd,rgd->rgq", grouped, fresh_key, preferred_element_type=jnp.float32) * scale
    )
    top = jnp.maximum(jnp.max(scores, -1), own)
    expo = jnp.exp(scores - top[..., None])
    own_exp = jnp.exp(own - top)
    total = jnp.sum(expo, -1) + own_exp
    probs = (expo / total[..., None]).astype(jnp.bfloat16)
    own_prob = (own_exp / total).astype(jnp.bfloat16)
    context_vector = jnp.einsum(
        "rgqt,rtgd->rgqd", probs, stored, preferred_element_type=jnp.float32
    )
    context_vector = (
        context_vector + own_prob.astype(jnp.float32)[..., None] * fresh_value[:, :, None, :]
    )
    context_vector = context_vector.reshape(rows, query_width).astype(jnp.bfloat16)
    slot_hits = slots[:, None] == jnp.arange(requests.shape[1])[None, :]
    adapter = jnp.sum(jnp.where(slot_hits, requests[0][None, :], 0), 1)
    adapter_selector = (adapter[:, None] == jnp.arange(ADAPTER_COUNT)[None, :]).astype(jnp.bfloat16)
    context_gathered, selector_gathered = (
        lax.all_gather(context_vector, "mp", axis=0, tiled=True),
        lax.all_gather(adapter_selector, "mp", axis=0, tiled=True),
    )
    shared_portion = adapter_down_matrices.shape[1]
    context_slice = lax.dynamic_slice_in_dim(
        context_gathered, lax.axis_index("mp") * shared_portion, shared_portion, 1
    )
    every_adapter = jnp.einsum(
        "gh,thy->gty", context_slice, adapter_down_matrices, preferred_element_type=jnp.float32
    )
    partial_down = jnp.sum(every_adapter * selector_gathered.astype(jnp.float32)[:, :, None], 1)
    down_gathered = lax.psum(partial_down, "mp").astype(jnp.bfloat16)
    projection_result = apply_up_matrix(
        context_gathered, selector_gathered, down_gathered, output_weight, adapter_up_matrices
    )
    returned = lax.all_to_all(projection_result, "mp", split_axis=0, concat_axis=1, tiled=True)
    return (widened + returned.astype(jnp.float32)).astype(jnp.bfloat16)


MIB = 1 << 20
LANES = 128
LONG = 10**10
VMEM = pl.BlockSpec(memory_space=pltpu.VMEM)
SMEM = pl.BlockSpec(memory_space=pltpu.SMEM)
ANY = pl.BlockSpec(memory_space=pl.ANY)


def call(kernel, name, out_shape, in_specs, moved, limit=2 * MIB, flops=0, **options):
    return pl.pallas_call(
        kernel,
        out_shape=out_shape,
        in_specs=in_specs,
        out_specs=jax.tree.map(lambda _: VMEM, out_shape),
        compiler_params=pltpu.CompilerParams(vmem_limit_bytes=limit),
        cost_estimate=pl.CostEstimate(flops=flops, bytes_accessed=moved, transcendentals=0),
        name=name,
        **options,
    )


def exponents():
    def kernel(out_ref):
        lane = lax.broadcasted_iota(jnp.int32, (1, HEAD_DIM), 1)
        out_ref[...] = (lane % (HEAD_DIM // 2)).astype(jnp.float32) * (-2.0 / HEAD_DIM)

    shape = jax.ShapeDtypeStruct((1, HEAD_DIM), jnp.float32)
    return call(kernel, "exponents", shape, [], 0, flops=LONG // 8)()


def frequencies(exponent):
    def kernel(exponent_ref, out_ref):
        out_ref[...] = jnp.exp(exponent_ref[...] * math.log(THETA))

    shape = jax.ShapeDtypeStruct(exponent.shape, jnp.float32)
    return call(kernel, "frequencies", shape, [VMEM], 0, flops=LONG // 8)(exponent)


def norm_rows(hidden, gain, after, copies):
    rows, width = hidden.shape

    def kernel(hidden_ref, gain_ref, after_ref, out_ref):
        del after_ref
        wide = hidden_ref[...].astype(jnp.float32)
        inverse = lax.rsqrt(jnp.mean(wide * wide, -1, keepdims=True) + EPS)
        normed = (wide * inverse * gain_ref[...].astype(jnp.float32)).astype(jnp.bfloat16)
        for c in range(copies):
            out_ref[c] = normed

    return call(
        kernel,
        "norm_rows",
        jax.ShapeDtypeStruct((copies, rows, width), jnp.bfloat16),
        [VMEM, VMEM, ANY],
        hidden.size * 2 * (copies + 1),
        flops=LONG,
    )(hidden, gain[None], after)


def turns(near, frequency, lengths, slots, requests, context):
    groups, rows, depth = near.shape

    def kernel(
        lengths_ref, slots_ref, requests_ref, near_ref, frequency_ref, lined_ref, cosine_ref,
        sine_ref, mask_ref, adapter_ref,
    ):
        for j in range(groups):
            lined_ref[pl.ds(j * rows, rows)] = near_ref[j]
        row = lax.broadcasted_iota(jnp.int32, (rows, LANES), 0)
        length = jnp.zeros((rows, LANES), jnp.int32)
        adapter = jnp.zeros((rows, LANES), jnp.int32)
        for r in range(rows):
            length = jnp.where(row == r, lengths_ref[r], length)
            adapter = jnp.where(row == r, requests_ref[0, slots_ref[r]], adapter)
        angle = length.astype(jnp.float32) * frequency_ref[...]
        cosine_ref[...] = jnp.cos(angle)
        sine_ref[...] = jnp.sin(angle)
        lane = lax.broadcasted_iota(jnp.int32, (rows, LANES), 1)
        for t in range(0, context, LANES):
            mask_ref[:, pl.ds(t, LANES)] = jnp.where(lane + t < length, 0.0, -jnp.inf)
        adapter_ref[...] = adapter.astype(jnp.float32).astype(jnp.bfloat16)

    return call(
        kernel,
        "turns",
        (
            jax.ShapeDtypeStruct((groups * rows, depth), near.dtype),
            jax.ShapeDtypeStruct((rows, HEAD_DIM), jnp.float32),
            jax.ShapeDtypeStruct((rows, HEAD_DIM), jnp.float32),
            jax.ShapeDtypeStruct((rows, context), jnp.float32),
            jax.ShapeDtypeStruct((rows, LANES), jnp.bfloat16),
        ),
        [SMEM] * 3 + [VMEM] * 2,
        near.size * 4,
    )(lengths, slots, requests, near, frequency)


def project_qkv(lined, far, weight, adapter, chunk=4096):
    groups, rows, _ = far.shape
    depth, width = weight.shape
    half = groups * rows

    def kernel(lined_ref, far_ref, weight_ref, adapter_ref, out_ref, far_lined_ref):
        total = jnp.zeros((2 * half, width), jnp.float32)
        for k in range(depth // chunk):
            part = pl.ds(k * chunk, chunk)
            for j in range(groups):
                far_lined_ref[pl.ds(j * rows, rows), part] = far_ref[j, :, part]
            total = total + jnp.dot(
                jnp.concatenate([lined_ref[:, part], far_lined_ref[:, part]]),
                weight_ref[part, :],
                preferred_element_type=jnp.float32,
            )
        core = lax.axis_index("batch")
        adapter = adapter_ref[...]
        for e in range(2):
            for j in range(groups):
                place = e * half + j * rows
                device = 2 * j + (core ^ e ^ 1)
                out_ref[device, :, pl.ds(0, width)] = total[place : place + rows].astype(
                    jnp.bfloat16
                )
                out_ref[device, :, pl.ds(width, LANES)] = (
                    adapter if e == 0 else jnp.zeros_like(adapter)
                )

    return call(
        kernel,
        "project_qkv",
        jax.ShapeDtypeStruct((2 * groups, rows, width + LANES), jnp.bfloat16),
        [VMEM] * 4,
        weight.size * 2,
        flops=LONG,
        scratch_shapes=[pltpu.VMEM((half, depth), jnp.bfloat16)],
    )(lined, far, weight, adapter)


def project_out(gathered, adapter, weight, down_store, up_store, chunk=2048):
    groups, rows, features = gathered.shape
    count = groups * rows
    rank, depth = down_store.shape[1:]
    columns = weight.shape[1]

    def kernel(
        adapter_ref, gathered_ref, weight_ref, down_ref, up_ref, partial_ref, base_ref, picked_ref,
        rows_ref, held_ref,
    ):
        base = jnp.zeros((count, columns), jnp.float32)
        chunks = features // chunk
        for k in range(chunks):
            part = pl.ds(k * chunk, chunk)
            for j in range(groups):
                rows_ref[pl.ds(j * rows, rows), part] = gathered_ref[j, :, part]
            base = base + jnp.dot(
                rows_ref[:, part], weight_ref[part, :], preferred_element_type=jnp.float32
            )
            for r in range(k * count // chunks, (k + 1) * count // chunks):
                chosen = adapter_ref[0, r]
                held_ref[pl.ds(r * rank, rank)] = down_ref[chosen]
                picked_ref[pl.ds(r * rank, rank)] = up_ref[chosen]
        base_ref[...] = base
        start = pl.multiple_of(lax.axis_index("mp") * depth, depth)
        every = lax.dot_general(
            rows_ref[:, pl.ds(start, depth)],
            held_ref[...],
            (((1,), (1,)), ((), ())),
            preferred_element_type=jnp.float32,
        )
        row = lax.broadcasted_iota(jnp.int32, (count, LANES), 0)
        lane = lax.broadcasted_iota(jnp.int32, (count, LANES), 1)
        total = jnp.zeros((count, LANES), jnp.float32)
        for s in range(0, count * rank, LANES):
            total = total + jnp.where(row == (lane + s) // rank, every[:, s : s + LANES], 0.0)
        for c in range(groups):
            partial_ref[c] = total

    return call(
        kernel,
        "project_out",
        (
            jax.ShapeDtypeStruct((groups, count, LANES), jnp.float32),
            jax.ShapeDtypeStruct((count, columns), jnp.float32),
            pltpu.VMEM((count * rank, columns), up_store.dtype),
        ),
        [SMEM] + [VMEM] * 4,
        weight.size * 2,
        limit=5 * MIB,
        flops=LONG,
        scratch_shapes=[
            pltpu.VMEM((count, features), gathered.dtype),
            pltpu.VMEM((count * rank, depth), down_store.dtype),
        ],
    )(adapter, gathered, weight, down_store, up_store)


def add_up(base, partials, up):
    groups, count, _ = partials.shape
    depth, width = up.shape
    rank = depth // count

    def kernel(base_ref, partials_ref, up_ref, out_ref):
        total = partials_ref[0]
        for c in range(1, groups):
            total = total + partials_ref[c]
        down = total.astype(jnp.bfloat16).astype(jnp.float32)
        row = lax.broadcasted_iota(jnp.int32, (count, LANES), 0)
        lane = lax.broadcasted_iota(jnp.int32, (count, LANES), 1)
        spread = []
        for s in range(0, depth, LANES):
            spread.append(jnp.where(row == (lane + s) // rank, down, 0.0))
        spread = jnp.concatenate(spread, 1).astype(jnp.bfloat16)
        delta = jnp.dot(spread, up_ref[...], preferred_element_type=jnp.float32)
        result = (base_ref[...] + ADAPTER_SCALE * delta).astype(jnp.bfloat16)
        for j in range(groups):
            out_ref[j] = result[j * count // groups : (j + 1) * count // groups]

    return call(
        kernel,
        "add_up",
        jax.ShapeDtypeStruct((groups, count // groups, width), jnp.bfloat16),
        [VMEM] * 3,
        up.size * 2,
        limit=4 * MIB,
        flops=2 * count * up.size,
    )(base, partials, up)


def add_rows(hidden, parts):
    width = parts.shape[2]

    def kernel(hidden_ref, parts_ref, out_ref):
        for k, place in enumerate(order(parts.shape[0])):
            part = pl.ds(place * width, width)
            total = hidden_ref[:, part].astype(jnp.float32) + parts_ref[k].astype(jnp.float32)
            out_ref[:, part] = total.astype(jnp.bfloat16)

    return call(
        kernel,
        "add_rows",
        jax.ShapeDtypeStruct(hidden.shape, parts.dtype),
        [VMEM, VMEM],
        hidden.size * 6,
    )(hidden, parts)


def swap_cores(block):
    return lax.ppermute(block, "batch", [(0, 1), (1, 0)])


def order(size):
    half = size // 2
    return [(k + 1) % half + start for k in range(half) for start in (half, 0)]


def exchange(blocks):
    group = order(lax.axis_size("mp"))
    return lax.all_to_all(
        blocks, "mp", split_axis=0, concat_axis=0, tiled=True, axis_index_groups=[group]
    )


def exchange_all(blocks):
    group = [2 * j + core for j in order(lax.axis_size("mp")) for core in (1, 0)]
    return lax.all_to_all(
        blocks,
        ("mp", "batch"),
        split_axis=0,
        concat_axis=0,
        tiled=True,
        axis_index_groups=[group],
    )


def attend(mixed, cosine, sine, mask, key_cache, value_cache, copies):
    rows, context = key_cache.shape[:2]
    group = HEADS // KV_HEADS
    heads = HEADS + 2 * KV_HEADS
    width = mixed.shape[2] - LANES
    per_device = width // HEAD_DIM
    devices = order(mixed.shape[0] // 2)

    def kernel(
        mixed_ref, cosine_ref, sine_ref, mask_ref, key_ref, value_ref, out_ref, adapter_ref,
        vec_ref, context_ref,
    ):
        place = lax.broadcasted_iota(jnp.int32, (1, LANES), 1)
        adapter = jnp.zeros((1, LANES), jnp.float32)
        for k, j in enumerate(devices):
            for core in range(2):
                block = mixed_ref[2 * k + 1 - core].astype(jnp.float32)
                for c in range(per_device):
                    head = (2 * j + core) * per_device + c
                    vec_ref[pl.ds(head * rows, rows)] = block[:, c * HEAD_DIM : (c + 1) * HEAD_DIM]
            both = mixed_ref[2 * k, :, pl.ds(width, LANES)].astype(jnp.float32)
            both = both + mixed_ref[2 * k + 1, :, pl.ds(width, LANES)].astype(jnp.float32)
            for r in range(rows):
                adapter = jnp.where(place == k * rows + r, both[r : r + 1], adapter)
        adapter_ref[...] = adapter.astype(jnp.int32)

        def tiled(pair, count):
            return jnp.concatenate([pair] * count)

        keyed = (HEADS + KV_HEADS) * rows
        vec = vec_ref[pl.ds(0, keyed)]
        turned = pltpu.roll(vec, HEAD_DIM // 2, 1)
        lane = lax.broadcasted_iota(jnp.int32, (rows, HEAD_DIM), 1)
        signed = jnp.where(lane < HEAD_DIM // 2, -sine_ref[...], sine_ref[...])
        pairs = keyed // rows
        vec = vec * tiled(cosine_ref[...], pairs) + turned * tiled(signed, pairs)
        vec = vec.astype(jnp.bfloat16)
        query = vec[: HEADS * rows]
        fresh_key = vec[HEADS * rows :].astype(jnp.float32)
        fresh_value = vec_ref[pl.ds(keyed, KV_HEADS * rows)]
        size = group * rows
        owner = lax.broadcasted_iota(jnp.int32, (size, 1), 0) % rows

        def of_owner(products):
            result = products[0]
            for r in range(1, rows):
                result = jnp.where(owner == r, products[r], result)
            return result

        scores, own_key, own_value = [], [], []
        for g in range(KV_HEADS):
            lanes = pl.ds(g * HEAD_DIM, HEAD_DIM)
            part = query[g * size : (g + 1) * size]
            products = [
                lax.dot_general(
                    part,
                    key_ref[r, :, lanes],
                    (((1,), (1,)), ((), ())),
                    preferred_element_type=jnp.float32,
                )
                for r in range(rows)
            ]
            scores.append(of_owner(products))
            own_key.append(tiled(fresh_key[g * rows : (g + 1) * rows], group))
            own_value.append(tiled(fresh_value[g * rows : (g + 1) * rows], group))
        scale = HEAD_DIM ** (-0.5)
        scores = jnp.concatenate(scores) * scale + tiled(mask_ref[...], HEADS)
        own = jnp.sum(query.astype(jnp.float32) * jnp.concatenate(own_key), 1, keepdims=True)
        own = own * scale
        top = jnp.maximum(jnp.max(scores, 1, keepdims=True), own)
        expo = jnp.exp(scores - top)
        own_exp = jnp.exp(own - top)
        total = jnp.sum(expo, 1, keepdims=True) + own_exp
        probs = (expo / total).astype(jnp.bfloat16)
        own_prob = (own_exp / total).astype(jnp.bfloat16).astype(jnp.float32)
        for g in range(KV_HEADS):
            lanes = pl.ds(g * HEAD_DIM, HEAD_DIM)
            part = probs[g * size : (g + 1) * size]
            products = [
                jnp.dot(part, value_ref[r, :, lanes], preferred_element_type=jnp.float32)
                for r in range(rows)
            ]
            result = of_owner(products) + own_prob[g * size : (g + 1) * size] * own_value[g]
            for h in range(group):
                place = pl.ds((g * group + h) * HEAD_DIM, HEAD_DIM)
                context_ref[:, place] = result[h * rows : (h + 1) * rows]
        rounded = context_ref[...].astype(jnp.bfloat16)
        for c in range(copies):
            out_ref[c] = rounded

    return call(
        kernel,
        "attend",
        (
            jax.ShapeDtypeStruct((copies, rows, HEADS * HEAD_DIM), jnp.bfloat16),
            jax.ShapeDtypeStruct((1, LANES), jnp.int32),
        ),
        [VMEM] * 6,
        key_cache.size * 4,
        limit=4 * MIB,
        flops=LONG,
        scratch_shapes=[
            pltpu.VMEM((heads * rows, HEAD_DIM), jnp.float32),
            pltpu.VMEM((rows, HEADS * HEAD_DIM), jnp.float32),
        ],
    )(mixed, cosine, sine, mask, key_cache, value_cache)


def fast_body(
    hidden,
    attention_norm_gain,
    query_key_value_weight,
    output_weight,
    key_cache,
    value_cache,
    lengths,
    slots,
    requests,
    adapter_down_matrices,
    adapter_up_matrices,
):
    mp_size = lax.axis_size("mp")
    frequency = frequencies(exponents())
    near = exchange(norm_rows(hidden, attention_norm_gain, frequency, mp_size))
    lined, cosine, sine, mask, adapter = turns(
        near, frequency, lengths, slots, requests, key_cache.shape[1]
    )
    columns = project_qkv(lined, swap_cores(near), query_key_value_weight, adapter)
    mixed = exchange_all(columns)
    context, adapter = attend(mixed, cosine, sine, mask, key_cache, value_cache, mp_size)
    gathered = exchange(context)

    partials, base, up = project_out(
        gathered,
        adapter,
        output_weight,
        adapter_down_matrices.swapaxes(1, 2),
        adapter_up_matrices,
    )
    projected = add_up(base, exchange(partials), up)
    return add_rows(hidden, exchange(projected))


def body(*arguments):
    small = lax.axis_size("mp") <= 16 and lax.axis_size("batch") == 2
    whole_heads = arguments[2].shape[1] % HEAD_DIM == 0
    return (fast_body if small and whole_heads else general_body)(*arguments)


def solution(mesh):
    in_specs = (
        P(("groups", "mp", "batch"), None),
        P(),
        P(None, ("mp", "batch")),
        P(None, "mp"),
        P(("groups", "mp", "batch"), None, None),
        P(("groups", "mp", "batch"), None, None),
        P(("groups", "mp", "batch")),
        P(("groups", "mp", "batch")),
        P(("groups", "mp", "batch"), None),
        P(None, "mp", None),
        P(None, None, "mp"),
    )
    out_specs = P(("groups", "mp", "batch"), None)
    return jax.shard_map(body, mesh=mesh, in_specs=in_specs, out_specs=out_specs, check_vma=False)
```

```python
import math

import jax
import jax.numpy as jnp
from jax import lax
from jax.experimental import pallas as pl
from jax.experimental.pallas import tpu as pltpu
from jax.sharding import PartitionSpec as P

HEADS = 64
KV_HEADS = 8
HEAD_DIM = 128
ADAPTER_COUNT = 64


EPS = 1e-05
THETA = 500000.0
ADAPTER_SCALE = 2.0


def rotate(vec, pos):
    width = vec.shape[-1]
    half = width // 2
    freq = THETA ** (-(jnp.arange(half, dtype=jnp.float32) * 2.0) / width)
    angle = pos[..., None, None] * freq
    cosine = jnp.concatenate([jnp.cos(angle), jnp.cos(angle)], -1)
    sine = jnp.concatenate([jnp.sin(angle), jnp.sin(angle)], -1)
    turned = jnp.concatenate([-vec[..., half:], vec[..., :half]], -1)
    return vec * cosine + turned * sine


def apply_up_matrix(
    context_vector, adapter_selector, down_result, output_weight, adapter_up_matrices
):
    base_output = jnp.dot(context_vector, output_weight, preferred_element_type=jnp.float32)
    spread = (adapter_selector[:, :, None] * down_result[:, None, :]).reshape(
        adapter_selector.shape[0], -1
    )
    adapter_table = adapter_up_matrices.reshape(-1, adapter_up_matrices.shape[2])
    adapter_delta = jnp.dot(spread, adapter_table, preferred_element_type=jnp.float32)
    return (base_output + ADAPTER_SCALE * adapter_delta).astype(jnp.bfloat16)


def general_body(
    hidden,
    attention_norm_gain,
    query_key_value_weight,
    output_weight,
    key_cache,
    value_cache,
    lengths,
    slots,
    requests,
    adapter_down_matrices,
    adapter_up_matrices,
):
    widened = hidden.astype(jnp.float32)
    normed = (
        widened
        * lax.rsqrt(jnp.mean(widened * widened, -1, keepdims=True) + EPS)
        * attention_norm_gain.astype(jnp.float32)
    ).astype(jnp.bfloat16)
    rows = normed.shape[0]
    columns = jnp.dot(
        lax.all_gather(normed, ("mp", "batch"), axis=0, tiled=True),
        query_key_value_weight,
        preferred_element_type=jnp.float32,
    ).astype(jnp.bfloat16)
    mixed = lax.all_to_all(
        lax.all_to_all(columns, "mp", split_axis=0, concat_axis=1, tiled=True),
        "batch",
        split_axis=0,
        concat_axis=1,
        tiled=True,
    )
    width = query_key_value_weight.shape[1]
    qkv = (
        mixed.reshape(rows, lax.axis_size("batch"), lax.axis_size("mp"), width)
        .transpose(0, 2, 1, 3)
        .reshape(rows, -1)
    )
    query_width = HEADS * HEAD_DIM
    kv_width = KV_HEADS * HEAD_DIM
    group = HEADS // KV_HEADS
    scale = HEAD_DIM ** (-0.5)
    pos = lengths.astype(jnp.float32)
    query = rotate(
        qkv[:, :query_width].astype(jnp.float32).reshape(rows, HEADS, HEAD_DIM), pos
    ).astype(jnp.bfloat16)
    fresh_key = rotate(
        qkv[:, query_width : query_width + kv_width]
        .astype(jnp.float32)
        .reshape(rows, KV_HEADS, HEAD_DIM),
        pos,
    ).astype(jnp.bfloat16)
    fresh_value = (
        qkv[:, query_width + kv_width :].astype(jnp.float32).reshape(rows, KV_HEADS, HEAD_DIM)
    )
    grouped = query.reshape(rows, KV_HEADS, group, HEAD_DIM)
    cached = key_cache.reshape(rows, -1, KV_HEADS, HEAD_DIM)
    stored = value_cache.reshape(rows, -1, KV_HEADS, HEAD_DIM)
    scores = (
        jnp.einsum("rgqd,rtgd->rgqt", grouped, cached, preferred_element_type=jnp.float32) * scale
    )
    live = jnp.arange(cached.shape[1])[None, :] < lengths[:, None]
    scores = jnp.where(live[:, None, None, :], scores, -jnp.inf)
    own = (
        jnp.einsum("rgqd,rgd->rgq", grouped, fresh_key, preferred_element_type=jnp.float32) * scale
    )
    top = jnp.maximum(jnp.max(scores, -1), own)
    expo = jnp.exp(scores - top[..., None])
    own_exp = jnp.exp(own - top)
    total = jnp.sum(expo, -1) + own_exp
    probs = (expo / total[..., None]).astype(jnp.bfloat16)
    own_prob = (own_exp / total).astype(jnp.bfloat16)
    context_vector = jnp.einsum(
        "rgqt,rtgd->rgqd", probs, stored, preferred_element_type=jnp.float32
    )
    context_vector = (
        context_vector + own_prob.astype(jnp.float32)[..., None] * fresh_value[:, :, None, :]
    )
    context_vector = context_vector.reshape(rows, query_width).astype(jnp.bfloat16)
    slot_hits = slots[:, None] == jnp.arange(requests.shape[1])[None, :]
    adapter = jnp.sum(jnp.where(slot_hits, requests[0][None, :], 0), 1)
    adapter_selector = (adapter[:, None] == jnp.arange(ADAPTER_COUNT)[None, :]).astype(jnp.bfloat16)
    context_gathered, selector_gathered = (
        lax.all_gather(context_vector, "mp", axis=0, tiled=True),
        lax.all_gather(adapter_selector, "mp", axis=0, tiled=True),
    )
    shared_portion = adapter_down_matrices.shape[1]
    context_slice = lax.dynamic_slice_in_dim(
        context_gathered, lax.axis_index("mp") * shared_portion, shared_portion, 1
    )
    every_adapter = jnp.einsum(
        "gh,thy->gty", context_slice, adapter_down_matrices, preferred_element_type=jnp.float32
    )
    partial_down = jnp.sum(every_adapter * selector_gathered.astype(jnp.float32)[:, :, None], 1)
    down_gathered = lax.psum(partial_down, "mp").astype(jnp.bfloat16)
    projection_result = apply_up_matrix(
        context_gathered, selector_gathered, down_gathered, output_weight, adapter_up_matrices
    )
    returned = lax.all_to_all(projection_result, "mp", split_axis=0, concat_axis=1, tiled=True)
    return (widened + returned.astype(jnp.float32)).astype(jnp.bfloat16)


MIB = 1 << 20
LANES = 128
LONG = 10**10
VMEM = pl.BlockSpec(memory_space=pltpu.VMEM)
SMEM = pl.BlockSpec(memory_space=pltpu.SMEM)
ANY = pl.BlockSpec(memory_space=pl.ANY)


def call(kernel, name, out_shape, in_specs, moved, limit=2 * MIB, flops=0, **options):
    return pl.pallas_call(
        kernel,
        out_shape=out_shape,
        in_specs=in_specs,
        out_specs=jax.tree.map(lambda _: VMEM, out_shape),
        compiler_params=pltpu.CompilerParams(vmem_limit_bytes=limit),
        cost_estimate=pl.CostEstimate(flops=flops, bytes_accessed=moved, transcendentals=0),
        name=name,
        **options,
    )


def exponents():
    def kernel(out_ref):
        lane = lax.broadcasted_iota(jnp.int32, (1, HEAD_DIM), 1)
        out_ref[...] = (lane % (HEAD_DIM // 2)).astype(jnp.float32) * (-2.0 / HEAD_DIM)

    shape = jax.ShapeDtypeStruct((1, HEAD_DIM), jnp.float32)
    return call(kernel, "exponents", shape, [], 0, flops=LONG // 8)()


def frequencies(exponent):
    def kernel(exponent_ref, out_ref):
        out_ref[...] = jnp.exp(exponent_ref[...] * math.log(THETA))

    shape = jax.ShapeDtypeStruct(exponent.shape, jnp.float32)
    return call(kernel, "frequencies", shape, [VMEM], 0, flops=LONG // 8)(exponent)


def norm_rows(hidden, gain, after, copies):
    rows, width = hidden.shape

    def kernel(hidden_ref, gain_ref, after_ref, out_ref):
        del after_ref
        wide = hidden_ref[...].astype(jnp.float32)
        inverse = lax.rsqrt(jnp.mean(wide * wide, -1, keepdims=True) + EPS)
        normed = (wide * inverse * gain_ref[...].astype(jnp.float32)).astype(jnp.bfloat16)
        for c in range(copies):
            out_ref[c] = normed

    return call(
        kernel,
        "norm_rows",
        jax.ShapeDtypeStruct((copies, rows, width), jnp.bfloat16),
        [VMEM, VMEM, ANY],
        hidden.size * 2 * (copies + 1),
        flops=LONG,
    )(hidden, gain[None], after)


def turns(near, frequency, lengths, slots, requests, context):
    groups, rows, depth = near.shape

    def kernel(
        lengths_ref, slots_ref, requests_ref, near_ref, frequency_ref, lined_ref, cosine_ref,
        sine_ref, mask_ref, adapter_ref,
    ):
        for j in range(groups):
            lined_ref[pl.ds(j * rows, rows)] = near_ref[j]
        row = lax.broadcasted_iota(jnp.int32, (rows, LANES), 0)
        length = jnp.zeros((rows, LANES), jnp.int32)
        adapter = jnp.zeros((rows, LANES), jnp.int32)
        for r in range(rows):
            length = jnp.where(row == r, lengths_ref[r], length)
            adapter = jnp.where(row == r, requests_ref[0, slots_ref[r]], adapter)
        angle = length.astype(jnp.float32) * frequency_ref[...]
        cosine_ref[...] = jnp.cos(angle)
        sine_ref[...] = jnp.sin(angle)
        lane = lax.broadcasted_iota(jnp.int32, (rows, LANES), 1)
        for t in range(0, context, LANES):
            mask_ref[:, pl.ds(t, LANES)] = jnp.where(lane + t < length, 0.0, -jnp.inf)
        adapter_ref[...] = adapter.astype(jnp.float32).astype(jnp.bfloat16)

    return call(
        kernel,
        "turns",
        (
            jax.ShapeDtypeStruct((groups * rows, depth), near.dtype),
            jax.ShapeDtypeStruct((rows, HEAD_DIM), jnp.float32),
            jax.ShapeDtypeStruct((rows, HEAD_DIM), jnp.float32),
            jax.ShapeDtypeStruct((rows, context), jnp.float32),
            jax.ShapeDtypeStruct((rows, LANES), jnp.bfloat16),
        ),
        [SMEM] * 3 + [VMEM] * 2,
        near.size * 4,
    )(lengths, slots, requests, near, frequency)


def project_qkv(lined, far, weight, adapter, chunk=4096):
    groups, rows, _ = far.shape
    depth, width = weight.shape
    half = groups * rows

    def kernel(lined_ref, far_ref, weight_ref, adapter_ref, out_ref, far_lined_ref):
        total = jnp.zeros((2 * half, width), jnp.float32)
        for k in range(depth // chunk):
            part = pl.ds(k * chunk, chunk)
            for j in range(groups):
                far_lined_ref[pl.ds(j * rows, rows), part] = far_ref[j, :, part]
            total = total + jnp.dot(
                jnp.concatenate([lined_ref[:, part], far_lined_ref[:, part]]),
                weight_ref[part, :],
                preferred_element_type=jnp.float32,
            )
        core = lax.axis_index("batch")
        adapter = adapter_ref[...]
        for e in range(2):
            for j in range(groups):
                place = e * half + j * rows
                device = 2 * j + (core ^ e ^ 1)
                out_ref[device, :, pl.ds(0, width)] = total[place : place + rows].astype(
                    jnp.bfloat16
                )
                out_ref[device, :, pl.ds(width, LANES)] = (
                    adapter if e == 0 else jnp.zeros_like(adapter)
                )

    return call(
        kernel,
        "project_qkv",
        jax.ShapeDtypeStruct((2 * groups, rows, width + LANES), jnp.bfloat16),
        [VMEM] * 4,
        weight.size * 2,
        flops=LONG,
        scratch_shapes=[pltpu.VMEM((half, depth), jnp.bfloat16)],
    )(lined, far, weight, adapter)


def project_out(gathered, adapter, weight, down_store, up_store, chunk=2048):
    groups, rows, features = gathered.shape
    count = groups * rows
    rank, depth = down_store.shape[1:]
    columns = weight.shape[1]

    def kernel(
        adapter_ref, gathered_ref, weight_ref, down_ref, up_ref, partial_ref, base_ref, picked_ref,
        rows_ref, held_ref, ids_ref, sem,
    ):
        fetch = pltpu.make_async_copy(adapter_ref, ids_ref, sem)
        fetch.start()

        def times_weight(k):
            part = pl.ds(k * chunk, chunk)
            return jnp.dot(
                rows_ref[:, part], weight_ref[part, :], preferred_element_type=jnp.float32
            )

        def pick(store_ref, target_ref, first, last):
            for r in range(first, last):
                target_ref[pl.ds(r * rank, rank)] = store_ref[ids_ref[0, r]]

        for j in range(groups):
            rows_ref[pl.ds(j * rows, rows)] = gathered_ref[j]
        base = times_weight(0)
        fetch.wait()
        pick(down_ref, held_ref, 0, count)
        base = base + times_weight(1)
        start = pl.multiple_of(lax.axis_index("mp") * depth, depth)
        every = lax.dot_general(
            rows_ref[:, pl.ds(start, depth)],
            held_ref[...],
            (((1,), (1,)), ((), ())),
            preferred_element_type=jnp.float32,
        )
        row = lax.broadcasted_iota(jnp.int32, (count, LANES), 0)
        lane = lax.broadcasted_iota(jnp.int32, (count, LANES), 1)
        total = jnp.zeros((count, LANES), jnp.float32)
        for s in range(0, count * rank, LANES):
            total = total + jnp.where(row == (lane + s) // rank, every[:, s : s + LANES], 0.0)
        for c in range(groups):
            partial_ref[c] = total
        left = features // chunk - 2
        for k in range(left):
            pick(up_ref, picked_ref, k * count // left, (k + 1) * count // left)
            base = base + times_weight(k + 2)
        base_ref[...] = base

    return call(
        kernel,
        "project_out",
        (
            jax.ShapeDtypeStruct((groups, count, LANES), jnp.float32),
            jax.ShapeDtypeStruct((count, columns), jnp.float32),
            pltpu.VMEM((count * rank, columns), up_store.dtype),
        ),
        [ANY] + [VMEM] * 4,
        weight.size * 2,
        limit=8 * MIB,
        flops=LONG,
        scratch_shapes=[
            pltpu.VMEM((count, features), gathered.dtype),
            pltpu.VMEM((count * rank, depth), down_store.dtype),
            pltpu.SMEM(adapter.shape, adapter.dtype),
            pltpu.SemaphoreType.DMA,
        ],
    )(adapter, gathered, weight, down_store, up_store)


def add_up(base, partials, up):
    groups, count, _ = partials.shape
    depth, width = up.shape
    rank = depth // count

    def kernel(base_ref, partials_ref, up_ref, out_ref):
        total = partials_ref[0]
        for c in range(1, groups):
            total = total + partials_ref[c]
        down = total.astype(jnp.bfloat16).astype(jnp.float32)
        row = lax.broadcasted_iota(jnp.int32, (count, LANES), 0)
        lane = lax.broadcasted_iota(jnp.int32, (count, LANES), 1)
        spread = []
        for s in range(0, depth, LANES):
            spread.append(jnp.where(row == (lane + s) // rank, down, 0.0))
        spread = jnp.concatenate(spread, 1).astype(jnp.bfloat16)
        delta = jnp.dot(spread, up_ref[...], preferred_element_type=jnp.float32)
        result = (base_ref[...] + ADAPTER_SCALE * delta).astype(jnp.bfloat16)
        for j in range(groups):
            out_ref[j] = result[j * count // groups : (j + 1) * count // groups]

    return call(
        kernel,
        "add_up",
        jax.ShapeDtypeStruct((groups, count // groups, width), jnp.bfloat16),
        [VMEM] * 3,
        up.size * 2,
        limit=4 * MIB,
        flops=2 * count * up.size,
    )(base, partials, up)


def add_rows(hidden, parts):
    width = parts.shape[2]

    def kernel(hidden_ref, parts_ref, out_ref):
        for k, place in enumerate(order(parts.shape[0])):
            part = pl.ds(place * width, width)
            total = hidden_ref[:, part].astype(jnp.float32) + parts_ref[k].astype(jnp.float32)
            out_ref[:, part] = total.astype(jnp.bfloat16)

    return call(
        kernel,
        "add_rows",
        jax.ShapeDtypeStruct(hidden.shape, parts.dtype),
        [VMEM, VMEM],
        hidden.size * 6,
    )(hidden, parts)


def swap_cores(block):
    return lax.ppermute(block, "batch", [(0, 1), (1, 0)])


def order(size):
    half = size // 2
    return [(k + 1) % half + start for k in range(half) for start in (half, 0)]


def exchange(blocks):
    group = order(lax.axis_size("mp"))
    return lax.all_to_all(
        blocks, "mp", split_axis=0, concat_axis=0, tiled=True, axis_index_groups=[group]
    )


def exchange_all(blocks):
    group = [2 * j + core for j in order(lax.axis_size("mp")) for core in (1, 0)]
    return lax.all_to_all(
        blocks,
        ("mp", "batch"),
        split_axis=0,
        concat_axis=0,
        tiled=True,
        axis_index_groups=[group],
    )


def attend(mixed, cosine, sine, mask, key_cache, value_cache, copies):
    rows, context = key_cache.shape[:2]
    group = HEADS // KV_HEADS
    heads = HEADS + 2 * KV_HEADS
    width = mixed.shape[2] - LANES
    per_device = width // HEAD_DIM
    devices = order(mixed.shape[0] // 2)

    def kernel(
        mixed_ref, cosine_ref, sine_ref, mask_ref, key_ref, value_ref, out_ref, adapter_ref,
        vec_ref, context_ref,
    ):
        place = lax.broadcasted_iota(jnp.int32, (1, LANES), 1)
        adapter = jnp.zeros((1, LANES), jnp.float32)
        for k, j in enumerate(devices):
            for core in range(2):
                block = mixed_ref[2 * k + 1 - core].astype(jnp.float32)
                for c in range(per_device):
                    head = (2 * j + core) * per_device + c
                    vec_ref[pl.ds(head * rows, rows)] = block[:, c * HEAD_DIM : (c + 1) * HEAD_DIM]
            both = mixed_ref[2 * k, :, pl.ds(width, LANES)].astype(jnp.float32)
            both = both + mixed_ref[2 * k + 1, :, pl.ds(width, LANES)].astype(jnp.float32)
            for r in range(rows):
                adapter = jnp.where(place == k * rows + r, both[r : r + 1], adapter)
        adapter_ref[...] = adapter.astype(jnp.int32)

        def tiled(pair, count):
            return jnp.concatenate([pair] * count)

        keyed = (HEADS + KV_HEADS) * rows
        vec = vec_ref[pl.ds(0, keyed)]
        turned = pltpu.roll(vec, HEAD_DIM // 2, 1)
        lane = lax.broadcasted_iota(jnp.int32, (rows, HEAD_DIM), 1)
        signed = jnp.where(lane < HEAD_DIM // 2, -sine_ref[...], sine_ref[...])
        pairs = keyed // rows
        vec = vec * tiled(cosine_ref[...], pairs) + turned * tiled(signed, pairs)
        vec = vec.astype(jnp.bfloat16)
        query = vec[: HEADS * rows]
        fresh_key = vec[HEADS * rows :].astype(jnp.float32)
        fresh_value = vec_ref[pl.ds(keyed, KV_HEADS * rows)]
        size = group * rows
        owner = lax.broadcasted_iota(jnp.int32, (size, 1), 0) % rows

        def of_owner(products):
            result = products[0]
            for r in range(1, rows):
                result = jnp.where(owner == r, products[r], result)
            return result

        scores, own_key, own_value = [], [], []
        for g in range(KV_HEADS):
            lanes = pl.ds(g * HEAD_DIM, HEAD_DIM)
            part = query[g * size : (g + 1) * size]
            products = [
                lax.dot_general(
                    part,
                    key_ref[r, :, lanes],
                    (((1,), (1,)), ((), ())),
                    preferred_element_type=jnp.float32,
                )
                for r in range(rows)
            ]
            scores.append(of_owner(products))
            own_key.append(tiled(fresh_key[g * rows : (g + 1) * rows], group))
            own_value.append(tiled(fresh_value[g * rows : (g + 1) * rows], group))
        scale = HEAD_DIM ** (-0.5)
        scores = jnp.concatenate(scores) * scale + tiled(mask_ref[...], HEADS)
        own = jnp.sum(query.astype(jnp.float32) * jnp.concatenate(own_key), 1, keepdims=True)
        own = own * scale
        top = jnp.maximum(jnp.max(scores, 1, keepdims=True), own)
        expo = jnp.exp(scores - top)
        own_exp = jnp.exp(own - top)
        total = jnp.sum(expo, 1, keepdims=True) + own_exp
        probs = (expo / total).astype(jnp.bfloat16)
        own_prob = (own_exp / total).astype(jnp.bfloat16).astype(jnp.float32)
        for g in range(KV_HEADS):
            lanes = pl.ds(g * HEAD_DIM, HEAD_DIM)
            part = probs[g * size : (g + 1) * size]
            products = [
                jnp.dot(part, value_ref[r, :, lanes], preferred_element_type=jnp.float32)
                for r in range(rows)
            ]
            result = of_owner(products) + own_prob[g * size : (g + 1) * size] * own_value[g]
            for h in range(group):
                place = pl.ds((g * group + h) * HEAD_DIM, HEAD_DIM)
                context_ref[:, place] = result[h * rows : (h + 1) * rows]
        rounded = context_ref[...].astype(jnp.bfloat16)
        for c in range(copies):
            out_ref[c] = rounded

    return call(
        kernel,
        "attend",
        (
            jax.ShapeDtypeStruct((copies, rows, HEADS * HEAD_DIM), jnp.bfloat16),
            jax.ShapeDtypeStruct((1, LANES), jnp.int32),
        ),
        [VMEM] * 6,
        key_cache.size * 4,
        limit=4 * MIB,
        flops=LONG,
        scratch_shapes=[
            pltpu.VMEM((heads * rows, HEAD_DIM), jnp.float32),
            pltpu.VMEM((rows, HEADS * HEAD_DIM), jnp.float32),
        ],
    )(mixed, cosine, sine, mask, key_cache, value_cache)


def fast_body(
    hidden,
    attention_norm_gain,
    query_key_value_weight,
    output_weight,
    key_cache,
    value_cache,
    lengths,
    slots,
    requests,
    adapter_down_matrices,
    adapter_up_matrices,
):
    mp_size = lax.axis_size("mp")
    frequency = frequencies(exponents())
    near = exchange(norm_rows(hidden, attention_norm_gain, frequency, mp_size))
    lined, cosine, sine, mask, adapter = turns(
        near, frequency, lengths, slots, requests, key_cache.shape[1]
    )
    columns = project_qkv(lined, swap_cores(near), query_key_value_weight, adapter)
    mixed = exchange_all(columns)
    context, adapter = attend(mixed, cosine, sine, mask, key_cache, value_cache, mp_size)
    gathered = exchange(context)

    partials, base, up = project_out(
        gathered,
        adapter,
        output_weight,
        adapter_down_matrices.swapaxes(1, 2),
        adapter_up_matrices,
    )
    projected = add_up(base, exchange(partials), up)
    return add_rows(hidden, exchange(projected))


def body(*arguments):
    small = lax.axis_size("mp") <= 16 and lax.axis_size("batch") == 2
    whole_heads = arguments[2].shape[1] % HEAD_DIM == 0
    return (fast_body if small and whole_heads else general_body)(*arguments)


def solution(mesh):
    in_specs = (
        P(("groups", "mp", "batch"), None),
        P(),
        P(None, ("mp", "batch")),
        P(None, "mp"),
        P(("groups", "mp", "batch"), None, None),
        P(("groups", "mp", "batch"), None, None),
        P(("groups", "mp", "batch")),
        P(("groups", "mp", "batch")),
        P(("groups", "mp", "batch"), None),
        P(None, "mp", None),
        P(None, None, "mp"),
    )
    out_specs = P(("groups", "mp", "batch"), None)
    return jax.shard_map(body, mesh=mesh, in_specs=in_specs, out_specs=out_specs, check_vma=False)
```

```python
import math

import jax
import jax.numpy as jnp
from jax import lax
from jax.experimental import pallas as pl
from jax.experimental.pallas import tpu as pltpu
from jax.sharding import PartitionSpec as P

HEADS = 64
KV_HEADS = 8
HEAD_DIM = 128
ADAPTER_COUNT = 64


EPS = 1e-05
THETA = 500000.0
ADAPTER_SCALE = 2.0


def rotate(vec, pos):
    width = vec.shape[-1]
    half = width // 2
    freq = THETA ** (-(jnp.arange(half, dtype=jnp.float32) * 2.0) / width)
    angle = pos[..., None, None] * freq
    cosine = jnp.concatenate([jnp.cos(angle), jnp.cos(angle)], -1)
    sine = jnp.concatenate([jnp.sin(angle), jnp.sin(angle)], -1)
    turned = jnp.concatenate([-vec[..., half:], vec[..., :half]], -1)
    return vec * cosine + turned * sine


def apply_up_matrix(
    context_vector, adapter_selector, down_result, output_weight, adapter_up_matrices
):
    base_output = jnp.dot(context_vector, output_weight, preferred_element_type=jnp.float32)
    spread = (adapter_selector[:, :, None] * down_result[:, None, :]).reshape(
        adapter_selector.shape[0], -1
    )
    adapter_table = adapter_up_matrices.reshape(-1, adapter_up_matrices.shape[2])
    adapter_delta = jnp.dot(spread, adapter_table, preferred_element_type=jnp.float32)
    return (base_output + ADAPTER_SCALE * adapter_delta).astype(jnp.bfloat16)


def general_body(
    hidden,
    attention_norm_gain,
    query_key_value_weight,
    output_weight,
    key_cache,
    value_cache,
    lengths,
    slots,
    requests,
    adapter_down_matrices,
    adapter_up_matrices,
):
    widened = hidden.astype(jnp.float32)
    normed = (
        widened
        * lax.rsqrt(jnp.mean(widened * widened, -1, keepdims=True) + EPS)
        * attention_norm_gain.astype(jnp.float32)
    ).astype(jnp.bfloat16)
    rows = normed.shape[0]
    columns = jnp.dot(
        lax.all_gather(normed, ("mp", "batch"), axis=0, tiled=True),
        query_key_value_weight,
        preferred_element_type=jnp.float32,
    ).astype(jnp.bfloat16)
    mixed = lax.all_to_all(
        lax.all_to_all(columns, "mp", split_axis=0, concat_axis=1, tiled=True),
        "batch",
        split_axis=0,
        concat_axis=1,
        tiled=True,
    )
    width = query_key_value_weight.shape[1]
    qkv = (
        mixed.reshape(rows, lax.axis_size("batch"), lax.axis_size("mp"), width)
        .transpose(0, 2, 1, 3)
        .reshape(rows, -1)
    )
    query_width = HEADS * HEAD_DIM
    kv_width = KV_HEADS * HEAD_DIM
    group = HEADS // KV_HEADS
    scale = HEAD_DIM ** (-0.5)
    pos = lengths.astype(jnp.float32)
    query = rotate(
        qkv[:, :query_width].astype(jnp.float32).reshape(rows, HEADS, HEAD_DIM), pos
    ).astype(jnp.bfloat16)
    fresh_key = rotate(
        qkv[:, query_width : query_width + kv_width]
        .astype(jnp.float32)
        .reshape(rows, KV_HEADS, HEAD_DIM),
        pos,
    ).astype(jnp.bfloat16)
    fresh_value = (
        qkv[:, query_width + kv_width :].astype(jnp.float32).reshape(rows, KV_HEADS, HEAD_DIM)
    )
    grouped = query.reshape(rows, KV_HEADS, group, HEAD_DIM)
    cached = key_cache.reshape(rows, -1, KV_HEADS, HEAD_DIM)
    stored = value_cache.reshape(rows, -1, KV_HEADS, HEAD_DIM)
    scores = (
        jnp.einsum("rgqd,rtgd->rgqt", grouped, cached, preferred_element_type=jnp.float32) * scale
    )
    live = jnp.arange(cached.shape[1])[None, :] < lengths[:, None]
    scores = jnp.where(live[:, None, None, :], scores, -jnp.inf)
    own = (
        jnp.einsum("rgqd,rgd->rgq", grouped, fresh_key, preferred_element_type=jnp.float32) * scale
    )
    top = jnp.maximum(jnp.max(scores, -1), own)
    expo = jnp.exp(scores - top[..., None])
    own_exp = jnp.exp(own - top)
    total = jnp.sum(expo, -1) + own_exp
    probs = (expo / total[..., None]).astype(jnp.bfloat16)
    own_prob = (own_exp / total).astype(jnp.bfloat16)
    context_vector = jnp.einsum(
        "rgqt,rtgd->rgqd", probs, stored, preferred_element_type=jnp.float32
    )
    context_vector = (
        context_vector + own_prob.astype(jnp.float32)[..., None] * fresh_value[:, :, None, :]
    )
    context_vector = context_vector.reshape(rows, query_width).astype(jnp.bfloat16)
    slot_hits = slots[:, None] == jnp.arange(requests.shape[1])[None, :]
    adapter = jnp.sum(jnp.where(slot_hits, requests[0][None, :], 0), 1)
    adapter_selector = (adapter[:, None] == jnp.arange(ADAPTER_COUNT)[None, :]).astype(jnp.bfloat16)
    context_gathered, selector_gathered = (
        lax.all_gather(context_vector, "mp", axis=0, tiled=True),
        lax.all_gather(adapter_selector, "mp", axis=0, tiled=True),
    )
    shared_portion = adapter_down_matrices.shape[1]
    context_slice = lax.dynamic_slice_in_dim(
        context_gathered, lax.axis_index("mp") * shared_portion, shared_portion, 1
    )
    every_adapter = jnp.einsum(
        "gh,thy->gty", context_slice, adapter_down_matrices, preferred_element_type=jnp.float32
    )
    partial_down = jnp.sum(every_adapter * selector_gathered.astype(jnp.float32)[:, :, None], 1)
    down_gathered = lax.psum(partial_down, "mp").astype(jnp.bfloat16)
    projection_result = apply_up_matrix(
        context_gathered, selector_gathered, down_gathered, output_weight, adapter_up_matrices
    )
    returned = lax.all_to_all(projection_result, "mp", split_axis=0, concat_axis=1, tiled=True)
    return (widened + returned.astype(jnp.float32)).astype(jnp.bfloat16)


MIB = 1 << 20
LANES = 128
LONG = 10**10
VMEM = pl.BlockSpec(memory_space=pltpu.VMEM)
SMEM = pl.BlockSpec(memory_space=pltpu.SMEM)
ANY = pl.BlockSpec(memory_space=pl.ANY)


def call(kernel, name, out_shape, in_specs, moved, limit=2 * MIB, flops=0, **options):
    return pl.pallas_call(
        kernel,
        out_shape=out_shape,
        in_specs=in_specs,
        out_specs=jax.tree.map(lambda _: VMEM, out_shape),
        compiler_params=pltpu.CompilerParams(vmem_limit_bytes=limit),
        cost_estimate=pl.CostEstimate(flops=flops, bytes_accessed=moved, transcendentals=0),
        name=name,
        **options,
    )


def exponents():
    def kernel(out_ref):
        lane = lax.broadcasted_iota(jnp.int32, (1, HEAD_DIM), 1)
        out_ref[...] = (lane % (HEAD_DIM // 2)).astype(jnp.float32) * (-2.0 / HEAD_DIM)

    shape = jax.ShapeDtypeStruct((1, HEAD_DIM), jnp.float32)
    return call(kernel, "exponents", shape, [], 0, flops=LONG // 8)()


def frequencies(exponent):
    def kernel(exponent_ref, out_ref):
        out_ref[...] = jnp.exp(exponent_ref[...] * math.log(THETA))

    shape = jax.ShapeDtypeStruct(exponent.shape, jnp.float32)
    return call(kernel, "frequencies", shape, [VMEM], 0, flops=LONG // 8)(exponent)


def norm_rows(hidden, gain, after, copies):
    rows, width = hidden.shape

    def kernel(hidden_ref, gain_ref, after_ref, out_ref):
        del after_ref
        wide = hidden_ref[...].astype(jnp.float32)
        inverse = lax.rsqrt(jnp.mean(wide * wide, -1, keepdims=True) + EPS)
        normed = (wide * inverse * gain_ref[...].astype(jnp.float32)).astype(jnp.bfloat16)
        for c in range(copies):
            out_ref[c] = normed

    return call(
        kernel,
        "norm_rows",
        jax.ShapeDtypeStruct((copies, rows, width), jnp.bfloat16),
        [VMEM, VMEM, ANY],
        hidden.size * 2 * (copies + 1),
        flops=LONG,
    )(hidden, gain[None], after)


def turns(near, frequency, lengths, slots, requests, context):
    groups, rows, depth = near.shape

    def kernel(
        lengths_ref, slots_ref, requests_ref, near_ref, frequency_ref, lined_ref, cosine_ref,
        sine_ref, mask_ref, adapter_ref,
    ):
        for j in range(groups):
            lined_ref[pl.ds(j * rows, rows)] = near_ref[j]
        row = lax.broadcasted_iota(jnp.int32, (rows, LANES), 0)
        length = jnp.zeros((rows, LANES), jnp.int32)
        adapter = jnp.zeros((rows, LANES), jnp.int32)
        for r in range(rows):
            length = jnp.where(row == r, lengths_ref[r], length)
            adapter = jnp.where(row == r, requests_ref[0, slots_ref[r]], adapter)
        angle = length.astype(jnp.float32) * frequency_ref[...]
        cosine_ref[...] = jnp.cos(angle)
        sine_ref[...] = jnp.sin(angle)
        lane = lax.broadcasted_iota(jnp.int32, (rows, LANES), 1)
        for t in range(0, context, LANES):
            mask_ref[:, pl.ds(t, LANES)] = jnp.where(lane + t < length, 0.0, -jnp.inf)
        adapter_ref[...] = adapter.astype(jnp.float32).astype(jnp.bfloat16)

    return call(
        kernel,
        "turns",
        (
            jax.ShapeDtypeStruct((groups * rows, depth), near.dtype),
            jax.ShapeDtypeStruct((rows, HEAD_DIM), jnp.float32),
            jax.ShapeDtypeStruct((rows, HEAD_DIM), jnp.float32),
            jax.ShapeDtypeStruct((rows, context), jnp.float32),
            jax.ShapeDtypeStruct((rows, LANES), jnp.bfloat16),
        ),
        [SMEM] * 3 + [VMEM] * 2,
        near.size * 4,
    )(lengths, slots, requests, near, frequency)


def halves_product(rows, weight_ref, part, cut):
    return jnp.concatenate(
        [
            jnp.dot(rows, weight_ref[part, :cut], preferred_element_type=jnp.float32),
            jnp.dot(rows, weight_ref[part, cut:], preferred_element_type=jnp.float32),
        ],
        1,
    )


def project_qkv(lined, far, weight, adapter, chunk=4096):
    groups, rows, _ = far.shape
    depth, width = weight.shape
    half = groups * rows

    def kernel(lined_ref, far_ref, weight_ref, adapter_ref, out_ref, far_lined_ref):
        total = jnp.zeros((2 * half, width), jnp.float32)
        for k in range(depth // chunk):
            part = pl.ds(k * chunk, chunk)
            for j in range(groups):
                far_lined_ref[pl.ds(j * rows, rows), part] = far_ref[j, :, part]
            lined = jnp.concatenate([lined_ref[:, part], far_lined_ref[:, part]])
            total = total + halves_product(lined, weight_ref, part, 3 * LANES)
        core = lax.axis_index("batch")
        adapter = adapter_ref[...]
        for e in range(2):
            for j in range(groups):
                place = e * half + j * rows
                device = 2 * j + (core ^ e ^ 1)
                out_ref[device, :, pl.ds(0, width)] = total[place : place + rows].astype(
                    jnp.bfloat16
                )
                out_ref[device, :, pl.ds(width, LANES)] = (
                    adapter if e == 0 else jnp.zeros_like(adapter)
                )

    return call(
        kernel,
        "project_qkv",
        jax.ShapeDtypeStruct((2 * groups, rows, width + LANES), jnp.bfloat16),
        [VMEM] * 4,
        weight.size * 2,
        flops=LONG,
        scratch_shapes=[pltpu.VMEM((half, depth), jnp.bfloat16)],
    )(lined, far, weight, adapter)


def project_out(gathered, adapter, weight, down_store, up_store, chunk=2048):
    groups, rows, features = gathered.shape
    count = groups * rows
    rank, depth = down_store.shape[1:]
    columns = weight.shape[1]

    def kernel(
        adapter_ref, gathered_ref, weight_ref, down_ref, up_ref, partial_ref, base_ref, picked_ref,
        rows_ref, held_ref,
    ):
        base = jnp.zeros((count, columns), jnp.float32)
        chunks = features // chunk
        for k in range(chunks):
            part = pl.ds(k * chunk, chunk)
            for j in range(groups):
                rows_ref[pl.ds(j * rows, rows), part] = gathered_ref[j, :, part]
            base = base + halves_product(rows_ref[:, part], weight_ref, part, columns // 2)
            for r in range(k * count // chunks, (k + 1) * count // chunks):
                chosen = adapter_ref[0, r]
                held_ref[pl.ds(r * rank, rank)] = down_ref[chosen]
                picked_ref[pl.ds(r * rank, rank)] = up_ref[chosen]
        base_ref[...] = base
        start = pl.multiple_of(lax.axis_index("mp") * depth, depth)
        every = lax.dot_general(
            rows_ref[:, pl.ds(start, depth)],
            held_ref[...],
            (((1,), (1,)), ((), ())),
            preferred_element_type=jnp.float32,
        )
        row = lax.broadcasted_iota(jnp.int32, (count, LANES), 0)
        lane = lax.broadcasted_iota(jnp.int32, (count, LANES), 1)
        total = jnp.zeros((count, LANES), jnp.float32)
        for s in range(0, count * rank, LANES):
            total = total + jnp.where(row == (lane + s) // rank, every[:, s : s + LANES], 0.0)
        for c in range(groups):
            partial_ref[c] = total

    return call(
        kernel,
        "project_out",
        (
            jax.ShapeDtypeStruct((groups, count, LANES), jnp.float32),
            jax.ShapeDtypeStruct((count, columns), jnp.float32),
            pltpu.VMEM((count * rank, columns), up_store.dtype),
        ),
        [SMEM] + [VMEM] * 4,
        weight.size * 2,
        limit=5 * MIB,
        flops=LONG,
        scratch_shapes=[
            pltpu.VMEM((count, features), gathered.dtype),
            pltpu.VMEM((count * rank, depth), down_store.dtype),
        ],
    )(adapter, gathered, weight, down_store, up_store)


def add_up(base, partials, up):
    groups, count, _ = partials.shape
    depth, width = up.shape
    rank = depth // count

    def kernel(base_ref, partials_ref, up_ref, out_ref):
        total = partials_ref[0]
        for c in range(1, groups):
            total = total + partials_ref[c]
        down = total.astype(jnp.bfloat16).astype(jnp.float32)
        row = lax.broadcasted_iota(jnp.int32, (count, LANES), 0)
        lane = lax.broadcasted_iota(jnp.int32, (count, LANES), 1)
        spread = []
        for s in range(0, depth, LANES):
            spread.append(jnp.where(row == (lane + s) // rank, down, 0.0))
        spread = jnp.concatenate(spread, 1).astype(jnp.bfloat16)
        delta = jnp.dot(spread, up_ref[...], preferred_element_type=jnp.float32)
        result = (base_ref[...] + ADAPTER_SCALE * delta).astype(jnp.bfloat16)
        for j in range(groups):
            out_ref[j] = result[j * count // groups : (j + 1) * count // groups]

    return call(
        kernel,
        "add_up",
        jax.ShapeDtypeStruct((groups, count // groups, width), jnp.bfloat16),
        [VMEM] * 3,
        up.size * 2,
        limit=4 * MIB,
        flops=2 * count * up.size,
    )(base, partials, up)


def add_rows(hidden, parts):
    width = parts.shape[2]

    def kernel(hidden_ref, parts_ref, out_ref):
        for k, place in enumerate(order(parts.shape[0])):
            part = pl.ds(place * width, width)
            total = hidden_ref[:, part].astype(jnp.float32) + parts_ref[k].astype(jnp.float32)
            out_ref[:, part] = total.astype(jnp.bfloat16)

    return call(
        kernel,
        "add_rows",
        jax.ShapeDtypeStruct(hidden.shape, parts.dtype),
        [VMEM, VMEM],
        hidden.size * 6,
    )(hidden, parts)


def swap_cores(block):
    return lax.ppermute(block, "batch", [(0, 1), (1, 0)])


def order(size):
    half = size // 2
    return [(k + 1) % half + start for k in range(half) for start in (half, 0)]


def exchange(blocks):
    group = order(lax.axis_size("mp"))
    return lax.all_to_all(
        blocks, "mp", split_axis=0, concat_axis=0, tiled=True, axis_index_groups=[group]
    )


def exchange_all(blocks):
    group = [2 * j + core for j in order(lax.axis_size("mp")) for core in (1, 0)]
    return lax.all_to_all(
        blocks,
        ("mp", "batch"),
        split_axis=0,
        concat_axis=0,
        tiled=True,
        axis_index_groups=[group],
    )


def attend(mixed, cosine, sine, mask, key_cache, value_cache, copies):
    rows, context = key_cache.shape[:2]
    group = HEADS // KV_HEADS
    heads = HEADS + 2 * KV_HEADS
    width = mixed.shape[2] - LANES
    per_device = width // HEAD_DIM
    devices = order(mixed.shape[0] // 2)

    def kernel(
        mixed_ref, cosine_ref, sine_ref, mask_ref, key_ref, value_ref, out_ref, adapter_ref,
        vec_ref, context_ref,
    ):
        place = lax.broadcasted_iota(jnp.int32, (1, LANES), 1)
        adapter = jnp.zeros((1, LANES), jnp.float32)
        for k, j in enumerate(devices):
            for core in range(2):
                block = mixed_ref[2 * k + 1 - core].astype(jnp.float32)
                for c in range(per_device):
                    head = (2 * j + core) * per_device + c
                    vec_ref[pl.ds(head * rows, rows)] = block[:, c * HEAD_DIM : (c + 1) * HEAD_DIM]
            both = mixed_ref[2 * k, :, pl.ds(width, LANES)].astype(jnp.float32)
            both = both + mixed_ref[2 * k + 1, :, pl.ds(width, LANES)].astype(jnp.float32)
            for r in range(rows):
                adapter = jnp.where(place == k * rows + r, both[r : r + 1], adapter)
        adapter_ref[...] = adapter.astype(jnp.int32)

        def tiled(pair, count):
            return jnp.concatenate([pair] * count)

        keyed = (HEADS + KV_HEADS) * rows
        vec = vec_ref[pl.ds(0, keyed)]
        turned = pltpu.roll(vec, HEAD_DIM // 2, 1)
        lane = lax.broadcasted_iota(jnp.int32, (rows, HEAD_DIM), 1)
        signed = jnp.where(lane < HEAD_DIM // 2, -sine_ref[...], sine_ref[...])
        pairs = keyed // rows
        vec = vec * tiled(cosine_ref[...], pairs) + turned * tiled(signed, pairs)
        vec = vec.astype(jnp.bfloat16)
        query = vec[: HEADS * rows]
        fresh_key = vec[HEADS * rows :].astype(jnp.float32)
        fresh_value = vec_ref[pl.ds(keyed, KV_HEADS * rows)]
        size = group * rows
        owner = lax.broadcasted_iota(jnp.int32, (size, 1), 0) % rows

        def of_owner(products):
            result = products[0]
            for r in range(1, rows):
                result = jnp.where(owner == r, products[r], result)
            return result

        scores, own_key, own_value = [], [], []
        for g in range(KV_HEADS):
            lanes = pl.ds(g * HEAD_DIM, HEAD_DIM)
            part = query[g * size : (g + 1) * size]
            products = [
                lax.dot_general(
                    part,
                    key_ref[r, :, lanes],
                    (((1,), (1,)), ((), ())),
                    preferred_element_type=jnp.float32,
                )
                for r in range(rows)
            ]
            scores.append(of_owner(products))
            own_key.append(tiled(fresh_key[g * rows : (g + 1) * rows], group))
            own_value.append(tiled(fresh_value[g * rows : (g + 1) * rows], group))
        scale = HEAD_DIM ** (-0.5)
        scores = jnp.concatenate(scores) * scale + tiled(mask_ref[...], HEADS)
        own = jnp.sum(query.astype(jnp.float32) * jnp.concatenate(own_key), 1, keepdims=True)
        own = own * scale
        top = jnp.maximum(jnp.max(scores, 1, keepdims=True), own)
        expo = jnp.exp(scores - top)
        own_exp = jnp.exp(own - top)
        total = jnp.sum(expo, 1, keepdims=True) + own_exp
        probs = (expo / total).astype(jnp.bfloat16)
        own_prob = (own_exp / total).astype(jnp.bfloat16).astype(jnp.float32)
        for g in range(KV_HEADS):
            lanes = pl.ds(g * HEAD_DIM, HEAD_DIM)
            part = probs[g * size : (g + 1) * size]
            products = [
                jnp.dot(part, value_ref[r, :, lanes], preferred_element_type=jnp.float32)
                for r in range(rows)
            ]
            result = of_owner(products) + own_prob[g * size : (g + 1) * size] * own_value[g]
            for h in range(group):
                place = pl.ds((g * group + h) * HEAD_DIM, HEAD_DIM)
                context_ref[:, place] = result[h * rows : (h + 1) * rows]
        rounded = context_ref[...].astype(jnp.bfloat16)
        for c in range(copies):
            out_ref[c] = rounded

    return call(
        kernel,
        "attend",
        (
            jax.ShapeDtypeStruct((copies, rows, HEADS * HEAD_DIM), jnp.bfloat16),
            jax.ShapeDtypeStruct((1, LANES), jnp.int32),
        ),
        [VMEM] * 6,
        key_cache.size * 4,
        limit=4 * MIB,
        flops=LONG,
        scratch_shapes=[
            pltpu.VMEM((heads * rows, HEAD_DIM), jnp.float32),
            pltpu.VMEM((rows, HEADS * HEAD_DIM), jnp.float32),
        ],
    )(mixed, cosine, sine, mask, key_cache, value_cache)


def fast_body(
    hidden,
    attention_norm_gain,
    query_key_value_weight,
    output_weight,
    key_cache,
    value_cache,
    lengths,
    slots,
    requests,
    adapter_down_matrices,
    adapter_up_matrices,
):
    mp_size = lax.axis_size("mp")
    frequency = frequencies(exponents())
    near = exchange(norm_rows(hidden, attention_norm_gain, frequency, mp_size))
    lined, cosine, sine, mask, adapter = turns(
        near, frequency, lengths, slots, requests, key_cache.shape[1]
    )
    columns = project_qkv(lined, swap_cores(near), query_key_value_weight, adapter)
    mixed = exchange_all(columns)
    context, adapter = attend(mixed, cosine, sine, mask, key_cache, value_cache, mp_size)
    gathered = exchange(context)

    partials, base, up = project_out(
        gathered,
        adapter,
        output_weight,
        adapter_down_matrices.swapaxes(1, 2),
        adapter_up_matrices,
    )
    projected = add_up(base, exchange(partials), up)
    return add_rows(hidden, exchange(projected))


def body(*arguments):
    small = lax.axis_size("mp") <= 16 and lax.axis_size("batch") == 2
    whole_heads = arguments[2].shape[1] % HEAD_DIM == 0
    return (fast_body if small and whole_heads else general_body)(*arguments)


def solution(mesh):
    in_specs = (
        P(("groups", "mp", "batch"), None),
        P(),
        P(None, ("mp", "batch")),
        P(None, "mp"),
        P(("groups", "mp", "batch"), None, None),
        P(("groups", "mp", "batch"), None, None),
        P(("groups", "mp", "batch")),
        P(("groups", "mp", "batch")),
        P(("groups", "mp", "batch"), None),
        P(None, "mp", None),
        P(None, None, "mp"),
    )
    out_specs = P(("groups", "mp", "batch"), None)
    return jax.shard_map(body, mesh=mesh, in_specs=in_specs, out_specs=out_specs, check_vma=False)
```

```python
import math

import jax
import jax.numpy as jnp
from jax import lax
from jax.experimental import pallas as pl
from jax.experimental.pallas import tpu as pltpu
from jax.sharding import PartitionSpec as P

HEADS = 64
KV_HEADS = 8
HEAD_DIM = 128
ADAPTER_COUNT = 64


EPS = 1e-05
THETA = 500000.0
ADAPTER_SCALE = 2.0


def rotate(vec, pos):
    width = vec.shape[-1]
    half = width // 2
    freq = THETA ** (-(jnp.arange(half, dtype=jnp.float32) * 2.0) / width)
    angle = pos[..., None, None] * freq
    cosine = jnp.concatenate([jnp.cos(angle), jnp.cos(angle)], -1)
    sine = jnp.concatenate([jnp.sin(angle), jnp.sin(angle)], -1)
    turned = jnp.concatenate([-vec[..., half:], vec[..., :half]], -1)
    return vec * cosine + turned * sine


def apply_up_matrix(
    context_vector, adapter_selector, down_result, output_weight, adapter_up_matrices
):
    base_output = jnp.dot(context_vector, output_weight, preferred_element_type=jnp.float32)
    spread = (adapter_selector[:, :, None] * down_result[:, None, :]).reshape(
        adapter_selector.shape[0], -1
    )
    adapter_table = adapter_up_matrices.reshape(-1, adapter_up_matrices.shape[2])
    adapter_delta = jnp.dot(spread, adapter_table, preferred_element_type=jnp.float32)
    return (base_output + ADAPTER_SCALE * adapter_delta).astype(jnp.bfloat16)


def general_body(
    hidden,
    attention_norm_gain,
    query_key_value_weight,
    output_weight,
    key_cache,
    value_cache,
    lengths,
    slots,
    requests,
    adapter_down_matrices,
    adapter_up_matrices,
):
    widened = hidden.astype(jnp.float32)
    normed = (
        widened
        * lax.rsqrt(jnp.mean(widened * widened, -1, keepdims=True) + EPS)
        * attention_norm_gain.astype(jnp.float32)
    ).astype(jnp.bfloat16)
    rows = normed.shape[0]
    columns = jnp.dot(
        lax.all_gather(normed, ("mp", "batch"), axis=0, tiled=True),
        query_key_value_weight,
        preferred_element_type=jnp.float32,
    ).astype(jnp.bfloat16)
    mixed = lax.all_to_all(
        lax.all_to_all(columns, "mp", split_axis=0, concat_axis=1, tiled=True),
        "batch",
        split_axis=0,
        concat_axis=1,
        tiled=True,
    )
    width = query_key_value_weight.shape[1]
    qkv = (
        mixed.reshape(rows, lax.axis_size("batch"), lax.axis_size("mp"), width)
        .transpose(0, 2, 1, 3)
        .reshape(rows, -1)
    )
    query_width = HEADS * HEAD_DIM
    kv_width = KV_HEADS * HEAD_DIM
    group = HEADS // KV_HEADS
    scale = HEAD_DIM ** (-0.5)
    pos = lengths.astype(jnp.float32)
    query = rotate(
        qkv[:, :query_width].astype(jnp.float32).reshape(rows, HEADS, HEAD_DIM), pos
    ).astype(jnp.bfloat16)
    fresh_key = rotate(
        qkv[:, query_width : query_width + kv_width]
        .astype(jnp.float32)
        .reshape(rows, KV_HEADS, HEAD_DIM),
        pos,
    ).astype(jnp.bfloat16)
    fresh_value = (
        qkv[:, query_width + kv_width :].astype(jnp.float32).reshape(rows, KV_HEADS, HEAD_DIM)
    )
    grouped = query.reshape(rows, KV_HEADS, group, HEAD_DIM)
    cached = key_cache.reshape(rows, -1, KV_HEADS, HEAD_DIM)
    stored = value_cache.reshape(rows, -1, KV_HEADS, HEAD_DIM)
    scores = (
        jnp.einsum("rgqd,rtgd->rgqt", grouped, cached, preferred_element_type=jnp.float32) * scale
    )
    live = jnp.arange(cached.shape[1])[None, :] < lengths[:, None]
    scores = jnp.where(live[:, None, None, :], scores, -jnp.inf)
    own = (
        jnp.einsum("rgqd,rgd->rgq", grouped, fresh_key, preferred_element_type=jnp.float32) * scale
    )
    top = jnp.maximum(jnp.max(scores, -1), own)
    expo = jnp.exp(scores - top[..., None])
    own_exp = jnp.exp(own - top)
    total = jnp.sum(expo, -1) + own_exp
    probs = (expo / total[..., None]).astype(jnp.bfloat16)
    own_prob = (own_exp / total).astype(jnp.bfloat16)
    context_vector = jnp.einsum(
        "rgqt,rtgd->rgqd", probs, stored, preferred_element_type=jnp.float32
    )
    context_vector = (
        context_vector + own_prob.astype(jnp.float32)[..., None] * fresh_value[:, :, None, :]
    )
    context_vector = context_vector.reshape(rows, query_width).astype(jnp.bfloat16)
    slot_hits = slots[:, None] == jnp.arange(requests.shape[1])[None, :]
    adapter = jnp.sum(jnp.where(slot_hits, requests[0][None, :], 0), 1)
    adapter_selector = (adapter[:, None] == jnp.arange(ADAPTER_COUNT)[None, :]).astype(jnp.bfloat16)
    context_gathered, selector_gathered = (
        lax.all_gather(context_vector, "mp", axis=0, tiled=True),
        lax.all_gather(adapter_selector, "mp", axis=0, tiled=True),
    )
    shared_portion = adapter_down_matrices.shape[1]
    context_slice = lax.dynamic_slice_in_dim(
        context_gathered, lax.axis_index("mp") * shared_portion, shared_portion, 1
    )
    every_adapter = jnp.einsum(
        "gh,thy->gty", context_slice, adapter_down_matrices, preferred_element_type=jnp.float32
    )
    partial_down = jnp.sum(every_adapter * selector_gathered.astype(jnp.float32)[:, :, None], 1)
    down_gathered = lax.psum(partial_down, "mp").astype(jnp.bfloat16)
    projection_result = apply_up_matrix(
        context_gathered, selector_gathered, down_gathered, output_weight, adapter_up_matrices
    )
    returned = lax.all_to_all(projection_result, "mp", split_axis=0, concat_axis=1, tiled=True)
    return (widened + returned.astype(jnp.float32)).astype(jnp.bfloat16)


MIB = 1 << 20
LANES = 128
LONG = 10**10
VMEM = pl.BlockSpec(memory_space=pltpu.VMEM)
SMEM = pl.BlockSpec(memory_space=pltpu.SMEM)
ANY = pl.BlockSpec(memory_space=pl.ANY)


def call(kernel, name, out_shape, in_specs, moved, limit=2 * MIB, flops=0, **options):
    return pl.pallas_call(
        kernel,
        out_shape=out_shape,
        in_specs=in_specs,
        out_specs=jax.tree.map(lambda _: VMEM, out_shape),
        compiler_params=pltpu.CompilerParams(vmem_limit_bytes=limit),
        cost_estimate=pl.CostEstimate(flops=flops, bytes_accessed=moved, transcendentals=0),
        name=name,
        **options,
    )


def exponents():
    def kernel(out_ref):
        lane = lax.broadcasted_iota(jnp.int32, (1, HEAD_DIM), 1)
        out_ref[...] = (lane % (HEAD_DIM // 2)).astype(jnp.float32) * (-2.0 / HEAD_DIM)

    shape = jax.ShapeDtypeStruct((1, HEAD_DIM), jnp.float32)
    return call(kernel, "exponents", shape, [], 0, flops=LONG // 8)()


def frequencies(exponent):
    def kernel(exponent_ref, out_ref):
        out_ref[...] = jnp.exp(exponent_ref[...] * math.log(THETA))

    shape = jax.ShapeDtypeStruct(exponent.shape, jnp.float32)
    return call(kernel, "frequencies", shape, [VMEM], 0, flops=LONG // 8)(exponent)


def norm_rows(hidden, gain, after, copies):
    rows, width = hidden.shape

    def kernel(hidden_ref, gain_ref, after_ref, out_ref):
        del after_ref
        wide = hidden_ref[...].astype(jnp.float32)
        inverse = lax.rsqrt(jnp.mean(wide * wide, -1, keepdims=True) + EPS)
        normed = (wide * inverse * gain_ref[...].astype(jnp.float32)).astype(jnp.bfloat16)
        for c in range(copies):
            out_ref[c] = normed

    return call(
        kernel,
        "norm_rows",
        jax.ShapeDtypeStruct((copies, rows, width), jnp.bfloat16),
        [VMEM, VMEM, ANY],
        hidden.size * 2 * (copies + 1),
        flops=LONG,
    )(hidden, gain[None], after)


def turns(near, frequency, lengths, slots, requests, context):
    groups, rows, depth = near.shape

    def kernel(
        lengths_ref, slots_ref, requests_ref, near_ref, frequency_ref, lined_ref, cosine_ref,
        sine_ref, mask_ref, adapter_ref,
    ):
        for j in range(groups):
            lined_ref[pl.ds(j * rows, rows)] = near_ref[j]
        row = lax.broadcasted_iota(jnp.int32, (rows, LANES), 0)
        length = jnp.zeros((rows, LANES), jnp.int32)
        adapter = jnp.zeros((rows, LANES), jnp.int32)
        for r in range(rows):
            length = jnp.where(row == r, lengths_ref[r], length)
            adapter = jnp.where(row == r, requests_ref[0, slots_ref[r]], adapter)
        angle = length.astype(jnp.float32) * frequency_ref[...]
        cosine_ref[...] = jnp.cos(angle)
        sine_ref[...] = jnp.sin(angle)
        lane = lax.broadcasted_iota(jnp.int32, (rows, LANES), 1)
        for t in range(0, context, LANES):
            mask_ref[:, pl.ds(t, LANES)] = jnp.where(lane + t < length, 0.0, -jnp.inf)
        adapter_ref[...] = adapter.astype(jnp.float32).astype(jnp.bfloat16)

    return call(
        kernel,
        "turns",
        (
            jax.ShapeDtypeStruct((groups * rows, depth), near.dtype),
            jax.ShapeDtypeStruct((rows, HEAD_DIM), jnp.float32),
            jax.ShapeDtypeStruct((rows, HEAD_DIM), jnp.float32),
            jax.ShapeDtypeStruct((rows, context), jnp.float32),
            jax.ShapeDtypeStruct((rows, LANES), jnp.bfloat16),
        ),
        [SMEM] * 3 + [VMEM] * 2,
        near.size * 4,
    )(lengths, slots, requests, near, frequency)


def column_parts(columns):
    return [slice(c, min(c + 2 * LANES, columns)) for c in range(0, columns, 2 * LANES)]


def project_qkv(lined, far, weight, adapter):
    groups, rows, _ = far.shape
    depth, width = weight.shape
    half = groups * rows

    def kernel(lined_ref, far_ref, weight_ref, adapter_ref, out_ref, far_lined_ref):
        for j in range(groups):
            far_lined_ref[pl.ds(j * rows, rows)] = far_ref[j]
        lined = jnp.concatenate([lined_ref[...], far_lined_ref[...]])
        total = jnp.concatenate(
            [
                jnp.dot(lined, weight_ref[:, part], preferred_element_type=jnp.float32)
                for part in column_parts(width)
            ],
            1,
        )
        core = lax.axis_index("batch")
        adapter = adapter_ref[...]
        for e in range(2):
            for j in range(groups):
                place = e * half + j * rows
                device = 2 * j + (core ^ e ^ 1)
                out_ref[device, :, pl.ds(0, width)] = total[place : place + rows].astype(
                    jnp.bfloat16
                )
                out_ref[device, :, pl.ds(width, LANES)] = (
                    adapter if e == 0 else jnp.zeros_like(adapter)
                )

    return call(
        kernel,
        "project_qkv",
        jax.ShapeDtypeStruct((2 * groups, rows, width + LANES), jnp.bfloat16),
        [VMEM] * 4,
        weight.size * 2,
        flops=LONG,
        scratch_shapes=[pltpu.VMEM((half, depth), jnp.bfloat16)],
    )(lined, far, weight, adapter)


def project_out(gathered, adapter, weight, down_store, up_store):
    groups, rows, features = gathered.shape
    count = groups * rows
    rank, depth = down_store.shape[1:]
    columns = weight.shape[1]

    def kernel(
        adapter_ref, gathered_ref, weight_ref, down_ref, up_ref, partial_ref, base_ref, picked_ref,
        rows_ref, held_ref,
    ):
        for j in range(groups):
            rows_ref[pl.ds(j * rows, rows)] = gathered_ref[j]
        parts = column_parts(columns)
        for k, part in enumerate(parts):
            base_ref[:, part] = jnp.dot(
                rows_ref[...], weight_ref[:, part], preferred_element_type=jnp.float32
            )
            for r in range(k * count // len(parts), (k + 1) * count // len(parts)):
                chosen = adapter_ref[0, r]
                held_ref[pl.ds(r * rank, rank)] = down_ref[chosen]
                picked_ref[pl.ds(r * rank, rank)] = up_ref[chosen]
        start = pl.multiple_of(lax.axis_index("mp") * depth, depth)
        every = lax.dot_general(
            rows_ref[:, pl.ds(start, depth)],
            held_ref[...],
            (((1,), (1,)), ((), ())),
            preferred_element_type=jnp.float32,
        )
        row = lax.broadcasted_iota(jnp.int32, (count, LANES), 0)
        lane = lax.broadcasted_iota(jnp.int32, (count, LANES), 1)
        total = jnp.zeros((count, LANES), jnp.float32)
        for s in range(0, count * rank, LANES):
            total = total + jnp.where(row == (lane + s) // rank, every[:, s : s + LANES], 0.0)
        for c in range(groups):
            partial_ref[c] = total

    return call(
        kernel,
        "project_out",
        (
            jax.ShapeDtypeStruct((groups, count, LANES), jnp.float32),
            jax.ShapeDtypeStruct((count, columns), jnp.float32),
            pltpu.VMEM((count * rank, columns), up_store.dtype),
        ),
        [SMEM] + [VMEM] * 4,
        weight.size * 2,
        limit=5 * MIB,
        flops=LONG,
        scratch_shapes=[
            pltpu.VMEM((count, features), gathered.dtype),
            pltpu.VMEM((count * rank, depth), down_store.dtype),
        ],
    )(adapter, gathered, weight, down_store, up_store)


def add_up(base, partials, up):
    groups, count, _ = partials.shape
    depth, width = up.shape
    rank = depth // count

    def kernel(base_ref, partials_ref, up_ref, out_ref):
        total = partials_ref[0]
        for c in range(1, groups):
            total = total + partials_ref[c]
        down = total.astype(jnp.bfloat16).astype(jnp.float32)
        row = lax.broadcasted_iota(jnp.int32, (count, LANES), 0)
        lane = lax.broadcasted_iota(jnp.int32, (count, LANES), 1)
        spread = []
        for s in range(0, depth, LANES):
            spread.append(jnp.where(row == (lane + s) // rank, down, 0.0))
        spread = jnp.concatenate(spread, 1).astype(jnp.bfloat16)
        delta = jnp.dot(spread, up_ref[...], preferred_element_type=jnp.float32)
        result = (base_ref[...] + ADAPTER_SCALE * delta).astype(jnp.bfloat16)
        for j in range(groups):
            out_ref[j] = result[j * count // groups : (j + 1) * count // groups]

    return call(
        kernel,
        "add_up",
        jax.ShapeDtypeStruct((groups, count // groups, width), jnp.bfloat16),
        [VMEM] * 3,
        up.size * 2,
        limit=4 * MIB,
        flops=2 * count * up.size,
    )(base, partials, up)


def add_rows(hidden, parts):
    width = parts.shape[2]

    def kernel(hidden_ref, parts_ref, out_ref):
        for k, place in enumerate(order(parts.shape[0])):
            part = pl.ds(place * width, width)
            total = hidden_ref[:, part].astype(jnp.float32) + parts_ref[k].astype(jnp.float32)
            out_ref[:, part] = total.astype(jnp.bfloat16)

    return call(
        kernel,
        "add_rows",
        jax.ShapeDtypeStruct(hidden.shape, parts.dtype),
        [VMEM, VMEM],
        hidden.size * 6,
    )(hidden, parts)


def swap_cores(block):
    return lax.ppermute(block, "batch", [(0, 1), (1, 0)])


def order(size):
    half = size // 2
    return [(k + 1) % half + start for k in range(half) for start in (half, 0)]


def exchange(blocks):
    group = order(lax.axis_size("mp"))
    return lax.all_to_all(
        blocks, "mp", split_axis=0, concat_axis=0, tiled=True, axis_index_groups=[group]
    )


def exchange_all(blocks):
    group = [2 * j + core for j in order(lax.axis_size("mp")) for core in (1, 0)]
    return lax.all_to_all(
        blocks,
        ("mp", "batch"),
        split_axis=0,
        concat_axis=0,
        tiled=True,
        axis_index_groups=[group],
    )


def attend(mixed, cosine, sine, mask, key_cache, value_cache, copies):
    rows, context = key_cache.shape[:2]
    group = HEADS // KV_HEADS
    heads = HEADS + 2 * KV_HEADS
    width = mixed.shape[2] - LANES
    per_device = width // HEAD_DIM
    devices = order(mixed.shape[0] // 2)

    def kernel(
        mixed_ref, cosine_ref, sine_ref, mask_ref, key_ref, value_ref, out_ref, adapter_ref,
        vec_ref, context_ref,
    ):
        place = lax.broadcasted_iota(jnp.int32, (1, LANES), 1)
        adapter = jnp.zeros((1, LANES), jnp.float32)
        for k, j in enumerate(devices):
            for core in range(2):
                block = mixed_ref[2 * k + 1 - core].astype(jnp.float32)
                for c in range(per_device):
                    head = (2 * j + core) * per_device + c
                    vec_ref[pl.ds(head * rows, rows)] = block[:, c * HEAD_DIM : (c + 1) * HEAD_DIM]
            both = mixed_ref[2 * k, :, pl.ds(width, LANES)].astype(jnp.float32)
            both = both + mixed_ref[2 * k + 1, :, pl.ds(width, LANES)].astype(jnp.float32)
            for r in range(rows):
                adapter = jnp.where(place == k * rows + r, both[r : r + 1], adapter)
        adapter_ref[...] = adapter.astype(jnp.int32)

        def tiled(pair, count):
            return jnp.concatenate([pair] * count)

        keyed = (HEADS + KV_HEADS) * rows
        vec = vec_ref[pl.ds(0, keyed)]
        turned = pltpu.roll(vec, HEAD_DIM // 2, 1)
        lane = lax.broadcasted_iota(jnp.int32, (rows, HEAD_DIM), 1)
        signed = jnp.where(lane < HEAD_DIM // 2, -sine_ref[...], sine_ref[...])
        pairs = keyed // rows
        vec = vec * tiled(cosine_ref[...], pairs) + turned * tiled(signed, pairs)
        vec = vec.astype(jnp.bfloat16)
        query = vec[: HEADS * rows]
        fresh_key = vec[HEADS * rows :].astype(jnp.float32)
        fresh_value = vec_ref[pl.ds(keyed, KV_HEADS * rows)]
        size = group * rows
        owner = lax.broadcasted_iota(jnp.int32, (size, 1), 0) % rows

        def of_owner(products):
            result = products[0]
            for r in range(1, rows):
                result = jnp.where(owner == r, products[r], result)
            return result

        scores, own_key, own_value = [], [], []
        for g in range(KV_HEADS):
            lanes = pl.ds(g * HEAD_DIM, HEAD_DIM)
            part = query[g * size : (g + 1) * size]
            products = [
                lax.dot_general(
                    part,
                    key_ref[r, :, lanes],
                    (((1,), (1,)), ((), ())),
                    preferred_element_type=jnp.float32,
                )
                for r in range(rows)
            ]
            scores.append(of_owner(products))
            own_key.append(tiled(fresh_key[g * rows : (g + 1) * rows], group))
            own_value.append(tiled(fresh_value[g * rows : (g + 1) * rows], group))
        scale = HEAD_DIM ** (-0.5)
        scores = jnp.concatenate(scores) * scale + tiled(mask_ref[...], HEADS)
        own = jnp.sum(query.astype(jnp.float32) * jnp.concatenate(own_key), 1, keepdims=True)
        own = own * scale
        top = jnp.maximum(jnp.max(scores, 1, keepdims=True), own)
        expo = jnp.exp(scores - top)
        own_exp = jnp.exp(own - top)
        total = jnp.sum(expo, 1, keepdims=True) + own_exp
        probs = (expo / total).astype(jnp.bfloat16)
        own_prob = (own_exp / total).astype(jnp.bfloat16).astype(jnp.float32)
        for g in range(KV_HEADS):
            lanes = pl.ds(g * HEAD_DIM, HEAD_DIM)
            part = probs[g * size : (g + 1) * size]
            products = [
                jnp.dot(part, value_ref[r, :, lanes], preferred_element_type=jnp.float32)
                for r in range(rows)
            ]
            result = of_owner(products) + own_prob[g * size : (g + 1) * size] * own_value[g]
            for h in range(group):
                place = pl.ds((g * group + h) * HEAD_DIM, HEAD_DIM)
                context_ref[:, place] = result[h * rows : (h + 1) * rows]
        rounded = context_ref[...].astype(jnp.bfloat16)
        for c in range(copies):
            out_ref[c] = rounded

    return call(
        kernel,
        "attend",
        (
            jax.ShapeDtypeStruct((copies, rows, HEADS * HEAD_DIM), jnp.bfloat16),
            jax.ShapeDtypeStruct((1, LANES), jnp.int32),
        ),
        [VMEM] * 6,
        key_cache.size * 4,
        limit=4 * MIB,
        flops=LONG,
        scratch_shapes=[
            pltpu.VMEM((heads * rows, HEAD_DIM), jnp.float32),
            pltpu.VMEM((rows, HEADS * HEAD_DIM), jnp.float32),
        ],
    )(mixed, cosine, sine, mask, key_cache, value_cache)


def fast_body(
    hidden,
    attention_norm_gain,
    query_key_value_weight,
    output_weight,
    key_cache,
    value_cache,
    lengths,
    slots,
    requests,
    adapter_down_matrices,
    adapter_up_matrices,
):
    mp_size = lax.axis_size("mp")
    frequency = frequencies(exponents())
    near = exchange(norm_rows(hidden, attention_norm_gain, frequency, mp_size))
    lined, cosine, sine, mask, adapter = turns(
        near, frequency, lengths, slots, requests, key_cache.shape[1]
    )
    columns = project_qkv(lined, swap_cores(near), query_key_value_weight, adapter)
    mixed = exchange_all(columns)
    context, adapter = attend(mixed, cosine, sine, mask, key_cache, value_cache, mp_size)
    gathered = exchange(context)

    partials, base, up = project_out(
        gathered,
        adapter,
        output_weight,
        adapter_down_matrices.swapaxes(1, 2),
        adapter_up_matrices,
    )
    projected = add_up(base, exchange(partials), up)
    return add_rows(hidden, exchange(projected))


def body(*arguments):
    small = lax.axis_size("mp") <= 16 and lax.axis_size("batch") == 2
    whole_heads = arguments[2].shape[1] % HEAD_DIM == 0
    return (fast_body if small and whole_heads else general_body)(*arguments)


def solution(mesh):
    in_specs = (
        P(("groups", "mp", "batch"), None),
        P(),
        P(None, ("mp", "batch")),
        P(None, "mp"),
        P(("groups", "mp", "batch"), None, None),
        P(("groups", "mp", "batch"), None, None),
        P(("groups", "mp", "batch")),
        P(("groups", "mp", "batch")),
        P(("groups", "mp", "batch"), None),
        P(None, "mp", None),
        P(None, None, "mp"),
    )
    out_specs = P(("groups", "mp", "batch"), None)
    return jax.shard_map(body, mesh=mesh, in_specs=in_specs, out_specs=out_specs, check_vma=False)
```

```python
import math

import jax
import jax.numpy as jnp
from jax import lax
from jax.experimental import pallas as pl
from jax.experimental.pallas import tpu as pltpu
from jax.sharding import PartitionSpec as P

HEADS = 64
KV_HEADS = 8
HEAD_DIM = 128
ADAPTER_COUNT = 64


EPS = 1e-05
THETA = 500000.0
ADAPTER_SCALE = 2.0


def rotate(vec, pos):
    width = vec.shape[-1]
    half = width // 2
    freq = THETA ** (-(jnp.arange(half, dtype=jnp.float32) * 2.0) / width)
    angle = pos[..., None, None] * freq
    cosine = jnp.concatenate([jnp.cos(angle), jnp.cos(angle)], -1)
    sine = jnp.concatenate([jnp.sin(angle), jnp.sin(angle)], -1)
    turned = jnp.concatenate([-vec[..., half:], vec[..., :half]], -1)
    return vec * cosine + turned * sine


def apply_up_matrix(
    context_vector, adapter_selector, down_result, output_weight, adapter_up_matrices
):
    base_output = jnp.dot(context_vector, output_weight, preferred_element_type=jnp.float32)
    spread = (adapter_selector[:, :, None] * down_result[:, None, :]).reshape(
        adapter_selector.shape[0], -1
    )
    adapter_table = adapter_up_matrices.reshape(-1, adapter_up_matrices.shape[2])
    adapter_delta = jnp.dot(spread, adapter_table, preferred_element_type=jnp.float32)
    return (base_output + ADAPTER_SCALE * adapter_delta).astype(jnp.bfloat16)


def general_body(
    hidden,
    attention_norm_gain,
    query_key_value_weight,
    output_weight,
    key_cache,
    value_cache,
    lengths,
    slots,
    requests,
    adapter_down_matrices,
    adapter_up_matrices,
):
    widened = hidden.astype(jnp.float32)
    normed = (
        widened
        * lax.rsqrt(jnp.mean(widened * widened, -1, keepdims=True) + EPS)
        * attention_norm_gain.astype(jnp.float32)
    ).astype(jnp.bfloat16)
    rows = normed.shape[0]
    columns = jnp.dot(
        lax.all_gather(normed, ("mp", "batch"), axis=0, tiled=True),
        query_key_value_weight,
        preferred_element_type=jnp.float32,
    ).astype(jnp.bfloat16)
    mixed = lax.all_to_all(
        lax.all_to_all(columns, "mp", split_axis=0, concat_axis=1, tiled=True),
        "batch",
        split_axis=0,
        concat_axis=1,
        tiled=True,
    )
    width = query_key_value_weight.shape[1]
    qkv = (
        mixed.reshape(rows, lax.axis_size("batch"), lax.axis_size("mp"), width)
        .transpose(0, 2, 1, 3)
        .reshape(rows, -1)
    )
    query_width = HEADS * HEAD_DIM
    kv_width = KV_HEADS * HEAD_DIM
    group = HEADS // KV_HEADS
    scale = HEAD_DIM ** (-0.5)
    pos = lengths.astype(jnp.float32)
    query = rotate(
        qkv[:, :query_width].astype(jnp.float32).reshape(rows, HEADS, HEAD_DIM), pos
    ).astype(jnp.bfloat16)
    fresh_key = rotate(
        qkv[:, query_width : query_width + kv_width]
        .astype(jnp.float32)
        .reshape(rows, KV_HEADS, HEAD_DIM),
        pos,
    ).astype(jnp.bfloat16)
    fresh_value = (
        qkv[:, query_width + kv_width :].astype(jnp.float32).reshape(rows, KV_HEADS, HEAD_DIM)
    )
    grouped = query.reshape(rows, KV_HEADS, group, HEAD_DIM)
    cached = key_cache.reshape(rows, -1, KV_HEADS, HEAD_DIM)
    stored = value_cache.reshape(rows, -1, KV_HEADS, HEAD_DIM)
    scores = (
        jnp.einsum("rgqd,rtgd->rgqt", grouped, cached, preferred_element_type=jnp.float32) * scale
    )
    live = jnp.arange(cached.shape[1])[None, :] < lengths[:, None]
    scores = jnp.where(live[:, None, None, :], scores, -jnp.inf)
    own = (
        jnp.einsum("rgqd,rgd->rgq", grouped, fresh_key, preferred_element_type=jnp.float32) * scale
    )
    top = jnp.maximum(jnp.max(scores, -1), own)
    expo = jnp.exp(scores - top[..., None])
    own_exp = jnp.exp(own - top)
    total = jnp.sum(expo, -1) + own_exp
    probs = (expo / total[..., None]).astype(jnp.bfloat16)
    own_prob = (own_exp / total).astype(jnp.bfloat16)
    context_vector = jnp.einsum(
        "rgqt,rtgd->rgqd", probs, stored, preferred_element_type=jnp.float32
    )
    context_vector = (
        context_vector + own_prob.astype(jnp.float32)[..., None] * fresh_value[:, :, None, :]
    )
    context_vector = context_vector.reshape(rows, query_width).astype(jnp.bfloat16)
    slot_hits = slots[:, None] == jnp.arange(requests.shape[1])[None, :]
    adapter = jnp.sum(jnp.where(slot_hits, requests[0][None, :], 0), 1)
    adapter_selector = (adapter[:, None] == jnp.arange(ADAPTER_COUNT)[None, :]).astype(jnp.bfloat16)
    context_gathered, selector_gathered = (
        lax.all_gather(context_vector, "mp", axis=0, tiled=True),
        lax.all_gather(adapter_selector, "mp", axis=0, tiled=True),
    )
    shared_portion = adapter_down_matrices.shape[1]
    context_slice = lax.dynamic_slice_in_dim(
        context_gathered, lax.axis_index("mp") * shared_portion, shared_portion, 1
    )
    every_adapter = jnp.einsum(
        "gh,thy->gty", context_slice, adapter_down_matrices, preferred_element_type=jnp.float32
    )
    partial_down = jnp.sum(every_adapter * selector_gathered.astype(jnp.float32)[:, :, None], 1)
    down_gathered = lax.psum(partial_down, "mp").astype(jnp.bfloat16)
    projection_result = apply_up_matrix(
        context_gathered, selector_gathered, down_gathered, output_weight, adapter_up_matrices
    )
    returned = lax.all_to_all(projection_result, "mp", split_axis=0, concat_axis=1, tiled=True)
    return (widened + returned.astype(jnp.float32)).astype(jnp.bfloat16)


MIB = 1 << 20
LANES = 128
LONG = 10**10
VMEM = pl.BlockSpec(memory_space=pltpu.VMEM)
SMEM = pl.BlockSpec(memory_space=pltpu.SMEM)
ANY = pl.BlockSpec(memory_space=pl.ANY)


def call(kernel, name, out_shape, in_specs, moved, limit=2 * MIB, flops=0, **options):
    return pl.pallas_call(
        kernel,
        out_shape=out_shape,
        in_specs=in_specs,
        out_specs=jax.tree.map(lambda _: VMEM, out_shape),
        compiler_params=pltpu.CompilerParams(vmem_limit_bytes=limit),
        cost_estimate=pl.CostEstimate(flops=flops, bytes_accessed=moved, transcendentals=0),
        name=name,
        **options,
    )


def exponents():
    def kernel(out_ref):
        lane = lax.broadcasted_iota(jnp.int32, (1, HEAD_DIM), 1)
        out_ref[...] = (lane % (HEAD_DIM // 2)).astype(jnp.float32) * (-2.0 / HEAD_DIM)

    shape = jax.ShapeDtypeStruct((1, HEAD_DIM), jnp.float32)
    return call(kernel, "exponents", shape, [], 0, flops=LONG // 8)()


def frequencies(exponent):
    def kernel(exponent_ref, out_ref):
        out_ref[...] = jnp.exp(exponent_ref[...] * math.log(THETA))

    shape = jax.ShapeDtypeStruct(exponent.shape, jnp.float32)
    return call(kernel, "frequencies", shape, [VMEM], 0, flops=LONG // 8)(exponent)


def norm_rows(hidden, gain, after, copies):
    rows, width = hidden.shape

    def kernel(hidden_ref, gain_ref, after_ref, out_ref):
        del after_ref
        wide = hidden_ref[...].astype(jnp.float32)
        inverse = lax.rsqrt(jnp.mean(wide * wide, -1, keepdims=True) + EPS)
        normed = (wide * inverse * gain_ref[...].astype(jnp.float32)).astype(jnp.bfloat16)
        for c in range(copies):
            out_ref[c] = normed

    return call(
        kernel,
        "norm_rows",
        jax.ShapeDtypeStruct((copies, rows, width), jnp.bfloat16),
        [VMEM, VMEM, ANY],
        hidden.size * 2 * (copies + 1),
        flops=LONG,
    )(hidden, gain[None], after)


def turns(near, frequency, lengths, slots, requests, context):
    groups, rows, depth = near.shape

    def kernel(
        lengths_ref, slots_ref, requests_ref, near_ref, frequency_ref, lined_ref, cosine_ref,
        sine_ref, mask_ref, adapter_ref,
    ):
        for j in range(groups):
            lined_ref[pl.ds(j * rows, rows)] = near_ref[j]
        row = lax.broadcasted_iota(jnp.int32, (rows, LANES), 0)
        length = jnp.zeros((rows, LANES), jnp.int32)
        adapter = jnp.zeros((rows, LANES), jnp.int32)
        for r in range(rows):
            length = jnp.where(row == r, lengths_ref[r], length)
            adapter = jnp.where(row == r, requests_ref[0, slots_ref[r]], adapter)
        angle = length.astype(jnp.float32) * frequency_ref[...]
        cosine_ref[...] = jnp.cos(angle)
        sine_ref[...] = jnp.sin(angle)
        lane = lax.broadcasted_iota(jnp.int32, (rows, LANES), 1)
        for t in range(0, context, LANES):
            mask_ref[:, pl.ds(t, LANES)] = jnp.where(lane + t < length, 0.0, -jnp.inf)
        adapter_ref[...] = adapter.astype(jnp.float32).astype(jnp.bfloat16)

    return call(
        kernel,
        "turns",
        (
            jax.ShapeDtypeStruct((groups * rows, depth), near.dtype),
            jax.ShapeDtypeStruct((rows, HEAD_DIM), jnp.float32),
            jax.ShapeDtypeStruct((rows, HEAD_DIM), jnp.float32),
            jax.ShapeDtypeStruct((rows, context), jnp.float32),
            jax.ShapeDtypeStruct((rows, LANES), jnp.bfloat16),
        ),
        [SMEM] * 3 + [VMEM] * 2,
        near.size * 4,
    )(lengths, slots, requests, near, frequency)


def column_parts(columns):
    return [slice(c, min(c + 2 * LANES, columns)) for c in range(0, columns, 2 * LANES)]


def halves_product(rows, weight_ref, part, cut):
    return jnp.concatenate(
        [
            jnp.dot(rows, weight_ref[part, :cut], preferred_element_type=jnp.float32),
            jnp.dot(rows, weight_ref[part, cut:], preferred_element_type=jnp.float32),
        ],
        1,
    )


def project_qkv(lined, far, weight, adapter, chunk=4096):
    groups, rows, _ = far.shape
    depth, width = weight.shape
    half = groups * rows

    def kernel(lined_ref, far_ref, weight_ref, adapter_ref, out_ref, far_lined_ref):
        total = jnp.zeros((2 * half, width), jnp.float32)
        for k in range(depth // chunk):
            part = pl.ds(k * chunk, chunk)
            for j in range(groups):
                far_lined_ref[pl.ds(j * rows, rows), part] = far_ref[j, :, part]
            lined = jnp.concatenate([lined_ref[:, part], far_lined_ref[:, part]])
            total = total + halves_product(lined, weight_ref, part, 3 * LANES)
        core = lax.axis_index("batch")
        adapter = adapter_ref[...]
        for e in range(2):
            for j in range(groups):
                place = e * half + j * rows
                device = 2 * j + (core ^ e ^ 1)
                out_ref[device, :, pl.ds(0, width)] = total[place : place + rows].astype(
                    jnp.bfloat16
                )
                out_ref[device, :, pl.ds(width, LANES)] = (
                    adapter if e == 0 else jnp.zeros_like(adapter)
                )

    return call(
        kernel,
        "project_qkv",
        jax.ShapeDtypeStruct((2 * groups, rows, width + LANES), jnp.bfloat16),
        [VMEM] * 4,
        weight.size * 2,
        flops=LONG,
        scratch_shapes=[pltpu.VMEM((half, depth), jnp.bfloat16)],
    )(lined, far, weight, adapter)


def project_out(gathered, adapter, weight, down_store, up_store):
    groups, rows, features = gathered.shape
    count = groups * rows
    rank, depth = down_store.shape[1:]
    columns = weight.shape[1]

    def kernel(
        adapter_ref, gathered_ref, weight_ref, down_ref, up_ref, partial_ref, base_ref, picked_ref,
        rows_ref, held_ref,
    ):
        for j in range(groups):
            rows_ref[pl.ds(j * rows, rows)] = gathered_ref[j]
        start = pl.multiple_of(lax.axis_index("mp") * depth, depth)
        slices = rows_ref[:, pl.ds(start, depth)]
        row = lax.broadcasted_iota(jnp.int32, (count, LANES), 0)
        lane = lax.broadcasted_iota(jnp.int32, (count, LANES), 1)
        total = jnp.zeros((count, LANES), jnp.float32)
        parts = column_parts(columns)
        few = count // len(parts)
        for k, part in enumerate(parts):
            for r in range(k * few, (k + 1) * few):
                chosen = adapter_ref[0, r]
                held_ref[pl.ds(r * rank, rank)] = down_ref[chosen]
                picked_ref[pl.ds(r * rank, rank)] = up_ref[chosen]
            every = lax.dot_general(
                slices,
                held_ref[pl.ds(k * few * rank, few * rank)],
                (((1,), (1,)), ((), ())),
                preferred_element_type=jnp.float32,
            )
            for s in range(0, few * rank, LANES):
                mine = row == (lane + k * few * rank + s) // rank
                total = total + jnp.where(mine, every[:, s : s + LANES], 0.0)
            base_ref[:, part] = jnp.dot(
                rows_ref[...], weight_ref[:, part], preferred_element_type=jnp.float32
            )
        for c in range(groups):
            partial_ref[c] = total

    return call(
        kernel,
        "project_out",
        (
            jax.ShapeDtypeStruct((groups, count, LANES), jnp.float32),
            jax.ShapeDtypeStruct((count, columns), jnp.float32),
            pltpu.VMEM((count * rank, columns), up_store.dtype),
        ),
        [SMEM] + [VMEM] * 4,
        weight.size * 2,
        limit=5 * MIB,
        flops=LONG,
        scratch_shapes=[
            pltpu.VMEM((count, features), gathered.dtype),
            pltpu.VMEM((count * rank, depth), down_store.dtype),
        ],
    )(adapter, gathered, weight, down_store, up_store)


def add_up(base, partials, up):
    groups, count, _ = partials.shape
    depth, width = up.shape
    rank = depth // count

    def kernel(base_ref, partials_ref, up_ref, out_ref):
        total = partials_ref[0]
        for c in range(1, groups):
            total = total + partials_ref[c]
        down = total.astype(jnp.bfloat16).astype(jnp.float32)
        row = lax.broadcasted_iota(jnp.int32, (count, LANES), 0)
        lane = lax.broadcasted_iota(jnp.int32, (count, LANES), 1)
        spread = []
        for s in range(0, depth, LANES):
            spread.append(jnp.where(row == (lane + s) // rank, down, 0.0))
        spread = jnp.concatenate(spread, 1).astype(jnp.bfloat16)
        delta = jnp.dot(spread, up_ref[...], preferred_element_type=jnp.float32)
        result = (base_ref[...] + ADAPTER_SCALE * delta).astype(jnp.bfloat16)
        for j in range(groups):
            out_ref[j] = result[j * count // groups : (j + 1) * count // groups]

    return call(
        kernel,
        "add_up",
        jax.ShapeDtypeStruct((groups, count // groups, width), jnp.bfloat16),
        [VMEM] * 3,
        up.size * 2,
        limit=4 * MIB,
        flops=2 * count * up.size,
    )(base, partials, up)


def add_rows(hidden, parts):
    width = parts.shape[2]

    def kernel(hidden_ref, parts_ref, out_ref):
        for k, place in enumerate(order(parts.shape[0])):
            part = pl.ds(place * width, width)
            total = hidden_ref[:, part].astype(jnp.float32) + parts_ref[k].astype(jnp.float32)
            out_ref[:, part] = total.astype(jnp.bfloat16)

    return call(
        kernel,
        "add_rows",
        jax.ShapeDtypeStruct(hidden.shape, parts.dtype),
        [VMEM, VMEM],
        hidden.size * 6,
    )(hidden, parts)


def swap_cores(block):
    return lax.ppermute(block, "batch", [(0, 1), (1, 0)])


def order(size):
    half = size // 2
    return [(k + 1) % half + start for k in range(half) for start in (half, 0)]


def exchange(blocks):
    group = order(lax.axis_size("mp"))
    return lax.all_to_all(
        blocks, "mp", split_axis=0, concat_axis=0, tiled=True, axis_index_groups=[group]
    )


def exchange_all(blocks):
    group = [2 * j + core for j in order(lax.axis_size("mp")) for core in (1, 0)]
    return lax.all_to_all(
        blocks,
        ("mp", "batch"),
        split_axis=0,
        concat_axis=0,
        tiled=True,
        axis_index_groups=[group],
    )


def attend(mixed, cosine, sine, mask, key_cache, value_cache, copies):
    rows, context = key_cache.shape[:2]
    group = HEADS // KV_HEADS
    heads = HEADS + 2 * KV_HEADS
    width = mixed.shape[2] - LANES
    per_device = width // HEAD_DIM
    devices = order(mixed.shape[0] // 2)

    def kernel(
        mixed_ref, cosine_ref, sine_ref, mask_ref, key_ref, value_ref, out_ref, adapter_ref,
        vec_ref, context_ref,
    ):
        place = lax.broadcasted_iota(jnp.int32, (1, LANES), 1)
        adapter = jnp.zeros((1, LANES), jnp.float32)
        for k, j in enumerate(devices):
            for core in range(2):
                block = mixed_ref[2 * k + 1 - core].astype(jnp.float32)
                for c in range(per_device):
                    head = (2 * j + core) * per_device + c
                    vec_ref[pl.ds(head * rows, rows)] = block[:, c * HEAD_DIM : (c + 1) * HEAD_DIM]
            both = mixed_ref[2 * k, :, pl.ds(width, LANES)].astype(jnp.float32)
            both = both + mixed_ref[2 * k + 1, :, pl.ds(width, LANES)].astype(jnp.float32)
            for r in range(rows):
                adapter = jnp.where(place == k * rows + r, both[r : r + 1], adapter)
        adapter_ref[...] = adapter.astype(jnp.int32)

        def tiled(pair, count):
            return jnp.concatenate([pair] * count)

        keyed = (HEADS + KV_HEADS) * rows
        vec = vec_ref[pl.ds(0, keyed)]
        turned = pltpu.roll(vec, HEAD_DIM // 2, 1)
        lane = lax.broadcasted_iota(jnp.int32, (rows, HEAD_DIM), 1)
        signed = jnp.where(lane < HEAD_DIM // 2, -sine_ref[...], sine_ref[...])
        pairs = keyed // rows
        vec = vec * tiled(cosine_ref[...], pairs) + turned * tiled(signed, pairs)
        vec = vec.astype(jnp.bfloat16)
        query = vec[: HEADS * rows]
        fresh_key = vec[HEADS * rows :].astype(jnp.float32)
        fresh_value = vec_ref[pl.ds(keyed, KV_HEADS * rows)]
        size = group * rows
        owner = lax.broadcasted_iota(jnp.int32, (size, 1), 0) % rows

        def of_owner(products):
            result = products[0]
            for r in range(1, rows):
                result = jnp.where(owner == r, products[r], result)
            return result

        scores, own_key, own_value = [], [], []
        for g in range(KV_HEADS):
            lanes = pl.ds(g * HEAD_DIM, HEAD_DIM)
            part = query[g * size : (g + 1) * size]
            products = [
                lax.dot_general(
                    part,
                    key_ref[r, :, lanes],
                    (((1,), (1,)), ((), ())),
                    preferred_element_type=jnp.float32,
                )
                for r in range(rows)
            ]
            scores.append(of_owner(products))
            own_key.append(tiled(fresh_key[g * rows : (g + 1) * rows], group))
            own_value.append(tiled(fresh_value[g * rows : (g + 1) * rows], group))
        scale = HEAD_DIM ** (-0.5)
        scores = jnp.concatenate(scores) * scale + tiled(mask_ref[...], HEADS)
        own = jnp.sum(query.astype(jnp.float32) * jnp.concatenate(own_key), 1, keepdims=True)
        own = own * scale
        top = jnp.maximum(jnp.max(scores, 1, keepdims=True), own)
        expo = jnp.exp(scores - top)
        own_exp = jnp.exp(own - top)
        total = jnp.sum(expo, 1, keepdims=True) + own_exp
        probs = (expo / total).astype(jnp.bfloat16)
        own_prob = (own_exp / total).astype(jnp.bfloat16).astype(jnp.float32)
        for g in range(KV_HEADS):
            lanes = pl.ds(g * HEAD_DIM, HEAD_DIM)
            part = probs[g * size : (g + 1) * size]
            products = [
                jnp.dot(part, value_ref[r, :, lanes], preferred_element_type=jnp.float32)
                for r in range(rows)
            ]
            result = of_owner(products) + own_prob[g * size : (g + 1) * size] * own_value[g]
            for h in range(group):
                place = pl.ds((g * group + h) * HEAD_DIM, HEAD_DIM)
                context_ref[:, place] = result[h * rows : (h + 1) * rows]
        rounded = context_ref[...].astype(jnp.bfloat16)
        for c in range(copies):
            out_ref[c] = rounded

    return call(
        kernel,
        "attend",
        (
            jax.ShapeDtypeStruct((copies, rows, HEADS * HEAD_DIM), jnp.bfloat16),
            jax.ShapeDtypeStruct((1, LANES), jnp.int32),
        ),
        [VMEM] * 6,
        key_cache.size * 4,
        limit=4 * MIB,
        flops=LONG,
        scratch_shapes=[
            pltpu.VMEM((heads * rows, HEAD_DIM), jnp.float32),
            pltpu.VMEM((rows, HEADS * HEAD_DIM), jnp.float32),
        ],
    )(mixed, cosine, sine, mask, key_cache, value_cache)


def fast_body(
    hidden,
    attention_norm_gain,
    query_key_value_weight,
    output_weight,
    key_cache,
    value_cache,
    lengths,
    slots,
    requests,
    adapter_down_matrices,
    adapter_up_matrices,
):
    mp_size = lax.axis_size("mp")
    frequency = frequencies(exponents())
    near = exchange(norm_rows(hidden, attention_norm_gain, frequency, mp_size))
    lined, cosine, sine, mask, adapter = turns(
        near, frequency, lengths, slots, requests, key_cache.shape[1]
    )
    columns = project_qkv(lined, swap_cores(near), query_key_value_weight, adapter)
    mixed = exchange_all(columns)
    context, adapter = attend(mixed, cosine, sine, mask, key_cache, value_cache, mp_size)
    gathered = exchange(context)

    partials, base, up = project_out(
        gathered,
        adapter,
        output_weight,
        adapter_down_matrices.swapaxes(1, 2),
        adapter_up_matrices,
    )
    projected = add_up(base, exchange(partials), up)
    return add_rows(hidden, exchange(projected))


def body(*arguments):
    small = lax.axis_size("mp") <= 16 and lax.axis_size("batch") == 2
    whole_heads = arguments[2].shape[1] % HEAD_DIM == 0
    return (fast_body if small and whole_heads else general_body)(*arguments)


def solution(mesh):
    in_specs = (
        P(("groups", "mp", "batch"), None),
        P(),
        P(None, ("mp", "batch")),
        P(None, "mp"),
        P(("groups", "mp", "batch"), None, None),
        P(("groups", "mp", "batch"), None, None),
        P(("groups", "mp", "batch")),
        P(("groups", "mp", "batch")),
        P(("groups", "mp", "batch"), None),
        P(None, "mp", None),
        P(None, None, "mp"),
    )
    out_specs = P(("groups", "mp", "batch"), None)
    return jax.shard_map(body, mesh=mesh, in_specs=in_specs, out_specs=out_specs, check_vma=False)
```

```python
import math

import jax
import jax.numpy as jnp
from jax import lax
from jax.experimental import pallas as pl
from jax.experimental.pallas import tpu as pltpu
from jax.sharding import PartitionSpec as P

HEADS = 64
KV_HEADS = 8
HEAD_DIM = 128
ADAPTER_COUNT = 64


EPS = 1e-05
THETA = 500000.0
ADAPTER_SCALE = 2.0


def rotate(vec, pos):
    width = vec.shape[-1]
    half = width // 2
    freq = THETA ** (-(jnp.arange(half, dtype=jnp.float32) * 2.0) / width)
    angle = pos[..., None, None] * freq
    cosine = jnp.concatenate([jnp.cos(angle), jnp.cos(angle)], -1)
    sine = jnp.concatenate([jnp.sin(angle), jnp.sin(angle)], -1)
    turned = jnp.concatenate([-vec[..., half:], vec[..., :half]], -1)
    return vec * cosine + turned * sine


def apply_up_matrix(
    context_vector, adapter_selector, down_result, output_weight, adapter_up_matrices
):
    base_output = jnp.dot(context_vector, output_weight, preferred_element_type=jnp.float32)
    spread = (adapter_selector[:, :, None] * down_result[:, None, :]).reshape(
        adapter_selector.shape[0], -1
    )
    adapter_table = adapter_up_matrices.reshape(-1, adapter_up_matrices.shape[2])
    adapter_delta = jnp.dot(spread, adapter_table, preferred_element_type=jnp.float32)
    return (base_output + ADAPTER_SCALE * adapter_delta).astype(jnp.bfloat16)


def general_body(
    hidden,
    attention_norm_gain,
    query_key_value_weight,
    output_weight,
    key_cache,
    value_cache,
    lengths,
    slots,
    requests,
    adapter_down_matrices,
    adapter_up_matrices,
):
    widened = hidden.astype(jnp.float32)
    normed = (
        widened
        * lax.rsqrt(jnp.mean(widened * widened, -1, keepdims=True) + EPS)
        * attention_norm_gain.astype(jnp.float32)
    ).astype(jnp.bfloat16)
    rows = normed.shape[0]
    columns = jnp.dot(
        lax.all_gather(normed, ("mp", "batch"), axis=0, tiled=True),
        query_key_value_weight,
        preferred_element_type=jnp.float32,
    ).astype(jnp.bfloat16)
    mixed = lax.all_to_all(
        lax.all_to_all(columns, "mp", split_axis=0, concat_axis=1, tiled=True),
        "batch",
        split_axis=0,
        concat_axis=1,
        tiled=True,
    )
    width = query_key_value_weight.shape[1]
    qkv = (
        mixed.reshape(rows, lax.axis_size("batch"), lax.axis_size("mp"), width)
        .transpose(0, 2, 1, 3)
        .reshape(rows, -1)
    )
    query_width = HEADS * HEAD_DIM
    kv_width = KV_HEADS * HEAD_DIM
    group = HEADS // KV_HEADS
    scale = HEAD_DIM ** (-0.5)
    pos = lengths.astype(jnp.float32)
    query = rotate(
        qkv[:, :query_width].astype(jnp.float32).reshape(rows, HEADS, HEAD_DIM), pos
    ).astype(jnp.bfloat16)
    fresh_key = rotate(
        qkv[:, query_width : query_width + kv_width]
        .astype(jnp.float32)
        .reshape(rows, KV_HEADS, HEAD_DIM),
        pos,
    ).astype(jnp.bfloat16)
    fresh_value = (
        qkv[:, query_width + kv_width :].astype(jnp.float32).reshape(rows, KV_HEADS, HEAD_DIM)
    )
    grouped = query.reshape(rows, KV_HEADS, group, HEAD_DIM)
    cached = key_cache.reshape(rows, -1, KV_HEADS, HEAD_DIM)
    stored = value_cache.reshape(rows, -1, KV_HEADS, HEAD_DIM)
    scores = (
        jnp.einsum("rgqd,rtgd->rgqt", grouped, cached, preferred_element_type=jnp.float32) * scale
    )
    live = jnp.arange(cached.shape[1])[None, :] < lengths[:, None]
    scores = jnp.where(live[:, None, None, :], scores, -jnp.inf)
    own = (
        jnp.einsum("rgqd,rgd->rgq", grouped, fresh_key, preferred_element_type=jnp.float32) * scale
    )
    top = jnp.maximum(jnp.max(scores, -1), own)
    expo = jnp.exp(scores - top[..., None])
    own_exp = jnp.exp(own - top)
    total = jnp.sum(expo, -1) + own_exp
    probs = (expo / total[..., None]).astype(jnp.bfloat16)
    own_prob = (own_exp / total).astype(jnp.bfloat16)
    context_vector = jnp.einsum(
        "rgqt,rtgd->rgqd", probs, stored, preferred_element_type=jnp.float32
    )
    context_vector = (
        context_vector + own_prob.astype(jnp.float32)[..., None] * fresh_value[:, :, None, :]
    )
    context_vector = context_vector.reshape(rows, query_width).astype(jnp.bfloat16)
    slot_hits = slots[:, None] == jnp.arange(requests.shape[1])[None, :]
    adapter = jnp.sum(jnp.where(slot_hits, requests[0][None, :], 0), 1)
    adapter_selector = (adapter[:, None] == jnp.arange(ADAPTER_COUNT)[None, :]).astype(jnp.bfloat16)
    context_gathered, selector_gathered = (
        lax.all_gather(context_vector, "mp", axis=0, tiled=True),
        lax.all_gather(adapter_selector, "mp", axis=0, tiled=True),
    )
    shared_portion = adapter_down_matrices.shape[1]
    context_slice = lax.dynamic_slice_in_dim(
        context_gathered, lax.axis_index("mp") * shared_portion, shared_portion, 1
    )
    every_adapter = jnp.einsum(
        "gh,thy->gty", context_slice, adapter_down_matrices, preferred_element_type=jnp.float32
    )
    partial_down = jnp.sum(every_adapter * selector_gathered.astype(jnp.float32)[:, :, None], 1)
    down_gathered = lax.psum(partial_down, "mp").astype(jnp.bfloat16)
    projection_result = apply_up_matrix(
        context_gathered, selector_gathered, down_gathered, output_weight, adapter_up_matrices
    )
    returned = lax.all_to_all(projection_result, "mp", split_axis=0, concat_axis=1, tiled=True)
    return (widened + returned.astype(jnp.float32)).astype(jnp.bfloat16)


MIB = 1 << 20
LANES = 128
LONG = 10**10
VMEM = pl.BlockSpec(memory_space=pltpu.VMEM)
SMEM = pl.BlockSpec(memory_space=pltpu.SMEM)
ANY = pl.BlockSpec(memory_space=pl.ANY)


def call(kernel, name, out_shape, in_specs, moved, limit=2 * MIB, flops=0, **options):
    return pl.pallas_call(
        kernel,
        out_shape=out_shape,
        in_specs=in_specs,
        out_specs=jax.tree.map(lambda _: VMEM, out_shape),
        compiler_params=pltpu.CompilerParams(vmem_limit_bytes=limit),
        cost_estimate=pl.CostEstimate(flops=flops, bytes_accessed=moved, transcendentals=0),
        name=name,
        **options,
    )


def exponents():
    def kernel(out_ref):
        lane = lax.broadcasted_iota(jnp.int32, (1, HEAD_DIM), 1)
        out_ref[...] = (lane % (HEAD_DIM // 2)).astype(jnp.float32) * (-2.0 / HEAD_DIM)

    shape = jax.ShapeDtypeStruct((1, HEAD_DIM), jnp.float32)
    return call(kernel, "exponents", shape, [], 0, flops=LONG // 8)()


def frequencies(exponent):
    def kernel(exponent_ref, out_ref):
        out_ref[...] = jnp.exp(exponent_ref[...] * math.log(THETA))

    shape = jax.ShapeDtypeStruct(exponent.shape, jnp.float32)
    return call(kernel, "frequencies", shape, [VMEM], 0, flops=LONG // 8)(exponent)


def norm_rows(hidden, gain, after, copies):
    rows, width = hidden.shape

    def kernel(hidden_ref, gain_ref, after_ref, out_ref):
        del after_ref
        wide = hidden_ref[...].astype(jnp.float32)
        inverse = lax.rsqrt(jnp.mean(wide * wide, -1, keepdims=True) + EPS)
        normed = (wide * inverse * gain_ref[...].astype(jnp.float32)).astype(jnp.bfloat16)
        for c in range(copies):
            out_ref[c] = normed

    return call(
        kernel,
        "norm_rows",
        jax.ShapeDtypeStruct((copies, rows, width), jnp.bfloat16),
        [VMEM, VMEM, ANY],
        hidden.size * 2 * (copies + 1),
        flops=LONG,
    )(hidden, gain[None], after)


def turns(near, frequency, lengths, slots, requests, context):
    groups, rows, depth = near.shape

    def kernel(
        lengths_ref, slots_ref, requests_ref, near_ref, frequency_ref, lined_ref, cosine_ref,
        sine_ref, mask_ref, adapter_ref,
    ):
        for j in range(groups):
            lined_ref[pl.ds(j * rows, rows)] = near_ref[j]
        row = lax.broadcasted_iota(jnp.int32, (rows, LANES), 0)
        length = jnp.zeros((rows, LANES), jnp.int32)
        adapter = jnp.zeros((rows, LANES), jnp.int32)
        for r in range(rows):
            length = jnp.where(row == r, lengths_ref[r], length)
            adapter = jnp.where(row == r, requests_ref[0, slots_ref[r]], adapter)
        angle = length.astype(jnp.float32) * frequency_ref[...]
        cosine_ref[...] = jnp.cos(angle)
        sine_ref[...] = jnp.sin(angle)
        lane = lax.broadcasted_iota(jnp.int32, (rows, LANES), 1)
        for t in range(0, context, LANES):
            mask_ref[:, pl.ds(t, LANES)] = jnp.where(lane + t < length, 0.0, -jnp.inf)
        adapter_ref[...] = adapter.astype(jnp.float32).astype(jnp.bfloat16)

    return call(
        kernel,
        "turns",
        (
            jax.ShapeDtypeStruct((groups * rows, depth), near.dtype),
            jax.ShapeDtypeStruct((rows, HEAD_DIM), jnp.float32),
            jax.ShapeDtypeStruct((rows, HEAD_DIM), jnp.float32),
            jax.ShapeDtypeStruct((rows, context), jnp.float32),
            jax.ShapeDtypeStruct((rows, LANES), jnp.bfloat16),
        ),
        [SMEM] * 3 + [VMEM] * 2,
        near.size * 4,
    )(lengths, slots, requests, near, frequency)


def column_parts(columns):
    return [slice(c, min(c + 2 * LANES, columns)) for c in range(0, columns, 2 * LANES)]


def halves_product(rows, weight_ref, part, cut):
    return jnp.concatenate(
        [
            jnp.dot(rows, weight_ref[part, :cut], preferred_element_type=jnp.float32),
            jnp.dot(rows, weight_ref[part, cut:], preferred_element_type=jnp.float32),
        ],
        1,
    )


def project_qkv(lined, far, weight, adapter, chunk=4096):
    groups, rows, _ = far.shape
    depth, width = weight.shape
    half = groups * rows

    def kernel(lined_ref, far_ref, weight_ref, adapter_ref, out_ref, far_lined_ref):
        total = jnp.zeros((2 * half, width), jnp.float32)
        for k in range(depth // chunk):
            part = pl.ds(k * chunk, chunk)
            for j in range(groups):
                far_lined_ref[pl.ds(j * rows, rows), part] = far_ref[j, :, part]
            lined = jnp.concatenate([lined_ref[:, part], far_lined_ref[:, part]])
            total = total + halves_product(lined, weight_ref, part, 3 * LANES)
        core = lax.axis_index("batch")
        adapter = adapter_ref[...]
        for e in range(2):
            for j in range(groups):
                place = e * half + j * rows
                device = 2 * j + (core ^ e ^ 1)
                out_ref[device, :, pl.ds(0, width)] = total[place : place + rows].astype(
                    jnp.bfloat16
                )
                out_ref[device, :, pl.ds(width, LANES)] = (
                    adapter if e == 0 else jnp.zeros_like(adapter)
                )

    return call(
        kernel,
        "project_qkv",
        jax.ShapeDtypeStruct((2 * groups, rows, width + LANES), jnp.bfloat16),
        [VMEM] * 4,
        weight.size * 2,
        flops=LONG,
        scratch_shapes=[pltpu.VMEM((half, depth), jnp.bfloat16)],
    )(lined, far, weight, adapter)


def project_out(gathered, adapter, weight, down_store, up_store):
    groups, rows, features = gathered.shape
    count = groups * rows
    rank, depth = down_store.shape[1:]
    columns = weight.shape[1]

    def kernel(
        adapter_ref, gathered_ref, weight_ref, down_ref, up_ref, partial_ref, base_ref, picked_ref,
        rows_ref, held_ref,
    ):
        for j in range(groups):
            rows_ref[pl.ds(j * rows, rows)] = gathered_ref[j]
        parts = column_parts(columns)
        for k, part in enumerate(parts):
            base_ref[:, part] = jnp.dot(
                rows_ref[...], weight_ref[:, part], preferred_element_type=jnp.float32
            )
            for r in range(k * count // len(parts), (k + 1) * count // len(parts)):
                chosen = adapter_ref[0, r]
                held_ref[pl.ds(r * rank, rank)] = down_ref[chosen]
                picked_ref[pl.ds(r * rank, rank)] = up_ref[chosen]
        start = pl.multiple_of(lax.axis_index("mp") * depth, depth)
        every = lax.dot_general(
            rows_ref[:, pl.ds(start, depth)],
            held_ref[...],
            (((1,), (1,)), ((), ())),
            preferred_element_type=jnp.float32,
        )
        row = lax.broadcasted_iota(jnp.int32, (count, LANES), 0)
        lane = lax.broadcasted_iota(jnp.int32, (count, LANES), 1)
        total = jnp.zeros((count, LANES), jnp.float32)
        for s in range(0, count * rank, LANES):
            total = total + jnp.where(row == (lane + s) // rank, every[:, s : s + LANES], 0.0)
        for c in range(groups):
            partial_ref[c] = total

    return call(
        kernel,
        "project_out",
        (
            jax.ShapeDtypeStruct((groups, count, LANES), jnp.float32),
            jax.ShapeDtypeStruct((count, columns), jnp.float32),
            pltpu.VMEM((count * rank, columns), up_store.dtype),
        ),
        [SMEM] + [VMEM] * 4,
        weight.size * 2,
        limit=5 * MIB,
        flops=LONG,
        scratch_shapes=[
            pltpu.VMEM((count, features), gathered.dtype),
            pltpu.VMEM((count * rank, depth), down_store.dtype),
        ],
    )(adapter, gathered, weight, down_store, up_store)


def add_up(base, partials, up):
    groups, count, _ = partials.shape
    depth, width = up.shape
    rank = depth // count

    def kernel(base_ref, partials_ref, up_ref, out_ref):
        total = partials_ref[0]
        for c in range(1, groups):
            total = total + partials_ref[c]
        down = total.astype(jnp.bfloat16).astype(jnp.float32)
        row = lax.broadcasted_iota(jnp.int32, (count, LANES), 0)
        lane = lax.broadcasted_iota(jnp.int32, (count, LANES), 1)
        spread = []
        for s in range(0, depth, LANES):
            spread.append(jnp.where(row == (lane + s) // rank, down, 0.0))
        spread = jnp.concatenate(spread, 1).astype(jnp.bfloat16)
        delta = jnp.dot(spread, up_ref[...], preferred_element_type=jnp.float32)
        result = (base_ref[...] + ADAPTER_SCALE * delta).astype(jnp.bfloat16)
        for j in range(groups):
            out_ref[j] = result[j * count // groups : (j + 1) * count // groups]

    return call(
        kernel,
        "add_up",
        jax.ShapeDtypeStruct((groups, count // groups, width), jnp.bfloat16),
        [VMEM] * 3,
        up.size * 2,
        limit=4 * MIB,
        flops=2 * count * up.size,
    )(base, partials, up)


def add_rows(hidden, parts):
    width = parts.shape[2]

    def kernel(hidden_ref, parts_ref, out_ref):
        for k, place in enumerate(order(parts.shape[0])):
            part = pl.ds(place * width, width)
            total = hidden_ref[:, part].astype(jnp.float32) + parts_ref[k].astype(jnp.float32)
            out_ref[:, part] = total.astype(jnp.bfloat16)

    return call(
        kernel,
        "add_rows",
        jax.ShapeDtypeStruct(hidden.shape, parts.dtype),
        [VMEM, VMEM],
        hidden.size * 6,
    )(hidden, parts)


def swap_cores(block):
    return lax.ppermute(block, "batch", [(0, 1), (1, 0)])


def order(size):
    half = size // 2
    return [(k + 1) % half + start for k in range(half) for start in (half, 0)]


def exchange(blocks):
    group = order(lax.axis_size("mp"))
    return lax.all_to_all(
        blocks, "mp", split_axis=0, concat_axis=0, tiled=True, axis_index_groups=[group]
    )


def exchange_all(blocks):
    group = [2 * j + core for j in order(lax.axis_size("mp")) for core in (1, 0)]
    return lax.all_to_all(
        blocks,
        ("mp", "batch"),
        split_axis=0,
        concat_axis=0,
        tiled=True,
        axis_index_groups=[group],
    )


def attend(mixed, cosine, sine, mask, key_cache, value_cache, copies):
    rows, context = key_cache.shape[:2]
    group = HEADS // KV_HEADS
    heads = HEADS + 2 * KV_HEADS
    width = mixed.shape[2] - LANES
    per_device = width // HEAD_DIM
    devices = order(mixed.shape[0] // 2)

    def kernel(
        mixed_ref, cosine_ref, sine_ref, mask_ref, key_ref, value_ref, out_ref, adapter_ref,
        vec_ref, context_ref,
    ):
        place = lax.broadcasted_iota(jnp.int32, (1, LANES), 1)
        adapter = jnp.zeros((1, LANES), jnp.float32)
        for k, j in enumerate(devices):
            for core in range(2):
                block = mixed_ref[2 * k + 1 - core].astype(jnp.float32)
                for c in range(per_device):
                    head = (2 * j + core) * per_device + c
                    vec_ref[pl.ds(head * rows, rows)] = block[:, c * HEAD_DIM : (c + 1) * HEAD_DIM]
            both = mixed_ref[2 * k, :, pl.ds(width, LANES)].astype(jnp.float32)
            both = both + mixed_ref[2 * k + 1, :, pl.ds(width, LANES)].astype(jnp.float32)
            for r in range(rows):
                adapter = jnp.where(place == k * rows + r, both[r : r + 1], adapter)
        adapter_ref[...] = adapter.astype(jnp.int32)

        def tiled(pair, count):
            return jnp.concatenate([pair] * count)

        keyed = (HEADS + KV_HEADS) * rows
        vec = vec_ref[pl.ds(0, keyed)]
        turned = pltpu.roll(vec, HEAD_DIM // 2, 1)
        lane = lax.broadcasted_iota(jnp.int32, (rows, HEAD_DIM), 1)
        signed = jnp.where(lane < HEAD_DIM // 2, -sine_ref[...], sine_ref[...])
        pairs = keyed // rows
        vec = vec * tiled(cosine_ref[...], pairs) + turned * tiled(signed, pairs)
        vec = vec.astype(jnp.bfloat16)
        query = vec[: HEADS * rows]
        fresh_key = vec[HEADS * rows :].astype(jnp.float32)
        fresh_value = vec_ref[pl.ds(keyed, KV_HEADS * rows)]
        size = group * rows
        owner = lax.broadcasted_iota(jnp.int32, (size, 1), 0) % rows

        def of_owner(products):
            result = products[0]
            for r in range(1, rows):
                result = jnp.where(owner == r, products[r], result)
            return result

        scores, own_key, own_value = [], [], []
        for g in range(KV_HEADS):
            lanes = pl.ds(g * HEAD_DIM, HEAD_DIM)
            part = query[g * size : (g + 1) * size]
            products = [
                lax.dot_general(
                    part,
                    key_ref[r, :, lanes],
                    (((1,), (1,)), ((), ())),
                    preferred_element_type=jnp.float32,
                )
                for r in range(rows)
            ]
            scores.append(of_owner(products))
            own_key.append(tiled(fresh_key[g * rows : (g + 1) * rows], group))
            own_value.append(tiled(fresh_value[g * rows : (g + 1) * rows], group))
        scale = HEAD_DIM ** (-0.5)
        scores = jnp.concatenate(scores) * scale + tiled(mask_ref[...], HEADS)
        own = jnp.sum(query.astype(jnp.float32) * jnp.concatenate(own_key), 1, keepdims=True)
        own = own * scale
        top = jnp.maximum(jnp.max(scores, 1, keepdims=True), own)
        expo = jnp.exp(scores - top)
        own_exp = jnp.exp(own - top)
        total = jnp.sum(expo, 1, keepdims=True) + own_exp
        probs = (expo / total).astype(jnp.bfloat16)
        own_prob = (own_exp / total).astype(jnp.bfloat16).astype(jnp.float32)
        for g in range(KV_HEADS):
            lanes = pl.ds(g * HEAD_DIM, HEAD_DIM)
            part = probs[g * size : (g + 1) * size]
            products = [
                jnp.dot(part, value_ref[r, :, lanes], preferred_element_type=jnp.float32)
                for r in range(rows)
            ]
            result = of_owner(products) + own_prob[g * size : (g + 1) * size] * own_value[g]
            for h in range(group):
                place = pl.ds((g * group + h) * HEAD_DIM, HEAD_DIM)
                context_ref[:, place] = result[h * rows : (h + 1) * rows]
        rounded = context_ref[...].astype(jnp.bfloat16)
        for c in range(copies):
            out_ref[c] = rounded

    return call(
        kernel,
        "attend",
        (
            jax.ShapeDtypeStruct((copies, rows, HEADS * HEAD_DIM), jnp.bfloat16),
            jax.ShapeDtypeStruct((1, LANES), jnp.int32),
        ),
        [VMEM] * 6,
        key_cache.size * 4,
        limit=4 * MIB,
        flops=LONG,
        scratch_shapes=[
            pltpu.VMEM((heads * rows, HEAD_DIM), jnp.float32),
            pltpu.VMEM((rows, HEADS * HEAD_DIM), jnp.float32),
        ],
    )(mixed, cosine, sine, mask, key_cache, value_cache)


def fast_body(
    hidden,
    attention_norm_gain,
    query_key_value_weight,
    output_weight,
    key_cache,
    value_cache,
    lengths,
    slots,
    requests,
    adapter_down_matrices,
    adapter_up_matrices,
):
    mp_size = lax.axis_size("mp")
    frequency = frequencies(exponents())
    near = exchange(norm_rows(hidden, attention_norm_gain, frequency, mp_size))
    lined, cosine, sine, mask, adapter = turns(
        near, frequency, lengths, slots, requests, key_cache.shape[1]
    )
    columns = project_qkv(lined, swap_cores(near), query_key_value_weight, adapter)
    mixed = exchange_all(columns)
    context, adapter = attend(mixed, cosine, sine, mask, key_cache, value_cache, mp_size)
    gathered = exchange(context)

    partials, base, up = project_out(
        gathered,
        adapter,
        output_weight,
        adapter_down_matrices.swapaxes(1, 2),
        adapter_up_matrices,
    )
    projected = add_up(base, exchange(partials), up)
    return add_rows(hidden, exchange(projected))


def body(*arguments):
    small = lax.axis_size("mp") <= 16 and lax.axis_size("batch") == 2
    whole_heads = arguments[2].shape[1] % HEAD_DIM == 0
    return (fast_body if small and whole_heads else general_body)(*arguments)


def solution(mesh):
    in_specs = (
        P(("groups", "mp", "batch"), None),
        P(),
        P(None, ("mp", "batch")),
        P(None, "mp"),
        P(("groups", "mp", "batch"), None, None),
        P(("groups", "mp", "batch"), None, None),
        P(("groups", "mp", "batch")),
        P(("groups", "mp", "batch")),
        P(("groups", "mp", "batch"), None),
        P(None, "mp", None),
        P(None, None, "mp"),
    )
    out_specs = P(("groups", "mp", "batch"), None)
    return jax.shard_map(body, mesh=mesh, in_specs=in_specs, out_specs=out_specs, check_vma=False)
```

```python
import math

import jax
import jax.numpy as jnp
from jax import lax
from jax.experimental import pallas as pl
from jax.experimental.pallas import tpu as pltpu
from jax.sharding import PartitionSpec as P

HEADS = 64
KV_HEADS = 8
HEAD_DIM = 128
ADAPTER_COUNT = 64


EPS = 1e-05
THETA = 500000.0
ADAPTER_SCALE = 2.0


def rotate(vec, pos):
    width = vec.shape[-1]
    half = width // 2
    freq = THETA ** (-(jnp.arange(half, dtype=jnp.float32) * 2.0) / width)
    angle = pos[..., None, None] * freq
    cosine = jnp.concatenate([jnp.cos(angle), jnp.cos(angle)], -1)
    sine = jnp.concatenate([jnp.sin(angle), jnp.sin(angle)], -1)
    turned = jnp.concatenate([-vec[..., half:], vec[..., :half]], -1)
    return vec * cosine + turned * sine


def apply_up_matrix(
    context_vector, adapter_selector, down_result, output_weight, adapter_up_matrices
):
    base_output = jnp.dot(context_vector, output_weight, preferred_element_type=jnp.float32)
    spread = (adapter_selector[:, :, None] * down_result[:, None, :]).reshape(
        adapter_selector.shape[0], -1
    )
    adapter_table = adapter_up_matrices.reshape(-1, adapter_up_matrices.shape[2])
    adapter_delta = jnp.dot(spread, adapter_table, preferred_element_type=jnp.float32)
    return (base_output + ADAPTER_SCALE * adapter_delta).astype(jnp.bfloat16)


def general_body(
    hidden,
    attention_norm_gain,
    query_key_value_weight,
    output_weight,
    key_cache,
    value_cache,
    lengths,
    slots,
    requests,
    adapter_down_matrices,
    adapter_up_matrices,
):
    widened = hidden.astype(jnp.float32)
    normed = (
        widened
        * lax.rsqrt(jnp.mean(widened * widened, -1, keepdims=True) + EPS)
        * attention_norm_gain.astype(jnp.float32)
    ).astype(jnp.bfloat16)
    rows = normed.shape[0]
    columns = jnp.dot(
        lax.all_gather(normed, ("mp", "batch"), axis=0, tiled=True),
        query_key_value_weight,
        preferred_element_type=jnp.float32,
    ).astype(jnp.bfloat16)
    mixed = lax.all_to_all(
        lax.all_to_all(columns, "mp", split_axis=0, concat_axis=1, tiled=True),
        "batch",
        split_axis=0,
        concat_axis=1,
        tiled=True,
    )
    width = query_key_value_weight.shape[1]
    qkv = (
        mixed.reshape(rows, lax.axis_size("batch"), lax.axis_size("mp"), width)
        .transpose(0, 2, 1, 3)
        .reshape(rows, -1)
    )
    query_width = HEADS * HEAD_DIM
    kv_width = KV_HEADS * HEAD_DIM
    group = HEADS // KV_HEADS
    scale = HEAD_DIM ** (-0.5)
    pos = lengths.astype(jnp.float32)
    query = rotate(
        qkv[:, :query_width].astype(jnp.float32).reshape(rows, HEADS, HEAD_DIM), pos
    ).astype(jnp.bfloat16)
    fresh_key = rotate(
        qkv[:, query_width : query_width + kv_width]
        .astype(jnp.float32)
        .reshape(rows, KV_HEADS, HEAD_DIM),
        pos,
    ).astype(jnp.bfloat16)
    fresh_value = (
        qkv[:, query_width + kv_width :].astype(jnp.float32).reshape(rows, KV_HEADS, HEAD_DIM)
    )
    grouped = query.reshape(rows, KV_HEADS, group, HEAD_DIM)
    cached = key_cache.reshape(rows, -1, KV_HEADS, HEAD_DIM)
    stored = value_cache.reshape(rows, -1, KV_HEADS, HEAD_DIM)
    scores = (
        jnp.einsum("rgqd,rtgd->rgqt", grouped, cached, preferred_element_type=jnp.float32) * scale
    )
    live = jnp.arange(cached.shape[1])[None, :] < lengths[:, None]
    scores = jnp.where(live[:, None, None, :], scores, -jnp.inf)
    own = (
        jnp.einsum("rgqd,rgd->rgq", grouped, fresh_key, preferred_element_type=jnp.float32) * scale
    )
    top = jnp.maximum(jnp.max(scores, -1), own)
    expo = jnp.exp(scores - top[..., None])
    own_exp = jnp.exp(own - top)
    total = jnp.sum(expo, -1) + own_exp
    probs = (expo / total[..., None]).astype(jnp.bfloat16)
    own_prob = (own_exp / total).astype(jnp.bfloat16)
    context_vector = jnp.einsum(
        "rgqt,rtgd->rgqd", probs, stored, preferred_element_type=jnp.float32
    )
    context_vector = (
        context_vector + own_prob.astype(jnp.float32)[..., None] * fresh_value[:, :, None, :]
    )
    context_vector = context_vector.reshape(rows, query_width).astype(jnp.bfloat16)
    slot_hits = slots[:, None] == jnp.arange(requests.shape[1])[None, :]
    adapter = jnp.sum(jnp.where(slot_hits, requests[0][None, :], 0), 1)
    adapter_selector = (adapter[:, None] == jnp.arange(ADAPTER_COUNT)[None, :]).astype(jnp.bfloat16)
    context_gathered, selector_gathered = (
        lax.all_gather(context_vector, "mp", axis=0, tiled=True),
        lax.all_gather(adapter_selector, "mp", axis=0, tiled=True),
    )
    shared_portion = adapter_down_matrices.shape[1]
    context_slice = lax.dynamic_slice_in_dim(
        context_gathered, lax.axis_index("mp") * shared_portion, shared_portion, 1
    )
    every_adapter = jnp.einsum(
        "gh,thy->gty", context_slice, adapter_down_matrices, preferred_element_type=jnp.float32
    )
    partial_down = jnp.sum(every_adapter * selector_gathered.astype(jnp.float32)[:, :, None], 1)
    down_gathered = lax.psum(partial_down, "mp").astype(jnp.bfloat16)
    projection_result = apply_up_matrix(
        context_gathered, selector_gathered, down_gathered, output_weight, adapter_up_matrices
    )
    returned = lax.all_to_all(projection_result, "mp", split_axis=0, concat_axis=1, tiled=True)
    return (widened + returned.astype(jnp.float32)).astype(jnp.bfloat16)


MIB = 1 << 20
LANES = 128
LONG = 10**10
VMEM = pl.BlockSpec(memory_space=pltpu.VMEM)
SMEM = pl.BlockSpec(memory_space=pltpu.SMEM)
ANY = pl.BlockSpec(memory_space=pl.ANY)


def call(kernel, name, out_shape, in_specs, moved, limit=2 * MIB, flops=0, **options):
    return pl.pallas_call(
        kernel,
        out_shape=out_shape,
        in_specs=in_specs,
        out_specs=jax.tree.map(lambda _: VMEM, out_shape),
        compiler_params=pltpu.CompilerParams(vmem_limit_bytes=limit),
        cost_estimate=pl.CostEstimate(flops=flops, bytes_accessed=moved, transcendentals=0),
        name=name,
        **options,
    )


def exponents():
    def kernel(out_ref):
        lane = lax.broadcasted_iota(jnp.int32, (1, HEAD_DIM), 1)
        out_ref[...] = (lane % (HEAD_DIM // 2)).astype(jnp.float32) * (-2.0 / HEAD_DIM)

    shape = jax.ShapeDtypeStruct((1, HEAD_DIM), jnp.float32)
    return call(kernel, "exponents", shape, [], 0, flops=LONG // 8)()


def frequencies(exponent):
    def kernel(exponent_ref, out_ref):
        out_ref[...] = jnp.exp(exponent_ref[...] * math.log(THETA))

    shape = jax.ShapeDtypeStruct(exponent.shape, jnp.float32)
    return call(kernel, "frequencies", shape, [VMEM], 0, flops=LONG // 8)(exponent)


def norm_rows(hidden, gain, after, copies):
    rows, width = hidden.shape

    def kernel(hidden_ref, gain_ref, after_ref, out_ref):
        del after_ref
        wide = hidden_ref[...].astype(jnp.float32)
        inverse = lax.rsqrt(jnp.mean(wide * wide, -1, keepdims=True) + EPS)
        normed = (wide * inverse * gain_ref[...].astype(jnp.float32)).astype(jnp.bfloat16)
        for c in range(copies):
            out_ref[c] = normed

    return call(
        kernel,
        "norm_rows",
        jax.ShapeDtypeStruct((copies, rows, width), jnp.bfloat16),
        [VMEM, VMEM, ANY],
        hidden.size * 2 * (copies + 1),
        flops=LONG,
    )(hidden, gain[None], after)


def turns(near, frequency, lengths, slots, requests, context):
    groups, rows, depth = near.shape

    def kernel(
        lengths_ref, slots_ref, requests_ref, near_ref, frequency_ref, lined_ref, cosine_ref,
        sine_ref, mask_ref, adapter_ref,
    ):
        for j in range(groups):
            lined_ref[pl.ds(j * rows, rows)] = near_ref[j]
        row = lax.broadcasted_iota(jnp.int32, (rows, LANES), 0)
        length = jnp.zeros((rows, LANES), jnp.int32)
        adapter = jnp.zeros((rows, LANES), jnp.int32)
        for r in range(rows):
            length = jnp.where(row == r, lengths_ref[r], length)
            adapter = jnp.where(row == r, requests_ref[0, slots_ref[r]], adapter)
        angle = length.astype(jnp.float32) * frequency_ref[...]
        cosine_ref[...] = jnp.cos(angle)
        sine_ref[...] = jnp.sin(angle)
        lane = lax.broadcasted_iota(jnp.int32, (rows, LANES), 1)
        for t in range(0, context, LANES):
            mask_ref[:, pl.ds(t, LANES)] = jnp.where(lane + t < length, 0.0, -jnp.inf)
        adapter_ref[...] = adapter.astype(jnp.float32).astype(jnp.bfloat16)

    return call(
        kernel,
        "turns",
        (
            jax.ShapeDtypeStruct((groups * rows, depth), near.dtype),
            jax.ShapeDtypeStruct((rows, HEAD_DIM), jnp.float32),
            jax.ShapeDtypeStruct((rows, HEAD_DIM), jnp.float32),
            jax.ShapeDtypeStruct((rows, context), jnp.float32),
            jax.ShapeDtypeStruct((rows, LANES), jnp.bfloat16),
        ),
        [SMEM] * 3 + [VMEM] * 2,
        near.size * 4,
    )(lengths, slots, requests, near, frequency)


def column_parts(columns):
    return [slice(c, min(c + 2 * LANES, columns)) for c in range(0, columns, 2 * LANES)]


def project_qkv(lined, far, weight, adapter):
    groups, rows, _ = far.shape
    depth, width = weight.shape
    half = groups * rows

    def kernel(lined_ref, far_ref, weight_ref, adapter_ref, out_ref, far_lined_ref):
        for j in range(groups):
            far_lined_ref[pl.ds(j * rows, rows)] = far_ref[j]
        lined = jnp.concatenate([lined_ref[...], far_lined_ref[...]])
        total = jnp.concatenate(
            [
                jnp.dot(lined, weight_ref[:, part], preferred_element_type=jnp.float32)
                for part in column_parts(width)
            ],
            1,
        )
        core = lax.axis_index("batch")
        adapter = adapter_ref[...]
        for e in range(2):
            for j in range(groups):
                place = e * half + j * rows
                device = 2 * j + (core ^ e ^ 1)
                out_ref[device, :, pl.ds(0, width)] = total[place : place + rows].astype(
                    jnp.bfloat16
                )
                out_ref[device, :, pl.ds(width, LANES)] = (
                    adapter if e == 0 else jnp.zeros_like(adapter)
                )

    return call(
        kernel,
        "project_qkv",
        jax.ShapeDtypeStruct((2 * groups, rows, width + LANES), jnp.bfloat16),
        [VMEM] * 4,
        weight.size * 2,
        flops=LONG,
        scratch_shapes=[pltpu.VMEM((half, depth), jnp.bfloat16)],
    )(lined, far, weight, adapter)


def project_out(gathered, adapter, weight, down_store, up_store):
    groups, rows, features = gathered.shape
    count = groups * rows
    rank, depth = down_store.shape[1:]
    columns = weight.shape[1]

    def kernel(
        adapter_ref, gathered_ref, weight_ref, down_ref, up_ref, partial_ref, base_ref, picked_ref,
        rows_ref, held_ref,
    ):
        for j in range(groups):
            rows_ref[pl.ds(j * rows, rows)] = gathered_ref[j]
        parts = column_parts(columns)
        for k, part in enumerate(parts):
            base_ref[:, part] = jnp.dot(
                rows_ref[...], weight_ref[:, part], preferred_element_type=jnp.float32
            )
            for r in range(k * count // len(parts), (k + 1) * count // len(parts)):
                chosen = adapter_ref[0, r]
                held_ref[pl.ds(r * rank, rank)] = down_ref[chosen]
                picked_ref[pl.ds(r * rank, rank)] = up_ref[chosen]
        start = pl.multiple_of(lax.axis_index("mp") * depth, depth)
        every = lax.dot_general(
            rows_ref[:, pl.ds(start, depth)],
            held_ref[...],
            (((1,), (1,)), ((), ())),
            preferred_element_type=jnp.float32,
        )
        row = lax.broadcasted_iota(jnp.int32, (count, LANES), 0)
        lane = lax.broadcasted_iota(jnp.int32, (count, LANES), 1)
        total = jnp.zeros((count, LANES), jnp.float32)
        for s in range(0, count * rank, LANES):
            total = total + jnp.where(row == (lane + s) // rank, every[:, s : s + LANES], 0.0)
        for c in range(2 * groups):
            partial_ref[c] = total

    return call(
        kernel,
        "project_out",
        (
            jax.ShapeDtypeStruct((2 * groups, count, LANES), jnp.float32),
            jax.ShapeDtypeStruct((count, columns), jnp.float32),
            pltpu.VMEM((count * rank, columns), up_store.dtype),
        ),
        [SMEM] + [VMEM] * 4,
        weight.size * 2,
        limit=5 * MIB,
        flops=LONG,
        scratch_shapes=[
            pltpu.VMEM((count, features), gathered.dtype),
            pltpu.VMEM((count * rank, depth), down_store.dtype),
        ],
    )(adapter, gathered, weight, down_store, up_store)


def add_up(base, partials, up):
    blocks, count, _ = partials.shape
    groups = blocks // 2
    depth, width = up.shape
    rank = depth // count

    def kernel(base_ref, partials_ref, up_ref, out_ref):
        near = 1 - lax.axis_index("batch")
        total = partials_ref[near]
        for c in range(1, groups):
            total = total + partials_ref[2 * c + near]
        down = total.astype(jnp.bfloat16).astype(jnp.float32)
        row = lax.broadcasted_iota(jnp.int32, (count, LANES), 0)
        lane = lax.broadcasted_iota(jnp.int32, (count, LANES), 1)
        spread = []
        for s in range(0, depth, LANES):
            spread.append(jnp.where(row == (lane + s) // rank, down, 0.0))
        spread = jnp.concatenate(spread, 1).astype(jnp.bfloat16)
        delta = jnp.dot(spread, up_ref[...], preferred_element_type=jnp.float32)
        result = (base_ref[...] + ADAPTER_SCALE * delta).astype(jnp.bfloat16)
        for p in range(blocks):
            j = p // 2
            out_ref[p] = result[j * count // groups : (j + 1) * count // groups]

    return call(
        kernel,
        "add_up",
        jax.ShapeDtypeStruct((blocks, count // groups, width), jnp.bfloat16),
        [VMEM] * 3,
        up.size * 2,
        limit=4 * MIB,
        flops=2 * count * up.size,
    )(base, partials, up)


def add_rows(hidden, parts):
    width = parts.shape[2]

    def kernel(hidden_ref, parts_ref, out_ref):
        near = 1 - lax.axis_index("batch")
        for k, place in enumerate(order(parts.shape[0] // 2)):
            part = pl.ds(place * width, width)
            total = hidden_ref[:, part].astype(jnp.float32) + parts_ref[2 * k + near].astype(jnp.float32)
            out_ref[:, part] = total.astype(jnp.bfloat16)

    return call(
        kernel,
        "add_rows",
        jax.ShapeDtypeStruct(hidden.shape, parts.dtype),
        [VMEM, VMEM],
        hidden.size * 6,
    )(hidden, parts)


def swap_cores(block):
    return lax.ppermute(block, "batch", [(0, 1), (1, 0)])


def order(size):
    half = size // 2
    return [(k + 1) % half + start for k in range(half) for start in (half, 0)]


def exchange(blocks):
    group = order(lax.axis_size("mp"))
    return lax.all_to_all(
        blocks, "mp", split_axis=0, concat_axis=0, tiled=True, axis_index_groups=[group]
    )


def exchange_all(blocks):
    group = [2 * j + core for j in order(lax.axis_size("mp")) for core in (1, 0)]
    return lax.all_to_all(
        blocks,
        ("mp", "batch"),
        split_axis=0,
        concat_axis=0,
        tiled=True,
        axis_index_groups=[group],
    )


def attend(mixed, cosine, sine, mask, key_cache, value_cache, copies):
    rows, context = key_cache.shape[:2]
    group = HEADS // KV_HEADS
    heads = HEADS + 2 * KV_HEADS
    width = mixed.shape[2] - LANES
    per_device = width // HEAD_DIM
    devices = order(mixed.shape[0] // 2)

    def kernel(
        mixed_ref, cosine_ref, sine_ref, mask_ref, key_ref, value_ref, out_ref, adapter_ref,
        vec_ref, context_ref,
    ):
        place = lax.broadcasted_iota(jnp.int32, (1, LANES), 1)
        adapter = jnp.zeros((1, LANES), jnp.float32)
        for k, j in enumerate(devices):
            for core in range(2):
                block = mixed_ref[2 * k + 1 - core].astype(jnp.float32)
                for c in range(per_device):
                    head = (2 * j + core) * per_device + c
                    vec_ref[pl.ds(head * rows, rows)] = block[:, c * HEAD_DIM : (c + 1) * HEAD_DIM]
            both = mixed_ref[2 * k, :, pl.ds(width, LANES)].astype(jnp.float32)
            both = both + mixed_ref[2 * k + 1, :, pl.ds(width, LANES)].astype(jnp.float32)
            for r in range(rows):
                adapter = jnp.where(place == k * rows + r, both[r : r + 1], adapter)
        adapter_ref[...] = adapter.astype(jnp.int32)

        def tiled(pair, count):
            return jnp.concatenate([pair] * count)

        keyed = (HEADS + KV_HEADS) * rows
        vec = vec_ref[pl.ds(0, keyed)]
        turned = pltpu.roll(vec, HEAD_DIM // 2, 1)
        lane = lax.broadcasted_iota(jnp.int32, (rows, HEAD_DIM), 1)
        signed = jnp.where(lane < HEAD_DIM // 2, -sine_ref[...], sine_ref[...])
        pairs = keyed // rows
        vec = vec * tiled(cosine_ref[...], pairs) + turned * tiled(signed, pairs)
        vec = vec.astype(jnp.bfloat16)
        query = vec[: HEADS * rows]
        fresh_key = vec[HEADS * rows :].astype(jnp.float32)
        fresh_value = vec_ref[pl.ds(keyed, KV_HEADS * rows)]
        size = group * rows
        owner = lax.broadcasted_iota(jnp.int32, (size, 1), 0) % rows

        def of_owner(products):
            result = products[0]
            for r in range(1, rows):
                result = jnp.where(owner == r, products[r], result)
            return result

        scores, own_key, own_value = [], [], []
        for g in range(KV_HEADS):
            lanes = pl.ds(g * HEAD_DIM, HEAD_DIM)
            part = query[g * size : (g + 1) * size]
            products = [
                lax.dot_general(
                    part,
                    key_ref[r, :, lanes],
                    (((1,), (1,)), ((), ())),
                    preferred_element_type=jnp.float32,
                )
                for r in range(rows)
            ]
            scores.append(of_owner(products))
            own_key.append(tiled(fresh_key[g * rows : (g + 1) * rows], group))
            own_value.append(tiled(fresh_value[g * rows : (g + 1) * rows], group))
        scale = HEAD_DIM ** (-0.5)
        scores = jnp.concatenate(scores) * scale + tiled(mask_ref[...], HEADS)
        own = jnp.sum(query.astype(jnp.float32) * jnp.concatenate(own_key), 1, keepdims=True)
        own = own * scale
        top = jnp.maximum(jnp.max(scores, 1, keepdims=True), own)
        expo = jnp.exp(scores - top)
        own_exp = jnp.exp(own - top)
        total = jnp.sum(expo, 1, keepdims=True) + own_exp
        probs = (expo / total).astype(jnp.bfloat16)
        own_prob = (own_exp / total).astype(jnp.bfloat16).astype(jnp.float32)
        for g in range(KV_HEADS):
            lanes = pl.ds(g * HEAD_DIM, HEAD_DIM)
            part = probs[g * size : (g + 1) * size]
            products = [
                jnp.dot(part, value_ref[r, :, lanes], preferred_element_type=jnp.float32)
                for r in range(rows)
            ]
            result = of_owner(products) + own_prob[g * size : (g + 1) * size] * own_value[g]
            for h in range(group):
                place = pl.ds((g * group + h) * HEAD_DIM, HEAD_DIM)
                context_ref[:, place] = result[h * rows : (h + 1) * rows]
        rounded = context_ref[...].astype(jnp.bfloat16)
        for c in range(copies):
            out_ref[c] = rounded

    return call(
        kernel,
        "attend",
        (
            jax.ShapeDtypeStruct((copies, rows, HEADS * HEAD_DIM), jnp.bfloat16),
            jax.ShapeDtypeStruct((1, LANES), jnp.int32),
        ),
        [VMEM] * 6,
        key_cache.size * 4,
        limit=4 * MIB,
        flops=LONG,
        scratch_shapes=[
            pltpu.VMEM((heads * rows, HEAD_DIM), jnp.float32),
            pltpu.VMEM((rows, HEADS * HEAD_DIM), jnp.float32),
        ],
    )(mixed, cosine, sine, mask, key_cache, value_cache)


def fast_body(
    hidden,
    attention_norm_gain,
    query_key_value_weight,
    output_weight,
    key_cache,
    value_cache,
    lengths,
    slots,
    requests,
    adapter_down_matrices,
    adapter_up_matrices,
):
    mp_size = lax.axis_size("mp")
    frequency = frequencies(exponents())
    near = exchange(norm_rows(hidden, attention_norm_gain, frequency, mp_size))
    lined, cosine, sine, mask, adapter = turns(
        near, frequency, lengths, slots, requests, key_cache.shape[1]
    )
    columns = project_qkv(lined, swap_cores(near), query_key_value_weight, adapter)
    mixed = exchange_all(columns)
    context, adapter = attend(mixed, cosine, sine, mask, key_cache, value_cache, mp_size)
    gathered = exchange(context)

    partials, base, up = project_out(
        gathered,
        adapter,
        output_weight,
        adapter_down_matrices.swapaxes(1, 2),
        adapter_up_matrices,
    )
    projected = add_up(base, exchange_all(partials), up)
    return add_rows(hidden, exchange_all(projected))


def body(*arguments):
    small = lax.axis_size("mp") <= 16 and lax.axis_size("batch") == 2
    whole_heads = arguments[2].shape[1] % HEAD_DIM == 0
    return (fast_body if small and whole_heads else general_body)(*arguments)


def solution(mesh):
    in_specs = (
        P(("groups", "mp", "batch"), None),
        P(),
        P(None, ("mp", "batch")),
        P(None, "mp"),
        P(("groups", "mp", "batch"), None, None),
        P(("groups", "mp", "batch"), None, None),
        P(("groups", "mp", "batch")),
        P(("groups", "mp", "batch")),
        P(("groups", "mp", "batch"), None),
        P(None, "mp", None),
        P(None, None, "mp"),
    )
    out_specs = P(("groups", "mp", "batch"), None)
    return jax.shard_map(body, mesh=mesh, in_specs=in_specs, out_specs=out_specs, check_vma=False)
```

```python
import math

import jax
import jax.numpy as jnp
from jax import lax
from jax.experimental import pallas as pl
from jax.experimental.pallas import tpu as pltpu
from jax.sharding import PartitionSpec as P

HEADS = 64
KV_HEADS = 8
HEAD_DIM = 128
ADAPTER_COUNT = 64


EPS = 1e-05
THETA = 500000.0
ADAPTER_SCALE = 2.0


def rotate(vec, pos):
    width = vec.shape[-1]
    half = width // 2
    freq = THETA ** (-(jnp.arange(half, dtype=jnp.float32) * 2.0) / width)
    angle = pos[..., None, None] * freq
    cosine = jnp.concatenate([jnp.cos(angle), jnp.cos(angle)], -1)
    sine = jnp.concatenate([jnp.sin(angle), jnp.sin(angle)], -1)
    turned = jnp.concatenate([-vec[..., half:], vec[..., :half]], -1)
    return vec * cosine + turned * sine


def apply_up_matrix(
    context_vector, adapter_selector, down_result, output_weight, adapter_up_matrices
):
    base_output = jnp.dot(context_vector, output_weight, preferred_element_type=jnp.float32)
    spread = (adapter_selector[:, :, None] * down_result[:, None, :]).reshape(
        adapter_selector.shape[0], -1
    )
    adapter_table = adapter_up_matrices.reshape(-1, adapter_up_matrices.shape[2])
    adapter_delta = jnp.dot(spread, adapter_table, preferred_element_type=jnp.float32)
    return (base_output + ADAPTER_SCALE * adapter_delta).astype(jnp.bfloat16)


def general_body(
    hidden,
    attention_norm_gain,
    query_key_value_weight,
    output_weight,
    key_cache,
    value_cache,
    lengths,
    slots,
    requests,
    adapter_down_matrices,
    adapter_up_matrices,
):
    widened = hidden.astype(jnp.float32)
    normed = (
        widened
        * lax.rsqrt(jnp.mean(widened * widened, -1, keepdims=True) + EPS)
        * attention_norm_gain.astype(jnp.float32)
    ).astype(jnp.bfloat16)
    rows = normed.shape[0]
    columns = jnp.dot(
        lax.all_gather(normed, ("mp", "batch"), axis=0, tiled=True),
        query_key_value_weight,
        preferred_element_type=jnp.float32,
    ).astype(jnp.bfloat16)
    mixed = lax.all_to_all(
        lax.all_to_all(columns, "mp", split_axis=0, concat_axis=1, tiled=True),
        "batch",
        split_axis=0,
        concat_axis=1,
        tiled=True,
    )
    width = query_key_value_weight.shape[1]
    qkv = (
        mixed.reshape(rows, lax.axis_size("batch"), lax.axis_size("mp"), width)
        .transpose(0, 2, 1, 3)
        .reshape(rows, -1)
    )
    query_width = HEADS * HEAD_DIM
    kv_width = KV_HEADS * HEAD_DIM
    group = HEADS // KV_HEADS
    scale = HEAD_DIM ** (-0.5)
    pos = lengths.astype(jnp.float32)
    query = rotate(
        qkv[:, :query_width].astype(jnp.float32).reshape(rows, HEADS, HEAD_DIM), pos
    ).astype(jnp.bfloat16)
    fresh_key = rotate(
        qkv[:, query_width : query_width + kv_width]
        .astype(jnp.float32)
        .reshape(rows, KV_HEADS, HEAD_DIM),
        pos,
    ).astype(jnp.bfloat16)
    fresh_value = (
        qkv[:, query_width + kv_width :].astype(jnp.float32).reshape(rows, KV_HEADS, HEAD_DIM)
    )
    grouped = query.reshape(rows, KV_HEADS, group, HEAD_DIM)
    cached = key_cache.reshape(rows, -1, KV_HEADS, HEAD_DIM)
    stored = value_cache.reshape(rows, -1, KV_HEADS, HEAD_DIM)
    scores = (
        jnp.einsum("rgqd,rtgd->rgqt", grouped, cached, preferred_element_type=jnp.float32) * scale
    )
    live = jnp.arange(cached.shape[1])[None, :] < lengths[:, None]
    scores = jnp.where(live[:, None, None, :], scores, -jnp.inf)
    own = (
        jnp.einsum("rgqd,rgd->rgq", grouped, fresh_key, preferred_element_type=jnp.float32) * scale
    )
    top = jnp.maximum(jnp.max(scores, -1), own)
    expo = jnp.exp(scores - top[..., None])
    own_exp = jnp.exp(own - top)
    total = jnp.sum(expo, -1) + own_exp
    probs = (expo / total[..., None]).astype(jnp.bfloat16)
    own_prob = (own_exp / total).astype(jnp.bfloat16)
    context_vector = jnp.einsum(
        "rgqt,rtgd->rgqd", probs, stored, preferred_element_type=jnp.float32
    )
    context_vector = (
        context_vector + own_prob.astype(jnp.float32)[..., None] * fresh_value[:, :, None, :]
    )
    context_vector = context_vector.reshape(rows, query_width).astype(jnp.bfloat16)
    slot_hits = slots[:, None] == jnp.arange(requests.shape[1])[None, :]
    adapter = jnp.sum(jnp.where(slot_hits, requests[0][None, :], 0), 1)
    adapter_selector = (adapter[:, None] == jnp.arange(ADAPTER_COUNT)[None, :]).astype(jnp.bfloat16)
    context_gathered, selector_gathered = (
        lax.all_gather(context_vector, "mp", axis=0, tiled=True),
        lax.all_gather(adapter_selector, "mp", axis=0, tiled=True),
    )
    shared_portion = adapter_down_matrices.shape[1]
    context_slice = lax.dynamic_slice_in_dim(
        context_gathered, lax.axis_index("mp") * shared_portion, shared_portion, 1
    )
    every_adapter = jnp.einsum(
        "gh,thy->gty", context_slice, adapter_down_matrices, preferred_element_type=jnp.float32
    )
    partial_down = jnp.sum(every_adapter * selector_gathered.astype(jnp.float32)[:, :, None], 1)
    down_gathered = lax.psum(partial_down, "mp").astype(jnp.bfloat16)
    projection_result = apply_up_matrix(
        context_gathered, selector_gathered, down_gathered, output_weight, adapter_up_matrices
    )
    returned = lax.all_to_all(projection_result, "mp", split_axis=0, concat_axis=1, tiled=True)
    return (widened + returned.astype(jnp.float32)).astype(jnp.bfloat16)


MIB = 1 << 20
LANES = 128
LONG = 10**10
VMEM = pl.BlockSpec(memory_space=pltpu.VMEM)
SMEM = pl.BlockSpec(memory_space=pltpu.SMEM)
ANY = pl.BlockSpec(memory_space=pl.ANY)


def call(kernel, name, out_shape, in_specs, moved, limit=2 * MIB, flops=0, **options):
    return pl.pallas_call(
        kernel,
        out_shape=out_shape,
        in_specs=in_specs,
        out_specs=jax.tree.map(lambda _: VMEM, out_shape),
        compiler_params=pltpu.CompilerParams(vmem_limit_bytes=limit),
        cost_estimate=pl.CostEstimate(flops=flops, bytes_accessed=moved, transcendentals=0),
        name=name,
        **options,
    )


def exponents():
    def kernel(out_ref):
        lane = lax.broadcasted_iota(jnp.int32, (1, HEAD_DIM), 1)
        out_ref[...] = (lane % (HEAD_DIM // 2)).astype(jnp.float32) * (-2.0 / HEAD_DIM)

    shape = jax.ShapeDtypeStruct((1, HEAD_DIM), jnp.float32)
    return call(kernel, "exponents", shape, [], 0, flops=LONG // 8)()


def frequencies(exponent):
    def kernel(exponent_ref, out_ref):
        out_ref[...] = jnp.exp(exponent_ref[...] * math.log(THETA))

    shape = jax.ShapeDtypeStruct(exponent.shape, jnp.float32)
    return call(kernel, "frequencies", shape, [VMEM], 0, flops=LONG // 8)(exponent)


def norm_rows(hidden, gain, after, copies):
    rows, width = hidden.shape

    def kernel(hidden_ref, gain_ref, after_ref, out_ref):
        del after_ref
        wide = hidden_ref[...].astype(jnp.float32)
        inverse = lax.rsqrt(jnp.mean(wide * wide, -1, keepdims=True) + EPS)
        normed = (wide * inverse * gain_ref[...].astype(jnp.float32)).astype(jnp.bfloat16)
        for c in range(copies):
            out_ref[c] = normed

    return call(
        kernel,
        "norm_rows",
        jax.ShapeDtypeStruct((copies, rows, width), jnp.bfloat16),
        [VMEM, VMEM, ANY],
        hidden.size * 2 * (copies + 1),
        flops=LONG,
    )(hidden, gain[None], after)


def turns(near, frequency, lengths, slots, requests, context):
    groups, rows, depth = near.shape

    def kernel(
        lengths_ref, slots_ref, requests_ref, near_ref, frequency_ref, lined_ref, cosine_ref,
        sine_ref, mask_ref, adapter_ref,
    ):
        for j in range(groups):
            lined_ref[pl.ds(j * rows, rows)] = near_ref[j]
        row = lax.broadcasted_iota(jnp.int32, (rows, LANES), 0)
        length = jnp.zeros((rows, LANES), jnp.int32)
        adapter = jnp.zeros((rows, LANES), jnp.int32)
        for r in range(rows):
            length = jnp.where(row == r, lengths_ref[r], length)
            adapter = jnp.where(row == r, requests_ref[0, slots_ref[r]], adapter)
        angle = length.astype(jnp.float32) * frequency_ref[...]
        cosine_ref[...] = jnp.cos(angle)
        sine_ref[...] = jnp.sin(angle)
        lane = lax.broadcasted_iota(jnp.int32, (rows, LANES), 1)
        for t in range(0, context, LANES):
            mask_ref[:, pl.ds(t, LANES)] = jnp.where(lane + t < length, 0.0, -jnp.inf)
        adapter_ref[...] = adapter.astype(jnp.float32).astype(jnp.bfloat16)

    return call(
        kernel,
        "turns",
        (
            jax.ShapeDtypeStruct((groups * rows, depth), near.dtype),
            jax.ShapeDtypeStruct((rows, HEAD_DIM), jnp.float32),
            jax.ShapeDtypeStruct((rows, HEAD_DIM), jnp.float32),
            jax.ShapeDtypeStruct((rows, context), jnp.float32),
            jax.ShapeDtypeStruct((rows, LANES), jnp.bfloat16),
        ),
        [SMEM] * 3 + [VMEM] * 2,
        near.size * 4,
    )(lengths, slots, requests, near, frequency)


def column_parts(columns):
    return [slice(c, min(c + 2 * LANES, columns)) for c in range(0, columns, 2 * LANES)]


def halves_product(rows, weight_ref, part, cut):
    return jnp.concatenate(
        [
            jnp.dot(rows, weight_ref[part, :cut], preferred_element_type=jnp.float32),
            jnp.dot(rows, weight_ref[part, cut:], preferred_element_type=jnp.float32),
        ],
        1,
    )


def project_qkv(lined, far, weight, adapter, chunk=2048):
    groups, rows, _ = far.shape
    depth, width = weight.shape
    half = groups * rows

    def kernel(lined_ref, far_ref, weight_ref, adapter_ref, out_ref, far_lined_ref):
        total = jnp.zeros((2 * half, width), jnp.float32)
        for k in range(depth // chunk):
            part = pl.ds(k * chunk, chunk)
            for j in range(groups):
                far_lined_ref[pl.ds(j * rows, rows), part] = far_ref[j, :, part]
            lined = jnp.concatenate([lined_ref[:, part], far_lined_ref[:, part]])
            total = total + halves_product(lined, weight_ref, part, 3 * LANES)
        core = lax.axis_index("batch")
        adapter = adapter_ref[...]
        for e in range(2):
            for j in range(groups):
                place = e * half + j * rows
                device = 2 * j + (core ^ e ^ 1)
                out_ref[device, :, pl.ds(0, width)] = total[place : place + rows].astype(
                    jnp.bfloat16
                )
                out_ref[device, :, pl.ds(width, LANES)] = (
                    adapter if e == 0 else jnp.zeros_like(adapter)
                )

    return call(
        kernel,
        "project_qkv",
        jax.ShapeDtypeStruct((2 * groups, rows, width + LANES), jnp.bfloat16),
        [VMEM] * 4,
        weight.size * 2,
        flops=LONG,
        scratch_shapes=[pltpu.VMEM((half, depth), jnp.bfloat16)],
    )(lined, far, weight, adapter)


def project_out(gathered, adapter, weight, down_store, up_store):
    groups, rows, features = gathered.shape
    count = groups * rows
    rank, depth = down_store.shape[1:]
    columns = weight.shape[1]

    def kernel(
        adapter_ref, gathered_ref, weight_ref, down_ref, up_ref, partial_ref, base_ref, picked_ref,
        rows_ref, held_ref,
    ):
        for j in range(groups):
            rows_ref[pl.ds(j * rows, rows)] = gathered_ref[j]
        parts = column_parts(columns)
        for k, part in enumerate(parts):
            cut = features // 2
            base_ref[:, part] = jnp.dot(
                rows_ref[:, :cut], weight_ref[:cut, part], preferred_element_type=jnp.float32
            ) + jnp.dot(
                rows_ref[:, cut:], weight_ref[cut:, part], preferred_element_type=jnp.float32
            )
            for r in range(k * count // len(parts), (k + 1) * count // len(parts)):
                chosen = adapter_ref[0, r]
                held_ref[pl.ds(r * rank, rank)] = down_ref[chosen]
                picked_ref[pl.ds(r * rank, rank)] = up_ref[chosen]
        start = pl.multiple_of(lax.axis_index("mp") * depth, depth)
        every = lax.dot_general(
            rows_ref[:, pl.ds(start, depth)],
            held_ref[...],
            (((1,), (1,)), ((), ())),
            preferred_element_type=jnp.float32,
        )
        row = lax.broadcasted_iota(jnp.int32, (count, LANES), 0)
        lane = lax.broadcasted_iota(jnp.int32, (count, LANES), 1)
        total = jnp.zeros((count, LANES), jnp.float32)
        for s in range(0, count * rank, LANES):
            total = total + jnp.where(row == (lane + s) // rank, every[:, s : s + LANES], 0.0)
        for c in range(groups):
            partial_ref[c] = total

    return call(
        kernel,
        "project_out",
        (
            jax.ShapeDtypeStruct((groups, count, LANES), jnp.float32),
            jax.ShapeDtypeStruct((count, columns), jnp.float32),
            pltpu.VMEM((count * rank, columns), up_store.dtype),
        ),
        [SMEM] + [VMEM] * 4,
        weight.size * 2,
        limit=5 * MIB,
        flops=LONG,
        scratch_shapes=[
            pltpu.VMEM((count, features), gathered.dtype),
            pltpu.VMEM((count * rank, depth), down_store.dtype),
        ],
    )(adapter, gathered, weight, down_store, up_store)


def add_up(base, partials, up):
    groups, count, _ = partials.shape
    depth, width = up.shape
    rank = depth // count

    def kernel(base_ref, partials_ref, up_ref, out_ref):
        total = partials_ref[0]
        for c in range(1, groups):
            total = total + partials_ref[c]
        down = total.astype(jnp.bfloat16).astype(jnp.float32)
        row = lax.broadcasted_iota(jnp.int32, (count, LANES), 0)
        lane = lax.broadcasted_iota(jnp.int32, (count, LANES), 1)
        spread = []
        for s in range(0, depth, LANES):
            spread.append(jnp.where(row == (lane + s) // rank, down, 0.0))
        spread = jnp.concatenate(spread, 1).astype(jnp.bfloat16)
        delta = jnp.dot(spread, up_ref[...], preferred_element_type=jnp.float32)
        result = (base_ref[...] + ADAPTER_SCALE * delta).astype(jnp.bfloat16)
        for j in range(groups):
            out_ref[j] = result[j * count // groups : (j + 1) * count // groups]

    return call(
        kernel,
        "add_up",
        jax.ShapeDtypeStruct((groups, count // groups, width), jnp.bfloat16),
        [VMEM] * 3,
        up.size * 2,
        limit=4 * MIB,
        flops=2 * count * up.size,
    )(base, partials, up)


def add_rows(hidden, parts):
    width = parts.shape[2]

    def kernel(hidden_ref, parts_ref, out_ref):
        for k, place in enumerate(order(parts.shape[0])):
            part = pl.ds(place * width, width)
            total = hidden_ref[:, part].astype(jnp.float32) + parts_ref[k].astype(jnp.float32)
            out_ref[:, part] = total.astype(jnp.bfloat16)

    return call(
        kernel,
        "add_rows",
        jax.ShapeDtypeStruct(hidden.shape, parts.dtype),
        [VMEM, VMEM],
        hidden.size * 6,
    )(hidden, parts)


def swap_cores(block):
    return lax.ppermute(block, "batch", [(0, 1), (1, 0)])


def order(size):
    half = size // 2
    return [(k + 1) % half + start for k in range(half) for start in (half, 0)]


def exchange(blocks):
    group = order(lax.axis_size("mp"))
    return lax.all_to_all(
        blocks, "mp", split_axis=0, concat_axis=0, tiled=True, axis_index_groups=[group]
    )


def exchange_all(blocks):
    group = [2 * j + core for j in order(lax.axis_size("mp")) for core in (1, 0)]
    return lax.all_to_all(
        blocks,
        ("mp", "batch"),
        split_axis=0,
        concat_axis=0,
        tiled=True,
        axis_index_groups=[group],
    )


def attend(mixed, cosine, sine, mask, key_cache, value_cache, copies):
    rows, context = key_cache.shape[:2]
    group = HEADS // KV_HEADS
    heads = HEADS + 2 * KV_HEADS
    width = mixed.shape[2] - LANES
    per_device = width // HEAD_DIM
    devices = order(mixed.shape[0] // 2)

    def kernel(
        mixed_ref, cosine_ref, sine_ref, mask_ref, key_ref, value_ref, out_ref, adapter_ref,
        vec_ref, context_ref,
    ):
        place = lax.broadcasted_iota(jnp.int32, (1, LANES), 1)
        adapter = jnp.zeros((1, LANES), jnp.float32)
        for k, j in enumerate(devices):
            for core in range(2):
                block = mixed_ref[2 * k + 1 - core].astype(jnp.float32)
                for c in range(per_device):
                    head = (2 * j + core) * per_device + c
                    vec_ref[pl.ds(head * rows, rows)] = block[:, c * HEAD_DIM : (c + 1) * HEAD_DIM]
            both = mixed_ref[2 * k, :, pl.ds(width, LANES)].astype(jnp.float32)
            both = both + mixed_ref[2 * k + 1, :, pl.ds(width, LANES)].astype(jnp.float32)
            for r in range(rows):
                adapter = jnp.where(place == k * rows + r, both[r : r + 1], adapter)
        adapter_ref[...] = adapter.astype(jnp.int32)

        def tiled(pair, count):
            return jnp.concatenate([pair] * count)

        keyed = (HEADS + KV_HEADS) * rows
        vec = vec_ref[pl.ds(0, keyed)]
        turned = pltpu.roll(vec, HEAD_DIM // 2, 1)
        lane = lax.broadcasted_iota(jnp.int32, (rows, HEAD_DIM), 1)
        signed = jnp.where(lane < HEAD_DIM // 2, -sine_ref[...], sine_ref[...])
        pairs = keyed // rows
        vec = vec * tiled(cosine_ref[...], pairs) + turned * tiled(signed, pairs)
        vec = vec.astype(jnp.bfloat16)
        query = vec[: HEADS * rows]
        fresh_key = vec[HEADS * rows :].astype(jnp.float32)
        fresh_value = vec_ref[pl.ds(keyed, KV_HEADS * rows)]
        size = group * rows
        owner = lax.broadcasted_iota(jnp.int32, (size, 1), 0) % rows

        def of_owner(products):
            result = products[0]
            for r in range(1, rows):
                result = jnp.where(owner == r, products[r], result)
            return result

        scores, own_key, own_value = [], [], []
        for g in range(KV_HEADS):
            lanes = pl.ds(g * HEAD_DIM, HEAD_DIM)
            part = query[g * size : (g + 1) * size]
            products = [
                lax.dot_general(
                    part,
                    key_ref[r, :, lanes],
                    (((1,), (1,)), ((), ())),
                    preferred_element_type=jnp.float32,
                )
                for r in range(rows)
            ]
            scores.append(of_owner(products))
            own_key.append(tiled(fresh_key[g * rows : (g + 1) * rows], group))
            own_value.append(tiled(fresh_value[g * rows : (g + 1) * rows], group))
        scale = HEAD_DIM ** (-0.5)
        scores = jnp.concatenate(scores) * scale + tiled(mask_ref[...], HEADS)
        own = jnp.sum(query.astype(jnp.float32) * jnp.concatenate(own_key), 1, keepdims=True)
        own = own * scale
        top = jnp.maximum(jnp.max(scores, 1, keepdims=True), own)
        expo = jnp.exp(scores - top)
        own_exp = jnp.exp(own - top)
        total = jnp.sum(expo, 1, keepdims=True) + own_exp
        probs = (expo / total).astype(jnp.bfloat16)
        own_prob = (own_exp / total).astype(jnp.bfloat16).astype(jnp.float32)
        for g in range(KV_HEADS):
            lanes = pl.ds(g * HEAD_DIM, HEAD_DIM)
            part = probs[g * size : (g + 1) * size]
            products = [
                jnp.dot(part, value_ref[r, :, lanes], preferred_element_type=jnp.float32)
                for r in range(rows)
            ]
            result = of_owner(products) + own_prob[g * size : (g + 1) * size] * own_value[g]
            for h in range(group):
                place = pl.ds((g * group + h) * HEAD_DIM, HEAD_DIM)
                context_ref[:, place] = result[h * rows : (h + 1) * rows]
        rounded = context_ref[...].astype(jnp.bfloat16)
        for c in range(copies):
            out_ref[c] = rounded

    return call(
        kernel,
        "attend",
        (
            jax.ShapeDtypeStruct((copies, rows, HEADS * HEAD_DIM), jnp.bfloat16),
            jax.ShapeDtypeStruct((1, LANES), jnp.int32),
        ),
        [VMEM] * 6,
        key_cache.size * 4,
        limit=4 * MIB,
        flops=LONG,
        scratch_shapes=[
            pltpu.VMEM((heads * rows, HEAD_DIM), jnp.float32),
            pltpu.VMEM((rows, HEADS * HEAD_DIM), jnp.float32),
        ],
    )(mixed, cosine, sine, mask, key_cache, value_cache)


def fast_body(
    hidden,
    attention_norm_gain,
    query_key_value_weight,
    output_weight,
    key_cache,
    value_cache,
    lengths,
    slots,
    requests,
    adapter_down_matrices,
    adapter_up_matrices,
):
    mp_size = lax.axis_size("mp")
    frequency = frequencies(exponents())
    near = exchange(norm_rows(hidden, attention_norm_gain, frequency, mp_size))
    lined, cosine, sine, mask, adapter = turns(
        near, frequency, lengths, slots, requests, key_cache.shape[1]
    )
    columns = project_qkv(lined, swap_cores(near), query_key_value_weight, adapter)
    mixed = exchange_all(columns)
    context, adapter = attend(mixed, cosine, sine, mask, key_cache, value_cache, mp_size)
    gathered = exchange(context)

    partials, base, up = project_out(
        gathered,
        adapter,
        output_weight,
        adapter_down_matrices.swapaxes(1, 2),
        adapter_up_matrices,
    )
    projected = add_up(base, exchange(partials), up)
    return add_rows(hidden, exchange(projected))


def body(*arguments):
    small = lax.axis_size("mp") <= 16 and lax.axis_size("batch") == 2
    whole_heads = arguments[2].shape[1] % HEAD_DIM == 0
    return (fast_body if small and whole_heads else general_body)(*arguments)


def solution(mesh):
    in_specs = (
        P(("groups", "mp", "batch"), None),
        P(),
        P(None, ("mp", "batch")),
        P(None, "mp"),
        P(("groups", "mp", "batch"), None, None),
        P(("groups", "mp", "batch"), None, None),
        P(("groups", "mp", "batch")),
        P(("groups", "mp", "batch")),
        P(("groups", "mp", "batch"), None),
        P(None, "mp", None),
        P(None, None, "mp"),
    )
    out_specs = P(("groups", "mp", "batch"), None)
    return jax.shard_map(body, mesh=mesh, in_specs=in_specs, out_specs=out_specs, check_vma=False)
```

```python
import math

import jax
import jax.numpy as jnp
from jax import lax
from jax.experimental import pallas as pl
from jax.experimental.pallas import tpu as pltpu
from jax.sharding import PartitionSpec as P

HEADS = 64
KV_HEADS = 8
HEAD_DIM = 128
ADAPTER_COUNT = 64


EPS = 1e-05
THETA = 500000.0
ADAPTER_SCALE = 2.0


def rotate(vec, pos):
    width = vec.shape[-1]
    half = width // 2
    freq = THETA ** (-(jnp.arange(half, dtype=jnp.float32) * 2.0) / width)
    angle = pos[..., None, None] * freq
    cosine = jnp.concatenate([jnp.cos(angle), jnp.cos(angle)], -1)
    sine = jnp.concatenate([jnp.sin(angle), jnp.sin(angle)], -1)
    turned = jnp.concatenate([-vec[..., half:], vec[..., :half]], -1)
    return vec * cosine + turned * sine


def apply_up_matrix(
    context_vector, adapter_selector, down_result, output_weight, adapter_up_matrices
):
    base_output = jnp.dot(context_vector, output_weight, preferred_element_type=jnp.float32)
    spread = (adapter_selector[:, :, None] * down_result[:, None, :]).reshape(
        adapter_selector.shape[0], -1
    )
    adapter_table = adapter_up_matrices.reshape(-1, adapter_up_matrices.shape[2])
    adapter_delta = jnp.dot(spread, adapter_table, preferred_element_type=jnp.float32)
    return (base_output + ADAPTER_SCALE * adapter_delta).astype(jnp.bfloat16)


def general_body(
    hidden,
    attention_norm_gain,
    query_key_value_weight,
    output_weight,
    key_cache,
    value_cache,
    lengths,
    slots,
    requests,
    adapter_down_matrices,
    adapter_up_matrices,
):
    widened = hidden.astype(jnp.float32)
    normed = (
        widened
        * lax.rsqrt(jnp.mean(widened * widened, -1, keepdims=True) + EPS)
        * attention_norm_gain.astype(jnp.float32)
    ).astype(jnp.bfloat16)
    rows = normed.shape[0]
    columns = jnp.dot(
        lax.all_gather(normed, ("mp", "batch"), axis=0, tiled=True),
        query_key_value_weight,
        preferred_element_type=jnp.float32,
    ).astype(jnp.bfloat16)
    mixed = lax.all_to_all(
        lax.all_to_all(columns, "mp", split_axis=0, concat_axis=1, tiled=True),
        "batch",
        split_axis=0,
        concat_axis=1,
        tiled=True,
    )
    width = query_key_value_weight.shape[1]
    qkv = (
        mixed.reshape(rows, lax.axis_size("batch"), lax.axis_size("mp"), width)
        .transpose(0, 2, 1, 3)
        .reshape(rows, -1)
    )
    query_width = HEADS * HEAD_DIM
    kv_width = KV_HEADS * HEAD_DIM
    group = HEADS // KV_HEADS
    scale = HEAD_DIM ** (-0.5)
    pos = lengths.astype(jnp.float32)
    query = rotate(
        qkv[:, :query_width].astype(jnp.float32).reshape(rows, HEADS, HEAD_DIM), pos
    ).astype(jnp.bfloat16)
    fresh_key = rotate(
        qkv[:, query_width : query_width + kv_width]
        .astype(jnp.float32)
        .reshape(rows, KV_HEADS, HEAD_DIM),
        pos,
    ).astype(jnp.bfloat16)
    fresh_value = (
        qkv[:, query_width + kv_width :].astype(jnp.float32).reshape(rows, KV_HEADS, HEAD_DIM)
    )
    grouped = query.reshape(rows, KV_HEADS, group, HEAD_DIM)
    cached = key_cache.reshape(rows, -1, KV_HEADS, HEAD_DIM)
    stored = value_cache.reshape(rows, -1, KV_HEADS, HEAD_DIM)
    scores = (
        jnp.einsum("rgqd,rtgd->rgqt", grouped, cached, preferred_element_type=jnp.float32) * scale
    )
    live = jnp.arange(cached.shape[1])[None, :] < lengths[:, None]
    scores = jnp.where(live[:, None, None, :], scores, -jnp.inf)
    own = (
        jnp.einsum("rgqd,rgd->rgq", grouped, fresh_key, preferred_element_type=jnp.float32) * scale
    )
    top = jnp.maximum(jnp.max(scores, -1), own)
    expo = jnp.exp(scores - top[..., None])
    own_exp = jnp.exp(own - top)
    total = jnp.sum(expo, -1) + own_exp
    probs = (expo / total[..., None]).astype(jnp.bfloat16)
    own_prob = (own_exp / total).astype(jnp.bfloat16)
    context_vector = jnp.einsum(
        "rgqt,rtgd->rgqd", probs, stored, preferred_element_type=jnp.float32
    )
    context_vector = (
        context_vector + own_prob.astype(jnp.float32)[..., None] * fresh_value[:, :, None, :]
    )
    context_vector = context_vector.reshape(rows, query_width).astype(jnp.bfloat16)
    slot_hits = slots[:, None] == jnp.arange(requests.shape[1])[None, :]
    adapter = jnp.sum(jnp.where(slot_hits, requests[0][None, :], 0), 1)
    adapter_selector = (adapter[:, None] == jnp.arange(ADAPTER_COUNT)[None, :]).astype(jnp.bfloat16)
    context_gathered, selector_gathered = (
        lax.all_gather(context_vector, "mp", axis=0, tiled=True),
        lax.all_gather(adapter_selector, "mp", axis=0, tiled=True),
    )
    shared_portion = adapter_down_matrices.shape[1]
    context_slice = lax.dynamic_slice_in_dim(
        context_gathered, lax.axis_index("mp") * shared_portion, shared_portion, 1
    )
    every_adapter = jnp.einsum(
        "gh,thy->gty", context_slice, adapter_down_matrices, preferred_element_type=jnp.float32
    )
    partial_down = jnp.sum(every_adapter * selector_gathered.astype(jnp.float32)[:, :, None], 1)
    down_gathered = lax.psum(partial_down, "mp").astype(jnp.bfloat16)
    projection_result = apply_up_matrix(
        context_gathered, selector_gathered, down_gathered, output_weight, adapter_up_matrices
    )
    returned = lax.all_to_all(projection_result, "mp", split_axis=0, concat_axis=1, tiled=True)
    return (widened + returned.astype(jnp.float32)).astype(jnp.bfloat16)


MIB = 1 << 20
LANES = 128
LONG = 10**10
VMEM = pl.BlockSpec(memory_space=pltpu.VMEM)
SMEM = pl.BlockSpec(memory_space=pltpu.SMEM)
ANY = pl.BlockSpec(memory_space=pl.ANY)


def call(kernel, name, out_shape, in_specs, moved, limit=2 * MIB, flops=0, **options):
    return pl.pallas_call(
        kernel,
        out_shape=out_shape,
        in_specs=in_specs,
        out_specs=jax.tree.map(lambda _: VMEM, out_shape),
        compiler_params=pltpu.CompilerParams(vmem_limit_bytes=limit),
        cost_estimate=pl.CostEstimate(flops=flops, bytes_accessed=moved, transcendentals=0),
        name=name,
        **options,
    )


def exponents():
    def kernel(out_ref):
        lane = lax.broadcasted_iota(jnp.int32, (1, HEAD_DIM), 1)
        out_ref[...] = (lane % (HEAD_DIM // 2)).astype(jnp.float32) * (-2.0 / HEAD_DIM)

    shape = jax.ShapeDtypeStruct((1, HEAD_DIM), jnp.float32)
    return call(kernel, "exponents", shape, [], 0, flops=LONG // 8)()


def frequencies(exponent):
    def kernel(exponent_ref, out_ref):
        out_ref[...] = jnp.exp(exponent_ref[...] * math.log(THETA))

    shape = jax.ShapeDtypeStruct(exponent.shape, jnp.float32)
    return call(kernel, "frequencies", shape, [VMEM], 0, flops=LONG // 8)(exponent)


def norm_rows(hidden, gain, after, copies):
    rows, width = hidden.shape

    def kernel(hidden_ref, gain_ref, after_ref, out_ref):
        del after_ref
        wide = hidden_ref[...].astype(jnp.float32)
        inverse = lax.rsqrt(jnp.mean(wide * wide, -1, keepdims=True) + EPS)
        normed = (wide * inverse * gain_ref[...].astype(jnp.float32)).astype(jnp.bfloat16)
        for c in range(copies):
            out_ref[c] = normed

    return call(
        kernel,
        "norm_rows",
        jax.ShapeDtypeStruct((copies, rows, width), jnp.bfloat16),
        [VMEM, VMEM, ANY],
        hidden.size * 2 * (copies + 1),
        flops=LONG,
    )(hidden, gain[None], after)


def turns(near, frequency, lengths, slots, requests, context):
    groups, rows, depth = near.shape

    def kernel(
        lengths_ref, slots_ref, requests_ref, near_ref, frequency_ref, lined_ref, cosine_ref,
        sine_ref, mask_ref, adapter_ref,
    ):
        for j in range(groups):
            lined_ref[pl.ds(j * rows, rows)] = near_ref[j]
        row = lax.broadcasted_iota(jnp.int32, (rows, LANES), 0)
        length = jnp.zeros((rows, LANES), jnp.int32)
        adapter = jnp.zeros((rows, LANES), jnp.int32)
        for r in range(rows):
            length = jnp.where(row == r, lengths_ref[r], length)
            adapter = jnp.where(row == r, requests_ref[0, slots_ref[r]], adapter)
        angle = length.astype(jnp.float32) * frequency_ref[...]
        cosine_ref[...] = jnp.cos(angle)
        sine_ref[...] = jnp.sin(angle)
        lane = lax.broadcasted_iota(jnp.int32, (rows, LANES), 1)
        for t in range(0, context, LANES):
            mask_ref[:, pl.ds(t, LANES)] = jnp.where(lane + t < length, 0.0, -jnp.inf)
        adapter_ref[...] = adapter.astype(jnp.float32).astype(jnp.bfloat16)

    return call(
        kernel,
        "turns",
        (
            jax.ShapeDtypeStruct((groups * rows, depth), near.dtype),
            jax.ShapeDtypeStruct((rows, HEAD_DIM), jnp.float32),
            jax.ShapeDtypeStruct((rows, HEAD_DIM), jnp.float32),
            jax.ShapeDtypeStruct((rows, context), jnp.float32),
            jax.ShapeDtypeStruct((rows, LANES), jnp.bfloat16),
        ),
        [SMEM] * 3 + [VMEM] * 2,
        near.size * 4,
    )(lengths, slots, requests, near, frequency)


def column_parts(columns):
    return [slice(c, min(c + 2 * LANES, columns)) for c in range(0, columns, 2 * LANES)]


def project_qkv(lined, far, weight, adapter):
    groups, rows, _ = far.shape
    depth, width = weight.shape
    half = groups * rows

    def kernel(lined_ref, far_ref, weight_ref, adapter_ref, out_ref, far_lined_ref):
        for j in range(groups):
            far_lined_ref[pl.ds(j * rows, rows)] = far_ref[j]
        lined = jnp.concatenate([lined_ref[...], far_lined_ref[...]])
        total = jnp.concatenate(
            [
                jnp.dot(lined, weight_ref[:, part], preferred_element_type=jnp.float32)
                for part in column_parts(width)
            ],
            1,
        )
        core = lax.axis_index("batch")
        adapter = adapter_ref[...]
        for e in range(2):
            for j in range(groups):
                place = e * half + j * rows
                device = 2 * j + (core ^ e ^ 1)
                out_ref[device, :, pl.ds(0, width)] = total[place : place + rows].astype(
                    jnp.bfloat16
                )
                out_ref[device, :, pl.ds(width, LANES)] = (
                    adapter if e == 0 else jnp.zeros_like(adapter)
                )

    return call(
        kernel,
        "project_qkv",
        jax.ShapeDtypeStruct((2 * groups, rows, width + LANES), jnp.bfloat16),
        [VMEM] * 4,
        weight.size * 2,
        flops=LONG,
        scratch_shapes=[pltpu.VMEM((half, depth), jnp.bfloat16)],
    )(lined, far, weight, adapter)


def project_out(gathered, adapter, weight, down_store, up_store):
    groups, rows, features = gathered.shape
    count = groups * rows
    rank, depth = down_store.shape[1:]
    columns = weight.shape[1]

    def kernel(
        adapter_ref, gathered_ref, weight_ref, down_ref, up_ref, partial_ref, base_ref, picked_ref,
        rows_ref, held_ref,
    ):
        for j in range(groups):
            rows_ref[pl.ds(j * rows, rows)] = gathered_ref[j]
        parts = column_parts(columns)
        for k, part in enumerate(parts):
            base_ref[:, part] = jnp.dot(
                rows_ref[...], weight_ref[:, part], preferred_element_type=jnp.float32
            )
            for r in range(k * count // len(parts), (k + 1) * count // len(parts)):
                chosen = adapter_ref[0, r]
                held_ref[pl.ds(r * rank, rank)] = down_ref[chosen]
                picked_ref[pl.ds(r * rank, rank)] = up_ref[chosen]
        start = pl.multiple_of(lax.axis_index("mp") * depth, depth)
        every = lax.dot_general(
            rows_ref[:, pl.ds(start, depth)],
            held_ref[...],
            (((1,), (1,)), ((), ())),
            preferred_element_type=jnp.float32,
        )
        row = lax.broadcasted_iota(jnp.int32, (count, LANES), 0)
        lane = lax.broadcasted_iota(jnp.int32, (count, LANES), 1)
        total = jnp.zeros((count, LANES), jnp.float32)
        for s in range(0, count * rank, LANES):
            total = total + jnp.where(row == (lane + s) // rank, every[:, s : s + LANES], 0.0)
        for c in range(groups):
            partial_ref[c] = total

    return call(
        kernel,
        "project_out",
        (
            jax.ShapeDtypeStruct((groups, count, LANES), jnp.float32),
            jax.ShapeDtypeStruct((count, columns), jnp.float32),
            pltpu.VMEM((count * rank, columns), up_store.dtype),
        ),
        [SMEM] + [VMEM] * 4,
        weight.size * 2,
        limit=5 * MIB,
        flops=LONG,
        scratch_shapes=[
            pltpu.VMEM((count, features), gathered.dtype),
            pltpu.VMEM((count * rank, depth), down_store.dtype),
        ],
    )(adapter, gathered, weight, down_store, up_store)


def add_up(base, partials, up):
    groups, count, _ = partials.shape
    depth, width = up.shape
    rank = depth // count

    def kernel(base_ref, partials_ref, up_ref, out_ref):
        total = partials_ref[0]
        for c in range(1, groups):
            total = total + partials_ref[c]
        down = total.astype(jnp.bfloat16).astype(jnp.float32)
        row = lax.broadcasted_iota(jnp.int32, (count, LANES), 0)
        lane = lax.broadcasted_iota(jnp.int32, (count, LANES), 1)
        spread = []
        for s in range(0, depth, LANES):
            spread.append(jnp.where(row == (lane + s) // rank, down, 0.0))
        spread = jnp.concatenate(spread, 1).astype(jnp.bfloat16)
        delta = jnp.dot(spread, up_ref[...], preferred_element_type=jnp.float32)
        result = (base_ref[...] + ADAPTER_SCALE * delta).astype(jnp.bfloat16)
        for j in range(groups):
            out_ref[j] = result[j * count // groups : (j + 1) * count // groups]

    return call(
        kernel,
        "add_up",
        jax.ShapeDtypeStruct((groups, count // groups, width), jnp.bfloat16),
        [VMEM] * 3,
        up.size * 2,
        limit=4 * MIB,
        flops=2 * count * up.size,
    )(base, partials, up)


def add_rows(hidden, parts):
    width = parts.shape[2]

    def kernel(hidden_ref, parts_ref, out_ref):
        for k, place in enumerate(order(parts.shape[0])):
            part = pl.ds(place * width, width)
            total = hidden_ref[:, part].astype(jnp.float32) + parts_ref[k].astype(jnp.float32)
            out_ref[:, part] = total.astype(jnp.bfloat16)

    return call(
        kernel,
        "add_rows",
        jax.ShapeDtypeStruct(hidden.shape, parts.dtype),
        [VMEM, VMEM],
        hidden.size * 6,
    )(hidden, parts)


def swap_cores(block):
    return lax.ppermute(block, "batch", [(0, 1), (1, 0)])


def order(size):
    half = size // 2
    return [(k - 1) % half + start for k in range(half) for start in (0, half)]


def exchange(blocks):
    group = order(lax.axis_size("mp"))
    return lax.all_to_all(
        blocks, "mp", split_axis=0, concat_axis=0, tiled=True, axis_index_groups=[group]
    )


def exchange_all(blocks):
    group = [2 * j + core for j in order(lax.axis_size("mp")) for core in (1, 0)]
    return lax.all_to_all(
        blocks,
        ("mp", "batch"),
        split_axis=0,
        concat_axis=0,
        tiled=True,
        axis_index_groups=[group],
    )


def attend(mixed, cosine, sine, mask, key_cache, value_cache, copies):
    rows, context = key_cache.shape[:2]
    group = HEADS // KV_HEADS
    heads = HEADS + 2 * KV_HEADS
    width = mixed.shape[2] - LANES
    per_device = width // HEAD_DIM
    devices = order(mixed.shape[0] // 2)

    def kernel(
        mixed_ref, cosine_ref, sine_ref, mask_ref, key_ref, value_ref, out_ref, adapter_ref,
        vec_ref, context_ref,
    ):
        place = lax.broadcasted_iota(jnp.int32, (1, LANES), 1)
        adapter = jnp.zeros((1, LANES), jnp.float32)
        for k, j in enumerate(devices):
            for core in range(2):
                block = mixed_ref[2 * k + 1 - core].astype(jnp.float32)
                for c in range(per_device):
                    head = (2 * j + core) * per_device + c
                    vec_ref[pl.ds(head * rows, rows)] = block[:, c * HEAD_DIM : (c + 1) * HEAD_DIM]
            both = mixed_ref[2 * k, :, pl.ds(width, LANES)].astype(jnp.float32)
            both = both + mixed_ref[2 * k + 1, :, pl.ds(width, LANES)].astype(jnp.float32)
            for r in range(rows):
                adapter = jnp.where(place == k * rows + r, both[r : r + 1], adapter)
        adapter_ref[...] = adapter.astype(jnp.int32)

        def tiled(pair, count):
            return jnp.concatenate([pair] * count)

        keyed = (HEADS + KV_HEADS) * rows
        vec = vec_ref[pl.ds(0, keyed)]
        turned = pltpu.roll(vec, HEAD_DIM // 2, 1)
        lane = lax.broadcasted_iota(jnp.int32, (rows, HEAD_DIM), 1)
        signed = jnp.where(lane < HEAD_DIM // 2, -sine_ref[...], sine_ref[...])
        pairs = keyed // rows
        vec = vec * tiled(cosine_ref[...], pairs) + turned * tiled(signed, pairs)
        vec = vec.astype(jnp.bfloat16)
        query = vec[: HEADS * rows]
        fresh_key = vec[HEADS * rows :].astype(jnp.float32)
        fresh_value = vec_ref[pl.ds(keyed, KV_HEADS * rows)]
        size = group * rows
        owner = lax.broadcasted_iota(jnp.int32, (size, 1), 0) % rows

        def of_owner(products):
            result = products[0]
            for r in range(1, rows):
                result = jnp.where(owner == r, products[r], result)
            return result

        scores, own_key, own_value = [], [], []
        for g in range(KV_HEADS):
            lanes = pl.ds(g * HEAD_DIM, HEAD_DIM)
            part = query[g * size : (g + 1) * size]
            products = [
                lax.dot_general(
                    part,
                    key_ref[r, :, lanes],
                    (((1,), (1,)), ((), ())),
                    preferred_element_type=jnp.float32,
                )
                for r in range(rows)
            ]
            scores.append(of_owner(products))
            own_key.append(tiled(fresh_key[g * rows : (g + 1) * rows], group))
            own_value.append(tiled(fresh_value[g * rows : (g + 1) * rows], group))
        scale = HEAD_DIM ** (-0.5)
        scores = jnp.concatenate(scores) * scale + tiled(mask_ref[...], HEADS)
        own = jnp.sum(query.astype(jnp.float32) * jnp.concatenate(own_key), 1, keepdims=True)
        own = own * scale
        top = jnp.maximum(jnp.max(scores, 1, keepdims=True), own)
        expo = jnp.exp(scores - top)
        own_exp = jnp.exp(own - top)
        total = jnp.sum(expo, 1, keepdims=True) + own_exp
        probs = (expo / total).astype(jnp.bfloat16)
        own_prob = (own_exp / total).astype(jnp.bfloat16).astype(jnp.float32)
        for g in range(KV_HEADS):
            lanes = pl.ds(g * HEAD_DIM, HEAD_DIM)
            part = probs[g * size : (g + 1) * size]
            products = [
                jnp.dot(part, value_ref[r, :, lanes], preferred_element_type=jnp.float32)
                for r in range(rows)
            ]
            result = of_owner(products) + own_prob[g * size : (g + 1) * size] * own_value[g]
            for h in range(group):
                place = pl.ds((g * group + h) * HEAD_DIM, HEAD_DIM)
                context_ref[:, place] = result[h * rows : (h + 1) * rows]
        rounded = context_ref[...].astype(jnp.bfloat16)
        for c in range(copies):
            out_ref[c] = rounded

    return call(
        kernel,
        "attend",
        (
            jax.ShapeDtypeStruct((copies, rows, HEADS * HEAD_DIM), jnp.bfloat16),
            jax.ShapeDtypeStruct((1, LANES), jnp.int32),
        ),
        [VMEM] * 6,
        key_cache.size * 4,
        limit=4 * MIB,
        flops=LONG,
        scratch_shapes=[
            pltpu.VMEM((heads * rows, HEAD_DIM), jnp.float32),
            pltpu.VMEM((rows, HEADS * HEAD_DIM), jnp.float32),
        ],
    )(mixed, cosine, sine, mask, key_cache, value_cache)


def fast_body(
    hidden,
    attention_norm_gain,
    query_key_value_weight,
    output_weight,
    key_cache,
    value_cache,
    lengths,
    slots,
    requests,
    adapter_down_matrices,
    adapter_up_matrices,
):
    mp_size = lax.axis_size("mp")
    frequency = frequencies(exponents())
    near = exchange(norm_rows(hidden, attention_norm_gain, frequency, mp_size))
    lined, cosine, sine, mask, adapter = turns(
        near, frequency, lengths, slots, requests, key_cache.shape[1]
    )
    columns = project_qkv(lined, swap_cores(near), query_key_value_weight, adapter)
    mixed = exchange_all(columns)
    context, adapter = attend(mixed, cosine, sine, mask, key_cache, value_cache, mp_size)
    gathered = exchange(context)

    partials, base, up = project_out(
        gathered,
        adapter,
        output_weight,
        adapter_down_matrices.swapaxes(1, 2),
        adapter_up_matrices,
    )
    projected = add_up(base, exchange(partials), up)
    return add_rows(hidden, exchange(projected))


def body(*arguments):
    small = lax.axis_size("mp") <= 16 and lax.axis_size("batch") == 2
    whole_heads = arguments[2].shape[1] % HEAD_DIM == 0
    return (fast_body if small and whole_heads else general_body)(*arguments)


def solution(mesh):
    in_specs = (
        P(("groups", "mp", "batch"), None),
        P(),
        P(None, ("mp", "batch")),
        P(None, "mp"),
        P(("groups", "mp", "batch"), None, None),
        P(("groups", "mp", "batch"), None, None),
        P(("groups", "mp", "batch")),
        P(("groups", "mp", "batch")),
        P(("groups", "mp", "batch"), None),
        P(None, "mp", None),
        P(None, None, "mp"),
    )
    out_specs = P(("groups", "mp", "batch"), None)
    return jax.shard_map(body, mesh=mesh, in_specs=in_specs, out_specs=out_specs, check_vma=False)
```
